32 devices in a mesh: ctx: 8 (over y, x, core), wsh: 4 (over z).
Axes of the slice: x: 2, y: 2, z: 4, core: 2. Of those that a mesh axis runs over, the one named last changes fastest.
Arguments:
- tokens: bfloat16 [4, 2048, 1280], P('wsh', 'ctx'), may hold values from -6 to 6
- cotangent: bfloat16 [4, 2048, 1280], P('wsh', 'ctx'), may hold values from -6 to 6
- block_lengths: int32 [4, 8], P('wsh'), may hold values from 1 to 512, 2048 in all within a row
- group_order: int32 [8], replicated, may hold values from 0 to 7, each once
- w_query: bfloat16 [1280, 1280], P('wsh'), may hold values from -0.15625 to 0.15625
- w_key: bfloat16 [1280, 1280], P('wsh'), may hold values from -0.15625 to 0.15625
- w_value: bfloat16 [1280, 1280], P('wsh'), may hold values from -0.15625 to 0.15625
- w_out: bfloat16 [1280, 1280], P('wsh'), may hold values from -1 to 1
- w_up: bfloat16 [1280, 1280], P('wsh'), may hold values from -0.15625 to 0.15625
- w_down: bfloat16 [1280, 1280], P('wsh'), may hold values from -0.15625 to 0.15625
- gain_attn: bfloat16 [1280], P('wsh'), may hold values from 0.099609375 to 1.8984375
- gain_mlp: bfloat16 [1280], P('wsh'), may hold values from 0.099609375 to 1.8984375
- query_scale: bfloat16 [80], P('wsh'), may hold values from -3 to 3
Outputs:
- output: bfloat16 [4, 2048, 1280], P('wsh', 'ctx')
- grad_tokens: bfloat16 [4, 2048, 1280], P('wsh', 'ctx')
- grad_w_query: float32 [1280, 1280], P('wsh')
- grad_w_key: float32 [1280, 1280], P('wsh')
- grad_w_value: float32 [1280, 1280], P('wsh')
- grad_w_out: float32 [1280, 1280], P('wsh')
- grad_w_up: float32 [1280, 1280], P('wsh')
- grad_w_down: float32 [1280, 1280], P('wsh')
- grad_gain_attn: float32 [1280], P('wsh')
- grad_gain_mlp: float32 [1280], P('wsh')
- grad_query_scale: float32 [80], P('wsh')
The draws below stay inside these ranges and needn't reach their ends.
Inputs may be any that keep to these rules, and one draw needn't show every extreme that they name: `block_lengths`: each row sums to 2048; its largest entry is exactly 512. `group_order`: A permutation of the stored groups.
All inputs are finite; a program needn't handle non-finite values.
Results may differ from the reference program's by a relative error of at most 0.023.
Values may be sent and summed in bfloat16 or wider, within the bound.
A program may use at most 384 MiB of HBM per device.

```python
import math
import jax
import jax.numpy as jnp
import numpy as np
from jax import lax

D = 1280
H = 16
HD = 80
FF = 1280
TOK_DEV = 256
BLOCK = 256
SEQS = 4
LENGTH = 2048
NBLK = 8
N_CTX = 8


def levels(rng, dims, pieces, low, top_value):
    level = 1.0
    for position, shards_of in pieces:
        steps = jax.random.uniform(jax.random.fold_in(jax.random.fold_in(rng, 6), position), (shards_of,), jnp.float32, low / len(pieces), top_value / len(pieces))
        level = level * jnp.repeat(jnp.exp(steps), dims[position] // shards_of).reshape((-1,) + (1,) * (len(dims) - 1 - position))
    return level


def length_profile(amount, total, bound, slope):
    weights = [(1 << 20) // math.isqrt(rank ** slope) + 1 for rank in range(2, amount + 1)]
    spare, holding = total - bound - (amount - 1), [1] * (amount - 1)
    while spare > 0:
        candidates = [i for i in range(amount - 1) if holding[i] < bound]
        whole, budget = sum([weights[i] for i in candidates]), spare
        for i in candidates:
            more = min(bound - holding[i], max(1, budget * weights[i] // whole), spare)
            holding[i] = holding[i] + more
            spare = spare - more
    return np.array([bound] + holding)


def ragged_sizes(own_key, amount, total, bound, slope):
    if amount == 2:
        one = jax.random.randint(own_key, (), max(1, total - bound), min(bound, total - 1) + 1)
        return jnp.stack([one, total - one])
    tallies = jnp.asarray(length_profile(amount, total, bound, slope), jnp.int32)
    couples = (amount - 1) // 2
    giver, taker = tallies[1:1 + 2 * couples:2], tallies[2:2 + 2 * couples:2]
    margin = jnp.minimum(giver - 1, bound - taker)
    shifted = jax.random.randint(jax.random.fold_in(own_key, 1), (couples,), 0, 1 << 20) % (margin + 1)
    tallies = tallies.at[1:1 + 2 * couples:2].set(giver - shifted).at[2:2 + 2 * couples:2].set(taker + shifted)
    return tallies[jax.random.permutation(jax.random.fold_in(own_key, 2), amount)]


def scatter_about(stream_key, dims, width, reach, split=(), kind=jnp.bfloat16):
    values = jax.random.normal(stream_key, dims, jnp.float32) * width
    if len(split) > 0:
        values = levels(stream_key, dims, split, -0.22, 0.18) * values
    return jnp.clip(values, min=-reach, max=reach).astype(kind)


def setup_inputs(seed: int = 0) -> dict:
    splits = jax.random.split(jax.random.key(seed), 14)
    tokens = scatter_about(splits[0], (SEQS, LENGTH, D), 1.0, 6.0, ((0, 4), (1, 8)))
    cotangent = scatter_about(splits[1], (SEQS, LENGTH, D), 1.0, 6.0, ((0, 4), (1, 8)))
    block_lengths = jax.vmap(lambda own: ragged_sizes(own, NBLK, LENGTH, 2 * BLOCK, 1))(jax.random.split(splits[2], SEQS)).reshape((SEQS, NBLK)).astype(jnp.int32)
    group_order = jax.random.permutation(splits[3], N_CTX).astype(jnp.int32)
    w_query = scatter_about(splits[4], (D, D), D ** -0.5, 0.15625, ((0, 4),))
    w_key = scatter_about(splits[5], (D, D), D ** -0.5, 0.15625, ((0, 4),))
    w_value = scatter_about(splits[6], (D, D), D ** -0.5, 0.15625, ((0, 4),))
    w_out = scatter_about(splits[7], (D, D), (D // 32) ** -0.5, 1.0, ((0, 4),))
    w_up = scatter_about(splits[8], (D, FF), D ** -0.5, 0.15625, ((0, 4),))
    w_down = scatter_about(splits[9], (FF, D), FF ** -0.5, 0.15625, ((0, 4),))
    gain_attn = jnp.clip(1.0 + 0.18 * jax.random.normal(splits[10], (D,), jnp.float32), 0.099609375, 1.8984375).astype(jnp.bfloat16)
    gain_mlp = jnp.clip(1.0 + 0.18 * jax.random.normal(splits[11], (D,), jnp.float32), 0.099609375, 1.8984375).astype(jnp.bfloat16)
    query_scale = scatter_about(splits[12], (HD,), 0.5, 3.0, ((0, 4),))
    return dict(tokens=tokens, cotangent=cotangent, block_lengths=block_lengths, group_order=group_order, w_query=w_query, w_key=w_key, w_value=w_value, w_out=w_out, w_up=w_up, w_down=w_down, gain_attn=gain_attn, gain_mlp=gain_mlp, query_scale=query_scale)


EPS = 1e-06
LOG_BASE = 1.442695041

@jax.custom_vjp
def low(v):
    return lax.optimization_barrier(v.astype(jnp.bfloat16)).astype(jnp.float32)

@jax.custom_vjp
def low_back(v):
    return v

def low_keep(v):
    return (low(v), None)

def low_pass(kept, grad):
    return (grad,)

def back_keep(v):
    return (v, None)

def back_low(kept, grad):
    return (low(grad),)
low.defvjp(low_keep, low_pass)
low_back.defvjp(back_keep, back_low)

def matmul(left, right):
    return jnp.dot(left, right, precision=lax.Precision.HIGHEST, preferred_element_type=jnp.float32)

def rms_norm(values, gain):
    return values * lax.rsqrt(lax.optimization_barrier(jnp.mean(values * values, -1, keepdims=True)) + EPS) * gain

def attention(query3, key3, value3, marks):
    length = query3.shape[0]
    step_rows = 512 if length % 512 == 0 else length
    blocks = length // step_rows

    def one_block(block_parts):
        query_rows, query_marks = block_parts
        scores = low_back(jnp.einsum('qhd,khd->hqk', query_rows, key3, precision=lax.Precision.HIGHEST))
        allowed = marks[None, None, :] <= query_marks[None, :, None]
        chances = jax.nn.softmax(jnp.where(allowed, scores, -jnp.inf), axis=-1)
        return jnp.einsum('hqk,khd->qhd', low(chances), value3, precision=lax.Precision.HIGHEST)
    result = lax.map(jax.checkpoint(one_block), (query3.reshape(blocks, step_rows, H, HD), marks.reshape(blocks, step_rows)))
    return result.reshape(length, H, HD)

def layer(inputs, weight_list, marks):
    w_query, w_key, w_value, w_out, w_up, w_down, gain_attn, gain_mlp, query_scale = weight_list
    length = inputs.shape[0]
    hidden_one = low(rms_norm(inputs, gain_attn))
    query_raw = low_back(matmul(hidden_one, w_query)).reshape(length, H, HD)
    query_gain = LOG_BASE / math.sqrt(HD) * jax.nn.softplus(query_scale)
    query3 = low(query_raw * query_gain)
    key3 = low_back(low(matmul(hidden_one, w_key))).reshape(length, H, HD)
    value3 = low_back(low(matmul(hidden_one, w_value))).reshape(length, H, HD)
    attended = attention(query3, key3, value3, marks).reshape(length, H * HD)
    attended = low_back(low(attended))
    mixed = inputs + low_back(matmul(attended, w_out))
    hidden_two = low(rms_norm(mixed, gain_mlp))
    up_raw = low_back(matmul(hidden_two, w_up))
    active = low(jax.nn.silu(up_raw))
    return mixed + low_back(matmul(active, w_down))

def block_marks(block_lengths, group_order):
    positions = (group_order[:, None] * TOK_DEV + jnp.arange(TOK_DEV, dtype=jnp.int32)[None, :]).reshape(-1)
    bounds = jnp.cumsum(block_lengths, -1)
    return lax.optimization_barrier(jnp.sum((bounds[:, None, :] <= positions[None, :, None]).astype(jnp.int32), -1)).astype(jnp.int32)

def reference(tokens, cotangent, block_lengths, group_order, w_query, w_key, w_value, w_out, w_up, w_down, gain_attn, gain_mlp, query_scale):
    weight_list = tuple((item.astype(jnp.float32) for item in (w_query, w_key, w_value, w_out, w_up, w_down, gain_attn, gain_mlp, query_scale)))
    marks_all = block_marks(block_lengths, group_order)

    def one_sequence(carried, seq_parts):
        seq_inputs, seq_grad, seq_marks = seq_parts
        outputs, pullback = jax.vjp(lambda inputs_f, *weights_f: layer(inputs_f, weights_f, seq_marks), seq_inputs.astype(jnp.float32), *weight_list)
        grads = pullback(seq_grad.astype(jnp.float32))
        summed = tuple((first + second for first, second in zip(carried, grads[1:])))
        return (summed, (outputs.astype(jnp.bfloat16), grads[0].astype(jnp.bfloat16)))
    zero_grads = tuple((jnp.zeros_like(item) for item in weight_list))
    totals, (outputs, grad_inputs) = lax.scan(one_sequence, zero_grads, (tokens, cotangent, marks_all))
    return (outputs, grad_inputs, totals[0], totals[1], totals[2], totals[3], totals[4], totals[5], totals[6], totals[7], totals[8])
```

```python
import functools
import math

import jax
import jax.numpy as jnp
from jax import lax
from jax.experimental import pallas as pl
from jax.experimental.pallas import tpu as pltpu
from jax.sharding import PartitionSpec as P

H = 16


EPS = 1e-06
LOG_BASE = 1.442695041


def row_step():
    return 512


def rows_at(array, block_no, step_rows):
    return lax.dynamic_slice_in_dim(array, block_no * step_rows, step_rows, 0)


def inverse_rms(values):
    return lax.rsqrt(jnp.mean(values * values, -1, keepdims=True) + EPS)


def norm_back(normed, inverse, grad):
    return inverse * (grad - normed * jnp.mean(grad * normed, -1, keepdims=True))


def split_heads(matrix):
    return matrix.reshape(matrix.shape[0], H, -1)


def outer_product(left, right):
    return lax.dot_general(
        left, right, (((0,), (0,)), ((), ())), preferred_element_type=jnp.float32
    )


def back_product(grad, weight):
    return lax.dot_general(
        grad, weight, (((1,), (1,)), ((), ())), preferred_element_type=jnp.float32
    )


def probabilities(query3, key3, query_marks, key_marks, log_totals):
    scores = jnp.einsum("qhd,khd->hqk", query3, key3, preferred_element_type=jnp.float32)
    allowed = key_marks[None, None, :] <= query_marks[None, :, None]
    return jnp.exp(jnp.where(allowed, scores - log_totals[:, :, None], -jnp.inf))


def score_grads(chances, grad_out3, value3, deltas):
    grad_chances = jnp.einsum("qhd,khd->hqk", grad_out3, value3, preferred_element_type=jnp.float32)
    return (chances * (grad_chances - deltas[:, :, None])).astype(jnp.bfloat16)


def per_device(
    tokens,
    cotangent,
    block_lengths,
    group_order,
    w_query,
    w_key,
    w_value,
    w_out,
    w_up,
    w_down,
    gain_attn,
    gain_mlp,
    query_scale,
):
    gathered = (
        lax.all_gather(w_query, "wsh", axis=0, tiled=True),
        lax.all_gather(w_key, "wsh", axis=0, tiled=True),
        lax.all_gather(w_value, "wsh", axis=0, tiled=True),
        lax.all_gather(w_out, "wsh", axis=0, tiled=True),
        lax.all_gather(w_up, "wsh", axis=0, tiled=True),
        lax.all_gather(w_down, "wsh", axis=0, tiled=True),
        lax.all_gather(gain_attn, "wsh", axis=0, tiled=True),
        lax.all_gather(gain_mlp, "wsh", axis=0, tiled=True),
        lax.all_gather(query_scale, "wsh", axis=0, tiled=True),
    )
    (
        full_query,
        full_key,
        full_value,
        full_out,
        full_up,
        full_down,
        norm_attn,
        norm_mlp,
        scale_param,
    ) = gathered
    tok_rows = tokens.shape[1]
    model_width = tokens.shape[2]
    length = tok_rows * lax.axis_size("ctx")
    device = lax.axis_index("ctx")
    head_size = scale_param.shape[0]
    f32 = jnp.float32
    bf16 = jnp.bfloat16
    inputs = tokens.reshape(tok_rows, model_width).astype(f32)
    positions = (
        group_order[:, None] * tok_rows + jnp.arange(tok_rows, dtype=jnp.int32)[None, :]
    ).reshape(length)
    bounds = jnp.cumsum(block_lengths[0])
    block_ids = jnp.sum((bounds[None, :] <= positions[:, None]).astype(jnp.int32), -1)
    query_ids = lax.dynamic_slice_in_dim(block_ids, device * tok_rows, tok_rows, 0)
    inverse_one = inverse_rms(inputs)
    normed_one = inputs * inverse_one
    hidden_one = (normed_one * norm_attn.astype(f32)).astype(bf16)
    query_raw = jnp.dot(hidden_one, full_query, preferred_element_type=f32).reshape(
        tok_rows, H, head_size
    )
    query_gain = LOG_BASE / math.sqrt(head_size) * jax.nn.softplus(scale_param.astype(f32))
    query3 = (query_raw * query_gain).astype(bf16)
    key_flat = jnp.dot(hidden_one, full_key, preferred_element_type=f32).astype(bf16)
    value_flat = jnp.dot(hidden_one, full_value, preferred_element_type=f32).astype(bf16)
    initial = (
        jnp.full((H, tok_rows), -1e30, f32),
        jnp.zeros((H, tok_rows), f32),
        jnp.zeros((tok_rows, H, head_size), f32),
    )
    key_rows = lax.all_gather(key_flat, "ctx", axis=0, tiled=True)
    value_rows = lax.all_gather(value_flat, "ctx", axis=0, tiled=True)
    row_count = key_rows.shape[0]
    step_rows = row_step()

    def one_block(block_no, looped):
        key_part = split_heads(rows_at(key_rows, block_no, step_rows))
        value_part = split_heads(rows_at(value_rows, block_no, step_rows))
        block_marks = rows_at(block_ids, block_no, step_rows)
        maxima, totals, running = looped
        scores = jnp.einsum("qhd,khd->hqk", query3, key_part, preferred_element_type=f32)
        allowed = block_marks[None, None, :] <= query_ids[None, :, None]
        scores = jnp.where(allowed, scores, -jnp.inf)
        raised = jnp.maximum(maxima, jnp.max(scores, -1))
        rescale = jnp.exp(maxima - raised)
        weights = jnp.exp(scores - raised[:, :, None])
        totals = totals * rescale + jnp.sum(weights, -1)
        running = running * rescale.T[:, :, None] + jnp.einsum(
            "hqk,khd->qhd", weights.astype(bf16), value_part, preferred_element_type=f32
        )
        return (raised, totals, running)

    maxima, totals, running = lax.fori_loop(0, row_count // step_rows, one_block, initial)
    log_totals = maxima + jnp.log(totals)
    attended = running / totals.T[:, :, None]
    attended_bf = attended.reshape(tok_rows, model_width).astype(bf16)
    mixed = inputs + jnp.dot(attended_bf, full_out, preferred_element_type=f32)
    inverse_two = inverse_rms(mixed)
    normed_two = mixed * inverse_two
    hidden_two = (normed_two * norm_mlp.astype(f32)).astype(bf16)
    up_raw = jnp.dot(hidden_two, full_up, preferred_element_type=f32)
    active = jax.nn.silu(up_raw).astype(bf16)
    outputs = mixed + jnp.dot(active, full_down, preferred_element_type=f32)
    grad_output = cotangent.reshape(tok_rows, model_width).astype(f32)
    grad_mlp = grad_output.astype(bf16)
    grad_active = back_product(grad_mlp, full_down)
    sigmoid_up = jax.nn.sigmoid(up_raw)
    grad_up_raw = (grad_active * sigmoid_up * (1.0 + up_raw * (1.0 - sigmoid_up))).astype(bf16)
    grad_hidden_two = back_product(grad_up_raw, full_up)
    grad_gain_mlp = jnp.sum(grad_hidden_two * normed_two, 0)
    grad_mixed = grad_output + norm_back(
        normed_two, inverse_two, grad_hidden_two * norm_mlp.astype(f32)
    )
    grad_branch = grad_mixed.astype(bf16)
    grad_att = back_product(grad_branch, full_out).astype(bf16)
    grad_att3 = split_heads(grad_att)
    deltas = jnp.sum(grad_att3.astype(f32) * attended, -1).T
    key_whole, value_whole = (
        lax.all_gather(key_flat, "ctx", axis=0, tiled=True),
        lax.all_gather(value_flat, "ctx", axis=0, tiled=True),
    )
    step_rows = row_step()
    block_total = length // step_rows

    def key_block(grad_q, block_parts):
        key_rows, value_rows, block_marks = block_parts
        key_part = split_heads(key_rows)
        value_part = split_heads(value_rows)
        zero_part = jnp.zeros((key_rows.shape[0], H, head_size), f32)
        chances = probabilities(query3, key_part, query_ids, block_marks, log_totals)
        slopes = score_grads(chances, grad_att3, value_part, deltas)
        new_grad = (grad_q, zero_part, zero_part)[0] + jnp.einsum(
            "hqk,khd->qhd", slopes, key_part, preferred_element_type=f32
        )
        grad_key_part = jnp.einsum("hqk,qhd->khd", slopes, query3, preferred_element_type=f32)
        grad_value_part = jnp.einsum(
            "hqk,qhd->khd", chances.astype(bf16), grad_att3, preferred_element_type=f32
        )
        return (new_grad, (grad_key_part, grad_value_part))

    grad_qs, (key_terms, value_terms) = lax.scan(
        key_block,
        jnp.zeros((tok_rows, H, head_size), f32),
        (
            key_whole.reshape(block_total, step_rows, model_width),
            value_whole.reshape(block_total, step_rows, model_width),
            block_ids.reshape(block_total, step_rows),
        ),
    )
    grad_key, grad_value = (
        lax.psum_scatter(
            key_terms.reshape(length, model_width).astype(jnp.bfloat16),
            "ctx",
            scatter_dimension=0,
            tiled=True,
        ).astype(jnp.float32),
        lax.psum_scatter(
            value_terms.reshape(length, model_width).astype(jnp.bfloat16),
            "ctx",
            scatter_dimension=0,
            tiled=True,
        ).astype(jnp.float32),
    )
    grad_key_bf = grad_key.astype(bf16)
    grad_value_bf = grad_value.astype(bf16)
    grad_query_bf = (grad_qs * query_gain).reshape(tok_rows, model_width).astype(bf16)
    grad_scale_param = (
        jnp.sum(grad_qs * query_raw, (0, 1))
        * (LOG_BASE / math.sqrt(head_size))
        * jax.nn.sigmoid(scale_param.astype(f32))
    )
    grad_hidden_one = (
        back_product(grad_query_bf, full_query)
        + back_product(grad_key_bf, full_key)
        + back_product(grad_value_bf, full_value)
    )
    grad_gain_attn = jnp.sum(grad_hidden_one * normed_one, 0)
    grad_inputs = grad_mixed + norm_back(
        normed_one, inverse_one, grad_hidden_one * norm_attn.astype(f32)
    )
    grad_queryw = outer_product(hidden_one, grad_query_bf)
    grad_keyw = outer_product(hidden_one, grad_key_bf)
    grad_valuew = outer_product(hidden_one, grad_value_bf)
    grad_outw = outer_product(attended_bf, grad_branch)
    grad_upw = outer_product(hidden_two, grad_up_raw)
    grad_downw = outer_product(active, grad_mlp)
    owned = (
        lax.psum_scatter(
            grad_queryw.astype(jnp.bfloat16), "wsh", scatter_dimension=0, tiled=True
        ).astype(jnp.float32),
        lax.psum_scatter(
            grad_keyw.astype(jnp.bfloat16), "wsh", scatter_dimension=0, tiled=True
        ).astype(jnp.float32),
        lax.psum_scatter(
            grad_valuew.astype(jnp.bfloat16), "wsh", scatter_dimension=0, tiled=True
        ).astype(jnp.float32),
        lax.psum_scatter(
            grad_outw.astype(jnp.bfloat16), "wsh", scatter_dimension=0, tiled=True
        ).astype(jnp.float32),
        lax.psum_scatter(
            grad_upw.astype(jnp.bfloat16), "wsh", scatter_dimension=0, tiled=True
        ).astype(jnp.float32),
        lax.psum_scatter(
            grad_downw.astype(jnp.bfloat16), "wsh", scatter_dimension=0, tiled=True
        ).astype(jnp.float32),
        lax.psum_scatter(
            grad_gain_attn.astype(jnp.bfloat16), "wsh", scatter_dimension=0, tiled=True
        ).astype(jnp.float32),
        lax.psum_scatter(
            grad_gain_mlp.astype(jnp.bfloat16), "wsh", scatter_dimension=0, tiled=True
        ).astype(jnp.float32),
        lax.psum_scatter(
            grad_scale_param.astype(jnp.bfloat16), "wsh", scatter_dimension=0, tiled=True
        ).astype(jnp.float32),
    )
    summed = (
        lax.psum(owned[0].astype(jnp.bfloat16), "ctx").astype(jnp.float32),
        lax.psum(owned[1].astype(jnp.bfloat16), "ctx").astype(jnp.float32),
        lax.psum(owned[2].astype(jnp.bfloat16), "ctx").astype(jnp.float32),
        lax.psum(owned[3].astype(jnp.bfloat16), "ctx").astype(jnp.float32),
        lax.psum(owned[4].astype(jnp.bfloat16), "ctx").astype(jnp.float32),
        lax.psum(owned[5].astype(jnp.bfloat16), "ctx").astype(jnp.float32),
        lax.psum(owned[6].astype(jnp.bfloat16), "ctx").astype(jnp.float32),
        lax.psum(owned[7].astype(jnp.bfloat16), "ctx").astype(jnp.float32),
        lax.psum(owned[8].astype(jnp.bfloat16), "ctx").astype(jnp.float32),
    )
    return (
        outputs.reshape(tokens.shape).astype(bf16),
        grad_inputs.reshape(tokens.shape).astype(bf16),
        summed[0],
        summed[1],
        summed[2],
        summed[3],
        summed[4],
        summed[5],
        summed[6],
        summed[7],
        summed[8],
    )


MESH = pl.DeviceIdType.MESH
NEG = -1e30
VMEM_BYTES = 60 * 1024 * 1024


def place():
    c, z = lax.axis_index("ctx"), lax.axis_index("wsh")
    core, x, y = lax.rem(c, 2), lax.rem(c // 2, 2), c // 4
    sib = c + 1 - 2 * core
    over_x, over_y = c + 2 - 4 * x, c + 4 - 8 * y
    first = over_x * (1 - core) + over_y * core
    second = over_y * (1 - core) + over_x * core
    diag = over_x + over_y - c
    return c, z, sib, first, second, diag


def enter(c, z, n_ctx, n_wsh):
    barrier = pltpu.get_barrier_semaphore()
    for k in range(1, n_ctx):
        pl.semaphore_signal(
            barrier, inc=1, device_id=(lax.rem(c + k, n_ctx), z), device_id_type=MESH
        )
    for k in range(1, n_wsh):
        pl.semaphore_signal(
            barrier, inc=1, device_id=(c, lax.rem(z + k, n_wsh)), device_id_type=MESH
        )
    pl.semaphore_wait(barrier, n_ctx + n_wsh - 2)


def send(src, dst, send_sem, recv_sem, c, z):
    copy = pltpu.make_async_remote_copy(
        src_ref=src, dst_ref=dst, send_sem=send_sem, recv_sem=recv_sem,
        device_id=(c, z), device_id_type=MESH,
    )
    copy.start()
    return copy


def arrive(dst, send_sem, recv_sem, c, z):
    pltpu.make_async_remote_copy(
        src_ref=dst, dst_ref=dst, send_sem=send_sem, recv_sem=recv_sem,
        device_id=(c, z), device_id_type=MESH,
    ).wait_recv()


def left(src, send_sem, recv_sem, c, z):
    pltpu.make_async_remote_copy(
        src_ref=src, dst_ref=src, send_sem=send_sem, recv_sem=recv_sem,
        device_id=(c, z), device_id_type=MESH,
    ).wait_send()


class Line:
    def __init__(self, at, c, z, n, send_sem, recv_sem):
        self.at, self.c, self.z, self.n = at, c, z, n
        self.send_sem, self.recv_sem = send_sem, recv_sem

    def start(self, own):
        c, z = self.c, self.z

        @pl.when(z < self.n - 1)
        def _():
            send(own, self.at(z), self.send_sem.at[0], self.recv_sem.at[z], c, z + 1)

        @pl.when(z > 0)
        def _():
            send(own, self.at(z), self.send_sem.at[1], self.recv_sem.at[z], c, z - 1)

    def forward(self, distance, then=None):
        c, z, n = self.c, self.z, self.n
        below, above = z - distance, z + distance

        @pl.when(below >= 0)
        def _():
            arrive(self.at(below), self.send_sem.at[0], self.recv_sem.at[below], c, z)

            @pl.when(z < n - 1)
            def _():
                send(self.at(below), self.at(below), self.send_sem.at[2 * distance], self.recv_sem.at[below], c, z + 1)

            if then is not None:
                then(below)

        @pl.when(above < n)
        def _():
            arrive(self.at(above), self.send_sem.at[0], self.recv_sem.at[above], c, z)

            @pl.when(z > 0)
            def _():
                send(self.at(above), self.at(above), self.send_sem.at[2 * distance + 1], self.recv_sem.at[above], c, z - 1)

            if then is not None:
                then(above)

    def finish(self, own):
        c, z, n = self.c, self.z, self.n

        @pl.when(z < n - 1)
        def _():
            left(own, self.send_sem.at[0], self.recv_sem.at[z], c, z)

        @pl.when(z > 0)
        def _():
            left(own, self.send_sem.at[1], self.recv_sem.at[z], c, z)

        for distance in range(1, n):
            below, above = z - distance, z + distance

            @pl.when((below >= 0) & (z < n - 1))
            def _():
                left(self.at(below), self.send_sem.at[2 * distance], self.recv_sem.at[below], c, z)

            @pl.when((above < n) & (z > 0))
            def _():
                left(self.at(above), self.send_sem.at[2 * distance + 1], self.recv_sem.at[above], c, z)


class Plane:
    def __init__(self, at, c, z, around, send_sem, recv_sem):
        self.at, self.c, self.z = at, c, z
        self.sib, self.first, self.second, self.diag = around
        self.send_sem, self.recv_sem = send_sem, recv_sem

    def push(self, slot, block, target, src=None):
        src = self.at(block) if src is None else src
        send(src, self.at(block), self.send_sem.at[slot], self.recv_sem.at[block], target, self.z)

    def wait(self, block):
        arrive(self.at(block), self.send_sem.at[0], self.recv_sem.at[block], self.c, self.z)

    def start(self, own=None):
        self.push(0, self.c, self.first, own)
        self.push(1, self.c, self.second, own)
        self.push(2, self.c, self.sib, own)

    def from_first(self):
        self.wait(self.first)
        self.push(3, self.first, self.second)
        self.push(4, self.first, self.sib)

    def from_second(self):
        self.wait(self.second)
        self.push(5, self.second, self.sib)

    def from_diag(self):
        self.wait(self.diag)
        self.push(6, self.diag, self.sib)

    def others(self):
        shift = self.sib - self.c
        return (self.sib, self.second + shift, self.first + shift, self.diag + shift)

    def finish(self):
        for slot in range(7):
            left(self.at(self.c), self.send_sem.at[slot], self.recv_sem.at[self.c], self.c, self.z)


def block_ids_of(block, order_ref, lengths_ref, rows):
    n_blk = lengths_ref.shape[1]
    position = order_ref[block] * rows + lax.broadcasted_iota(jnp.int32, (8, rows), 1)
    ids = jnp.zeros((8, rows), jnp.int32)
    bound = jnp.int32(0)
    for b in range(n_blk):
        bound = bound + lengths_ref[0, b]
        ids = ids + jnp.where(position >= bound, 1, 0)
    return ids, lax.broadcasted_iota(jnp.int32, (8, rows), 0)


def three_rows(value, rows):
    f32 = jnp.float32
    high = value.astype(jnp.bfloat16).astype(f32)
    rest = value - high
    mid = rest.astype(jnp.bfloat16).astype(f32)
    low = rest - mid
    row = lax.broadcasted_iota(jnp.int32, (8, rows), 0)
    return jnp.where(row == 0, high, 0.0) + jnp.where(row == 1, mid, 0.0) + jnp.where(row == 2, low, 0.0)


def forward_kernel(
    dims,
    tok_ref, wqkv_ref, w3_ref, pack_ref, order_ref, lengths_ref,
    h1_out, wc_out, kaug_out, vaug_out, kt_out, qaug_out, qraw_out, o_out, ob_out, full_out, gain_out,
    tok_all, h1_all, w_c, packs, gains, kaug, vaug, kt, vt, qaug, qraw, qneg, o_all, ob_stage, ob_land, s_buf,
    tok_send, tok_recv, wz_send, wz_recv, pk_send, pk_recv, ob_send, ob_recv,
    w3z_send, w3z_recv, w3p_send, w3p_recv, local_sem,
):
    n_ctx, n_wsh, hd, heads = dims
    f32, bf16 = jnp.float32, jnp.bfloat16
    c, z, sib, first, second, diag = place()
    around = (sib, first, second, diag)
    rows, width = tok_ref.shape
    span = hd * heads
    shard = w_c.shape[0] // n_wsh
    cut = shard // (n_ctx // 2)
    half = width // 2
    length = rows * n_ctx
    enter(c, z, n_ctx, n_wsh)

    tokens = Plane(lambda b: tok_all.at[b], c, z, around, tok_send, tok_recv)
    tokens.start(tok_ref)
    wline = Line(lambda s: w_c.at[pl.ds(pl.multiple_of(s * shard, 16), shard)], c, z, n_wsh, wz_send, wz_recv)
    for k in range(1, n_wsh):
        send(pack_ref, packs.at[z], pk_send.at[k], pk_recv.at[z], c, lax.rem(z + k, n_wsh))
    wline.start(wqkv_ref)
    own_tok = pltpu.make_async_copy(tok_ref, tok_all.at[c], local_sem.at[0])
    own_w = pltpu.make_async_copy(wqkv_ref, wline.at(z), local_sem.at[1])
    own_pack = pltpu.make_async_copy(pack_ref, packs.at[z], local_sem.at[2])
    own_full = pltpu.make_async_copy(
        w3_ref, full_out.at[:, pl.ds(pl.multiple_of(z * shard, 16), shard)], local_sem.at[3]
    )
    for copy in (own_tok, own_w, own_pack, own_full):
        copy.start()
    own_tok.wait()
    own_pack.wait()
    for k in range(1, n_wsh):
        other = lax.rem(z + k, n_wsh)
        arrive(packs.at[other], pk_send.at[0], pk_recv.at[other], c, z)

    row8 = lax.broadcasted_iota(jnp.int32, (8, width), 0)
    total = jnp.zeros((8, width), f32)
    for s in range(n_wsh):
        wide = jnp.concatenate([packs[s], jnp.zeros((8, width - packs.shape[2]), f32)], axis=1)
        by_shard = pltpu.roll(wide, s * shard, 1) if s else wide
        by_dim = pltpu.roll(wide, s * (hd // n_wsh), 1) if s else wide
        total = total + jnp.where(row8 < 2, by_shard, by_dim)
    gains[...] = total
    scale = jnp.concatenate([total[2:3, 0:128], jnp.zeros((7, 128), f32)], axis=0)
    soft = jnp.maximum(scale, 0.0) + jnp.log(1.0 + jnp.exp(-jnp.abs(scale)))
    gain_col = (LOG_BASE / math.sqrt(hd) * soft).T[0:hd, 0:1]

    def norm_block(b):
        gain = gains[0:1, :]

        def some_rows(i, _):
            at = pl.ds(pl.multiple_of(i * 32, 32), 32)
            t = tok_all[b, at, :].astype(f32)
            inverse = lax.rsqrt(jnp.mean(t * t, -1, keepdims=True) + EPS)
            h1_all[b, at, :] = (t * inverse * gain).astype(bf16)
            return 0

        lax.fori_loop(0, rows // 32, some_rows, 0)
        pltpu.make_async_copy(h1_all.at[b], h1_out.at[b], local_sem.at[5]).start()

    others = tokens.others()
    norm_block(c)
    tokens.wait(others[0])
    norm_block(others[0])
    wline.forward(1)
    tokens.from_first()
    norm_block(first)
    wline.forward(2)
    tokens.from_second()
    norm_block(second)
    tokens.wait(others[1])
    norm_block(others[1])
    tokens.wait(others[2])
    norm_block(others[2])
    wline.forward(3)
    tokens.from_diag()
    norm_block(diag)
    own_w.wait()

    def piece(s, b):
        top = pl.multiple_of(s * shard + (b // 2) * cut, 16)
        return full_out.at[:, pl.ds(top, cut), pl.ds(pl.multiple_of(lax.rem(b, 2) * half, 128), half)]

    my_piece = w3_ref.at[
        :, pl.ds(pl.multiple_of((c // 2) * cut, 16), cut), pl.ds(pl.multiple_of(lax.rem(c, 2) * half, 128), half)
    ]
    line3 = Line(lambda s: piece(s, c), c, z, n_wsh, w3z_send, w3z_recv)
    line3.start(my_piece)

    tokens.wait(others[3])
    norm_block(others[3])

    def project(b, _):
        raw = jnp.dot(h1_all[b], w_c[...], preferred_element_type=f32).T
        at = pl.ds(pl.multiple_of(b * rows, 128), rows)
        ids, row = block_ids_of(b, order_ref, lengths_ref, rows)
        hot = jnp.where(ids == row, 1.0, 0.0)
        neg = jnp.where(row > ids, NEG, 0.0)
        ones = jnp.ones((8, rows), f32)
        qneg[b] = neg
        qraw[b] = raw[0:span]
        for h in range(heads):
            q = raw[h * hd : (h + 1) * hd] * gain_col
            qaug[b, h, 0:hd, :] = q.astype(bf16)
            qaug[b, h, hd : hd + 16, :] = jnp.concatenate([neg, jnp.zeros((8, rows), f32)], axis=0).astype(bf16)
            qaug[b, h, hd + 16 : 128, :] = jnp.zeros((112 - hd, rows), bf16)
            k = raw[span + h * hd : span + (h + 1) * hd].astype(bf16)
            v = raw[2 * span + h * hd : 2 * span + (h + 1) * hd].astype(bf16)
            tail = jnp.zeros((112 - hd, rows), f32)
            kt[h, :, at] = k
            vt[h, 0:hd, at] = v
            vt[h, hd : hd + 16, at] = jnp.ones((16, rows), bf16)
            kaug[h, at, :] = jnp.concatenate([k.astype(f32), hot, ones, tail], axis=0).T.astype(bf16)
            vaug[h, at, :] = jnp.concatenate([v.astype(f32), ones, ones, tail], axis=0).T.astype(bf16)
        return 0

    lax.fori_loop(0, n_ctx, project, 0)
    saved = [
        pltpu.make_async_copy(w_c, wc_out, local_sem.at[6]),
        pltpu.make_async_copy(kaug, kaug_out, local_sem.at[7]),
        pltpu.make_async_copy(vaug, vaug_out, local_sem.at[8]),
        pltpu.make_async_copy(kt, kt_out, local_sem.at[9]),
        pltpu.make_async_copy(qraw, qraw_out, local_sem.at[10]),
        pltpu.make_async_copy(gains, gain_out, local_sem.at[11]),
    ]
    for copy in saved:
        copy.start()

    planes = [
        Plane(lambda b, s=lax.rem(z + k, n_wsh): piece(s, b), c, z, around, w3p_send.at[k], w3p_recv.at[k])
        for k in range(n_wsh)
    ]

    def plane_of(s):
        k = lax.rem(s - z + n_wsh, n_wsh)
        Plane(lambda b: piece(s, b), c, z, around, w3p_send.at[k], w3p_recv.at[k]).start()

    keys = length // 4

    def attend(i, _):
        g = lax.rem(c + 1 + i, n_ctx)
        for h in range(heads):
            q = qaug[g, h]
            top = jnp.full((1, rows), -jnp.inf, f32)
            for j in range(4):
                s = jnp.dot(kaug[h, j * keys : (j + 1) * keys, :], q, preferred_element_type=f32)
                s_buf[j * keys : (j + 1) * keys, :] = s
                top = jnp.maximum(top, jnp.max(s, axis=0, keepdims=True))
            out = jnp.zeros((hd + 16, rows), f32)
            for j in range(4):
                p = jnp.exp(s_buf[j * keys : (j + 1) * keys, :] - top).astype(bf16)
                out = out + jnp.dot(vt[h, :, j * keys : (j + 1) * keys], p, preferred_element_type=f32)
            total = out[hd : hd + 1]
            o = out[0:hd] / total
            lse = top + jnp.log(total)
            o_all[g, h * hd : (h + 1) * hd, :] = o
            ob_stage[g, h * hd : (h + 1) * hd, :] = o.astype(bf16)
            qaug[g, h, hd : hd + 16, :] = jnp.concatenate([qneg[g], three_rows(-lse, rows)], axis=0).astype(bf16)

        @pl.when(i < n_ctx - 1)
        def _():
            send(ob_stage.at[g], ob_land.at[c], ob_send.at[g], ob_recv.at[c], g, z)

        return 0

    lax.fori_loop(0, n_ctx, attend, 0)
    own_o = pltpu.make_async_copy(ob_stage.at[c], ob_land.at[c], local_sem.at[0])
    own_o.start()
    more = [
        pltpu.make_async_copy(qaug, qaug_out, local_sem.at[12]),
        pltpu.make_async_copy(o_all, o_out, local_sem.at[13]),
    ]
    for copy in more:
        copy.start()

    for distance in range(1, n_wsh):
        line3.forward(distance, plane_of)
    for k in range(1, n_wsh):
        planes[k].from_first()
    for k in range(1, n_wsh):
        planes[k].from_second()
    for k in range(1, n_wsh):
        planes[k].from_diag()
    for k in range(1, n_wsh):
        for b in others:
            planes[k].wait(b)
    own_o.wait()
    for k in range(1, n_ctx):
        g = lax.rem(c + k, n_ctx)
        arrive(ob_land.at[g], ob_send.at[0], ob_recv.at[g], c, z)
        left(ob_stage.at[g], ob_send.at[g], ob_recv.at[g], c, z)
    last = pltpu.make_async_copy(ob_land, ob_out, local_sem.at[4])
    last.start()
    tokens.finish()
    wline.finish(wqkv_ref)
    line3.finish(my_piece)
    for k in range(1, n_wsh):
        planes[k].finish()
        left(pack_ref, pk_send.at[k], pk_recv.at[z], c, z)
    for copy in saved + more:
        copy.wait()
    for k in range(n_ctx):
        pltpu.make_async_copy(h1_all.at[k], h1_out.at[k], local_sem.at[5]).wait()
    own_full.wait()
    last.wait()


def forward_call(dims, tok, wqkv, w3, pack, order, lengths):
    n_ctx, n_wsh, hd, heads = dims
    rows, width = tok.shape
    span, length = hd * heads, rows * n_ctx
    f32, bf16 = jnp.float32, jnp.bfloat16
    hbm = pl.BlockSpec(memory_space=pl.ANY)
    smem = pl.BlockSpec(memory_space=pltpu.SMEM)
    shape = jax.ShapeDtypeStruct
    dma = pltpu.SemaphoreType.DMA
    outs = (
        shape((n_ctx, rows, width), bf16),
        shape((width, wqkv.shape[1]), bf16),
        shape((heads, length, 128), bf16),
        shape((heads, length, 128), bf16),
        shape((heads, hd, length), bf16),
        shape((n_ctx, heads, 128, rows), bf16),
        shape((n_ctx, span, rows), f32),
        shape((n_ctx, span, rows), f32),
        shape((n_ctx, span, rows), bf16),
        shape((3, width, width), bf16),
        shape((8, width), f32),
    )
    scratch = [
        pltpu.VMEM((n_ctx, rows, width), bf16),
        pltpu.VMEM((n_ctx, rows, width), bf16),
        pltpu.VMEM((width, wqkv.shape[1]), bf16),
        pltpu.VMEM((n_wsh,) + pack.shape, f32),
        pltpu.VMEM((8, width), f32),
        pltpu.VMEM((heads, length, 128), bf16),
        pltpu.VMEM((heads, length, 128), bf16),
        pltpu.VMEM((heads, hd, length), bf16),
        pltpu.VMEM((heads, hd + 16, length), bf16),
        pltpu.VMEM((n_ctx, heads, 128, rows), bf16),
        pltpu.VMEM((n_ctx, span, rows), f32),
        pltpu.VMEM((n_ctx, 8, rows), f32),
        pltpu.VMEM((n_ctx, span, rows), f32),
        pltpu.VMEM((n_ctx, span, rows), bf16),
        pltpu.VMEM((n_ctx, span, rows), bf16),
        pltpu.VMEM((length, rows), f32),
        dma((7,)), dma((n_ctx,)),
        dma((2 * n_wsh,)), dma((n_wsh,)),
        dma((n_wsh,)), dma((n_wsh,)),
        dma((n_ctx,)), dma((n_ctx,)),
        dma((2 * n_wsh,)), dma((n_wsh,)),
        dma((n_wsh, 7)), dma((n_wsh, n_ctx)),
        dma((14,)),
    ]
    return pl.pallas_call(
        functools.partial(forward_kernel, dims),
        out_shape=outs,
        in_specs=[hbm] * 4 + [smem] * 2,
        out_specs=[hbm] * len(outs),
        scratch_shapes=scratch,
        compiler_params=pltpu.CompilerParams(
            collective_id=0, has_side_effects=True, vmem_limit_bytes=VMEM_BYTES
        ),
    )(tok, wqkv, w3, pack, order, lengths)


def add_rows(target, index, at, other, other_index, other_at, rows, step=16):
    f32 = jnp.float32

    def some_rows(i, _):
        here = pl.ds(pl.multiple_of(at + i * step, 16), step)
        there = pl.ds(pl.multiple_of(other_at + i * step, 16), step)
        left_part = target[index + (here, slice(None))].astype(f32)
        right_part = other[other_index + (there, slice(None))].astype(f32)
        target[index + (here, slice(None))] = (left_part + right_part).astype(target.dtype)
        return 0

    lax.fori_loop(0, rows // step, some_rows, 0)


def windows(width, n):
    part = width // n
    tiles = -(-part // 128) + (0 if part % 128 == 0 else 0)
    size = tiles * 128
    return [min(s * part // 128 * 128, width - size) for s in range(n)], size


def backward_kernel(
    dims,
    go_ref, dwo_ref, dwu_ref, dwd_ref, tok_ref, dx_ref, vec_ref, gain_ref,
    h1_ref, wc_ref, kaug_ref, vaug_ref, kt_ref, qaug_ref, qraw_ref, o_ref,
    gtok_out, dw3_out, dwqkv_out, vec_out,
    go_land, h1_all, w_c, kaug, vaug, kt, qaug, qraw, o_all, goaug, go_tm, q_tm, dk, dv, dqkv, scale_acc,
    win_out, win_land, fin_qkv, part, part_p, part_f, part_s,
    acc, land_p, land_f, land_s, land_z, fin3, dh, dx, tok, gains, gtok, vec, vec_plane, vec_line, vec_mid, vec_sum,
    go_send, go_recv, p_send, p_recv, f_send, f_recv, s_send, s_recv, z_send, z_recv, g_send, g_recv,
    hp_send, hp_recv, hf_send, hf_recv, hs_send, hs_recv, w_send, w_recv, wg_send, wg_recv,
    vp_send, vp_recv, vl_send, vl_recv, local_sem,
):
    n_ctx, n_wsh, hd, heads = dims
    f32, bf16 = jnp.float32, jnp.bfloat16
    c, z, sib, first, second, diag = place()
    around = (sib, first, second, diag)
    core, x, y = lax.rem(c, 2), lax.rem(c // 2, 2), c // 4
    f_bit, s_bit = x * (1 - core) + y * core, y * (1 - core) + x * core
    rows, width = tok_ref.shape
    span = hd * heads
    length = rows * n_ctx
    shard = width // n_wsh
    half = width // 2
    two, one = shard // 2, shard // 4
    weights = (dwo_ref, dwu_ref, dwd_ref)
    enter(c, z, n_ctx, n_wsh)

    for k in range(1, n_ctx):
        g = lax.rem(c + k, n_ctx)
        send(go_ref.at[g], go_land.at[c], go_send.at[k], go_recv.at[c], g, z)
    mine = pl.ds(pl.multiple_of(core * half, 128), half)
    theirs = pl.ds(pl.multiple_of((1 - core) * half, 128), half)
    order3 = (2, 1, 0)
    for w in order3:
        send(weights[w].at[:, :, theirs], land_p.at[w], p_send.at[w], p_recv.at[w], sib, z)
    loads = [
        (go_ref.at[c], go_land.at[c]), (qaug_ref, qaug), (o_ref, o_all), (kaug_ref, kaug), (vaug_ref, vaug), (kt_ref, kt),
        (qraw_ref, qraw), (gain_ref, gains),
    ]
    later = [
        (dwd_ref.at[:, :, mine], acc.at[2]), (dwu_ref.at[:, :, mine], acc.at[1]), (dwo_ref.at[:, :, mine], acc.at[0]),
        (h1_ref, h1_all), (wc_ref, w_c), (tok_ref, tok), (dx_ref, dx), (vec_ref, vec),
    ]
    loads = [pltpu.make_async_copy(a, b, local_sem.at[i]) for i, (a, b) in enumerate(loads)]
    later = [pltpu.make_async_copy(a, b, local_sem.at[i + 8]) for i, (a, b) in enumerate(later)]
    for copy in loads + later:
        copy.start()
    dk[...] = jnp.zeros_like(dk)
    dv[...] = jnp.zeros_like(dv)
    scale_acc[...] = jnp.zeros_like(scale_acc)
    dqkv[3 * span :, :] = jnp.zeros((dqkv.shape[0] - 3 * span, length), bf16)
    for copy in loads:
        copy.wait()

    scale = jnp.concatenate([gains[2:3, 0:128], jnp.zeros((7, 128), f32)], axis=0)
    soft = jnp.maximum(scale, 0.0) + jnp.log(1.0 + jnp.exp(-jnp.abs(scale)))
    gain_col = (LOG_BASE / math.sqrt(hd) * soft).T[0:hd, 0:1]

    def prepare(g):
        at = pl.ds(pl.multiple_of(g * rows, 16), rows)
        for h in range(heads):
            go = go_land[g, h * hd : (h + 1) * hd, :]
            wide = go.astype(f32)
            delta = jnp.sum(wide * o_all[g, h * hd : (h + 1) * hd, :], axis=0, keepdims=True)
            tail = jnp.concatenate([three_rows(-delta, rows), jnp.zeros((120 - hd, rows), f32)], axis=0)
            goaug[g, h, 0:hd, :] = go
            goaug[g, h, hd:128, :] = tail.astype(bf16)
            go_tm[h, at, :] = jnp.concatenate([wide, jnp.zeros((128 - hd, rows), f32)], axis=0).T.astype(bf16)
            q = qaug[g, h, 0:hd, :].astype(f32)
            q_tm[h, at, :] = jnp.concatenate([q, jnp.zeros((128 - hd, rows), f32)], axis=0).T.astype(bf16)

    def reduce_pair(w):
        arrive(land_p.at[w], p_send.at[w], p_recv.at[w], c, z)
        for s in range(n_wsh):
            add_rows(acc, (w, s), 0, land_p, (w, s), 0, shard)
        at = pl.ds(pl.multiple_of((1 - f_bit) * two, 16), two)
        send(acc.at[w, :, at], land_f.at[w], f_send.at[w], f_recv.at[w], first, z)

    def reduce_first(w):
        arrive(land_f.at[w], f_send.at[w], f_recv.at[w], c, z)
        for s in range(n_wsh):
            add_rows(acc, (w, s), f_bit * two, land_f, (w, s), 0, two)
        at = pl.ds(pl.multiple_of(f_bit * two + (1 - s_bit) * one, 16), one)
        send(acc.at[w, :, at], land_s.at[w], s_send.at[w], s_recv.at[w], second, z)

    my_top = f_bit * two + s_bit * one

    def reduce_second(w):
        arrive(land_s.at[w], s_send.at[w], s_recv.at[w], c, z)
        for s in range(n_wsh):
            add_rows(acc, (w, s), my_top, land_s, (w, s), 0, one)
        at = pl.ds(pl.multiple_of(my_top, 16), one)
        for k in range(1, n_wsh):
            s = lax.rem(z + k, n_wsh)
            send(acc.at[w, s, at], land_z.at[w, z], z_send.at[w, k], z_recv.at[w, z], c, s)

    def out_piece(w, b):
        b_core, b_x, b_y = lax.rem(b, 2), lax.rem(b // 2, 2), b // 4
        r = (1 - b_core) * (2 * b_x + b_y) + b_core * (2 * b_y + b_x)
        return dw3_out.at[
            w, pl.ds(pl.multiple_of(r * one, 16), one), pl.ds(pl.multiple_of(b_core * half, 128), half)
        ]

    planes = [
        Plane(lambda b, w=w: out_piece(w, b), c, z, around, g_send.at[w], g_recv.at[w]) for w in range(3)
    ]

    def reduce_line(w):
        for k in range(1, n_wsh):
            s = lax.rem(z + k, n_wsh)
            arrive(land_z.at[w, s], z_send.at[w, 0], z_recv.at[w, s], c, z)

        def some_rows(i, _):
            at = pl.ds(pl.multiple_of(i * 16, 16), 16)
            total = acc[w, z, pl.ds(pl.multiple_of(my_top + i * 16, 16), 16), :].astype(f32)
            for k in range(1, n_wsh):
                total = total + land_z[w, lax.rem(z + k, n_wsh), at, :].astype(f32)
            fin3[w, at, :] = total.astype(bf16)
            return 0

        lax.fori_loop(0, one // 16, some_rows, 0)
        planes[w].start(fin3.at[w])
        pltpu.make_async_copy(fin3.at[w], out_piece(w, c), local_sem.at[16]).start()

    for k in range(n_ctx):
        g = lax.rem(c + k, n_ctx)
        if k:
            arrive(go_land.at[g], go_send.at[0], go_recv.at[g], c, z)
        prepare(g)
    for copy in later:
        copy.wait()
    for w in order3:
        reduce_pair(w)

    chunk = length // 4

    def attend(g, _):
        at = pl.ds(pl.multiple_of(g * rows, 16), rows)
        for h in range(heads):
            dq = jnp.zeros((hd, rows), f32)
            for j in range(4):
                keys = slice(j * chunk, (j + 1) * chunk)
                p = jnp.exp(jnp.dot(kaug[h, keys, :], qaug[g, h], preferred_element_type=f32))
                ds = (p * jnp.dot(vaug[h, keys, :], goaug[g, h], preferred_element_type=f32)).astype(bf16)
                dq = dq + jnp.dot(kt[h, :, keys], ds, preferred_element_type=f32)
                dk[h, keys, :] += jnp.dot(ds, q_tm[h, at, :], preferred_element_type=f32)
                dv[h, keys, :] += jnp.dot(p.astype(bf16), go_tm[h, at, :], preferred_element_type=f32)
            scale_acc[...] += dq * qraw[g, h * hd : (h + 1) * hd, :]
            lanes = pl.ds(pl.multiple_of(g * rows, 128), rows)
            dqkv[h * hd : (h + 1) * hd, lanes] = (dq * gain_col).astype(bf16)

        for step, w in ((3, 2), (6, 1)):

            @pl.when(g == step)
            def _():
                reduce_first(w)

        return 0

    lax.fori_loop(0, n_ctx, attend, 0)

    def settle(g, _):
        at = pl.ds(pl.multiple_of(g * rows, 16), rows)
        lanes = pl.ds(pl.multiple_of(g * rows, 128), rows)
        for h in range(heads):
            for source, top in ((dk, span), (dv, 2 * span)):
                turned = source[h, at, :].T
                dqkv[top + h * hd : top + (h + 1) * hd, lanes] = turned[0:hd].astype(bf16)
        return 0

    lax.fori_loop(0, n_ctx, settle, 0)

    starts, size = windows(width, n_wsh)
    for s in range(n_wsh):
        total = jnp.zeros((3 * span, size), f32)
        for b in range(n_ctx):
            total = total + jnp.dot(
                dqkv[0 : 3 * span, b * rows : (b + 1) * rows], h1_all[b, :, starts[s] : starts[s] + size],
                preferred_element_type=f32,
            )
        win_out[s] = total.astype(bf16)

        @pl.when(z != s)
        def _():
            send(win_out.at[s], win_land.at[z], w_send.at[s], w_recv.at[z], c, s)

    def partial(b):
        lanes = pl.ds(pl.multiple_of(b * rows, 128), rows)
        part[b] = jnp.dot(w_c[...], dqkv[:, lanes], preferred_element_type=f32).astype(bf16)

    shift = sib - c

    def from_sib(i, _):
        b = lax.rem(2 * i + (1 - core), n_ctx)
        partial(b)
        send(part.at[b], part_p.at[i], hp_send.at[i], hp_recv.at[i], sib, z)
        return 0

    lax.fori_loop(0, n_ctx // 2, from_sib, 0)

    def own_core(i, _):
        partial(2 * i + core)
        return 0

    lax.fori_loop(0, n_ctx // 2, own_core, 0)
    reduce_first(0)
    reduce_second(2)

    for i, b in enumerate((first, diag, second, c)):
        arrive(part_p.at[b // 2], hp_send.at[0], hp_recv.at[b // 2], c, z)
        add_rows(part, (b,), 0, part_p, (b // 2,), 0, width)
        if i < 2:
            slot = s_bit if i == 0 else 1 - s_bit
            send(part.at[b], part_f.at[slot], hf_send.at[i], hf_recv.at[slot], first, z)
    reduce_second(1)
    arrive(part_f.at[1 - s_bit], hf_send.at[0], hf_recv.at[1 - s_bit], c, z)
    add_rows(part, (second,), 0, part_f, (1 - s_bit,), 0, width)
    send(part.at[second], part_s, hs_send.at[0], hs_recv.at[0], second, z)
    arrive(part_f.at[s_bit], hf_send.at[0], hf_recv.at[s_bit], c, z)
    add_rows(part, (c,), 0, part_f, (s_bit,), 0, width)
    reduce_second(0)
    reduce_line(2)
    reduce_line(1)

    for k in range(1, n_wsh):
        s = lax.rem(z + k, n_wsh)
        arrive(win_land.at[s], w_send.at[0], w_recv.at[s], c, z)

    def sum_windows(i, _):
        at = pl.ds(pl.multiple_of(i * 16, 16), 16)
        total = win_out[z, at, :].astype(f32)
        for k in range(1, n_wsh):
            total = total + win_land[lax.rem(z + k, n_wsh), at, :].astype(f32)
        fin_qkv[at, :] = total.astype(bf16)
        return 0

    lax.fori_loop(0, 3 * span // 16, sum_windows, 0)
    plane_w = Plane(lambda b: dwqkv_out.at[b], c, z, around, wg_send, wg_recv)
    plane_w.start(fin_qkv)
    own_fin = pltpu.make_async_copy(fin_qkv, dwqkv_out.at[c], local_sem.at[17])
    own_fin.start()
    reduce_line(0)

    arrive(part_s, hs_send.at[0], hs_recv.at[0], c, z)

    def turn(i, _):
        at = pl.ds(pl.multiple_of(i * 128, 128), 128)
        dh[:, at] = (part[c, at, :].astype(f32) + part_s[at, :].astype(f32)).T
        return 0

    lax.fori_loop(0, width // 128, turn, 0)

    def last_rows(i, total):
        at = pl.ds(pl.multiple_of(i * 16, 16), 16)
        t = tok[at, :].astype(f32)
        inverse = lax.rsqrt(jnp.mean(t * t, -1, keepdims=True) + EPS)
        normed = t * inverse
        grad = dh[at, :]
        both = grad * normed
        scaled = both * gains[0:1, :]
        slope = jnp.mean(scaled, -1, keepdims=True)
        gtok[at, :] = (dx[at, :] + inverse * (grad * gains[0:1, :] - normed * slope)).astype(bf16)
        return total + both

    gain_sum = lax.fori_loop(0, rows // 16, last_rows, jnp.zeros((16, width), f32))
    scale_sum = jnp.sum(scale_acc[...], axis=1, keepdims=True)
    scale_row = jnp.concatenate(
        [jnp.broadcast_to(scale_sum, (hd, 128)), jnp.zeros((128 - hd, 128), f32)], axis=0
    ).T[0:1, :]
    vec[0:1, :] = jnp.sum(gain_sum, axis=0, keepdims=True)
    vec[2:3, 0:128] = scale_row
    own_tok = pltpu.make_async_copy(gtok, gtok_out, local_sem.at[18])
    own_tok.start()
    for k in range(1, n_ctx):
        g = lax.rem(c + k, n_ctx)
        send(vec, vec_plane.at[c], vp_send.at[k], vp_recv.at[c], g, z)
    for w in order3:
        planes[w].from_first()
    plane_w.from_first()
    for w in order3:
        planes[w].from_second()
    plane_w.from_second()
    total = vec[...]
    for k in range(1, n_ctx):
        g = lax.rem(c + k, n_ctx)
        arrive(vec_plane.at[g], vp_send.at[0], vp_recv.at[g], c, z)
        total = total + vec_plane[g]
    vec_mid[...] = total
    for k in range(1, n_wsh):
        send(vec_mid, vec_line.at[z], vl_send.at[k], vl_recv.at[z], c, lax.rem(z + k, n_wsh))
    for w in order3:
        planes[w].from_diag()
    plane_w.from_diag()
    for k in range(1, n_wsh):
        s = lax.rem(z + k, n_wsh)
        arrive(vec_line.at[s], vl_send.at[0], vl_recv.at[s], c, z)
        total = total + vec_line[s]
    vec_sum[...] = total
    own_vec = pltpu.make_async_copy(vec_sum, vec_out, local_sem.at[19])
    own_vec.start()
    for plane in planes + [plane_w]:
        for b in plane.others():
            plane.wait(b)
        plane.finish()
    for w in range(3):
        pltpu.make_async_copy(fin3.at[w], out_piece(w, c), local_sem.at[16]).wait()
        left(land_p.at[w], p_send.at[w], p_recv.at[w], c, z)
        left(land_f.at[w], f_send.at[w], f_recv.at[w], c, z)
        left(land_s.at[w], s_send.at[w], s_recv.at[w], c, z)
        for k in range(1, n_wsh):
            left(land_z.at[w, 0], z_send.at[w, k], z_recv.at[w, 0], c, z)
    for k in range(1, n_ctx):
        left(go_land.at[0], go_send.at[k], go_recv.at[0], c, z)
        left(vec, vp_send.at[k], vp_recv.at[0], c, z)
    for k in range(1, n_wsh):
        left(vec, vl_send.at[k], vl_recv.at[0], c, z)
    for s in range(n_wsh):

        @pl.when(z != s)
        def _():
            left(win_out.at[s], w_send.at[s], w_recv.at[s], c, z)

    for i in range(n_ctx // 2):
        left(part.at[0], hp_send.at[i], hp_recv.at[i], c, z)
    for i in range(2):
        left(part.at[0], hf_send.at[i], hf_recv.at[i], c, z)
    left(part.at[0], hs_send.at[0], hs_recv.at[0], c, z)
    own_fin.wait()
    own_tok.wait()
    own_vec.wait()


def backward_call(dims, go, dw3, tok, dx, vec, gain, saved):
    n_ctx, n_wsh, hd, heads = dims
    rows, width = tok.shape
    span, length, shard = hd * heads, rows * n_ctx, width // n_wsh
    half, cut = width // 2, shard // 4
    f32, bf16 = jnp.float32, jnp.bfloat16
    hbm = pl.BlockSpec(memory_space=pl.ANY)
    shape = jax.ShapeDtypeStruct
    dma = pltpu.SemaphoreType.DMA
    vm = pltpu.VMEM
    size = windows(width, n_wsh)[1]
    outs = (
        shape((rows, width), bf16),
        shape((3, shard, width), bf16),
        shape((n_ctx, 3 * span, size), bf16),
        shape((8, width), f32),
    )
    scratch = [
        vm((n_ctx, span, rows), bf16), vm((n_ctx, rows, width), bf16), vm(saved[1].shape, bf16),
        vm((heads, length, 128), bf16), vm((heads, length, 128), bf16), vm((heads, hd, length), bf16),
        vm((n_ctx, heads, 128, rows), bf16), vm((n_ctx, span, rows), f32), vm((n_ctx, span, rows), f32),
        vm((n_ctx, heads, 128, rows), bf16), vm((heads, length, 128), bf16), vm((heads, length, 128), bf16),
        vm((heads, length, 128), f32), vm((heads, length, 128), f32), vm((saved[1].shape[1], length), bf16),
        vm((hd, rows), f32),
        vm((n_wsh, 3 * span, size), bf16), vm((n_wsh, 3 * span, size), bf16), vm((3 * span, size), bf16),
        vm((n_ctx, width, rows), bf16), vm((n_ctx // 2, width, rows), bf16), vm((2, width, rows), bf16),
        vm((width, rows), bf16),
        vm((3, n_wsh, shard, half), bf16), vm((3, n_wsh, shard, half), bf16), vm((3, n_wsh, 2 * cut, half), bf16),
        vm((3, n_wsh, cut, half), bf16), vm((3, n_wsh, cut, half), bf16), vm((3, cut, half), bf16),
        vm((rows, width), f32), vm((rows, width), f32), vm((rows, width), bf16), vm((8, width), f32),
        vm((rows, width), bf16), vm((8, width), f32), vm((n_ctx, 8, width), f32), vm((n_wsh, 8, width), f32),
        vm((8, width), f32), vm((8, width), f32),
        dma((n_ctx,)), dma((n_ctx,)), dma((3,)), dma((3,)), dma((3,)), dma((3,)), dma((3,)), dma((3,)),
        dma((3, n_wsh)), dma((3, n_wsh)), dma((3, 7)), dma((3, n_ctx)),
        dma((n_ctx // 2,)), dma((n_ctx // 2,)), dma((2,)), dma((2,)), dma((1,)), dma((1,)),
        dma((n_wsh,)), dma((n_wsh,)), dma((7,)), dma((n_ctx,)),
        dma((n_ctx,)), dma((n_ctx,)), dma((n_wsh,)), dma((n_wsh,)), dma((20,)),
    ]
    h1, wc, kaug, vaug, kt, qaug, qraw, o = saved
    operands = (go, *[w.reshape(n_wsh, shard, width) for w in dw3], tok, dx, vec, gain, *saved)
    return pl.pallas_call(
        functools.partial(backward_kernel, dims),
        out_shape=outs,
        in_specs=[hbm] * len(operands),
        out_specs=[hbm] * len(outs),
        scratch_shapes=scratch,
        compiler_params=pltpu.CompilerParams(
            collective_id=1, has_side_effects=True, vmem_limit_bytes=VMEM_BYTES
        ),
    )(*operands)


def head_split(
    tokens, cotangent, block_lengths, group_order, w_query, w_key, w_value, w_out, w_up, w_down,
    gain_attn, gain_mlp, query_scale,
):
    f32, bf16 = jnp.float32, jnp.bfloat16
    n_ctx, n_wsh = lax.axis_size("ctx"), lax.axis_size("wsh")
    c, z = lax.axis_index("ctx"), lax.axis_index("wsh")
    rows, width = tokens.shape[1:]
    hd, heads = width // H, H // n_ctx
    span, shard = hd * heads, width // n_wsh
    dims = (n_ctx, n_wsh, hd, heads)
    mine = [lax.dynamic_slice_in_dim(w, c * span, span, 1) for w in (w_query, w_key, w_value)]
    lanes = -(-3 * span // 128) * 128
    wqkv = jnp.pad(jnp.concatenate(mine, 1), ((0, 0), (0, lanes - 3 * span)))
    w3 = jnp.stack([w_out, w_up, w_down])
    lanes = -(-shard // 128) * 128
    pack = jnp.concatenate(
        [jnp.pad(v.astype(f32), (0, lanes - v.shape[0]))[None] for v in (gain_attn, gain_mlp, query_scale)]
        + [jnp.zeros((5, lanes), f32)]
    )
    *saved, ob, full, gains = forward_call(dims, tokens[0], wqkv, w3, pack, group_order, block_lengths)
    full_out, full_up, full_down = full[0], full[1], full[2]
    ob = ob.reshape(width, rows)
    inputs = tokens[0].astype(f32)
    norm_mlp = gains[1]
    mixed = inputs + lax.dot_general(ob, full_out, (((0,), (0,)), ((), ())), preferred_element_type=f32)
    inverse_two = inverse_rms(mixed)
    normed_two = mixed * inverse_two
    hidden_two = (normed_two * norm_mlp).astype(bf16)
    up_raw = jnp.dot(hidden_two, full_up, preferred_element_type=f32)
    active = jax.nn.silu(up_raw).astype(bf16)
    outputs = mixed + jnp.dot(active, full_down, preferred_element_type=f32)
    grad_mlp = cotangent[0]
    grad_output = grad_mlp.astype(f32)
    grad_active = back_product(grad_mlp, full_down)
    sigmoid_up = jax.nn.sigmoid(up_raw)
    grad_up_raw = (grad_active * sigmoid_up * (1.0 + up_raw * (1.0 - sigmoid_up))).astype(bf16)
    grad_hidden_two = back_product(grad_up_raw, full_up)
    grad_gain_mlp = jnp.sum(grad_hidden_two * normed_two, 0)
    grad_mixed = grad_output + norm_back(normed_two, inverse_two, grad_hidden_two * norm_mlp)
    grad_branch = grad_mixed.astype(bf16)
    go = lax.dot_general(
        full_out, grad_branch, (((1,), (1,)), ((), ())), preferred_element_type=f32
    ).astype(bf16)
    dw3 = (
        jnp.dot(ob, grad_branch, preferred_element_type=f32).astype(bf16),
        outer_product(hidden_two, grad_up_raw).astype(bf16),
        outer_product(active, grad_mlp).astype(bf16),
    )
    vec = jnp.pad(grad_gain_mlp[None], ((1, 6), (0, 0)))
    gtok, dw3_own, dwqkv, sums = backward_call(
        dims, go.reshape(n_ctx, span, rows), dw3, tokens[0], grad_mixed, vec, gains, saved
    )
    starts, size = windows(width, n_wsh)
    at = z * shard - jnp.asarray(starts, jnp.int32)[z]
    dwqkv = lax.dynamic_slice_in_dim(dwqkv.reshape(n_ctx, 3, span, size), at, shard, 3)
    dwqkv = dwqkv.transpose(1, 3, 0, 2).reshape(3, shard, width).astype(f32)
    dw3_own = dw3_own.astype(f32)
    own = [lax.dynamic_slice_in_dim(sums[i], z * shard, shard, 0) for i in (0, 1)]
    scale_grad = (
        lax.dynamic_slice_in_dim(sums[2], z * (hd // n_wsh), hd // n_wsh, 0)
        * (LOG_BASE / math.sqrt(hd))
        * jax.nn.sigmoid(query_scale.astype(f32))
    )
    return (
        outputs.reshape(tokens.shape).astype(bf16), gtok.reshape(tokens.shape),
        dwqkv[0], dwqkv[1], dwqkv[2], dw3_own[0], dw3_own[1], dw3_own[2], own[0], own[1], scale_grad,
    )


def solution(mesh):
    in_specs = (
        P("wsh", "ctx", None),
        P("wsh", "ctx", None),
        P("wsh", None),
        P(),
        P("wsh", None),
        P("wsh", None),
        P("wsh", None),
        P("wsh", None),
        P("wsh", None),
        P("wsh", None),
        P("wsh"),
        P("wsh"),
        P("wsh"),
    )
    out_specs = (
        P("wsh", "ctx", None),
        P("wsh", "ctx", None),
        P("wsh", None),
        P("wsh", None),
        P("wsh", None),
        P("wsh", None),
        P("wsh", None),
        P("wsh", None),
        P("wsh"),
        P("wsh"),
        P("wsh"),
    )
    n_ctx, n_wsh = mesh.shape["ctx"], mesh.shape["wsh"]
    plan = head_split if (n_ctx, n_wsh) == (8, 4) else per_device
    return jax.shard_map(
        plan, mesh=mesh, in_specs=in_specs, out_specs=out_specs, check_vma=False
    )
```

```python
import functools
import math

import jax
import jax.numpy as jnp
from jax import lax
from jax.experimental import pallas as pl
from jax.experimental.pallas import tpu as pltpu
from jax.sharding import PartitionSpec as P

H = 16


EPS = 1e-06
LOG_BASE = 1.442695041


def row_step():
    return 512


def rows_at(array, block_no, step_rows):
    return lax.dynamic_slice_in_dim(array, block_no * step_rows, step_rows, 0)


def inverse_rms(values):
    return lax.rsqrt(jnp.mean(values * values, -1, keepdims=True) + EPS)


def norm_back(normed, inverse, grad):
    return inverse * (grad - normed * jnp.mean(grad * normed, -1, keepdims=True))


def split_heads(matrix):
    return matrix.reshape(matrix.shape[0], H, -1)


def outer_product(left, right):
    return lax.dot_general(
        left, right, (((0,), (0,)), ((), ())), preferred_element_type=jnp.float32
    )


def back_product(grad, weight):
    return lax.dot_general(
        grad, weight, (((1,), (1,)), ((), ())), preferred_element_type=jnp.float32
    )


def probabilities(query3, key3, query_marks, key_marks, log_totals):
    scores = jnp.einsum("qhd,khd->hqk", query3, key3, preferred_element_type=jnp.float32)
    allowed = key_marks[None, None, :] <= query_marks[None, :, None]
    return jnp.exp(jnp.where(allowed, scores - log_totals[:, :, None], -jnp.inf))


def score_grads(chances, grad_out3, value3, deltas):
    grad_chances = jnp.einsum("qhd,khd->hqk", grad_out3, value3, preferred_element_type=jnp.float32)
    return (chances * (grad_chances - deltas[:, :, None])).astype(jnp.bfloat16)


def per_device(
    tokens,
    cotangent,
    block_lengths,
    group_order,
    w_query,
    w_key,
    w_value,
    w_out,
    w_up,
    w_down,
    gain_attn,
    gain_mlp,
    query_scale,
):
    gathered = (
        lax.all_gather(w_query, "wsh", axis=0, tiled=True),
        lax.all_gather(w_key, "wsh", axis=0, tiled=True),
        lax.all_gather(w_value, "wsh", axis=0, tiled=True),
        lax.all_gather(w_out, "wsh", axis=0, tiled=True),
        lax.all_gather(w_up, "wsh", axis=0, tiled=True),
        lax.all_gather(w_down, "wsh", axis=0, tiled=True),
        lax.all_gather(gain_attn, "wsh", axis=0, tiled=True),
        lax.all_gather(gain_mlp, "wsh", axis=0, tiled=True),
        lax.all_gather(query_scale, "wsh", axis=0, tiled=True),
    )
    (
        full_query,
        full_key,
        full_value,
        full_out,
        full_up,
        full_down,
        norm_attn,
        norm_mlp,
        scale_param,
    ) = gathered
    tok_rows = tokens.shape[1]
    model_width = tokens.shape[2]
    length = tok_rows * lax.axis_size("ctx")
    device = lax.axis_index("ctx")
    head_size = scale_param.shape[0]
    f32 = jnp.float32
    bf16 = jnp.bfloat16
    inputs = tokens.reshape(tok_rows, model_width).astype(f32)
    positions = (
        group_order[:, None] * tok_rows + jnp.arange(tok_rows, dtype=jnp.int32)[None, :]
    ).reshape(length)
    bounds = jnp.cumsum(block_lengths[0])
    block_ids = jnp.sum((bounds[None, :] <= positions[:, None]).astype(jnp.int32), -1)
    query_ids = lax.dynamic_slice_in_dim(block_ids, device * tok_rows, tok_rows, 0)
    inverse_one = inverse_rms(inputs)
    normed_one = inputs * inverse_one
    hidden_one = (normed_one * norm_attn.astype(f32)).astype(bf16)
    query_raw = jnp.dot(hidden_one, full_query, preferred_element_type=f32).reshape(
        tok_rows, H, head_size
    )
    query_gain = LOG_BASE / math.sqrt(head_size) * jax.nn.softplus(scale_param.astype(f32))
    query3 = (query_raw * query_gain).astype(bf16)
    key_flat = jnp.dot(hidden_one, full_key, preferred_element_type=f32).astype(bf16)
    value_flat = jnp.dot(hidden_one, full_value, preferred_element_type=f32).astype(bf16)
    initial = (
        jnp.full((H, tok_rows), -1e30, f32),
        jnp.zeros((H, tok_rows), f32),
        jnp.zeros((tok_rows, H, head_size), f32),
    )
    key_rows = lax.all_gather(key_flat, "ctx", axis=0, tiled=True)
    value_rows = lax.all_gather(value_flat, "ctx", axis=0, tiled=True)
    row_count = key_rows.shape[0]
    step_rows = row_step()

    def one_block(block_no, looped):
        key_part = split_heads(rows_at(key_rows, block_no, step_rows))
        value_part = split_heads(rows_at(value_rows, block_no, step_rows))
        block_marks = rows_at(block_ids, block_no, step_rows)
        maxima, totals, running = looped
        scores = jnp.einsum("qhd,khd->hqk", query3, key_part, preferred_element_type=f32)
        allowed = block_marks[None, None, :] <= query_ids[None, :, None]
        scores = jnp.where(allowed, scores, -jnp.inf)
        raised = jnp.maximum(maxima, jnp.max(scores, -1))
        rescale = jnp.exp(maxima - raised)
        weights = jnp.exp(scores - raised[:, :, None])
        totals = totals * rescale + jnp.sum(weights, -1)
        running = running * rescale.T[:, :, None] + jnp.einsum(
            "hqk,khd->qhd", weights.astype(bf16), value_part, preferred_element_type=f32
        )
        return (raised, totals, running)

    maxima, totals, running = lax.fori_loop(0, row_count // step_rows, one_block, initial)
    log_totals = maxima + jnp.log(totals)
    attended = running / totals.T[:, :, None]
    attended_bf = attended.reshape(tok_rows, model_width).astype(bf16)
    mixed = inputs + jnp.dot(attended_bf, full_out, preferred_element_type=f32)
    inverse_two = inverse_rms(mixed)
    normed_two = mixed * inverse_two
    hidden_two = (normed_two * norm_mlp.astype(f32)).astype(bf16)
    up_raw = jnp.dot(hidden_two, full_up, preferred_element_type=f32)
    active = jax.nn.silu(up_raw).astype(bf16)
    outputs = mixed + jnp.dot(active, full_down, preferred_element_type=f32)
    grad_output = cotangent.reshape(tok_rows, model_width).astype(f32)
    grad_mlp = grad_output.astype(bf16)
    grad_active = back_product(grad_mlp, full_down)
    sigmoid_up = jax.nn.sigmoid(up_raw)
    grad_up_raw = (grad_active * sigmoid_up * (1.0 + up_raw * (1.0 - sigmoid_up))).astype(bf16)
    grad_hidden_two = back_product(grad_up_raw, full_up)
    grad_gain_mlp = jnp.sum(grad_hidden_two * normed_two, 0)
    grad_mixed = grad_output + norm_back(
        normed_two, inverse_two, grad_hidden_two * norm_mlp.astype(f32)
    )
    grad_branch = grad_mixed.astype(bf16)
    grad_att = back_product(grad_branch, full_out).astype(bf16)
    grad_att3 = split_heads(grad_att)
    deltas = jnp.sum(grad_att3.astype(f32) * attended, -1).T
    key_whole, value_whole = (
        lax.all_gather(key_flat, "ctx", axis=0, tiled=True),
        lax.all_gather(value_flat, "ctx", axis=0, tiled=True),
    )
    step_rows = row_step()
    block_total = length // step_rows

    def key_block(grad_q, block_parts):
        key_rows, value_rows, block_marks = block_parts
        key_part = split_heads(key_rows)
        value_part = split_heads(value_rows)
        zero_part = jnp.zeros((key_rows.shape[0], H, head_size), f32)
        chances = probabilities(query3, key_part, query_ids, block_marks, log_totals)
        slopes = score_grads(chances, grad_att3, value_part, deltas)
        new_grad = (grad_q, zero_part, zero_part)[0] + jnp.einsum(
            "hqk,khd->qhd", slopes, key_part, preferred_element_type=f32
        )
        grad_key_part = jnp.einsum("hqk,qhd->khd", slopes, query3, preferred_element_type=f32)
        grad_value_part = jnp.einsum(
            "hqk,qhd->khd", chances.astype(bf16), grad_att3, preferred_element_type=f32
        )
        return (new_grad, (grad_key_part, grad_value_part))

    grad_qs, (key_terms, value_terms) = lax.scan(
        key_block,
        jnp.zeros((tok_rows, H, head_size), f32),
        (
            key_whole.reshape(block_total, step_rows, model_width),
            value_whole.reshape(block_total, step_rows, model_width),
            block_ids.reshape(block_total, step_rows),
        ),
    )
    grad_key, grad_value = (
        lax.psum_scatter(
            key_terms.reshape(length, model_width).astype(jnp.bfloat16),
            "ctx",
            scatter_dimension=0,
            tiled=True,
        ).astype(jnp.float32),
        lax.psum_scatter(
            value_terms.reshape(length, model_width).astype(jnp.bfloat16),
            "ctx",
            scatter_dimension=0,
            tiled=True,
        ).astype(jnp.float32),
    )
    grad_key_bf = grad_key.astype(bf16)
    grad_value_bf = grad_value.astype(bf16)
    grad_query_bf = (grad_qs * query_gain).reshape(tok_rows, model_width).astype(bf16)
    grad_scale_param = (
        jnp.sum(grad_qs * query_raw, (0, 1))
        * (LOG_BASE / math.sqrt(head_size))
        * jax.nn.sigmoid(scale_param.astype(f32))
    )
    grad_hidden_one = (
        back_product(grad_query_bf, full_query)
        + back_product(grad_key_bf, full_key)
        + back_product(grad_value_bf, full_value)
    )
    grad_gain_attn = jnp.sum(grad_hidden_one * normed_one, 0)
    grad_inputs = grad_mixed + norm_back(
        normed_one, inverse_one, grad_hidden_one * norm_attn.astype(f32)
    )
    grad_queryw = outer_product(hidden_one, grad_query_bf)
    grad_keyw = outer_product(hidden_one, grad_key_bf)
    grad_valuew = outer_product(hidden_one, grad_value_bf)
    grad_outw = outer_product(attended_bf, grad_branch)
    grad_upw = outer_product(hidden_two, grad_up_raw)
    grad_downw = outer_product(active, grad_mlp)
    owned = (
        lax.psum_scatter(
            grad_queryw.astype(jnp.bfloat16), "wsh", scatter_dimension=0, tiled=True
        ).astype(jnp.float32),
        lax.psum_scatter(
            grad_keyw.astype(jnp.bfloat16), "wsh", scatter_dimension=0, tiled=True
        ).astype(jnp.float32),
        lax.psum_scatter(
            grad_valuew.astype(jnp.bfloat16), "wsh", scatter_dimension=0, tiled=True
        ).astype(jnp.float32),
        lax.psum_scatter(
            grad_outw.astype(jnp.bfloat16), "wsh", scatter_dimension=0, tiled=True
        ).astype(jnp.float32),
        lax.psum_scatter(
            grad_upw.astype(jnp.bfloat16), "wsh", scatter_dimension=0, tiled=True
        ).astype(jnp.float32),
        lax.psum_scatter(
            grad_downw.astype(jnp.bfloat16), "wsh", scatter_dimension=0, tiled=True
        ).astype(jnp.float32),
        lax.psum_scatter(
            grad_gain_attn.astype(jnp.bfloat16), "wsh", scatter_dimension=0, tiled=True
        ).astype(jnp.float32),
        lax.psum_scatter(
            grad_gain_mlp.astype(jnp.bfloat16), "wsh", scatter_dimension=0, tiled=True
        ).astype(jnp.float32),
        lax.psum_scatter(
            grad_scale_param.astype(jnp.bfloat16), "wsh", scatter_dimension=0, tiled=True
        ).astype(jnp.float32),
    )
    summed = (
        lax.psum(owned[0].astype(jnp.bfloat16), "ctx").astype(jnp.float32),
        lax.psum(owned[1].astype(jnp.bfloat16), "ctx").astype(jnp.float32),
        lax.psum(owned[2].astype(jnp.bfloat16), "ctx").astype(jnp.float32),
        lax.psum(owned[3].astype(jnp.bfloat16), "ctx").astype(jnp.float32),
        lax.psum(owned[4].astype(jnp.bfloat16), "ctx").astype(jnp.float32),
        lax.psum(owned[5].astype(jnp.bfloat16), "ctx").astype(jnp.float32),
        lax.psum(owned[6].astype(jnp.bfloat16), "ctx").astype(jnp.float32),
        lax.psum(owned[7].astype(jnp.bfloat16), "ctx").astype(jnp.float32),
        lax.psum(owned[8].astype(jnp.bfloat16), "ctx").astype(jnp.float32),
    )
    return (
        outputs.reshape(tokens.shape).astype(bf16),
        grad_inputs.reshape(tokens.shape).astype(bf16),
        summed[0],
        summed[1],
        summed[2],
        summed[3],
        summed[4],
        summed[5],
        summed[6],
        summed[7],
        summed[8],
    )


MESH = pl.DeviceIdType.MESH
NEG = -1e30
VMEM_BYTES = 60 * 1024 * 1024


def place():
    c, z = lax.axis_index("ctx"), lax.axis_index("wsh")
    core, x, y = lax.rem(c, 2), lax.rem(c // 2, 2), c // 4
    sib = c + 1 - 2 * core
    over_x, over_y = c + 2 - 4 * x, c + 4 - 8 * y
    first = over_x * (1 - core) + over_y * core
    second = over_y * (1 - core) + over_x * core
    diag = over_x + over_y - c
    return c, z, sib, first, second, diag


def enter(c, z, n_ctx, n_wsh):
    barrier = pltpu.get_barrier_semaphore()
    for k in range(1, n_ctx):
        pl.semaphore_signal(
            barrier, inc=1, device_id=(lax.rem(c + k, n_ctx), z), device_id_type=MESH
        )
    for k in range(1, n_wsh):
        pl.semaphore_signal(
            barrier, inc=1, device_id=(c, lax.rem(z + k, n_wsh)), device_id_type=MESH
        )
    pl.semaphore_wait(barrier, n_ctx + n_wsh - 2)


def send(src, dst, send_sem, recv_sem, c, z):
    copy = pltpu.make_async_remote_copy(
        src_ref=src, dst_ref=dst, send_sem=send_sem, recv_sem=recv_sem,
        device_id=(c, z), device_id_type=MESH,
    )
    copy.start()
    return copy


def arrive(dst, send_sem, recv_sem, c, z):
    pltpu.make_async_remote_copy(
        src_ref=dst, dst_ref=dst, send_sem=send_sem, recv_sem=recv_sem,
        device_id=(c, z), device_id_type=MESH,
    ).wait_recv()


def left(src, send_sem, recv_sem, c, z):
    pltpu.make_async_remote_copy(
        src_ref=src, dst_ref=src, send_sem=send_sem, recv_sem=recv_sem,
        device_id=(c, z), device_id_type=MESH,
    ).wait_send()


class Line:
    def __init__(self, at, c, z, n, send_sem, recv_sem):
        self.at, self.c, self.z, self.n = at, c, z, n
        self.send_sem, self.recv_sem = send_sem, recv_sem

    def start(self, own):
        c, z = self.c, self.z

        @pl.when(z < self.n - 1)
        def _():
            send(own, self.at(z), self.send_sem.at[0], self.recv_sem.at[z], c, z + 1)

        @pl.when(z > 0)
        def _():
            send(own, self.at(z), self.send_sem.at[1], self.recv_sem.at[z], c, z - 1)

    def forward(self, distance, then=None):
        c, z, n = self.c, self.z, self.n
        below, above = z - distance, z + distance

        @pl.when(below >= 0)
        def _():
            arrive(self.at(below), self.send_sem.at[0], self.recv_sem.at[below], c, z)

            @pl.when(z < n - 1)
            def _():
                send(self.at(below), self.at(below), self.send_sem.at[2 * distance], self.recv_sem.at[below], c, z + 1)

            if then is not None:
                then(below)

        @pl.when(above < n)
        def _():
            arrive(self.at(above), self.send_sem.at[0], self.recv_sem.at[above], c, z)

            @pl.when(z > 0)
            def _():
                send(self.at(above), self.at(above), self.send_sem.at[2 * distance + 1], self.recv_sem.at[above], c, z - 1)

            if then is not None:
                then(above)

    def finish(self, own):
        c, z, n = self.c, self.z, self.n

        @pl.when(z < n - 1)
        def _():
            left(own, self.send_sem.at[0], self.recv_sem.at[z], c, z)

        @pl.when(z > 0)
        def _():
            left(own, self.send_sem.at[1], self.recv_sem.at[z], c, z)

        for distance in range(1, n):
            below, above = z - distance, z + distance

            @pl.when((below >= 0) & (z < n - 1))
            def _():
                left(self.at(below), self.send_sem.at[2 * distance], self.recv_sem.at[below], c, z)

            @pl.when((above < n) & (z > 0))
            def _():
                left(self.at(above), self.send_sem.at[2 * distance + 1], self.recv_sem.at[above], c, z)


class Plane:
    def __init__(self, at, c, z, around, send_sem, recv_sem):
        self.at, self.c, self.z = at, c, z
        self.sib, self.first, self.second, self.diag = around
        self.send_sem, self.recv_sem = send_sem, recv_sem

    def push(self, slot, block, target, src=None):
        src = self.at(block) if src is None else src
        send(src, self.at(block), self.send_sem.at[slot], self.recv_sem.at[block], target, self.z)

    def wait(self, block):
        arrive(self.at(block), self.send_sem.at[0], self.recv_sem.at[block], self.c, self.z)

    def start(self, own=None):
        self.push(0, self.c, self.first, own)
        self.push(1, self.c, self.second, own)
        self.push(2, self.c, self.sib, own)

    def from_first(self):
        self.wait(self.first)
        self.push(3, self.first, self.second)
        self.push(4, self.first, self.sib)

    def from_second(self):
        self.wait(self.second)
        self.push(5, self.second, self.sib)

    def from_diag(self):
        self.wait(self.diag)
        self.push(6, self.diag, self.sib)

    def others(self):
        shift = self.sib - self.c
        return (self.sib, self.second + shift, self.first + shift, self.diag + shift)

    def finish(self):
        for slot in range(7):
            left(self.at(self.c), self.send_sem.at[slot], self.recv_sem.at[self.c], self.c, self.z)


def block_ids_of(block, order_ref, lengths_ref, rows):
    n_blk = lengths_ref.shape[1]
    position = order_ref[block] * rows + lax.broadcasted_iota(jnp.int32, (8, rows), 1)
    ids = jnp.zeros((8, rows), jnp.int32)
    bound = jnp.int32(0)
    for b in range(n_blk):
        bound = bound + lengths_ref[0, b]
        ids = ids + jnp.where(position >= bound, 1, 0)
    return ids, lax.broadcasted_iota(jnp.int32, (8, rows), 0)


def three_rows(value, rows):
    f32 = jnp.float32
    high = value.astype(jnp.bfloat16).astype(f32)
    rest = value - high
    mid = rest.astype(jnp.bfloat16).astype(f32)
    low = rest - mid
    row = lax.broadcasted_iota(jnp.int32, (8, rows), 0)
    return jnp.where(row == 0, high, 0.0) + jnp.where(row == 1, mid, 0.0) + jnp.where(row == 2, low, 0.0)


def add_rows(target, index, at, other, other_index, other_at, rows, step=16):
    f32 = jnp.float32

    def some_rows(i, _):
        here = pl.ds(pl.multiple_of(at + i * step, 16), step)
        there = pl.ds(pl.multiple_of(other_at + i * step, 16), step)
        left_part = target[index + (here, slice(None))].astype(f32)
        right_part = other[other_index + (there, slice(None))].astype(f32)
        target[index + (here, slice(None))] = (left_part + right_part).astype(target.dtype)
        return 0

    lax.fori_loop(0, rows // step, some_rows, 0)


def windows(width, n):
    part = width // n
    tiles = -(-part // 128) + (0 if part % 128 == 0 else 0)
    size = tiles * 128
    return [min(s * part // 128 * 128, width - size) for s in range(n)], size


def whole_kernel(
    dims,
    tok_ref, cot_ref, wqkv_ref, wout_ref, wup_ref, wdown_ref, pack_ref, order_ref, lengths_ref,
    out_out, gtok_out, dwo_out, dwu_out, dwd_out, dwqkv_out, vec_out,
    tok_hbm, w_hbm, h1_hbm, land_p,
    w_c, packs, gains, kaug, vaug, kt, qaug, qraw, o_all, ob_stage, ob_land, go_stage, go_land,
    acc, land_f, land_s, land_z, fin3, win_out, win_land, fin_qkv, part_p, part_f, part_s,
    dx, dh, tok, cot, gtok, vec, vec_plane, vec_line, vec_mid, vec_sum, scale_acc,
    tok_send, tok_recv, wz_send, wz_recv, pk_send, pk_recv, ob_send, ob_recv,
    w3z_send, w3z_recv, w3p_send, w3p_recv,
    go_send, go_recv, p_send, p_recv, f_send, f_recv, s_send, s_recv, z_send, z_recv, g_send, g_recv,
    hp_send, hp_recv, hf_send, hf_recv, hs_send, hs_recv, w_send, w_recv, wg_send, wg_recv,
    vp_send, vp_recv, vl_send, vl_recv, local_sem, norm_sem, load_sem,
):
    n_ctx, n_wsh, hd, heads = dims
    f32, bf16 = jnp.float32, jnp.bfloat16
    c, z, sib, first, second, diag = place()
    around = (sib, first, second, diag)
    core, x, y = lax.rem(c, 2), lax.rem(c // 2, 2), c // 4
    f_bit, s_bit = x * (1 - core) + y * core, y * (1 - core) + x * core
    rows, width = tok_ref.shape
    span, length = hd * heads, rows * n_ctx
    shard, half = width // n_wsh, width // 2
    two, cut = shard // 2, shard // (n_ctx // 2)
    w3_refs = (wout_ref, wup_ref, wdown_ref)
    OUT, UP, DOWN = 0, 1, 2
    from_first, from_second, from_diag = Plane.from_first, Plane.from_second, Plane.from_diag
    enter(c, z, n_ctx, n_wsh)

    part_rows = rows // 2
    tokens = [
        Plane(
            lambda b, i=i: tok_hbm.at[b, pl.ds(i * part_rows, part_rows)], c, z, around,
            tok_send.at[i], tok_recv.at[i],
        )
        for i in range(2)
    ]
    for i in range(2):
        tokens[i].start(tok_ref.at[pl.ds(i * part_rows, part_rows)])
    wline = Line(lambda s: w_c.at[pl.ds(pl.multiple_of(s * shard, 16), shard)], c, z, n_wsh, wz_send, wz_recv)
    for k in range(1, n_wsh):
        send(pack_ref, packs.at[z], pk_send.at[k], pk_recv.at[z], c, lax.rem(z + k, n_wsh))
    wline.start(wqkv_ref)
    own_tok = pltpu.make_async_copy(tok_ref, tok, local_sem.at[0])
    own_w = pltpu.make_async_copy(wqkv_ref, wline.at(z), local_sem.at[1])
    own_pack = pltpu.make_async_copy(pack_ref, packs.at[z], local_sem.at[2])
    own_cot = pltpu.make_async_copy(cot_ref, cot, local_sem.at[3])
    for copy in (own_tok, own_pack, own_w, own_cot):
        copy.start()
    vec[...] = jnp.zeros_like(vec)
    scale_acc[...] = jnp.zeros_like(scale_acc)

    def columns(b):
        return pl.ds(pl.multiple_of(lax.rem(b, 2) * half, 128), half)

    def piece(w, s, b):
        top = pl.multiple_of(s * shard + (b // 2) * cut, 16)
        return w_hbm.at[w, pl.ds(top, cut), columns(b)]

    my_piece = [ref.at[pl.ds(pl.multiple_of((c // 2) * cut, 16), cut), columns(c)] for ref in w3_refs]
    lines = [
        Line(lambda s, w=w: piece(w, s, c), c, z, n_wsh, w3z_send.at[w], w3z_recv.at[w]) for w in range(3)
    ]

    def plane_of(w, s):
        k = lax.rem(s - z + n_wsh, n_wsh)
        return Plane(lambda b: piece(w, s, b), c, z, around, w3p_send.at[w, k], w3p_recv.at[w, k])

    def shards_at(distance, step, weights=(0, 1, 2)):
        below, above = z - distance, z + distance

        @pl.when(below >= 0)
        def _():
            for w in weights:
                step(plane_of(w, below))

        @pl.when(above < n_wsh)
        def _():
            for w in weights:
                step(plane_of(w, above))

    def spread(distance):
        for w in range(3):
            lines[w].forward(distance, lambda s, w=w: plane_of(w, s).start())

    def all_others(plane):
        for b in plane.others():
            plane.wait(b)

    own_tok.wait()
    own_pack.wait()
    for k in range(1, n_wsh):
        other = lax.rem(z + k, n_wsh)
        arrive(packs.at[other], pk_send.at[0], pk_recv.at[other], c, z)
    row8 = lax.broadcasted_iota(jnp.int32, (8, width), 0)
    total = jnp.zeros((8, width), f32)
    for s in range(n_wsh):
        wide = jnp.concatenate([packs[s], jnp.zeros((8, width - packs.shape[2]), f32)], axis=1)
        by_shard = pltpu.roll(wide, s * shard, 1) if s else wide
        by_dim = pltpu.roll(wide, s * (hd // n_wsh), 1) if s else wide
        total = total + jnp.where(row8 < 2, by_shard, by_dim)
    gains[...] = total

    def gain_column():
        scale = jnp.concatenate([gains[2:3, 0:128], jnp.zeros((7, 128), f32)], axis=0)
        soft = jnp.maximum(scale, 0.0) + jnp.log(1.0 + jnp.exp(-jnp.abs(scale)))
        return (LOG_BASE / math.sqrt(hd) * soft).T[0:hd, 0:1]

    def attention_forward(h1_all, tok_buf, vt, qneg, s_buf):
        def load(slot, b):
            return pltpu.make_async_copy(tok_hbm.at[b], tok_buf.at[slot], load_sem.at[slot])

        def norm_block(b, source):
            gain = gains[0:1, :]

            def some_rows(i, _):
                at = pl.ds(pl.multiple_of(i * 32, 32), 32)
                t = source[at, :].astype(f32)
                inverse = lax.rsqrt(jnp.mean(t * t, -1, keepdims=True) + EPS)
                h1_all[b, at, :] = (t * inverse * gain).astype(bf16)
                return 0

            lax.fori_loop(0, rows // 32, some_rows, 0)
            pltpu.make_async_copy(h1_all.at[b], h1_hbm.at[b], norm_sem.at[0]).start()

        def arrived(b):
            for i in range(2):
                tokens[i].wait(b)

        def norm_loaded(slot, b):
            load(slot, b).wait()
            norm_block(b, tok_buf.at[slot])

        others = tokens[0].others()
        norm_block(c, tok)
        arrived(others[0])
        load(0, others[0]).start()
        tokens[0].from_first()
        norm_loaded(0, others[0])
        wline.forward(1)
        tokens[1].from_first()
        load(1, first).start()
        tokens[0].from_second()
        norm_loaded(1, first)
        tokens[1].from_second()
        load(0, second).start()
        norm_loaded(0, second)
        wline.forward(2)
        for w in range(3):
            lines[w].start(my_piece[w])
        arrived(others[1])
        load(1, others[1]).start()
        norm_loaded(1, others[1])
        arrived(others[2])
        load(0, others[2]).start()
        norm_loaded(0, others[2])
        tokens[0].from_diag()
        tokens[1].from_diag()
        load(1, diag).start()
        norm_loaded(1, diag)
        arrived(others[3])
        load(0, others[3]).start()
        norm_loaded(0, others[3])
        wline.forward(3)
        own_w.wait()
        spread(1)
        gain_col = gain_column()

        def project(b, _):
            raw = jnp.dot(h1_all[b], w_c[...], preferred_element_type=f32).T
            at = pl.ds(pl.multiple_of(b * rows, 128), rows)
            ids, row = block_ids_of(b, order_ref, lengths_ref, rows)
            hot = jnp.where(ids == row, 1.0, 0.0)
            neg = jnp.where(row > ids, NEG, 0.0)
            ones = jnp.ones((8, rows), f32)
            qneg[b] = neg
            qraw[b] = raw[0:span]
            for h in range(heads):
                q = raw[h * hd : (h + 1) * hd] * gain_col
                qaug[b, h, 0:hd, :] = q.astype(bf16)
                qaug[b, h, hd : hd + 16, :] = jnp.concatenate([neg, jnp.zeros((8, rows), f32)], axis=0).astype(bf16)
                qaug[b, h, hd + 16 : 128, :] = jnp.zeros((112 - hd, rows), bf16)
                k = raw[span + h * hd : span + (h + 1) * hd].astype(bf16)
                v = raw[2 * span + h * hd : 2 * span + (h + 1) * hd].astype(bf16)
                tail = jnp.zeros((112 - hd, rows), f32)
                kt[h, :, at] = k
                vt[h, 0:hd, at] = v
                vt[h, hd : hd + 16, at] = jnp.ones((16, rows), bf16)
                kaug[h, at, :] = jnp.concatenate([k.astype(f32), hot, ones, tail], axis=0).T.astype(bf16)
                vaug[h, at, :] = jnp.concatenate([v.astype(f32), ones, ones, tail], axis=0).T.astype(bf16)
            return 0

        lax.fori_loop(0, n_ctx, project, 0)
        keys = length // 2
        events = (
            ((0, lambda: spread(2)), (2, lambda: shards_at(1, from_first)), (4, lambda: shards_at(1, from_second))),
            ((3, lambda: spread(3)), (5, lambda: shards_at(2, from_first)), (6, lambda: shards_at(1, from_diag))),
        )

        def attend(i, _):
            g = lax.rem(c + 1 + i, n_ctx)
            for h in range(heads):
                q = qaug[g, h]
                top = jnp.full((1, rows), -jnp.inf, f32)
                for j in range(2):
                    s = jnp.dot(kaug[h, j * keys : (j + 1) * keys, :], q, preferred_element_type=f32)
                    s_buf[j * keys : (j + 1) * keys, :] = s
                    top = jnp.maximum(top, jnp.max(s, axis=0, keepdims=True))
                out = jnp.zeros((hd + 16, rows), f32)
                for j in range(2):
                    p = jnp.exp(s_buf[j * keys : (j + 1) * keys, :] - top).astype(bf16)
                    out = out + jnp.dot(vt[h, :, j * keys : (j + 1) * keys], p, preferred_element_type=f32)
                total = out[hd : hd + 1]
                o = out[0:hd] / total
                lse = top + jnp.log(total)
                o_all[g, h * hd : (h + 1) * hd, :] = o
                ob_stage[g, h * hd : (h + 1) * hd, :] = o.astype(bf16)
                qaug[g, h, hd : hd + 16, :] = jnp.concatenate([qneg[g], three_rows(-lse, rows)], axis=0).astype(bf16)
                for step, event in events[h]:
                    pl.when(i == step)(event)

            @pl.when(i < n_ctx - 1)
            def _():
                send(ob_stage.at[g], my_heads(ob_land), ob_send.at[g], ob_recv.at[c], g, z)

            return 0

        lax.fori_loop(0, n_ctx, attend, 0)
        for b in range(n_ctx):
            pltpu.make_async_copy(h1_all.at[b], h1_hbm.at[b], norm_sem.at[0]).wait()

    def my_heads(ref):
        return ref.at[pl.ds(pl.multiple_of(c * span, 16), span)]

    def heads_of(ref, g):
        return ref.at[pl.ds(pl.multiple_of(g * span, 16), span)]

    vm = pltpu.VMEM
    pl.run_scoped(
        attention_forward,
        vm((n_ctx, rows, width), bf16), vm((2, rows, width), bf16), vm((heads, hd + 16, length), bf16),
        vm((n_ctx, 8, rows), f32), vm((length, rows), f32),
    )
    own_o = pltpu.make_async_copy(ob_stage.at[c], my_heads(ob_land), local_sem.at[4])
    own_o.start()

    mine = pl.ds(pl.multiple_of(core * half, 128), half)
    theirs = pl.ds(pl.multiple_of((1 - core) * half, 128), half)
    my_top = f_bit * two + s_bit * cut
    dw_outs = (dwo_out, dwu_out, dwd_out)

    def pair_sum(w, tmp):
        arrive(land_p.at[w], p_send.at[w], p_recv.at[w], c, z)
        copies = [
            pltpu.make_async_copy(land_p.at[w, s], tmp.at[s % 2], load_sem.at[s % 2]) for s in range(n_wsh)
        ]
        copies[0].start()
        for s in range(n_wsh):
            copies[s].wait()
            if s + 1 < n_wsh:
                copies[s + 1].start()
            add_rows(acc, (w, s), 0, tmp, (s % 2,), 0, shard, 64)
        at = pl.ds(pl.multiple_of((1 - f_bit) * two, 16), two)
        send(acc.at[w, :, at], land_f.at[w], f_send.at[w], f_recv.at[w], first, z)

    def first_sum(w):
        arrive(land_f.at[w], f_send.at[w], f_recv.at[w], c, z)
        for s in range(n_wsh):
            add_rows(acc, (w, s), f_bit * two, land_f, (w, s), 0, two, 80)
        at = pl.ds(pl.multiple_of(f_bit * two + (1 - s_bit) * cut, 16), cut)
        send(acc.at[w, :, at], land_s.at[w], s_send.at[w], s_recv.at[w], second, z)

    def second_sum(w):
        arrive(land_s.at[w], s_send.at[w], s_recv.at[w], c, z)
        for s in range(n_wsh):
            add_rows(acc, (w, s), my_top, land_s, (w, s), 0, cut, 80)
        at = pl.ds(pl.multiple_of(my_top, 16), cut)
        for k in range(1, n_wsh):
            s = lax.rem(z + k, n_wsh)
            send(acc.at[w, s, at], land_z.at[w, z], z_send.at[w, k], z_recv.at[w, z], c, s)

    def out_piece(w, b):
        b_core, b_x, b_y = lax.rem(b, 2), lax.rem(b // 2, 2), b // 4
        r = (1 - b_core) * (2 * b_x + b_y) + b_core * (2 * b_y + b_x)
        return dw_outs[w].at[pl.ds(pl.multiple_of(r * cut, 16), cut), columns(b)]

    planes = [
        Plane(lambda b, w=w: out_piece(w, b), c, z, around, g_send.at[w], g_recv.at[w]) for w in range(3)
    ]

    def line_sum(w):
        for k in range(1, n_wsh):
            s = lax.rem(z + k, n_wsh)
            arrive(land_z.at[w, s], z_send.at[w, 0], z_recv.at[w, s], c, z)

        def some_rows(i, _):
            at = pl.ds(pl.multiple_of(i * 16, 16), 16)
            total = acc[w, z, pl.ds(pl.multiple_of(my_top + i * 16, 16), 16), :].astype(f32)
            for k in range(1, n_wsh):
                total = total + land_z[w, lax.rem(z + k, n_wsh), at, :].astype(f32)
            fin3[w, at, :] = total.astype(bf16)
            return 0

        lax.fori_loop(0, cut // 16, some_rows, 0)
        planes[w].start(fin3.at[w])
        pltpu.make_async_copy(fin3.at[w], out_piece(w, c), local_sem.at[8 + w]).start()

    def feed_forward(w_full, x1, h2, a, gu, ob, turned, ga, inv2, outb, stage, tmp):
        def load(w, k):
            at = pl.ds(pl.multiple_of(lax.rem(z + k, n_wsh) * shard, 16), shard)
            source = w_hbm.at[w, at] if k else w3_refs[w]
            return pltpu.make_async_copy(source, w_full.at[w, at], load_sem.at[2 + n_wsh * w + k])

        def whole(w):
            for k in range(1, n_wsh):
                load(w, k).start()

        def ready(w):
            for k in range(n_wsh):
                load(w, k).wait()

        def tiles(step, size=256):
            def one(i, _):
                step(pl.ds(pl.multiple_of(i * size, size), size))
                return 0

            lax.fori_loop(0, width // size, one, 0)

        def turn(source, target):
            def one(at):
                target[at, :] = source[:, at].T

            tiles(one, 128)

        def weight_gradient(w, left_t, right):
            for s in range(n_wsh):
                at = slice(s * shard, (s + 1) * shard)
                stage[w, s] = jnp.dot(left_t[at, :], right[:, theirs], preferred_element_type=f32).astype(bf16)
            send(stage.at[w], land_p.at[w], p_send.at[w], p_recv.at[w], sib, z)
            for s in range(n_wsh):
                at = slice(s * shard, (s + 1) * shard)
                acc[w, s] = jnp.dot(left_t[at, :], right[:, mine], preferred_element_type=f32).astype(bf16)

        for w in range(3):
            load(w, 0).start()
        shards_at(3, from_first, (OUT,))
        shards_at(2, from_second, (OUT,))
        shards_at(3, from_second, (OUT,))
        shards_at(2, from_diag, (OUT,))
        shards_at(3, from_diag, (OUT,))
        shards_at(3, from_first, (UP, DOWN))
        shards_at(2, from_second, (UP, DOWN))
        for distance in range(1, n_wsh):
            shards_at(distance, all_others, (OUT,))
        whole(OUT)
        own_o.wait()
        for k in range(1, n_ctx):
            g = lax.rem(c + k, n_ctx)
            arrive(heads_of(ob_land, g), ob_send.at[0], ob_recv.at[g], c, z)

        def turn_ob(at):
            ob[:, at] = ob_land[at, :].T

        tiles(turn_ob, 128)
        shards_at(3, from_second, (UP, DOWN))
        shards_at(2, from_diag, (UP, DOWN))
        ready(OUT)

        def mix(at):
            x1[:, at] = tok[:, at].astype(f32) + jnp.dot(ob[...], w_full[OUT, :, at], preferred_element_type=f32)

        tiles(mix)
        shards_at(3, from_diag, (UP, DOWN))
        for distance in range(1, n_wsh):
            shards_at(distance, all_others, (UP, DOWN))
        whole(UP)
        whole(DOWN)

        def norm_rows(i, _):
            at = pl.ds(pl.multiple_of(i * 32, 32), 32)
            t = x1[at, :]
            inverse = lax.rsqrt(jnp.mean(t * t, -1, keepdims=True) + EPS)
            inv2[at, :] = jnp.broadcast_to(inverse, (32, 128))
            h2[at, :] = (t * inverse * gains[1:2, :]).astype(bf16)
            return 0

        lax.fori_loop(0, rows // 32, norm_rows, 0)
        own_cot.wait()
        ready(UP)
        ready(DOWN)

        def hidden(at):
            up = jnp.dot(h2[...], w_full[UP, :, at], preferred_element_type=f32)
            da = lax.dot_general(
                cot[...], w_full[DOWN, at, :], (((1,), (1,)), ((), ())), preferred_element_type=f32
            )
            sig = 1.0 / (1.0 + jnp.exp(-up))
            act = up * sig
            a[:, at] = act.astype(bf16)
            turned[at, :] = act.T.astype(bf16)
            gu[:, at] = (da * sig * (1.0 + up * (1.0 - sig))).astype(bf16)

        tiles(hidden)
        weight_gradient(DOWN, turned, cot)

        def back(at):
            dh[:, at] = lax.dot_general(
                gu[...], w_full[UP, at, :], (((1,), (1,)), ((), ())), preferred_element_type=f32
            )

        tiles(back)

        def norm_back_rows(i, total):
            at = pl.ds(pl.multiple_of(i * 16, 16), 16)
            inverse = inv2[at, 0:1]
            normed = x1[at, :] * inverse
            grad = dh[at, :]
            both = grad * normed
            slope = jnp.mean(both * gains[1:2, :], -1, keepdims=True)
            result = cot[at, :].astype(f32) + inverse * (grad * gains[1:2, :] - normed * slope)
            dx[at, :] = result
            ga[at, :] = result.astype(bf16)
            return total + both

        gain_sum = lax.fori_loop(0, rows // 16, norm_back_rows, jnp.zeros((16, width), f32))
        vec[1:2, :] = jnp.sum(gain_sum, axis=0, keepdims=True)

        def back_out(at):
            go_stage[at, :] = lax.dot_general(
                w_full[OUT, at, :], ga[...], (((1,), (1,)), ((), ())), preferred_element_type=f32
            ).astype(bf16)

        tiles(back_out)
        for k in range(1, n_ctx):
            g = lax.rem(c + k, n_ctx)
            send(heads_of(go_stage, g), go_land.at[c], go_send.at[k], go_recv.at[c], g, z)
        pltpu.make_async_copy(my_heads(go_stage), go_land.at[c], local_sem.at[5]).start()
        pair_sum(DOWN, tmp)
        turn(h2, turned)
        weight_gradient(UP, turned, gu)
        weight_gradient(OUT, ob_land, ga)

        def finish(at):
            outb[:, at] = (
                x1[:, at] + jnp.dot(a[...], w_full[DOWN, :, at], preferred_element_type=f32)
            ).astype(bf16)

        tiles(finish)
        own_out = pltpu.make_async_copy(outb, out_out, local_sem.at[6])
        own_out.start()
        pair_sum(UP, tmp)
        pair_sum(OUT, tmp)
        own_out.wait()
        for w in range(3):
            left(stage.at[w], p_send.at[w], p_recv.at[w], c, z)

    wide = (rows, width)
    pl.run_scoped(
        feed_forward,
        vm((3, width, width), bf16), vm(wide, f32), vm(wide, bf16), vm(wide, bf16), vm(wide, bf16), vm(wide, bf16),
        vm((width, rows), bf16), vm(wide, bf16), vm((rows, 128), f32), vm(wide, bf16),
        vm((3, n_wsh, shard, half), bf16), vm((2, shard, half), bf16),
    )

    def attention_backward(h1_all, goaug, go_tm, q_tm, dk, dv, dqkv, part):
        def reload(b):
            return pltpu.make_async_copy(h1_hbm.at[b], h1_all.at[b], norm_sem.at[1])

        for b in range(n_ctx):
            reload(b).start()
        dk[...] = jnp.zeros_like(dk)
        dv[...] = jnp.zeros_like(dv)
        dqkv[3 * span :, :] = jnp.zeros((dqkv.shape[0] - 3 * span, length), bf16)
        gain_col = gain_column()

        def prepare(g):
            at = pl.ds(pl.multiple_of(g * rows, 16), rows)
            for h in range(heads):
                go = go_land[g, h * hd : (h + 1) * hd, :]
                wide = go.astype(f32)
                delta = jnp.sum(wide * o_all[g, h * hd : (h + 1) * hd, :], axis=0, keepdims=True)
                tail = jnp.concatenate([three_rows(-delta, rows), jnp.zeros((120 - hd, rows), f32)], axis=0)
                goaug[g, h, 0:hd, :] = go
                goaug[g, h, hd:128, :] = tail.astype(bf16)
                go_tm[h, at, :] = jnp.concatenate([wide, jnp.zeros((128 - hd, rows), f32)], axis=0).T.astype(bf16)
                q = qaug[g, h, 0:hd, :].astype(f32)
                q_tm[h, at, :] = jnp.concatenate([q, jnp.zeros((128 - hd, rows), f32)], axis=0).T.astype(bf16)

        pltpu.make_async_copy(my_heads(go_stage), go_land.at[c], local_sem.at[5]).wait()
        prepare(c)

        def prepare_other(k, _):
            g = lax.rem(c + k, n_ctx)
            arrive(go_land.at[g], go_send.at[0], go_recv.at[g], c, z)
            prepare(g)
            return 0

        lax.fori_loop(1, n_ctx, prepare_other, 0)
        chunk = length // 2
        events = (
            ((1, lambda: first_sum(DOWN)), (4, lambda: first_sum(UP)), (6, lambda: line_sum(DOWN))),
            ((3, lambda: second_sum(DOWN)), (6, lambda: second_sum(UP)), (7, lambda: first_sum(OUT))),
        )

        def attend(g, _):
            at = pl.ds(pl.multiple_of(g * rows, 16), rows)
            for h in range(heads):
                dq = jnp.zeros((hd, rows), f32)
                for j in range(2):
                    keys = slice(j * chunk, (j + 1) * chunk)
                    p = jnp.exp(jnp.dot(kaug[h, keys, :], qaug[g, h], preferred_element_type=f32))
                    ds = (p * jnp.dot(vaug[h, keys, :], goaug[g, h], preferred_element_type=f32)).astype(bf16)
                    dq = dq + jnp.dot(kt[h, :, keys], ds, preferred_element_type=f32)
                    dk[h, keys, :] += jnp.dot(ds, q_tm[h, at, :], preferred_element_type=f32)
                    dv[h, keys, :] += jnp.dot(p.astype(bf16), go_tm[h, at, :], preferred_element_type=f32)
                scale_acc[...] += dq * qraw[g, h * hd : (h + 1) * hd, :]
                lanes = pl.ds(pl.multiple_of(g * rows, 128), rows)
                dqkv[h * hd : (h + 1) * hd, lanes] = (dq * gain_col).astype(bf16)
                for step, event in events[h]:
                    pl.when(g == step)(event)
            return 0

        lax.fori_loop(0, n_ctx, attend, 0)

        def settle(g, _):
            at = pl.ds(pl.multiple_of(g * rows, 16), rows)
            lanes = pl.ds(pl.multiple_of(g * rows, 128), rows)
            for h in range(heads):
                for source, top in ((dk, span), (dv, 2 * span)):
                    turned = source[h, at, :].T
                    dqkv[top + h * hd : top + (h + 1) * hd, lanes] = turned[0:hd].astype(bf16)
            return 0

        lax.fori_loop(0, n_ctx, settle, 0)

        def partial(b):
            lanes = pl.ds(pl.multiple_of(b * rows, 128), rows)
            part[b] = jnp.dot(w_c[...], dqkv[:, lanes], preferred_element_type=f32).astype(bf16)

        def to_sib(i, _):
            b = 2 * i + (1 - core)
            partial(b)
            send(part.at[b], part_p.at[i], hp_send.at[i], hp_recv.at[i], sib, z)
            return 0

        lax.fori_loop(0, n_ctx // 2, to_sib, 0)
        planes[DOWN].from_first()

        def own_core(i, _):
            partial(2 * i + core)
            return 0

        lax.fori_loop(0, n_ctx // 2, own_core, 0)

        def pair(i, b):
            arrive(part_p.at[b // 2], hp_send.at[0], hp_recv.at[b // 2], c, z)
            add_rows(part, (b,), 0, part_p, (b // 2,), 0, width, 128)
            if i < 2:
                slot = s_bit if i == 0 else 1 - s_bit
                send(part.at[b], part_f.at[slot], hf_send.at[i], hf_recv.at[slot], first, z)

        pair(1, diag)
        pair(0, first)
        second_sum(OUT)
        line_sum(UP)
        planes[DOWN].from_second()

        for b in range(n_ctx):
            reload(b).wait()
        starts, size = windows(width, n_wsh)
        for s in range(n_wsh):
            total = jnp.zeros((3 * span, size), f32)
            for b in range(n_ctx):
                total = total + jnp.dot(
                    dqkv[0 : 3 * span, b * rows : (b + 1) * rows], h1_all[b, :, starts[s] : starts[s] + size],
                    preferred_element_type=f32,
                )
            win_out[s] = total.astype(bf16)

            @pl.when(z != s)
            def _():
                send(win_out.at[s], win_land.at[z], w_send.at[s], w_recv.at[z], c, s)

        pair(2, second)
        planes[DOWN].from_diag()
        pair(3, c)
        planes[UP].from_first()
        arrive(part_f.at[1 - s_bit], hf_send.at[0], hf_recv.at[1 - s_bit], c, z)
        add_rows(part, (second,), 0, part_f, (1 - s_bit,), 0, width, 128)
        send(part.at[second], part_s, hs_send.at[0], hs_recv.at[0], second, z)
        line_sum(OUT)
        arrive(part_f.at[s_bit], hf_send.at[0], hf_recv.at[s_bit], c, z)
        add_rows(part, (c,), 0, part_f, (s_bit,), 0, width, 128)
        planes[UP].from_second()
        planes[UP].from_diag()

        for k in range(1, n_wsh):
            s = lax.rem(z + k, n_wsh)
            arrive(win_land.at[s], w_send.at[0], w_recv.at[s], c, z)

        def sum_windows(i, _):
            at = pl.ds(pl.multiple_of(i * 32, 32), 32)
            total = win_out[z, at, :].astype(f32)
            for k in range(1, n_wsh):
                total = total + win_land[lax.rem(z + k, n_wsh), at, :].astype(f32)
            fin_qkv[at, :] = total.astype(bf16)
            return 0

        lax.fori_loop(0, 3 * span // 32, sum_windows, 0)
        plane_w = Plane(lambda b: dwqkv_out.at[b], c, z, around, wg_send, wg_recv)
        plane_w.start(fin_qkv)
        own_fin = pltpu.make_async_copy(fin_qkv, dwqkv_out.at[c], local_sem.at[7])
        own_fin.start()
        planes[OUT].from_first()
        planes[OUT].from_second()
        arrive(part_s, hs_send.at[0], hs_recv.at[0], c, z)

        def turn_dh(i, _):
            at = pl.ds(pl.multiple_of(i * 128, 128), 128)
            dh[:, at] = (part[c, at, :].astype(f32) + part_s[at, :].astype(f32)).T
            return 0

        lax.fori_loop(0, width // 128, turn_dh, 0)

        def last_rows(i, total):
            at = pl.ds(pl.multiple_of(i * 16, 16), 16)
            t = tok[at, :].astype(f32)
            inverse = lax.rsqrt(jnp.mean(t * t, -1, keepdims=True) + EPS)
            normed = t * inverse
            grad = dh[at, :]
            both = grad * normed
            slope = jnp.mean(both * gains[0:1, :], -1, keepdims=True)
            gtok[at, :] = (dx[at, :] + inverse * (grad * gains[0:1, :] - normed * slope)).astype(bf16)
            return total + both

        gain_sum = lax.fori_loop(0, rows // 16, last_rows, jnp.zeros((16, width), f32))
        scale_sum = jnp.sum(scale_acc[...], axis=1, keepdims=True)
        scale_row = jnp.concatenate(
            [jnp.broadcast_to(scale_sum, (hd, 128)), jnp.zeros((128 - hd, 128), f32)], axis=0
        ).T[0:1, :]
        vec[0:1, :] = jnp.sum(gain_sum, axis=0, keepdims=True)
        vec[2:3, 0:128] = scale_row
        own_gtok = pltpu.make_async_copy(gtok, gtok_out, local_sem.at[11])
        own_gtok.start()
        for k in range(1, n_ctx):
            g = lax.rem(c + k, n_ctx)
            send(vec, vec_plane.at[c], vp_send.at[k], vp_recv.at[c], g, z)
        planes[OUT].from_diag()
        plane_w.from_first()
        plane_w.from_second()
        total = vec[...]
        for k in range(1, n_ctx):
            g = lax.rem(c + k, n_ctx)
            arrive(vec_plane.at[g], vp_send.at[0], vp_recv.at[g], c, z)
            total = total + vec_plane[g]
        vec_mid[...] = total
        for k in range(1, n_wsh):
            send(vec_mid, vec_line.at[z], vl_send.at[k], vl_recv.at[z], c, lax.rem(z + k, n_wsh))
        plane_w.from_diag()
        for k in range(1, n_wsh):
            s = lax.rem(z + k, n_wsh)
            arrive(vec_line.at[s], vl_send.at[0], vl_recv.at[s], c, z)
            total = total + vec_line[s]
        vec_sum[...] = total
        own_vec = pltpu.make_async_copy(vec_sum, vec_out, local_sem.at[12])
        own_vec.start()
        for plane in planes + [plane_w]:
            all_others(plane)
            plane.finish()
        for i in range(n_ctx // 2):
            left(part.at[0], hp_send.at[i], hp_recv.at[i], c, z)
        for i in range(2):
            left(part.at[0], hf_send.at[i], hf_recv.at[i], c, z)
        left(part.at[0], hs_send.at[0], hs_recv.at[0], c, z)
        for copy in (own_fin, own_gtok, own_vec):
            copy.wait()

    pl.run_scoped(
        attention_backward,
        vm((n_ctx, rows, width), bf16), vm((n_ctx, heads, 128, rows), bf16), vm((heads, length, 128), bf16),
        vm((heads, length, 128), bf16), vm((heads, length, 128), f32), vm((heads, length, 128), f32),
        vm((w_c.shape[1], length), bf16), vm((n_ctx, width, rows), bf16),
    )

    for i in range(2):
        tokens[i].finish()
    wline.finish(wqkv_ref)
    for w in range(3):
        lines[w].finish(my_piece[w])
    for distance in range(1, n_wsh):
        shards_at(distance, Plane.finish)
    for k in range(1, n_wsh):
        left(pack_ref, pk_send.at[k], pk_recv.at[z], c, z)
        left(vec, vl_send.at[k], vl_recv.at[0], c, z)
    for k in range(1, n_ctx):
        g = lax.rem(c + k, n_ctx)
        left(ob_stage.at[g], ob_send.at[g], ob_recv.at[g], c, z)
        left(go_land.at[0], go_send.at[k], go_recv.at[0], c, z)
        left(vec, vp_send.at[k], vp_recv.at[0], c, z)
    for w in range(3):
        pltpu.make_async_copy(fin3.at[w], out_piece(w, c), local_sem.at[8 + w]).wait()
        left(land_f.at[w], f_send.at[w], f_recv.at[w], c, z)
        left(land_s.at[w], s_send.at[w], s_recv.at[w], c, z)
        for k in range(1, n_wsh):
            left(land_z.at[w, 0], z_send.at[w, k], z_recv.at[w, 0], c, z)
    for s in range(n_wsh):

        @pl.when(z != s)
        def _():
            left(win_out.at[s], w_send.at[s], w_recv.at[s], c, z)


def whole_call(dims, tok, cot, wqkv, w3, pack, order, lengths):
    n_ctx, n_wsh, hd, heads = dims
    rows, width = tok.shape
    span, length, shard = hd * heads, rows * n_ctx, width // n_wsh
    half, cut = width // 2, shard // (n_ctx // 2)
    f32, bf16 = jnp.float32, jnp.bfloat16
    hbm = pl.BlockSpec(memory_space=pl.ANY)
    smem = pl.BlockSpec(memory_space=pltpu.SMEM)
    shape = jax.ShapeDtypeStruct
    dma = pltpu.SemaphoreType.DMA
    vm = pltpu.VMEM
    size = windows(width, n_wsh)[1]
    wide = (rows, width)
    outs = (
        shape(wide, bf16), shape(wide, bf16),
        shape((shard, width), bf16), shape((shard, width), bf16), shape((shard, width), bf16),
        shape((n_ctx, 3 * span, size), bf16), shape((8, width), f32),
        shape((n_ctx, rows, width), bf16), shape((3, width, width), bf16), shape((n_ctx, rows, width), bf16),
        shape((3, n_wsh, shard, half), bf16),
    )
    scratch = [
        vm(( width, wqkv.shape[1]), bf16), vm((n_wsh,) + pack.shape, f32), vm((8, width), f32),
        vm((heads, length, 128), bf16), vm((heads, length, 128), bf16), vm((heads, hd, length), bf16),
        vm((n_ctx, heads, 128, rows), bf16), vm((n_ctx, span, rows), f32), vm((n_ctx, span, rows), f32),
        vm((n_ctx, span, rows), bf16), vm((width, rows), bf16), vm((width, rows), bf16), vm((n_ctx, span, rows), bf16),
        vm((3, n_wsh, shard, half), bf16), vm((3, n_wsh, 2 * cut, half), bf16), vm((3, n_wsh, cut, half), bf16),
        vm((3, n_wsh, cut, half), bf16), vm((3, cut, half), bf16),
        vm((n_wsh, 3 * span, size), bf16), vm((n_wsh, 3 * span, size), bf16), vm((3 * span, size), bf16),
        vm((n_ctx // 2, width, rows), bf16), vm((2, width, rows), bf16), vm((width, rows), bf16),
        vm(wide, f32), vm(wide, f32), vm(wide, bf16), vm(wide, bf16), vm(wide, bf16),
        vm((8, width), f32), vm((n_ctx, 8, width), f32), vm((n_wsh, 8, width), f32), vm((8, width), f32),
        vm((8, width), f32), vm((hd, rows), f32),
        dma((2, 7)), dma((2, n_ctx)), dma((2 * n_wsh,)), dma((n_wsh,)), dma((n_wsh,)), dma((n_wsh,)),
        dma((n_ctx,)), dma((n_ctx,)), dma((3, 2 * n_wsh)), dma((3, n_wsh)),
        dma((3, n_wsh, 7)), dma((3, n_wsh, n_ctx)),
        dma((n_ctx,)), dma((n_ctx,)), dma((3,)), dma((3,)), dma((3,)), dma((3,)), dma((3,)), dma((3,)),
        dma((3, n_wsh)), dma((3, n_wsh)), dma((3, 7)), dma((3, n_ctx)),
        dma((n_ctx // 2,)), dma((n_ctx // 2,)), dma((2,)), dma((2,)), dma((1,)), dma((1,)),
        dma((n_wsh,)), dma((n_wsh,)), dma((7,)), dma((n_ctx,)),
        dma((n_ctx,)), dma((n_ctx,)), dma((n_wsh,)), dma((n_wsh,)), dma((13,)), dma((2,)), dma((2 + 3 * n_wsh,)),
    ]
    return pl.pallas_call(
        functools.partial(whole_kernel, dims),
        out_shape=outs,
        in_specs=[hbm] * 7 + [smem] * 2,
        out_specs=[hbm] * len(outs),
        scratch_shapes=scratch,
        compiler_params=pltpu.CompilerParams(
            collective_id=0, has_side_effects=True, vmem_limit_bytes=VMEM_BYTES
        ),
    )(tok, cot, wqkv, *w3, pack, order, lengths)


def head_split(
    tokens, cotangent, block_lengths, group_order, w_query, w_key, w_value, w_out, w_up, w_down,
    gain_attn, gain_mlp, query_scale,
):
    f32 = jnp.float32
    n_ctx, n_wsh = lax.axis_size("ctx"), lax.axis_size("wsh")
    c, z = lax.axis_index("ctx"), lax.axis_index("wsh")
    width = tokens.shape[2]
    hd, heads = width // H, H // n_ctx
    span, shard = hd * heads, width // n_wsh
    dims = (n_ctx, n_wsh, hd, heads)
    mine = [lax.dynamic_slice_in_dim(w, c * span, span, 1) for w in (w_query, w_key, w_value)]
    lanes = -(-3 * span // 128) * 128
    wqkv = jnp.pad(jnp.concatenate(mine, 1), ((0, 0), (0, lanes - 3 * span)))
    lanes = -(-shard // 128) * 128
    pack = jnp.concatenate(
        [jnp.pad(v.astype(f32), (0, lanes - v.shape[0]))[None] for v in (gain_attn, gain_mlp, query_scale)]
        + [jnp.zeros((5, lanes), f32)]
    )
    outputs, gtok, dwo, dwu, dwd, dwqkv, sums = whole_call(
        dims, tokens[0], cotangent[0], wqkv, (w_out, w_up, w_down), pack, group_order, block_lengths
    )[:7]
    starts, size = windows(width, n_wsh)
    at = z * shard - jnp.asarray(starts, jnp.int32)[z]
    dwqkv = dwqkv.reshape(n_ctx, 3, span, size)
    projections = [
        lax.dynamic_slice_in_dim(dwqkv[:, i], at, shard, 2).transpose(2, 0, 1).reshape(shard, width).astype(f32)
        for i in range(3)
    ]
    own = [lax.dynamic_slice_in_dim(sums[i], z * shard, shard, 0) for i in (0, 1)]
    scale_grad = (
        lax.dynamic_slice_in_dim(sums[2], z * (hd // n_wsh), hd // n_wsh, 0)
        * (LOG_BASE / math.sqrt(hd))
        * jax.nn.sigmoid(query_scale.astype(f32))
    )
    return (
        outputs.reshape(tokens.shape), gtok.reshape(tokens.shape), *projections,
        dwo.astype(f32), dwu.astype(f32), dwd.astype(f32), own[0], own[1], scale_grad,
    )


def solution(mesh):
    in_specs = (
        P("wsh", "ctx", None),
        P("wsh", "ctx", None),
        P("wsh", None),
        P(),
        P("wsh", None),
        P("wsh", None),
        P("wsh", None),
        P("wsh", None),
        P("wsh", None),
        P("wsh", None),
        P("wsh"),
        P("wsh"),
        P("wsh"),
    )
    out_specs = (
        P("wsh", "ctx", None),
        P("wsh", "ctx", None),
        P("wsh", None),
        P("wsh", None),
        P("wsh", None),
        P("wsh", None),
        P("wsh", None),
        P("wsh", None),
        P("wsh"),
        P("wsh"),
        P("wsh"),
    )
    n_ctx, n_wsh = mesh.shape["ctx"], mesh.shape["wsh"]
    plan = head_split if (n_ctx, n_wsh) == (8, 4) else per_device
    return jax.shard_map(
        plan, mesh=mesh, in_specs=in_specs, out_specs=out_specs, check_vma=False
    )
```

```python
import functools
import math

import jax
import jax.numpy as jnp
from jax import lax
from jax.experimental import pallas as pl
from jax.experimental.pallas import tpu as pltpu
from jax.sharding import PartitionSpec as P

H = 16


EPS = 1e-06
LOG_BASE = 1.442695041


def row_step():
    return 512


def rows_at(array, block_no, step_rows):
    return lax.dynamic_slice_in_dim(array, block_no * step_rows, step_rows, 0)


def inverse_rms(values):
    return lax.rsqrt(jnp.mean(values * values, -1, keepdims=True) + EPS)


def norm_back(normed, inverse, grad):
    return inverse * (grad - normed * jnp.mean(grad * normed, -1, keepdims=True))


def split_heads(matrix):
    return matrix.reshape(matrix.shape[0], H, -1)


def outer_product(left, right):
    return lax.dot_general(
        left, right, (((0,), (0,)), ((), ())), preferred_element_type=jnp.float32
    )


def back_product(grad, weight):
    return lax.dot_general(
        grad, weight, (((1,), (1,)), ((), ())), preferred_element_type=jnp.float32
    )


def probabilities(query3, key3, query_marks, key_marks, log_totals):
    scores = jnp.einsum("qhd,khd->hqk", query3, key3, preferred_element_type=jnp.float32)
    allowed = key_marks[None, None, :] <= query_marks[None, :, None]
    return jnp.exp(jnp.where(allowed, scores - log_totals[:, :, None], -jnp.inf))


def score_grads(chances, grad_out3, value3, deltas):
    grad_chances = jnp.einsum("qhd,khd->hqk", grad_out3, value3, preferred_element_type=jnp.float32)
    return (chances * (grad_chances - deltas[:, :, None])).astype(jnp.bfloat16)


def per_device(
    tokens,
    cotangent,
    block_lengths,
    group_order,
    w_query,
    w_key,
    w_value,
    w_out,
    w_up,
    w_down,
    gain_attn,
    gain_mlp,
    query_scale,
):
    gathered = (
        lax.all_gather(w_query, "wsh", axis=0, tiled=True),
        lax.all_gather(w_key, "wsh", axis=0, tiled=True),
        lax.all_gather(w_value, "wsh", axis=0, tiled=True),
        lax.all_gather(w_out, "wsh", axis=0, tiled=True),
        lax.all_gather(w_up, "wsh", axis=0, tiled=True),
        lax.all_gather(w_down, "wsh", axis=0, tiled=True),
        lax.all_gather(gain_attn, "wsh", axis=0, tiled=True),
        lax.all_gather(gain_mlp, "wsh", axis=0, tiled=True),
        lax.all_gather(query_scale, "wsh", axis=0, tiled=True),
    )
    (
        full_query,
        full_key,
        full_value,
        full_out,
        full_up,
        full_down,
        norm_attn,
        norm_mlp,
        scale_param,
    ) = gathered
    tok_rows = tokens.shape[1]
    model_width = tokens.shape[2]
    length = tok_rows * lax.axis_size("ctx")
    device = lax.axis_index("ctx")
    head_size = scale_param.shape[0]
    f32 = jnp.float32
    bf16 = jnp.bfloat16
    inputs = tokens.reshape(tok_rows, model_width).astype(f32)
    positions = (
        group_order[:, None] * tok_rows + jnp.arange(tok_rows, dtype=jnp.int32)[None, :]
    ).reshape(length)
    bounds = jnp.cumsum(block_lengths[0])
    block_ids = jnp.sum((bounds[None, :] <= positions[:, None]).astype(jnp.int32), -1)
    query_ids = lax.dynamic_slice_in_dim(block_ids, device * tok_rows, tok_rows, 0)
    inverse_one = inverse_rms(inputs)
    normed_one = inputs * inverse_one
    hidden_one = (normed_one * norm_attn.astype(f32)).astype(bf16)
    query_raw = jnp.dot(hidden_one, full_query, preferred_element_type=f32).reshape(
        tok_rows, H, head_size
    )
    query_gain = LOG_BASE / math.sqrt(head_size) * jax.nn.softplus(scale_param.astype(f32))
    query3 = (query_raw * query_gain).astype(bf16)
    key_flat = jnp.dot(hidden_one, full_key, preferred_element_type=f32).astype(bf16)
    value_flat = jnp.dot(hidden_one, full_value, preferred_element_type=f32).astype(bf16)
    initial = (
        jnp.full((H, tok_rows), -1e30, f32),
        jnp.zeros((H, tok_rows), f32),
        jnp.zeros((tok_rows, H, head_size), f32),
    )
    key_rows = lax.all_gather(key_flat, "ctx", axis=0, tiled=True)
    value_rows = lax.all_gather(value_flat, "ctx", axis=0, tiled=True)
    row_count = key_rows.shape[0]
    step_rows = row_step()

    def one_block(block_no, looped):
        key_part = split_heads(rows_at(key_rows, block_no, step_rows))
        value_part = split_heads(rows_at(value_rows, block_no, step_rows))
        block_marks = rows_at(block_ids, block_no, step_rows)
        maxima, totals, running = looped
        scores = jnp.einsum("qhd,khd->hqk", query3, key_part, preferred_element_type=f32)
        allowed = block_marks[None, None, :] <= query_ids[None, :, None]
        scores = jnp.where(allowed, scores, -jnp.inf)
        raised = jnp.maximum(maxima, jnp.max(scores, -1))
        rescale = jnp.exp(maxima - raised)
        weights = jnp.exp(scores - raised[:, :, None])
        totals = totals * rescale + jnp.sum(weights, -1)
        running = running * rescale.T[:, :, None] + jnp.einsum(
            "hqk,khd->qhd", weights.astype(bf16), value_part, preferred_element_type=f32
        )
        return (raised, totals, running)

    maxima, totals, running = lax.fori_loop(0, row_count // step_rows, one_block, initial)
    log_totals = maxima + jnp.log(totals)
    attended = running / totals.T[:, :, None]
    attended_bf = attended.reshape(tok_rows, model_width).astype(bf16)
    mixed = inputs + jnp.dot(attended_bf, full_out, preferred_element_type=f32)
    inverse_two = inverse_rms(mixed)
    normed_two = mixed * inverse_two
    hidden_two = (normed_two * norm_mlp.astype(f32)).astype(bf16)
    up_raw = jnp.dot(hidden_two, full_up, preferred_element_type=f32)
    active = jax.nn.silu(up_raw).astype(bf16)
    outputs = mixed + jnp.dot(active, full_down, preferred_element_type=f32)
    grad_output = cotangent.reshape(tok_rows, model_width).astype(f32)
    grad_mlp = grad_output.astype(bf16)
    grad_active = back_product(grad_mlp, full_down)
    sigmoid_up = jax.nn.sigmoid(up_raw)
    grad_up_raw = (grad_active * sigmoid_up * (1.0 + up_raw * (1.0 - sigmoid_up))).astype(bf16)
    grad_hidden_two = back_product(grad_up_raw, full_up)
    grad_gain_mlp = jnp.sum(grad_hidden_two * normed_two, 0)
    grad_mixed = grad_output + norm_back(
        normed_two, inverse_two, grad_hidden_two * norm_mlp.astype(f32)
    )
    grad_branch = grad_mixed.astype(bf16)
    grad_att = back_product(grad_branch, full_out).astype(bf16)
    grad_att3 = split_heads(grad_att)
    deltas = jnp.sum(grad_att3.astype(f32) * attended, -1).T
    key_whole, value_whole = (
        lax.all_gather(key_flat, "ctx", axis=0, tiled=True),
        lax.all_gather(value_flat, "ctx", axis=0, tiled=True),
    )
    step_rows = row_step()
    block_total = length // step_rows

    def key_block(grad_q, block_parts):
        key_rows, value_rows, block_marks = block_parts
        key_part = split_heads(key_rows)
        value_part = split_heads(value_rows)
        zero_part = jnp.zeros((key_rows.shape[0], H, head_size), f32)
        chances = probabilities(query3, key_part, query_ids, block_marks, log_totals)
        slopes = score_grads(chances, grad_att3, value_part, deltas)
        new_grad = (grad_q, zero_part, zero_part)[0] + jnp.einsum(
            "hqk,khd->qhd", slopes, key_part, preferred_element_type=f32
        )
        grad_key_part = jnp.einsum("hqk,qhd->khd", slopes, query3, preferred_element_type=f32)
        grad_value_part = jnp.einsum(
            "hqk,qhd->khd", chances.astype(bf16), grad_att3, preferred_element_type=f32
        )
        return (new_grad, (grad_key_part, grad_value_part))

    grad_qs, (key_terms, value_terms) = lax.scan(
        key_block,
        jnp.zeros((tok_rows, H, head_size), f32),
        (
            key_whole.reshape(block_total, step_rows, model_width),
            value_whole.reshape(block_total, step_rows, model_width),
            block_ids.reshape(block_total, step_rows),
        ),
    )
    grad_key, grad_value = (
        lax.psum_scatter(
            key_terms.reshape(length, model_width).astype(jnp.bfloat16),
            "ctx",
            scatter_dimension=0,
            tiled=True,
        ).astype(jnp.float32),
        lax.psum_scatter(
            value_terms.reshape(length, model_width).astype(jnp.bfloat16),
            "ctx",
            scatter_dimension=0,
            tiled=True,
        ).astype(jnp.float32),
    )
    grad_key_bf = grad_key.astype(bf16)
    grad_value_bf = grad_value.astype(bf16)
    grad_query_bf = (grad_qs * query_gain).reshape(tok_rows, model_width).astype(bf16)
    grad_scale_param = (
        jnp.sum(grad_qs * query_raw, (0, 1))
        * (LOG_BASE / math.sqrt(head_size))
        * jax.nn.sigmoid(scale_param.astype(f32))
    )
    grad_hidden_one = (
        back_product(grad_query_bf, full_query)
        + back_product(grad_key_bf, full_key)
        + back_product(grad_value_bf, full_value)
    )
    grad_gain_attn = jnp.sum(grad_hidden_one * normed_one, 0)
    grad_inputs = grad_mixed + norm_back(
        normed_one, inverse_one, grad_hidden_one * norm_attn.astype(f32)
    )
    grad_queryw = outer_product(hidden_one, grad_query_bf)
    grad_keyw = outer_product(hidden_one, grad_key_bf)
    grad_valuew = outer_product(hidden_one, grad_value_bf)
    grad_outw = outer_product(attended_bf, grad_branch)
    grad_upw = outer_product(hidden_two, grad_up_raw)
    grad_downw = outer_product(active, grad_mlp)
    owned = (
        lax.psum_scatter(
            grad_queryw.astype(jnp.bfloat16), "wsh", scatter_dimension=0, tiled=True
        ).astype(jnp.float32),
        lax.psum_scatter(
            grad_keyw.astype(jnp.bfloat16), "wsh", scatter_dimension=0, tiled=True
        ).astype(jnp.float32),
        lax.psum_scatter(
            grad_valuew.astype(jnp.bfloat16), "wsh", scatter_dimension=0, tiled=True
        ).astype(jnp.float32),
        lax.psum_scatter(
            grad_outw.astype(jnp.bfloat16), "wsh", scatter_dimension=0, tiled=True
        ).astype(jnp.float32),
        lax.psum_scatter(
            grad_upw.astype(jnp.bfloat16), "wsh", scatter_dimension=0, tiled=True
        ).astype(jnp.float32),
        lax.psum_scatter(
            grad_downw.astype(jnp.bfloat16), "wsh", scatter_dimension=0, tiled=True
        ).astype(jnp.float32),
        lax.psum_scatter(
            grad_gain_attn.astype(jnp.bfloat16), "wsh", scatter_dimension=0, tiled=True
        ).astype(jnp.float32),
        lax.psum_scatter(
            grad_gain_mlp.astype(jnp.bfloat16), "wsh", scatter_dimension=0, tiled=True
        ).astype(jnp.float32),
        lax.psum_scatter(
            grad_scale_param.astype(jnp.bfloat16), "wsh", scatter_dimension=0, tiled=True
        ).astype(jnp.float32),
    )
    summed = (
        lax.psum(owned[0].astype(jnp.bfloat16), "ctx").astype(jnp.float32),
        lax.psum(owned[1].astype(jnp.bfloat16), "ctx").astype(jnp.float32),
        lax.psum(owned[2].astype(jnp.bfloat16), "ctx").astype(jnp.float32),
        lax.psum(owned[3].astype(jnp.bfloat16), "ctx").astype(jnp.float32),
        lax.psum(owned[4].astype(jnp.bfloat16), "ctx").astype(jnp.float32),
        lax.psum(owned[5].astype(jnp.bfloat16), "ctx").astype(jnp.float32),
        lax.psum(owned[6].astype(jnp.bfloat16), "ctx").astype(jnp.float32),
        lax.psum(owned[7].astype(jnp.bfloat16), "ctx").astype(jnp.float32),
        lax.psum(owned[8].astype(jnp.bfloat16), "ctx").astype(jnp.float32),
    )
    return (
        outputs.reshape(tokens.shape).astype(bf16),
        grad_inputs.reshape(tokens.shape).astype(bf16),
        summed[0],
        summed[1],
        summed[2],
        summed[3],
        summed[4],
        summed[5],
        summed[6],
        summed[7],
        summed[8],
    )


MESH = pl.DeviceIdType.MESH
NEG = -1e30
VMEM_BYTES = 62 * 1024 * 1024


def place():
    c, z = lax.axis_index("ctx"), lax.axis_index("wsh")
    core, x, y = lax.rem(c, 2), lax.rem(c // 2, 2), c // 4
    sib = c + 1 - 2 * core
    over_x, over_y = c + 2 - 4 * x, c + 4 - 8 * y
    first = over_x * (1 - core) + over_y * core
    second = over_y * (1 - core) + over_x * core
    diag = over_x + over_y - c
    return c, z, sib, first, second, diag


def enter(c, z, n_ctx, n_wsh):
    barrier = pltpu.get_barrier_semaphore()
    for k in range(1, n_ctx):
        pl.semaphore_signal(
            barrier, inc=1, device_id=(lax.rem(c + k, n_ctx), z), device_id_type=MESH
        )
    for k in range(1, n_wsh):
        pl.semaphore_signal(
            barrier, inc=1, device_id=(c, lax.rem(z + k, n_wsh)), device_id_type=MESH
        )
    pl.semaphore_wait(barrier, n_ctx + n_wsh - 2)


def send(src, dst, send_sem, recv_sem, c, z):
    copy = pltpu.make_async_remote_copy(
        src_ref=src, dst_ref=dst, send_sem=send_sem, recv_sem=recv_sem,
        device_id=(c, z), device_id_type=MESH,
    )
    copy.start()
    return copy


def arrive(dst, send_sem, recv_sem, c, z):
    pltpu.make_async_remote_copy(
        src_ref=dst, dst_ref=dst, send_sem=send_sem, recv_sem=recv_sem,
        device_id=(c, z), device_id_type=MESH,
    ).wait_recv()


def left(src, send_sem, recv_sem, c, z):
    pltpu.make_async_remote_copy(
        src_ref=src, dst_ref=src, send_sem=send_sem, recv_sem=recv_sem,
        device_id=(c, z), device_id_type=MESH,
    ).wait_send()


class Line:
    def __init__(self, at, c, z, n, send_sem, recv_sem):
        self.at, self.c, self.z, self.n = at, c, z, n
        self.send_sem, self.recv_sem = send_sem, recv_sem

    def start(self, own):
        c, z = self.c, self.z

        @pl.when(z < self.n - 1)
        def _():
            send(own, self.at(z), self.send_sem.at[0], self.recv_sem.at[z], c, z + 1)

        @pl.when(z > 0)
        def _():
            send(own, self.at(z), self.send_sem.at[1], self.recv_sem.at[z], c, z - 1)

    def forward(self, distance, then=None):
        c, z, n = self.c, self.z, self.n
        below, above = z - distance, z + distance

        @pl.when(below >= 0)
        def _():
            arrive(self.at(below), self.send_sem.at[0], self.recv_sem.at[below], c, z)

            @pl.when(z < n - 1)
            def _():
                send(self.at(below), self.at(below), self.send_sem.at[2 * distance], self.recv_sem.at[below], c, z + 1)

            if then is not None:
                then(below)

        @pl.when(above < n)
        def _():
            arrive(self.at(above), self.send_sem.at[0], self.recv_sem.at[above], c, z)

            @pl.when(z > 0)
            def _():
                send(self.at(above), self.at(above), self.send_sem.at[2 * distance + 1], self.recv_sem.at[above], c, z - 1)

            if then is not None:
                then(above)

    def finish(self, own):
        c, z, n = self.c, self.z, self.n

        @pl.when(z < n - 1)
        def _():
            left(own, self.send_sem.at[0], self.recv_sem.at[z], c, z)

        @pl.when(z > 0)
        def _():
            left(own, self.send_sem.at[1], self.recv_sem.at[z], c, z)

        for distance in range(1, n):
            below, above = z - distance, z + distance

            @pl.when((below >= 0) & (z < n - 1))
            def _():
                left(self.at(below), self.send_sem.at[2 * distance], self.recv_sem.at[below], c, z)

            @pl.when((above < n) & (z > 0))
            def _():
                left(self.at(above), self.send_sem.at[2 * distance + 1], self.recv_sem.at[above], c, z)


class Plane:
    def __init__(self, at, c, z, around, send_sem, recv_sem):
        self.at, self.c, self.z = at, c, z
        self.sib, self.first, self.second, self.diag = around
        self.send_sem, self.recv_sem = send_sem, recv_sem

    def push(self, slot, block, target, src=None):
        src = self.at(block) if src is None else src
        send(src, self.at(block), self.send_sem.at[slot], self.recv_sem.at[block], target, self.z)

    def wait(self, block):
        arrive(self.at(block), self.send_sem.at[0], self.recv_sem.at[block], self.c, self.z)

    def start(self, own=None):
        self.push(0, self.c, self.first, own)
        self.push(1, self.c, self.second, own)
        self.push(2, self.c, self.sib, own)

    def from_first(self):
        self.wait(self.first)
        self.push(3, self.first, self.second)
        self.push(4, self.first, self.sib)

    def from_second(self):
        self.wait(self.second)
        self.push(5, self.second, self.sib)

    def from_diag(self):
        self.wait(self.diag)
        self.push(6, self.diag, self.sib)

    def others(self):
        shift = self.sib - self.c
        return (self.sib, self.second + shift, self.first + shift, self.diag + shift)

    def finish(self):
        for slot in range(7):
            left(self.at(self.c), self.send_sem.at[slot], self.recv_sem.at[self.c], self.c, self.z)


def block_ids_of(block, order_ref, lengths_ref, rows):
    n_blk = lengths_ref.shape[1]
    position = order_ref[block] * rows + lax.broadcasted_iota(jnp.int32, (8, rows), 1)
    ids = jnp.zeros((8, rows), jnp.int32)
    bound = jnp.int32(0)
    for b in range(n_blk):
        bound = bound + lengths_ref[0, b]
        ids = ids + jnp.where(position >= bound, 1, 0)
    return ids, lax.broadcasted_iota(jnp.int32, (8, rows), 0)


def three_rows(value, rows):
    f32 = jnp.float32
    high = value.astype(jnp.bfloat16).astype(f32)
    rest = value - high
    mid = rest.astype(jnp.bfloat16).astype(f32)
    low = rest - mid
    row = lax.broadcasted_iota(jnp.int32, (8, rows), 0)
    return jnp.where(row == 0, high, 0.0) + jnp.where(row == 1, mid, 0.0) + jnp.where(row == 2, low, 0.0)


def add_rows(target, at, other, other_at, rows, step):
    f32 = jnp.float32

    def some_rows(i, _):
        here = pl.ds(pl.multiple_of(at + i * step, 16), step)
        there = pl.ds(pl.multiple_of(other_at + i * step, 16), step)
        target[here, :] = (target[here, :].astype(f32) + other[there, :].astype(f32)).astype(target.dtype)
        return 0

    lax.fori_loop(0, rows // step, some_rows, 0)


def windows(width, n):
    part = width // n
    tiles = -(-part // 128) + (0 if part % 128 == 0 else 0)
    size = tiles * 128
    return [min(s * part // 128 * 128, width - size) for s in range(n)], size


def whole_kernel(
    dims,
    tok_ref, cot_ref, wqkv_ref, wout_ref, wup_ref, wdown_ref, pack_ref, order_ref, lengths_ref,
    out_out, gtok_out, dw3_out, dwqkv_out, vec_out,
    h1_all, w_full, big, w_c, packs, gains, kaug, vaug, kt, qaug, qraw, o_all, ob_stage, ob_land, go_stage, go_land,
    acc, land_f, land_s, land_near, land_far, win_out, win_near, win_far,
    dx, dh, tok, cot, gtok, vec, vec_plane, vec_line, vec_mid, vec_sum, scale_acc,
    tok_send, tok_recv, wz_send, wz_recv, pk_send, pk_recv, ob_send, ob_recv,
    w3z_send, w3z_recv, w3p_send, w3p_recv,
    go_send, go_recv, p_send, p_recv, f_send, f_recv, s_send, s_recv, zn_send, zn_recv, zf_send, zf_recv, g_send, g_recv,
    hp_send, hp_recv, hf_send, hf_recv, hs_send, hs_recv, wn_send, wn_recv, wf_send, wf_recv, wg_send, wg_recv,
    vp_send, vp_recv, vl_send, vl_recv, local_sem, load_sem,
):
    n_ctx, n_wsh, hd, heads = dims
    f32, bf16 = jnp.float32, jnp.bfloat16
    c, z, sib, first, second, diag = place()
    around = (sib, first, second, diag)
    core, x, y = lax.rem(c, 2), lax.rem(c // 2, 2), c // 4
    f_bit, s_bit = x * (1 - core) + y * core, y * (1 - core) + x * core
    rows, width = tok_ref.shape
    span, length = hd * heads, rows * n_ctx
    shard, half = width // n_wsh, width // 2
    two, cut = shard // 2, shard // (n_ctx // 2)
    w3_refs = (wout_ref, wup_ref, wdown_ref)
    OUT, UP, DOWN = 0, 1, 2
    from_first, from_second, from_diag = Plane.from_first, Plane.from_second, Plane.from_diag
    enter(c, z, n_ctx, n_wsh)

    part_rows = rows // 2
    tokens = [
        Plane(
            lambda b, i=i: big.at[pl.ds(pl.multiple_of(b * rows + i * part_rows, 16), part_rows)], c, z, around,
            tok_send.at[i], tok_recv.at[i],
        )
        for i in range(2)
    ]
    for i in range(2):
        tokens[i].start(tok_ref.at[pl.ds(i * part_rows, part_rows)])
    wline = Line(lambda s: w_c.at[pl.ds(pl.multiple_of(s * shard, 16), shard)], c, z, n_wsh, wz_send, wz_recv)
    for k in range(1, n_wsh):
        send(pack_ref, packs.at[z], pk_send.at[k], pk_recv.at[z], c, lax.rem(z + k, n_wsh))
    wline.start(wqkv_ref)
    own_tok = pltpu.make_async_copy(tok_ref, tok, local_sem.at[0])
    own_w = pltpu.make_async_copy(wqkv_ref, wline.at(z), local_sem.at[1])
    own_pack = pltpu.make_async_copy(pack_ref, packs.at[z], local_sem.at[2])
    own_cot = pltpu.make_async_copy(cot_ref, cot, local_sem.at[3])
    own_full = [
        pltpu.make_async_copy(
            w3_refs[w], w_full.at[w, pl.ds(pl.multiple_of(z * shard, 16), shard)], load_sem.at[heads + w]
        )
        for w in range(3)
    ]
    for copy in (own_tok, own_pack, own_w, own_cot, *own_full):
        copy.start()
    vec[...] = jnp.zeros_like(vec)
    scale_acc[...] = jnp.zeros_like(scale_acc)

    def columns(b):
        return pl.ds(pl.multiple_of(lax.rem(b, 2) * half, 128), half)

    def piece(w, s, b):
        top = pl.multiple_of(s * shard + (b // 2) * cut, 16)
        return w_full.at[w, pl.ds(top, cut), columns(b)]

    my_piece = [ref.at[pl.ds(pl.multiple_of((c // 2) * cut, 16), cut), columns(c)] for ref in w3_refs]
    lines = [
        Line(lambda s, w=w: piece(w, s, c), c, z, n_wsh, w3z_send.at[w], w3z_recv.at[w]) for w in range(3)
    ]

    def plane_of(w, s):
        k = lax.rem(s - z + n_wsh, n_wsh)
        return Plane(lambda b: piece(w, s, b), c, z, around, w3p_send.at[w, k], w3p_recv.at[w, k])

    def shards_at(distance, step, weights=(0, 1, 2)):
        below, above = z - distance, z + distance

        @pl.when(below >= 0)
        def _():
            for w in weights:
                step(plane_of(w, below))

        @pl.when(above < n_wsh)
        def _():
            for w in weights:
                step(plane_of(w, above))

    def spread(distance):
        for w in range(3):
            lines[w].forward(distance, lambda s, w=w: plane_of(w, s).start())

    def all_others(plane):
        for b in plane.others():
            plane.wait(b)

    own_tok.wait()
    own_pack.wait()
    for k in range(1, n_wsh):
        other = lax.rem(z + k, n_wsh)
        arrive(packs.at[other], pk_send.at[0], pk_recv.at[other], c, z)
    row8 = lax.broadcasted_iota(jnp.int32, (8, width), 0)
    total = jnp.zeros((8, width), f32)
    for s in range(n_wsh):
        wide = jnp.concatenate([packs[s], jnp.zeros((8, width - packs.shape[2]), f32)], axis=1)
        by_shard = pltpu.roll(wide, s * shard, 1) if s else wide
        by_dim = pltpu.roll(wide, s * (hd // n_wsh), 1) if s else wide
        total = total + jnp.where(row8 < 2, by_shard, by_dim)
    gains[...] = total

    def gain_column():
        scale = jnp.concatenate([gains[2:3, 0:128], jnp.zeros((7, 128), f32)], axis=0)
        soft = jnp.maximum(scale, 0.0) + jnp.log(1.0 + jnp.exp(-jnp.abs(scale)))
        return (LOG_BASE / math.sqrt(hd) * soft).T[0:hd, 0:1]

    def attention_forward(vt, qneg, s_buf):
        def norm_block(b, source, top):
            gain = gains[0:1, :]

            def some_rows(i, _):
                t = source[pl.ds(pl.multiple_of(top + i * 32, 32), 32), :].astype(f32)
                inverse = lax.rsqrt(jnp.mean(t * t, -1, keepdims=True) + EPS)
                h1_all[b, pl.ds(pl.multiple_of(i * 32, 32), 32), :] = (t * inverse * gain).astype(bf16)
                return 0

            lax.fori_loop(0, rows // 32, some_rows, 0)

        def norm_arrived(b):
            norm_block(b, big, b * rows)

        def arrived(b):
            for i in range(2):
                tokens[i].wait(b)
            norm_arrived(b)

        others = tokens[0].others()
        norm_block(c, tok, 0)
        arrived(others[0])
        tokens[0].from_first()
        wline.forward(1)
        tokens[1].from_first()
        norm_arrived(first)
        tokens[0].from_second()
        tokens[1].from_second()
        norm_arrived(second)
        wline.forward(2)
        for w in range(3):
            lines[w].start(my_piece[w])
        arrived(others[1])
        arrived(others[2])
        tokens[0].from_diag()
        tokens[1].from_diag()
        norm_arrived(diag)
        arrived(others[3])
        wline.forward(3)
        own_w.wait()
        spread(1)
        gain_col = gain_column()

        def project(b, _):
            raw = jnp.dot(h1_all[b], w_c[...], preferred_element_type=f32).T
            at = pl.ds(pl.multiple_of(b * rows, 128), rows)
            ids, row = block_ids_of(b, order_ref, lengths_ref, rows)
            hot = jnp.where(ids == row, 1.0, 0.0)
            neg = jnp.where(row > ids, NEG, 0.0)
            ones = jnp.ones((8, rows), f32)
            qneg[b] = neg
            for h in range(heads):
                top = 3 * h * hd
                q = raw[top : top + hd]
                qraw[b, h * hd : (h + 1) * hd, :] = q
                q = q * gain_col
                qaug[b, h, 0:hd, :] = q.astype(bf16)
                qaug[b, h, hd : hd + 16, :] = jnp.concatenate([neg, jnp.zeros((8, rows), f32)], axis=0).astype(bf16)
                qaug[b, h, hd + 16 : 128, :] = jnp.zeros((112 - hd, rows), bf16)
                k = raw[top + hd : top + 2 * hd].astype(bf16)
                v = raw[top + 2 * hd : top + 3 * hd].astype(bf16)
                tail = jnp.zeros((112 - hd, rows), f32)
                kt[h, :, at] = k
                vt[h, 0:hd, at] = v
                vt[h, hd : hd + 16, at] = jnp.ones((16, rows), bf16)
                kaug[h, at, :] = jnp.concatenate([k.astype(f32), hot, ones, tail], axis=0).T.astype(bf16)
                vaug[h, at, :] = jnp.concatenate([v.astype(f32), ones, ones, tail], axis=0).T.astype(bf16)
            return 0

        lax.fori_loop(0, n_ctx, project, 0)
        for i in range(2):
            tokens[i].finish()
        keys = length // 2
        events = (
            ((0, lambda: spread(2)), (2, lambda: shards_at(1, from_first)), (4, lambda: shards_at(1, from_second))),
            ((3, lambda: spread(3)), (5, lambda: shards_at(2, from_first)), (6, lambda: shards_at(1, from_diag))),
        )

        def attend(i, _):
            g = lax.rem(c + 1 + i, n_ctx)
            for h in range(heads):
                q = qaug[g, h]
                top = jnp.full((1, rows), -jnp.inf, f32)
                for j in range(2):
                    s = jnp.dot(kaug[h, j * keys : (j + 1) * keys, :], q, preferred_element_type=f32)
                    s_buf[j * keys : (j + 1) * keys, :] = s
                    top = jnp.maximum(top, jnp.max(s, axis=0, keepdims=True))
                out = jnp.zeros((hd + 16, rows), f32)
                for j in range(2):
                    p = jnp.exp(s_buf[j * keys : (j + 1) * keys, :] - top).astype(bf16)
                    out = out + jnp.dot(vt[h, :, j * keys : (j + 1) * keys], p, preferred_element_type=f32)
                total = out[hd : hd + 1]
                o = out[0:hd] / total
                lse = top + jnp.log(total)
                o_all[g, h * hd : (h + 1) * hd, :] = o
                ob_stage[g, h * hd : (h + 1) * hd, :] = o.astype(bf16)
                qaug[g, h, hd : hd + 16, :] = jnp.concatenate([qneg[g], three_rows(-lse, rows)], axis=0).astype(bf16)
                for step, event in events[h]:
                    pl.when(i == step)(event)

            @pl.when(i < n_ctx - 1)
            def _():
                send(ob_stage.at[g], my_heads(ob_land), ob_send.at[g], ob_recv.at[c], g, z)

            return 0

        lax.fori_loop(0, n_ctx, attend, 0)

    def my_heads(ref):
        return ref.at[pl.ds(pl.multiple_of(c * span, 16), span)]

    def heads_of(ref, g):
        return ref.at[pl.ds(pl.multiple_of(g * span, 16), span)]

    vm = pltpu.VMEM
    pl.run_scoped(
        attention_forward,
        vm((heads, hd + 16, length), bf16), vm((n_ctx, 8, rows), f32), vm((length, rows), f32),
    )
    own_o = pltpu.make_async_copy(ob_stage.at[c], my_heads(ob_land), local_sem.at[4])
    own_o.start()

    mine = pl.ds(pl.multiple_of(core * half, 128), half)
    theirs = pl.ds(pl.multiple_of((1 - core) * half, 128), half)
    my_top = f_bit * two + s_bit * cut
    near, far = z + 1 - 2 * lax.rem(z, 2), z + 2 - 4 * (z // 2)

    def pair_at(w):
        return big.at[pl.ds(2 * w * shard, 2 * shard)]

    def pair_sum(w):
        arrive(pair_at(w), p_send.at[w], p_recv.at[w], c, z)
        for s in range(n_wsh):
            other = big.at[:, pl.ds(s % 2 * half, half)]
            add_rows(acc.at[w, s], 0, other, (2 * w + s // 2) * shard, shard, 64)
        at = pl.ds(pl.multiple_of((1 - f_bit) * two, 16), two)
        send(acc.at[w, :, at], land_f.at[w], f_send.at[w], f_recv.at[w], first, z)

    def first_sum(w):
        arrive(land_f.at[w], f_send.at[w], f_recv.at[w], c, z)
        for s in range(n_wsh):
            add_rows(acc.at[w, s], f_bit * two, land_f.at[w, s], 0, two, 80)
        at = pl.ds(pl.multiple_of(f_bit * two + (1 - s_bit) * cut, 16), cut)
        send(acc.at[w, :, at], land_s.at[w], s_send.at[w], s_recv.at[w], second, z)

    def second_sum(w):
        arrive(land_s.at[w], s_send.at[w], s_recv.at[w], c, z)
        for s in range(n_wsh):
            add_rows(acc.at[w, s], my_top, land_s.at[w, s], 0, cut, 80)
        at = pl.ds(pl.multiple_of(my_top, 16), cut)
        for j in range(2):
            s = 2 * j + lax.rem(near, 2)
            send(acc.at[w, s, at], land_near.at[w, j], zn_send.at[w, j], zn_recv.at[w, j], c, near)

    def near_sum(w):
        for j in range(2):
            arrive(land_near.at[w, j], zn_send.at[w, j], zn_recv.at[w, j], c, z)
            add_rows(acc.at[w, 2 * j + lax.rem(z, 2)], my_top, land_near.at[w, j], 0, cut, 80)
        at = pl.ds(pl.multiple_of(my_top, 16), cut)
        send(acc.at[w, far, at], land_far.at[w], zf_send.at[w], zf_recv.at[w], c, far)

    def out_piece(w, b):
        b_core, b_x, b_y = lax.rem(b, 2), lax.rem(b // 2, 2), b // 4
        r = (1 - b_core) * (2 * b_x + b_y) + b_core * (2 * b_y + b_x)
        return dw3_out.at[w, pl.ds(pl.multiple_of(r * cut, 16), cut), columns(b)]

    planes = [
        Plane(lambda b, w=w: out_piece(w, b), c, z, around, g_send.at[w], g_recv.at[w]) for w in range(3)
    ]

    def final_piece(w):
        return acc.at[w, z, pl.ds(pl.multiple_of(my_top, 16), cut)]

    def far_sum(w):
        arrive(land_far.at[w], zf_send.at[w], zf_recv.at[w], c, z)
        add_rows(acc.at[w, z], my_top, land_far.at[w], 0, cut, 80)
        planes[w].start(final_piece(w))
        pltpu.make_async_copy(final_piece(w), out_piece(w, c), local_sem.at[8 + w]).start()

    def feed_forward(x1, h2, a, gu, ob, turned, ga, inv2, outb, stage):
        def tiles(step, size=256):
            def one(i, _):
                step(pl.ds(pl.multiple_of(i * size, size), size))
                return 0

            lax.fori_loop(0, width // size, one, 0)

        def turn(source, target):
            def one(at):
                target[at, :] = source[:, at].T

            tiles(one, 128)

        def weight_gradient(w, left_t, right):
            for s in range(n_wsh):
                stage[w, s // 2 * shard : (s // 2 + 1) * shard, s % 2 * half : (s % 2 + 1) * half] = jnp.dot(
                    left_t[s * shard : (s + 1) * shard, :], right[:, theirs], preferred_element_type=f32
                ).astype(bf16)
            send(stage.at[w], pair_at(w), p_send.at[w], p_recv.at[w], sib, z)
            for s in range(n_wsh):
                at = slice(s * shard, (s + 1) * shard)
                acc[w, s] = jnp.dot(left_t[at, :], right[:, mine], preferred_element_type=f32).astype(bf16)

        shards_at(3, from_first, (OUT,))
        shards_at(2, from_second, (OUT,))
        shards_at(3, from_second, (OUT,))
        shards_at(2, from_diag, (OUT,))
        shards_at(3, from_diag, (OUT,))
        shards_at(3, from_first, (UP, DOWN))
        shards_at(2, from_second, (UP, DOWN))
        for distance in range(1, n_wsh):
            shards_at(distance, all_others, (OUT,))
        own_o.wait()
        for k in range(1, n_ctx):
            g = lax.rem(c + k, n_ctx)
            arrive(heads_of(ob_land, g), ob_send.at[0], ob_recv.at[g], c, z)

        def turn_ob(at):
            ob[:, at] = ob_land[at, :].T

        tiles(turn_ob, 128)
        shards_at(3, from_second, (UP, DOWN))
        shards_at(2, from_diag, (UP, DOWN))
        own_full[OUT].wait()

        def mix(at):
            x1[:, at] = tok[:, at].astype(f32) + jnp.dot(ob[...], w_full[OUT, :, at], preferred_element_type=f32)

        tiles(mix)
        shards_at(3, from_diag, (UP, DOWN))
        for distance in range(1, n_wsh):
            shards_at(distance, all_others, (UP, DOWN))

        def norm_rows(i, _):
            at = pl.ds(pl.multiple_of(i * 32, 32), 32)
            t = x1[at, :]
            inverse = lax.rsqrt(jnp.mean(t * t, -1, keepdims=True) + EPS)
            inv2[at, :] = jnp.broadcast_to(inverse, (32, 128))
            h2[at, :] = (t * inverse * gains[1:2, :]).astype(bf16)
            return 0

        lax.fori_loop(0, rows // 32, norm_rows, 0)
        own_cot.wait()
        own_full[UP].wait()
        own_full[DOWN].wait()

        def hidden(at):
            up = jnp.dot(h2[...], w_full[UP, :, at], preferred_element_type=f32)
            da = lax.dot_general(
                cot[...], w_full[DOWN, at, :], (((1,), (1,)), ((), ())), preferred_element_type=f32
            )
            sig = 1.0 / (1.0 + jnp.exp(-up))
            act = up * sig
            a[:, at] = act.astype(bf16)
            turned[at, :] = act.T.astype(bf16)
            gu[:, at] = (da * sig * (1.0 + up * (1.0 - sig))).astype(bf16)

        tiles(hidden)
        weight_gradient(DOWN, turned, cot)

        def back(at):
            dh[:, at] = lax.dot_general(
                gu[...], w_full[UP, at, :], (((1,), (1,)), ((), ())), preferred_element_type=f32
            )

        tiles(back)

        def norm_back_rows(i, total):
            at = pl.ds(pl.multiple_of(i * 16, 16), 16)
            inverse = inv2[at, 0:1]
            normed = x1[at, :] * inverse
            grad = dh[at, :]
            both = grad * normed
            slope = jnp.mean(both * gains[1:2, :], -1, keepdims=True)
            result = cot[at, :].astype(f32) + inverse * (grad * gains[1:2, :] - normed * slope)
            dx[at, :] = result
            ga[at, :] = result.astype(bf16)
            return total + both

        gain_sum = lax.fori_loop(0, rows // 16, norm_back_rows, jnp.zeros((16, width), f32))
        vec[1:2, :] = jnp.sum(gain_sum, axis=0, keepdims=True)

        def back_out(at):
            go_stage[at, :] = lax.dot_general(
                w_full[OUT, at, :], ga[...], (((1,), (1,)), ((), ())), preferred_element_type=f32
            ).astype(bf16)

        tiles(back_out)
        for w in range(3):
            lines[w].finish(my_piece[w])
        for distance in range(1, n_wsh):
            shards_at(distance, Plane.finish)
        for k in range(1, n_ctx):
            g = lax.rem(c + k, n_ctx)
            send(heads_of(go_stage, g), go_land.at[c], go_send.at[k], go_recv.at[c], g, z)
        pltpu.make_async_copy(my_heads(go_stage), go_land.at[c], local_sem.at[5]).start()
        pair_sum(DOWN)
        turn(h2, turned)
        weight_gradient(UP, turned, gu)
        weight_gradient(OUT, ob_land, ga)

        def finish(at):
            outb[:, at] = (
                x1[:, at] + jnp.dot(a[...], w_full[DOWN, :, at], preferred_element_type=f32)
            ).astype(bf16)

        tiles(finish)
        own_out = pltpu.make_async_copy(outb, out_out, local_sem.at[6])
        own_out.start()
        pair_sum(UP)
        pair_sum(OUT)
        own_out.wait()
        for w in range(3):
            left(stage.at[w], p_send.at[w], p_recv.at[w], c, z)

    wide = (rows, width)
    pl.run_scoped(
        feed_forward,
        vm(wide, f32), vm(wide, bf16), vm(wide, bf16), vm(wide, bf16), vm(wide, bf16),
        vm((width, rows), bf16), vm(wide, bf16), vm((rows, 128), f32), vm(wide, bf16),
        vm((3, 2 * shard, width), bf16),
    )

    def attention_backward(goaug, go_tm, q_tm, dk, dv, dqkv):
        per = width // rows

        def block(i):
            return w_full.at[i // per, :, pl.ds(pl.multiple_of(lax.rem(i, per) * rows, 128), rows)]

        def part_p(i):
            return block(i)

        def part_f(i):
            return block(n_ctx // 2 + i)

        part_s = block(jnp.int32(n_ctx // 2 + 2))

        def part(b):
            return block(n_ctx // 2 + 3 + b)

        dk[...] = jnp.zeros_like(dk)
        dv[...] = jnp.zeros_like(dv)
        dqkv[3 * span :, :] = jnp.zeros((dqkv.shape[0] - 3 * span, length), bf16)
        gain_col = gain_column()

        def prepare(g):
            at = pl.ds(pl.multiple_of(g * rows, 16), rows)
            for h in range(heads):
                go = go_land[g, h * hd : (h + 1) * hd, :]
                wide = go.astype(f32)
                delta = jnp.sum(wide * o_all[g, h * hd : (h + 1) * hd, :], axis=0, keepdims=True)
                tail = jnp.concatenate([three_rows(-delta, rows), jnp.zeros((120 - hd, rows), f32)], axis=0)
                goaug[g, h, 0:hd, :] = go
                goaug[g, h, hd:128, :] = tail.astype(bf16)
                go_tm[h, at, :] = jnp.concatenate([wide, jnp.zeros((128 - hd, rows), f32)], axis=0).T.astype(bf16)
                q = qaug[g, h, 0:hd, :].astype(f32)
                q_tm[h, at, :] = jnp.concatenate([q, jnp.zeros((128 - hd, rows), f32)], axis=0).T.astype(bf16)

        pltpu.make_async_copy(my_heads(go_stage), go_land.at[c], local_sem.at[5]).wait()
        prepare(c)

        def prepare_other(k, _):
            g = lax.rem(c + k, n_ctx)
            arrive(go_land.at[g], go_send.at[0], go_recv.at[g], c, z)
            prepare(g)
            return 0

        lax.fori_loop(1, n_ctx, prepare_other, 0)
        chunk = length // 2
        three = 3 * hd
        starts, size = windows(width, n_wsh)

        def head_gradients(h, events):
            def attend(g, _):
                at = pl.ds(pl.multiple_of(g * rows, 16), rows)
                dq = jnp.zeros((hd, rows), f32)
                for j in range(2):
                    keys = slice(j * chunk, (j + 1) * chunk)
                    p = jnp.exp(jnp.dot(kaug[h, keys, :], qaug[g, h], preferred_element_type=f32))
                    ds = (p * jnp.dot(vaug[h, keys, :], goaug[g, h], preferred_element_type=f32)).astype(bf16)
                    dq = dq + jnp.dot(kt[h, :, keys], ds, preferred_element_type=f32)
                    dk[h, keys, :] += jnp.dot(ds, q_tm[h, at, :], preferred_element_type=f32)
                    dv[h, keys, :] += jnp.dot(p.astype(bf16), go_tm[h, at, :], preferred_element_type=f32)
                scale_acc[...] += dq * qraw[g, h * hd : (h + 1) * hd, :]
                lanes = pl.ds(pl.multiple_of(g * rows, 128), rows)
                dqkv[h * three : h * three + hd, lanes] = (dq * gain_col).astype(bf16)
                for step, event in events:
                    pl.when(g == step)(event)
                return 0

            lax.fori_loop(0, n_ctx, attend, 0)

            def settle(g, _):
                at = pl.ds(pl.multiple_of(g * rows, 16), rows)
                lanes = pl.ds(pl.multiple_of(g * rows, 128), rows)
                for i, source in enumerate((dk, dv)):
                    turned = source[h, at, :].T
                    top = h * three + (i + 1) * hd
                    dqkv[top : top + hd, lanes] = turned[0:hd].astype(bf16)
                return 0

            lax.fori_loop(0, n_ctx, settle, 0)
            for s in range(n_wsh):
                total = jnp.zeros((three, size), f32)
                for b in range(n_ctx):
                    total = total + jnp.dot(
                        dqkv[h * three : (h + 1) * three, b * rows : (b + 1) * rows],
                        h1_all[b, :, starts[s] : starts[s] + size], preferred_element_type=f32,
                    )
                win_out[h, s] = total.astype(bf16)
            for j in range(2):
                s = 2 * j + lax.rem(near, 2)
                send(win_out.at[h, s], win_near.at[h, j], wn_send.at[h, j], wn_recv.at[h, j], c, near)

        def near_window(h):
            for j in range(2):
                arrive(win_near.at[h, j], wn_send.at[h, j], wn_recv.at[h, j], c, z)
                add_rows(win_out.at[h, 2 * j + lax.rem(z, 2)], 0, win_near.at[h, j], 0, three, 80)
            send(win_out.at[h, far], win_far.at[h], wf_send.at[h], wf_recv.at[h], c, far)

        plane_w = [
            Plane(lambda b, h=h: dwqkv_out.at[b, h], c, z, around, wg_send.at[h], wg_recv.at[h]) for h in range(heads)
        ]

        def own_window(h):
            return pltpu.make_async_copy(win_out.at[h, z], dwqkv_out.at[c, h], load_sem.at[h])

        def far_window(h):
            arrive(win_far.at[h], wf_send.at[h], wf_recv.at[h], c, z)
            add_rows(win_out.at[h, z], 0, win_far.at[h], 0, three, 80)
            plane_w[h].start(win_out.at[h, z])
            own_window(h).start()

        head_gradients(0, ((3, lambda: first_sum(DOWN)), (7, lambda: second_sum(DOWN))))
        head_gradients(1, (
            (0, lambda: first_sum(UP)), (3, lambda: near_sum(DOWN)), (4, lambda: second_sum(UP)),
            (5, lambda: near_window(0)), (7, lambda: first_sum(OUT)),
        ))

        def partial(b):
            lanes = pl.ds(pl.multiple_of(b * rows, 128), rows)
            part(b)[...] = jnp.dot(w_c[...], dqkv[:, lanes], preferred_element_type=f32).astype(bf16)

        def to_sib(i, _):
            b = 2 * i + (1 - core)
            partial(b)
            send(part(b), part_p(i), hp_send.at[i], hp_recv.at[i], sib, z)
            return 0

        lax.fori_loop(0, n_ctx // 2, to_sib, 0)
        far_sum(DOWN)
        near_sum(UP)

        def own_core(i, _):
            partial(2 * i + core)
            return 0

        lax.fori_loop(0, n_ctx // 2, own_core, 0)

        def pair(i, b):
            arrive(part_p(b // 2), hp_send.at[0], hp_recv.at[b // 2], c, z)
            add_rows(part(b), 0, part_p(b // 2), 0, width, 128)
            if i < 2:
                slot = s_bit if i == 0 else 1 - s_bit
                send(part(b), part_f(slot), hf_send.at[i], hf_recv.at[slot], first, z)

        pair(1, diag)
        pair(0, first)
        second_sum(OUT)
        far_window(0)
        pair(2, second)
        pair(3, c)
        near_window(1)
        far_sum(UP)
        near_sum(OUT)
        arrive(part_f(1 - s_bit), hf_send.at[0], hf_recv.at[1 - s_bit], c, z)
        add_rows(part(second), 0, part_f(1 - s_bit), 0, width, 128)
        send(part(second), part_s, hs_send.at[0], hs_recv.at[0], second, z)
        planes[DOWN].from_first()
        planes[DOWN].from_second()
        arrive(part_f(s_bit), hf_send.at[0], hf_recv.at[s_bit], c, z)
        add_rows(part(c), 0, part_f(s_bit), 0, width, 128)
        far_window(1)
        far_sum(OUT)
        planes[DOWN].from_diag()
        plane_w[0].from_first()
        plane_w[0].from_second()
        planes[UP].from_first()
        planes[UP].from_second()
        arrive(part_s, hs_send.at[0], hs_recv.at[0], c, z)

        mine_part = part(c)

        def turn_dh(i, _):
            at = pl.ds(pl.multiple_of(i * 128, 128), 128)
            dh[:, at] = (mine_part[at, :].astype(f32) + part_s[at, :].astype(f32)).T
            return 0

        lax.fori_loop(0, width // 128, turn_dh, 0)

        def last_rows(i, total):
            at = pl.ds(pl.multiple_of(i * 16, 16), 16)
            t = tok[at, :].astype(f32)
            inverse = lax.rsqrt(jnp.mean(t * t, -1, keepdims=True) + EPS)
            normed = t * inverse
            grad = dh[at, :]
            both = grad * normed
            slope = jnp.mean(both * gains[0:1, :], -1, keepdims=True)
            gtok[at, :] = (dx[at, :] + inverse * (grad * gains[0:1, :] - normed * slope)).astype(bf16)
            return total + both

        gain_sum = lax.fori_loop(0, rows // 16, last_rows, jnp.zeros((16, width), f32))
        scale_sum = jnp.sum(scale_acc[...], axis=1, keepdims=True)
        scale_row = jnp.concatenate(
            [jnp.broadcast_to(scale_sum, (hd, 128)), jnp.zeros((128 - hd, 128), f32)], axis=0
        ).T[0:1, :]
        vec[0:1, :] = jnp.sum(gain_sum, axis=0, keepdims=True)
        vec[2:3, 0:128] = scale_row
        own_gtok = pltpu.make_async_copy(gtok, gtok_out, local_sem.at[11])
        own_gtok.start()
        for k in range(1, n_ctx):
            g = lax.rem(c + k, n_ctx)
            send(vec, vec_plane.at[c], vp_send.at[k], vp_recv.at[c], g, z)
        plane_w[0].from_diag()
        planes[UP].from_diag()
        plane_w[1].from_first()
        planes[OUT].from_first()
        plane_w[1].from_second()
        planes[OUT].from_second()
        total = vec[...]
        for k in range(1, n_ctx):
            g = lax.rem(c + k, n_ctx)
            arrive(vec_plane.at[g], vp_send.at[0], vp_recv.at[g], c, z)
            total = total + vec_plane[g]
        vec_mid[...] = total
        for k in range(1, n_wsh):
            send(vec_mid, vec_line.at[z], vl_send.at[k], vl_recv.at[z], c, lax.rem(z + k, n_wsh))
        plane_w[1].from_diag()
        planes[OUT].from_diag()
        for k in range(1, n_wsh):
            s = lax.rem(z + k, n_wsh)
            arrive(vec_line.at[s], vl_send.at[0], vl_recv.at[s], c, z)
            total = total + vec_line[s]
        vec_sum[...] = total
        own_vec = pltpu.make_async_copy(vec_sum, vec_out, local_sem.at[12])
        own_vec.start()
        for plane in planes + plane_w:
            all_others(plane)
            plane.finish()
        for i in range(n_ctx // 2):
            left(part(c), hp_send.at[i], hp_recv.at[i], c, z)
        for i in range(2):
            left(part(c), hf_send.at[i], hf_recv.at[i], c, z)
        left(part(c), hs_send.at[0], hs_recv.at[0], c, z)
        for copy in (own_gtok, own_vec, *[own_window(h) for h in range(heads)]):
            copy.wait()

    pl.run_scoped(
        attention_backward,
        vm((n_ctx, heads, 128, rows), bf16), vm((heads, length, 128), bf16), vm((heads, length, 128), bf16),
        vm((heads, length, 128), f32), vm((heads, length, 128), f32), vm((w_c.shape[1], length), bf16),
    )

    wline.finish(wqkv_ref)
    for k in range(1, n_wsh):
        left(pack_ref, pk_send.at[k], pk_recv.at[z], c, z)
        left(vec, vl_send.at[k], vl_recv.at[0], c, z)
    for k in range(1, n_ctx):
        g = lax.rem(c + k, n_ctx)
        left(ob_stage.at[g], ob_send.at[g], ob_recv.at[g], c, z)
        left(go_land.at[0], go_send.at[k], go_recv.at[0], c, z)
        left(vec, vp_send.at[k], vp_recv.at[0], c, z)
    for w in range(3):
        pltpu.make_async_copy(final_piece(w), out_piece(w, c), local_sem.at[8 + w]).wait()
        left(land_f.at[w], f_send.at[w], f_recv.at[w], c, z)
        left(land_s.at[w], s_send.at[w], s_recv.at[w], c, z)
        for j in range(2):
            left(land_near.at[w, j], zn_send.at[w, j], zn_recv.at[w, j], c, z)
        left(land_far.at[w], zf_send.at[w], zf_recv.at[w], c, z)
    for h in range(heads):
        for j in range(2):
            left(win_near.at[h, j], wn_send.at[h, j], wn_recv.at[h, j], c, z)
        left(win_far.at[h], wf_send.at[h], wf_recv.at[h], c, z)


def whole_call(dims, tok, cot, wqkv, w3, pack, order, lengths):
    n_ctx, n_wsh, hd, heads = dims
    rows, width = tok.shape
    span, length, shard = hd * heads, rows * n_ctx, width // n_wsh
    half, cut = width // 2, shard // (n_ctx // 2)
    f32, bf16 = jnp.float32, jnp.bfloat16
    hbm = pl.BlockSpec(memory_space=pl.ANY)
    smem = pl.BlockSpec(memory_space=pltpu.SMEM)
    shape = jax.ShapeDtypeStruct
    dma = pltpu.SemaphoreType.DMA
    vm = pltpu.VMEM
    size = windows(width, n_wsh)[1]
    wide = (rows, width)
    outs = (
        shape(wide, bf16), shape(wide, bf16),
        shape((3, shard, width), bf16), shape((n_ctx, heads, 3 * hd, size), bf16), shape((8, width), f32),
    )
    scratch = [
        vm((n_ctx, rows, width), bf16), vm((3, width, width), bf16), vm((length, width), bf16),
        vm((width, wqkv.shape[1]), bf16), vm((n_wsh,) + pack.shape, f32), vm((8, width), f32),
        vm((heads, length, 128), bf16), vm((heads, length, 128), bf16), vm((heads, hd, length), bf16),
        vm((n_ctx, heads, 128, rows), bf16), vm((n_ctx, span, rows), f32), vm((n_ctx, span, rows), f32),
        vm((n_ctx, span, rows), bf16), vm((width, rows), bf16), vm((width, rows), bf16), vm((n_ctx, span, rows), bf16),
        vm((3, n_wsh, shard, half), bf16), vm((3, n_wsh, 2 * cut, half), bf16), vm((3, n_wsh, cut, half), bf16),
        vm((3, 2, cut, half), bf16), vm((3, cut, half), bf16),
        vm((heads, n_wsh, 3 * hd, size), bf16), vm((heads, 2, 3 * hd, size), bf16), vm((heads, 3 * hd, size), bf16),
        vm(wide, f32), vm(wide, f32), vm(wide, bf16), vm(wide, bf16), vm(wide, bf16),
        vm((8, width), f32), vm((n_ctx, 8, width), f32), vm((n_wsh, 8, width), f32), vm((8, width), f32),
        vm((8, width), f32), vm((hd, rows), f32),
        dma((2, 7)), dma((2, n_ctx)), dma((2 * n_wsh,)), dma((n_wsh,)), dma((n_wsh,)), dma((n_wsh,)),
        dma((n_ctx,)), dma((n_ctx,)), dma((3, 2 * n_wsh)), dma((3, n_wsh)),
        dma((3, n_wsh, 7)), dma((3, n_wsh, n_ctx)),
        dma((n_ctx,)), dma((n_ctx,)), dma((3,)), dma((3,)), dma((3,)), dma((3,)), dma((3,)), dma((3,)),
        dma((3, 2)), dma((3, 2)), dma((3,)), dma((3,)), dma((3, 7)), dma((3, n_ctx)),
        dma((n_ctx // 2,)), dma((n_ctx // 2,)), dma((2,)), dma((2,)), dma((1,)), dma((1,)),
        dma((heads, 2)), dma((heads, 2)), dma((heads,)), dma((heads,)), dma((heads, 7)), dma((heads, n_ctx)),
        dma((n_ctx,)), dma((n_ctx,)), dma((n_wsh,)), dma((n_wsh,)), dma((13,)), dma((heads + 3,)),
    ]
    return pl.pallas_call(
        functools.partial(whole_kernel, dims),
        out_shape=outs,
        in_specs=[hbm] * 7 + [smem] * 2,
        out_specs=[hbm] * len(outs),
        scratch_shapes=scratch,
        compiler_params=pltpu.CompilerParams(
            collective_id=0, has_side_effects=True, vmem_limit_bytes=VMEM_BYTES
        ),
    )(tok, cot, wqkv, *w3, pack, order, lengths)


def finish_kernel(dims, dwqkv_ref, dw3_ref, *refs):
    outs, (pieces, plain, wide, turned, results, in_sem, out_sem) = refs[:6], refs[6:]
    n_ctx, n_wsh, hd, heads = dims
    z = lax.axis_index("wsh")
    f32 = jnp.float32
    shard, width = outs[0].shape
    starts, size = windows(width, n_wsh)
    offset = jnp.int32(0)
    for s in range(n_wsh):
        offset = jnp.where(z == s, s * shard - starts[s], offset)
    ins = [pltpu.make_async_copy(dw3_ref.at[w], plain.at[w], in_sem.at[w]) for w in range(3)]
    for i in range(3):
        at = pl.ds(i * hd, hd)
        ins.append(pltpu.make_async_copy(dwqkv_ref.at[:, :, at], pieces.at[i], in_sem.at[3 + i]))
    for copy in ins:
        copy.start()
    done = []

    def store(i):
        copy = pltpu.make_async_copy(results.at[i], outs[i], out_sem.at[i])
        copy.start()
        done.append(copy)

    for w in range(3):
        ins[w].wait()
        results[3 + w] = plain[w].astype(f32)
        store(3 + w)
    for i in range(3):
        ins[3 + i].wait()

        def lay(b, _):
            for h in range(heads):
                at = pl.ds(pl.multiple_of((b * heads + h) * hd, 16), hd)
                wide[at, :] = pieces[i, b, h].astype(f32)
            return 0

        lax.fori_loop(0, n_ctx, lay, 0)

        def turn(j, _):
            at = pl.ds(pl.multiple_of(j * 128, 128), 128)
            turned[:, at] = wide[at, :].T
            return 0

        lax.fori_loop(0, width // 128, turn, 0)
        results[i] = turned[pl.ds(pl.multiple_of(offset, 8), shard), :]
        store(i)
    for copy in done:
        copy.wait()


def finish_call(dims, dwqkv, dw3):
    n_ctx, n_wsh, hd, heads = dims
    shard, width = dw3.shape[1:]
    size = dwqkv.shape[3]
    f32, bf16 = jnp.float32, jnp.bfloat16
    hbm = pl.BlockSpec(memory_space=pl.ANY)
    dma = pltpu.SemaphoreType.DMA
    return pl.pallas_call(
        functools.partial(finish_kernel, dims),
        out_shape=(jax.ShapeDtypeStruct((shard, width), f32),) * 6,
        in_specs=[hbm] * 2,
        out_specs=[hbm] * 6,
        scratch_shapes=[
            pltpu.VMEM((3, n_ctx, heads, hd, size), bf16), pltpu.VMEM((3, shard, width), bf16),
            pltpu.VMEM((width, size), f32), pltpu.VMEM((size, width), f32), pltpu.VMEM((6, shard, width), f32),
            dma((6,)), dma((6,)),
        ],
        compiler_params=pltpu.CompilerParams(vmem_limit_bytes=VMEM_BYTES),
    )(dwqkv, dw3)


def head_split(
    tokens, cotangent, block_lengths, group_order, w_query, w_key, w_value, w_out, w_up, w_down,
    gain_attn, gain_mlp, query_scale,
):
    f32 = jnp.float32
    n_ctx, n_wsh = lax.axis_size("ctx"), lax.axis_size("wsh")
    c, z = lax.axis_index("ctx"), lax.axis_index("wsh")
    width = tokens.shape[2]
    hd, heads = width // H, H // n_ctx
    span, shard = hd * heads, width // n_wsh
    dims = (n_ctx, n_wsh, hd, heads)
    mine = [lax.dynamic_slice_in_dim(w, c * span, span, 1) for w in (w_query, w_key, w_value)]
    mine = [w[:, h * hd : (h + 1) * hd] for h in range(heads) for w in mine]
    lanes = -(-3 * span // 128) * 128
    wqkv = jnp.pad(jnp.concatenate(mine, 1), ((0, 0), (0, lanes - 3 * span)))
    lanes = -(-shard // 128) * 128
    pack = sum(
        jnp.pad(v.astype(f32)[None], ((i, 7 - i), (0, lanes - v.shape[0])))
        for i, v in enumerate((gain_attn, gain_mlp, query_scale))
    )
    outputs, gtok, dw3, dwqkv, sums = whole_call(
        dims, tokens[0], cotangent[0], wqkv, (w_out, w_up, w_down), pack, group_order, block_lengths
    )[:5]
    weight_grads = finish_call(dims, dwqkv, dw3)
    own = [lax.dynamic_slice_in_dim(sums[i], z * shard, shard, 0) for i in (0, 1)]
    scale_grad = (
        lax.dynamic_slice_in_dim(sums[2], z * (hd // n_wsh), hd // n_wsh, 0)
        * (LOG_BASE / math.sqrt(hd))
        * jax.nn.sigmoid(query_scale.astype(f32))
    )
    return (
        outputs.reshape(tokens.shape), gtok.reshape(tokens.shape), *weight_grads, own[0], own[1], scale_grad,
    )


def solution(mesh):
    in_specs = (
        P("wsh", "ctx", None),
        P("wsh", "ctx", None),
        P("wsh", None),
        P(),
        P("wsh", None),
        P("wsh", None),
        P("wsh", None),
        P("wsh", None),
        P("wsh", None),
        P("wsh", None),
        P("wsh"),
        P("wsh"),
        P("wsh"),
    )
    out_specs = (
        P("wsh", "ctx", None),
        P("wsh", "ctx", None),
        P("wsh", None),
        P("wsh", None),
        P("wsh", None),
        P("wsh", None),
        P("wsh", None),
        P("wsh", None),
        P("wsh"),
        P("wsh"),
        P("wsh"),
    )
    n_ctx, n_wsh = mesh.shape["ctx"], mesh.shape["wsh"]
    plan = head_split if (n_ctx, n_wsh) == (8, 4) else per_device
    return jax.shard_map(
        plan, mesh=mesh, in_specs=in_specs, out_specs=out_specs, check_vma=False
    )
```

```python
import functools
import math

import jax
import jax.numpy as jnp
from jax import lax
from jax.experimental import pallas as pl
from jax.experimental.pallas import tpu as pltpu
from jax.sharding import PartitionSpec as P

H = 16


EPS = 1e-06
LOG_BASE = 1.442695041


def row_step():
    return 512


def rows_at(array, block_no, step_rows):
    return lax.dynamic_slice_in_dim(array, block_no * step_rows, step_rows, 0)


def inverse_rms(values):
    return lax.rsqrt(jnp.mean(values * values, -1, keepdims=True) + EPS)


def norm_back(normed, inverse, grad):
    return inverse * (grad - normed * jnp.mean(grad * normed, -1, keepdims=True))


def split_heads(matrix):
    return matrix.reshape(matrix.shape[0], H, -1)


def outer_product(left, right):
    return lax.dot_general(
        left, right, (((0,), (0,)), ((), ())), preferred_element_type=jnp.float32
    )


def back_product(grad, weight):
    return lax.dot_general(
        grad, weight, (((1,), (1,)), ((), ())), preferred_element_type=jnp.float32
    )


def probabilities(query3, key3, query_marks, key_marks, log_totals):
    scores = jnp.einsum("qhd,khd->hqk", query3, key3, preferred_element_type=jnp.float32)
    allowed = key_marks[None, None, :] <= query_marks[None, :, None]
    return jnp.exp(jnp.where(allowed, scores - log_totals[:, :, None], -jnp.inf))


def score_grads(chances, grad_out3, value3, deltas):
    grad_chances = jnp.einsum("qhd,khd->hqk", grad_out3, value3, preferred_element_type=jnp.float32)
    return (chances * (grad_chances - deltas[:, :, None])).astype(jnp.bfloat16)


def per_device(
    tokens,
    cotangent,
    block_lengths,
    group_order,
    w_query,
    w_key,
    w_value,
    w_out,
    w_up,
    w_down,
    gain_attn,
    gain_mlp,
    query_scale,
):
    gathered = (
        lax.all_gather(w_query, "wsh", axis=0, tiled=True),
        lax.all_gather(w_key, "wsh", axis=0, tiled=True),
        lax.all_gather(w_value, "wsh", axis=0, tiled=True),
        lax.all_gather(w_out, "wsh", axis=0, tiled=True),
        lax.all_gather(w_up, "wsh", axis=0, tiled=True),
        lax.all_gather(w_down, "wsh", axis=0, tiled=True),
        lax.all_gather(gain_attn, "wsh", axis=0, tiled=True),
        lax.all_gather(gain_mlp, "wsh", axis=0, tiled=True),
        lax.all_gather(query_scale, "wsh", axis=0, tiled=True),
    )
    (
        full_query,
        full_key,
        full_value,
        full_out,
        full_up,
        full_down,
        norm_attn,
        norm_mlp,
        scale_param,
    ) = gathered
    tok_rows = tokens.shape[1]
    model_width = tokens.shape[2]
    length = tok_rows * lax.axis_size("ctx")
    device = lax.axis_index("ctx")
    head_size = scale_param.shape[0]
    f32 = jnp.float32
    bf16 = jnp.bfloat16
    inputs = tokens.reshape(tok_rows, model_width).astype(f32)
    positions = (
        group_order[:, None] * tok_rows + jnp.arange(tok_rows, dtype=jnp.int32)[None, :]
    ).reshape(length)
    bounds = jnp.cumsum(block_lengths[0])
    block_ids = jnp.sum((bounds[None, :] <= positions[:, None]).astype(jnp.int32), -1)
    query_ids = lax.dynamic_slice_in_dim(block_ids, device * tok_rows, tok_rows, 0)
    inverse_one = inverse_rms(inputs)
    normed_one = inputs * inverse_one
    hidden_one = (normed_one * norm_attn.astype(f32)).astype(bf16)
    query_raw = jnp.dot(hidden_one, full_query, preferred_element_type=f32).reshape(
        tok_rows, H, head_size
    )
    query_gain = LOG_BASE / math.sqrt(head_size) * jax.nn.softplus(scale_param.astype(f32))
    query3 = (query_raw * query_gain).astype(bf16)
    key_flat = jnp.dot(hidden_one, full_key, preferred_element_type=f32).astype(bf16)
    value_flat = jnp.dot(hidden_one, full_value, preferred_element_type=f32).astype(bf16)
    initial = (
        jnp.full((H, tok_rows), -1e30, f32),
        jnp.zeros((H, tok_rows), f32),
        jnp.zeros((tok_rows, H, head_size), f32),
    )
    key_rows = lax.all_gather(key_flat, "ctx", axis=0, tiled=True)
    value_rows = lax.all_gather(value_flat, "ctx", axis=0, tiled=True)
    row_count = key_rows.shape[0]
    step_rows = row_step()

    def one_block(block_no, looped):
        key_part = split_heads(rows_at(key_rows, block_no, step_rows))
        value_part = split_heads(rows_at(value_rows, block_no, step_rows))
        block_marks = rows_at(block_ids, block_no, step_rows)
        maxima, totals, running = looped
        scores = jnp.einsum("qhd,khd->hqk", query3, key_part, preferred_element_type=f32)
        allowed = block_marks[None, None, :] <= query_ids[None, :, None]
        scores = jnp.where(allowed, scores, -jnp.inf)
        raised = jnp.maximum(maxima, jnp.max(scores, -1))
        rescale = jnp.exp(maxima - raised)
        weights = jnp.exp(scores - raised[:, :, None])
        totals = totals * rescale + jnp.sum(weights, -1)
        running = running * rescale.T[:, :, None] + jnp.einsum(
            "hqk,khd->qhd", weights.astype(bf16), value_part, preferred_element_type=f32
        )
        return (raised, totals, running)

    maxima, totals, running = lax.fori_loop(0, row_count // step_rows, one_block, initial)
    log_totals = maxima + jnp.log(totals)
    attended = running / totals.T[:, :, None]
    attended_bf = attended.reshape(tok_rows, model_width).astype(bf16)
    mixed = inputs + jnp.dot(attended_bf, full_out, preferred_element_type=f32)
    inverse_two = inverse_rms(mixed)
    normed_two = mixed * inverse_two
    hidden_two = (normed_two * norm_mlp.astype(f32)).astype(bf16)
    up_raw = jnp.dot(hidden_two, full_up, preferred_element_type=f32)
    active = jax.nn.silu(up_raw).astype(bf16)
    outputs = mixed + jnp.dot(active, full_down, preferred_element_type=f32)
    grad_output = cotangent.reshape(tok_rows, model_width).astype(f32)
    grad_mlp = grad_output.astype(bf16)
    grad_active = back_product(grad_mlp, full_down)
    sigmoid_up = jax.nn.sigmoid(up_raw)
    grad_up_raw = (grad_active * sigmoid_up * (1.0 + up_raw * (1.0 - sigmoid_up))).astype(bf16)
    grad_hidden_two = back_product(grad_up_raw, full_up)
    grad_gain_mlp = jnp.sum(grad_hidden_two * normed_two, 0)
    grad_mixed = grad_output + norm_back(
        normed_two, inverse_two, grad_hidden_two * norm_mlp.astype(f32)
    )
    grad_branch = grad_mixed.astype(bf16)
    grad_att = back_product(grad_branch, full_out).astype(bf16)
    grad_att3 = split_heads(grad_att)
    deltas = jnp.sum(grad_att3.astype(f32) * attended, -1).T
    key_whole, value_whole = (
        lax.all_gather(key_flat, "ctx", axis=0, tiled=True),
        lax.all_gather(value_flat, "ctx", axis=0, tiled=True),
    )
    step_rows = row_step()
    block_total = length // step_rows

    def key_block(grad_q, block_parts):
        key_rows, value_rows, block_marks = block_parts
        key_part = split_heads(key_rows)
        value_part = split_heads(value_rows)
        zero_part = jnp.zeros((key_rows.shape[0], H, head_size), f32)
        chances = probabilities(query3, key_part, query_ids, block_marks, log_totals)
        slopes = score_grads(chances, grad_att3, value_part, deltas)
        new_grad = (grad_q, zero_part, zero_part)[0] + jnp.einsum(
            "hqk,khd->qhd", slopes, key_part, preferred_element_type=f32
        )
        grad_key_part = jnp.einsum("hqk,qhd->khd", slopes, query3, preferred_element_type=f32)
        grad_value_part = jnp.einsum(
            "hqk,qhd->khd", chances.astype(bf16), grad_att3, preferred_element_type=f32
        )
        return (new_grad, (grad_key_part, grad_value_part))

    grad_qs, (key_terms, value_terms) = lax.scan(
        key_block,
        jnp.zeros((tok_rows, H, head_size), f32),
        (
            key_whole.reshape(block_total, step_rows, model_width),
            value_whole.reshape(block_total, step_rows, model_width),
            block_ids.reshape(block_total, step_rows),
        ),
    )
    grad_key, grad_value = (
        lax.psum_scatter(
            key_terms.reshape(length, model_width).astype(jnp.bfloat16),
            "ctx",
            scatter_dimension=0,
            tiled=True,
        ).astype(jnp.float32),
        lax.psum_scatter(
            value_terms.reshape(length, model_width).astype(jnp.bfloat16),
            "ctx",
            scatter_dimension=0,
            tiled=True,
        ).astype(jnp.float32),
    )
    grad_key_bf = grad_key.astype(bf16)
    grad_value_bf = grad_value.astype(bf16)
    grad_query_bf = (grad_qs * query_gain).reshape(tok_rows, model_width).astype(bf16)
    grad_scale_param = (
        jnp.sum(grad_qs * query_raw, (0, 1))
        * (LOG_BASE / math.sqrt(head_size))
        * jax.nn.sigmoid(scale_param.astype(f32))
    )
    grad_hidden_one = (
        back_product(grad_query_bf, full_query)
        + back_product(grad_key_bf, full_key)
        + back_product(grad_value_bf, full_value)
    )
    grad_gain_attn = jnp.sum(grad_hidden_one * normed_one, 0)
    grad_inputs = grad_mixed + norm_back(
        normed_one, inverse_one, grad_hidden_one * norm_attn.astype(f32)
    )
    grad_queryw = outer_product(hidden_one, grad_query_bf)
    grad_keyw = outer_product(hidden_one, grad_key_bf)
    grad_valuew = outer_product(hidden_one, grad_value_bf)
    grad_outw = outer_product(attended_bf, grad_branch)
    grad_upw = outer_product(hidden_two, grad_up_raw)
    grad_downw = outer_product(active, grad_mlp)
    owned = (
        lax.psum_scatter(
            grad_queryw.astype(jnp.bfloat16), "wsh", scatter_dimension=0, tiled=True
        ).astype(jnp.float32),
        lax.psum_scatter(
            grad_keyw.astype(jnp.bfloat16), "wsh", scatter_dimension=0, tiled=True
        ).astype(jnp.float32),
        lax.psum_scatter(
            grad_valuew.astype(jnp.bfloat16), "wsh", scatter_dimension=0, tiled=True
        ).astype(jnp.float32),
        lax.psum_scatter(
            grad_outw.astype(jnp.bfloat16), "wsh", scatter_dimension=0, tiled=True
        ).astype(jnp.float32),
        lax.psum_scatter(
            grad_upw.astype(jnp.bfloat16), "wsh", scatter_dimension=0, tiled=True
        ).astype(jnp.float32),
        lax.psum_scatter(
            grad_downw.astype(jnp.bfloat16), "wsh", scatter_dimension=0, tiled=True
        ).astype(jnp.float32),
        lax.psum_scatter(
            grad_gain_attn.astype(jnp.bfloat16), "wsh", scatter_dimension=0, tiled=True
        ).astype(jnp.float32),
        lax.psum_scatter(
            grad_gain_mlp.astype(jnp.bfloat16), "wsh", scatter_dimension=0, tiled=True
        ).astype(jnp.float32),
        lax.psum_scatter(
            grad_scale_param.astype(jnp.bfloat16), "wsh", scatter_dimension=0, tiled=True
        ).astype(jnp.float32),
    )
    summed = (
        lax.psum(owned[0].astype(jnp.bfloat16), "ctx").astype(jnp.float32),
        lax.psum(owned[1].astype(jnp.bfloat16), "ctx").astype(jnp.float32),
        lax.psum(owned[2].astype(jnp.bfloat16), "ctx").astype(jnp.float32),
        lax.psum(owned[3].astype(jnp.bfloat16), "ctx").astype(jnp.float32),
        lax.psum(owned[4].astype(jnp.bfloat16), "ctx").astype(jnp.float32),
        lax.psum(owned[5].astype(jnp.bfloat16), "ctx").astype(jnp.float32),
        lax.psum(owned[6].astype(jnp.bfloat16), "ctx").astype(jnp.float32),
        lax.psum(owned[7].astype(jnp.bfloat16), "ctx").astype(jnp.float32),
        lax.psum(owned[8].astype(jnp.bfloat16), "ctx").astype(jnp.float32),
    )
    return (
        outputs.reshape(tokens.shape).astype(bf16),
        grad_inputs.reshape(tokens.shape).astype(bf16),
        summed[0],
        summed[1],
        summed[2],
        summed[3],
        summed[4],
        summed[5],
        summed[6],
        summed[7],
        summed[8],
    )


MESH = pl.DeviceIdType.MESH
NEG = -1e30
VMEM_BYTES = 62 * 1024 * 1024


def place():
    c, z = lax.axis_index("ctx"), lax.axis_index("wsh")
    core, x, y = lax.rem(c, 2), lax.rem(c // 2, 2), c // 4
    sib = c + 1 - 2 * core
    over_x, over_y = c + 2 - 4 * x, c + 4 - 8 * y
    first = over_x * (1 - core) + over_y * core
    second = over_y * (1 - core) + over_x * core
    diag = over_x + over_y - c
    return c, z, sib, first, second, diag


def enter(c, z, n_ctx, n_wsh):
    barrier = pltpu.get_barrier_semaphore()
    for k in range(1, n_ctx):
        pl.semaphore_signal(
            barrier, inc=1, device_id=(lax.rem(c + k, n_ctx), z), device_id_type=MESH
        )
    for k in range(1, n_wsh):
        pl.semaphore_signal(
            barrier, inc=1, device_id=(c, lax.rem(z + k, n_wsh)), device_id_type=MESH
        )
    pl.semaphore_wait(barrier, n_ctx + n_wsh - 2)


def send(src, dst, send_sem, recv_sem, c, z):
    copy = pltpu.make_async_remote_copy(
        src_ref=src, dst_ref=dst, send_sem=send_sem, recv_sem=recv_sem,
        device_id=(c, z), device_id_type=MESH,
    )
    copy.start()
    return copy


def arrive(dst, send_sem, recv_sem, c, z):
    pltpu.make_async_remote_copy(
        src_ref=dst, dst_ref=dst, send_sem=send_sem, recv_sem=recv_sem,
        device_id=(c, z), device_id_type=MESH,
    ).wait_recv()


def left(src, send_sem, recv_sem, c, z):
    pltpu.make_async_remote_copy(
        src_ref=src, dst_ref=src, send_sem=send_sem, recv_sem=recv_sem,
        device_id=(c, z), device_id_type=MESH,
    ).wait_send()


class Line:
    def __init__(self, at, c, z, n, send_sem, recv_sem):
        self.at, self.c, self.z, self.n = at, c, z, n
        self.send_sem, self.recv_sem = send_sem, recv_sem

    def start(self, own):
        c, z = self.c, self.z

        @pl.when(z < self.n - 1)
        def _():
            send(own, self.at(z), self.send_sem.at[0], self.recv_sem.at[z], c, z + 1)

        @pl.when(z > 0)
        def _():
            send(own, self.at(z), self.send_sem.at[1], self.recv_sem.at[z], c, z - 1)

    def forward(self, distance, then=None):
        c, z, n = self.c, self.z, self.n
        below, above = z - distance, z + distance

        @pl.when(below >= 0)
        def _():
            arrive(self.at(below), self.send_sem.at[0], self.recv_sem.at[below], c, z)

            @pl.when(z < n - 1)
            def _():
                send(self.at(below), self.at(below), self.send_sem.at[2 * distance], self.recv_sem.at[below], c, z + 1)

            if then is not None:
                then(below)

        @pl.when(above < n)
        def _():
            arrive(self.at(above), self.send_sem.at[0], self.recv_sem.at[above], c, z)

            @pl.when(z > 0)
            def _():
                send(self.at(above), self.at(above), self.send_sem.at[2 * distance + 1], self.recv_sem.at[above], c, z - 1)

            if then is not None:
                then(above)

    def finish(self, own):
        c, z, n = self.c, self.z, self.n

        @pl.when(z < n - 1)
        def _():
            left(own, self.send_sem.at[0], self.recv_sem.at[z], c, z)

        @pl.when(z > 0)
        def _():
            left(own, self.send_sem.at[1], self.recv_sem.at[z], c, z)

        for distance in range(1, n):
            below, above = z - distance, z + distance

            @pl.when((below >= 0) & (z < n - 1))
            def _():
                left(self.at(below), self.send_sem.at[2 * distance], self.recv_sem.at[below], c, z)

            @pl.when((above < n) & (z > 0))
            def _():
                left(self.at(above), self.send_sem.at[2 * distance + 1], self.recv_sem.at[above], c, z)


class Plane:
    def __init__(self, at, c, z, around, send_sem, recv_sem):
        self.at, self.c, self.z = at, c, z
        self.sib, self.first, self.second, self.diag = around
        self.send_sem, self.recv_sem = send_sem, recv_sem

    def push(self, slot, block, target, src=None):
        src = self.at(block) if src is None else src
        send(src, self.at(block), self.send_sem.at[slot], self.recv_sem.at[block], target, self.z)

    def wait(self, block):
        arrive(self.at(block), self.send_sem.at[0], self.recv_sem.at[block], self.c, self.z)

    def start(self, own=None):
        self.push(0, self.c, self.first, own)
        self.push(1, self.c, self.second, own)
        self.push(2, self.c, self.sib, own)

    def from_first(self):
        self.wait(self.first)
        self.push(3, self.first, self.second)
        self.push(4, self.first, self.sib)

    def from_second(self):
        self.wait(self.second)
        self.push(5, self.second, self.sib)

    def from_diag(self):
        self.wait(self.diag)
        self.push(6, self.diag, self.sib)

    def others(self):
        shift = self.sib - self.c
        return (self.sib, self.second + shift, self.first + shift, self.diag + shift)

    def finish(self):
        for slot in range(7):
            left(self.at(self.c), self.send_sem.at[slot], self.recv_sem.at[self.c], self.c, self.z)


def block_ids_of(block, order_ref, lengths_ref, rows):
    n_blk = lengths_ref.shape[1]
    position = order_ref[block] * rows + lax.broadcasted_iota(jnp.int32, (8, rows), 1)
    ids = jnp.zeros((8, rows), jnp.int32)
    bound = jnp.int32(0)
    for b in range(n_blk):
        bound = bound + lengths_ref[0, b]
        ids = ids + jnp.where(position >= bound, 1, 0)
    return ids, lax.broadcasted_iota(jnp.int32, (8, rows), 0)


def three_rows(value, rows):
    f32 = jnp.float32
    high = value.astype(jnp.bfloat16).astype(f32)
    rest = value - high
    mid = rest.astype(jnp.bfloat16).astype(f32)
    low = rest - mid
    row = lax.broadcasted_iota(jnp.int32, (8, rows), 0)
    return jnp.where(row == 0, high, 0.0) + jnp.where(row == 1, mid, 0.0) + jnp.where(row == 2, low, 0.0)


def add_rows(target, at, other, other_at, rows, step):
    f32 = jnp.float32

    def some_rows(i, _):
        here = pl.ds(pl.multiple_of(at + i * step, 16), step)
        there = pl.ds(pl.multiple_of(other_at + i * step, 16), step)
        target[here, :] = (target[here, :].astype(f32) + other[there, :].astype(f32)).astype(target.dtype)
        return 0

    lax.fori_loop(0, rows // step, some_rows, 0)


def windows(width, n):
    part = width // n
    tiles = -(-part // 128) + (0 if part % 128 == 0 else 0)
    size = tiles * 128
    return [min(s * part // 128 * 128, width - size) for s in range(n)], size


def whole_kernel(
    dims,
    tok_ref, cot_ref, wqkv_ref, wout_ref, wup_ref, wdown_ref, pack_ref, order_ref, lengths_ref,
    out_out, gtok_out, dw3_out, dwqkv_out, vec_out,
    h1_all, w_full, big, w_c, packs, gains, kaug, vaug, kt, qaug, qraw, o_all, ob_stage, ob_land, go_stage, go_land,
    acc, land_f, land_s, land_near, land_far, deep_near, deep_far, deep_f, deep_s, win_out, win_near, win_far,
    dx, dh, tok, cot, gtok, vec, vec_plane, vec_line, vec_mid, vec_sum, row, row_plane, row_line, row_mid, scale_acc,
    tok_send, tok_recv, wz_send, wz_recv, pk_send, pk_recv, ob_send, ob_recv,
    w3z_send, w3z_recv, w3p_send, w3p_recv,
    go_send, go_recv, p_send, p_recv, f_send, f_recv, s_send, s_recv, zn_send, zn_recv, zf_send, zf_recv, g_send, g_recv,
    hp_send, hp_recv, hf_send, hf_recv, hs_send, hs_recv, wn_send, wn_recv, wf_send, wf_recv, wg_send, wg_recv,
    vp_send, vp_recv, vl_send, vl_recv, rp_send, rp_recv, rl_send, rl_recv, local_sem, load_sem,
):
    n_ctx, n_wsh, hd, heads = dims
    f32, bf16 = jnp.float32, jnp.bfloat16
    c, z, sib, first, second, diag = place()
    around = (sib, first, second, diag)
    core, x, y = lax.rem(c, 2), lax.rem(c // 2, 2), c // 4
    f_bit, s_bit = x * (1 - core) + y * core, y * (1 - core) + x * core
    rows, width = tok_ref.shape
    span, length = hd * heads, rows * n_ctx
    shard, half = width // n_wsh, width // 2
    two, cut = shard // 2, shard // (n_ctx // 2)
    w3_refs = (wout_ref, wup_ref, wdown_ref)
    OUT, UP, DOWN = 0, 1, 2
    own_tok = pltpu.make_async_copy(tok_ref, tok, local_sem.at[0])
    own_w = pltpu.make_async_copy(wqkv_ref, w_c.at[pl.ds(pl.multiple_of(z * shard, 16), shard)], local_sem.at[1])
    own_pack = pltpu.make_async_copy(pack_ref, packs.at[z], local_sem.at[2])
    own_cot = pltpu.make_async_copy(cot_ref, cot, local_sem.at[3])
    own_full = [
        pltpu.make_async_copy(
            w3_refs[w], w_full.at[w, pl.ds(pl.multiple_of(z * shard, 16), shard)], load_sem.at[heads + w]
        )
        for w in range(3)
    ]
    for copy in (own_tok, own_pack, own_w, own_cot, *own_full):
        copy.start()
    enter(c, z, n_ctx, n_wsh)

    part_rows = rows // 2
    tokens = [
        Plane(
            lambda b, i=i: big.at[pl.ds(pl.multiple_of(b * rows + i * part_rows, 16), part_rows)], c, z, around,
            tok_send.at[i], tok_recv.at[i],
        )
        for i in range(2)
    ]
    for i in range(2):
        tokens[i].start(tok_ref.at[pl.ds(i * part_rows, part_rows)])
    wline = Line(lambda s: w_c.at[pl.ds(pl.multiple_of(s * shard, 16), shard)], c, z, n_wsh, wz_send, wz_recv)
    for k in range(1, n_wsh):
        send(pack_ref, packs.at[z], pk_send.at[k], pk_recv.at[z], c, lax.rem(z + k, n_wsh))
    wline.start(wqkv_ref)
    scale_acc[...] = jnp.zeros_like(scale_acc)

    def columns(b):
        return pl.ds(pl.multiple_of(lax.rem(b, 2) * half, 128), half)

    def piece(w, s, b):
        top = pl.multiple_of(s * shard + (b // 2) * cut, 16)
        return w_full.at[w, pl.ds(top, cut), columns(b)]

    my_piece = [ref.at[pl.ds(pl.multiple_of((c // 2) * cut, 16), cut), columns(c)] for ref in w3_refs]
    lines = [
        Line(lambda s, w=w: piece(w, s, c), c, z, n_wsh, w3z_send.at[w], w3z_recv.at[w]) for w in range(3)
    ]

    def plane_of(w, s):
        k = lax.rem(s - z + n_wsh, n_wsh)
        return Plane(lambda b: piece(w, s, b), c, z, around, w3p_send.at[w, k], w3p_recv.at[w, k])

    def shards_at(w, distance, step):
        below, above = z - distance, z + distance

        @pl.when(below >= 0)
        def _():
            step(plane_of(w, below))

        @pl.when(above < n_wsh)
        def _():
            step(plane_of(w, above))

    def spread(w, distance):
        lines[w].forward(distance, lambda s: plane_of(w, s).start())

    def step_of(step):
        return lambda w, distance: shards_at(w, distance, step)

    by_first, by_second, by_diag = step_of(Plane.from_first), step_of(Plane.from_second), step_of(Plane.from_diag)

    def all_others(plane):
        for b in plane.others():
            plane.wait(b)

    own_tok.wait()
    own_pack.wait()
    for k in range(1, n_wsh):
        other = lax.rem(z + k, n_wsh)
        arrive(packs.at[other], pk_send.at[0], pk_recv.at[other], c, z)
    row8 = lax.broadcasted_iota(jnp.int32, (8, width), 0)
    total = jnp.zeros((8, width), f32)
    for s in range(n_wsh):
        wide = jnp.concatenate([packs[s], jnp.zeros((8, width - packs.shape[2]), f32)], axis=1)
        by_shard = pltpu.roll(wide, s * shard, 1) if s else wide
        by_dim = pltpu.roll(wide, s * (hd // n_wsh), 1) if s else wide
        total = total + jnp.where(row8 < 2, by_shard, by_dim)
    gains[...] = total

    def gain_column():
        scale = jnp.concatenate([gains[2:3, 0:128], jnp.zeros((7, 128), f32)], axis=0)
        soft = jnp.maximum(scale, 0.0) + jnp.log(1.0 + jnp.exp(-jnp.abs(scale)))
        return (LOG_BASE / math.sqrt(hd) * soft).T[0:hd, 0:1]

    def attention_forward(vt, qneg, s_buf):
        def norm_block(b, source, top):
            gain = gains[0:1, :]

            def some_rows(i, _):
                t = source[pl.ds(pl.multiple_of(top + i * 32, 32), 32), :].astype(f32)
                inverse = lax.rsqrt(jnp.mean(t * t, -1, keepdims=True) + EPS)
                h1_all[b, pl.ds(pl.multiple_of(i * 32, 32), 32), :] = (t * inverse * gain).astype(bf16)
                return 0

            lax.fori_loop(0, rows // 32, some_rows, 0)

        def norm_arrived(b):
            norm_block(b, big, b * rows)

        def arrived(b):
            for i in range(2):
                tokens[i].wait(b)
            norm_arrived(b)

        others = tokens[0].others()
        lines[OUT].start(my_piece[OUT])
        norm_block(c, tok, 0)
        arrived(others[0])
        tokens[0].from_first()
        wline.forward(1)
        lines[UP].start(my_piece[UP])
        tokens[1].from_first()
        norm_arrived(first)
        tokens[0].from_second()
        tokens[1].from_second()
        norm_arrived(second)
        spread(OUT, 1)
        wline.forward(2)
        lines[DOWN].start(my_piece[DOWN])
        arrived(others[1])
        arrived(others[2])
        tokens[0].from_diag()
        tokens[1].from_diag()
        norm_arrived(diag)
        arrived(others[3])
        spread(OUT, 2)
        wline.forward(3)
        own_w.wait()
        spread(UP, 1)
        gain_col = gain_column()

        def project(b, _):
            raw = jnp.dot(h1_all[b], w_c[...], preferred_element_type=f32).T
            at = pl.ds(pl.multiple_of(b * rows, 128), rows)
            ids, row = block_ids_of(b, order_ref, lengths_ref, rows)
            hot = jnp.where(ids == row, 1.0, 0.0)
            neg = jnp.where(row > ids, NEG, 0.0)
            ones = jnp.ones((8, rows), f32)
            qneg[b] = neg
            for h in range(heads):
                top = 3 * h * hd
                q = raw[top : top + hd]
                qraw[b, h * hd : (h + 1) * hd, :] = q
                q = q * gain_col
                qaug[b, h, 0:hd, :] = q.astype(bf16)
                qaug[b, h, hd : hd + 16, :] = jnp.concatenate([neg, jnp.zeros((8, rows), f32)], axis=0).astype(bf16)
                qaug[b, h, hd + 16 : 128, :] = jnp.zeros((112 - hd, rows), bf16)
                k = raw[top + hd : top + 2 * hd].astype(bf16)
                v = raw[top + 2 * hd : top + 3 * hd].astype(bf16)
                tail = jnp.zeros((112 - hd, rows), f32)
                kt[h, :, at] = k
                vt[h, 0:hd, at] = v
                vt[h, hd : hd + 16, at] = jnp.ones((16, rows), bf16)
                kaug[h, at, :] = jnp.concatenate([k.astype(f32), hot, ones, tail], axis=0).T.astype(bf16)
                vaug[h, at, :] = jnp.concatenate([v.astype(f32), ones, ones, tail], axis=0).T.astype(bf16)
            return 0

        lax.fori_loop(0, n_ctx, project, 0)
        for i in range(2):
            tokens[i].finish()
        keys = length // 2
        plan = (
            (0, spread, OUT, 3), (0, by_first, OUT, 1), (1, by_first, OUT, 2), (1, spread, UP, 2),
            (2, by_second, OUT, 1), (2, by_second, OUT, 2), (3, spread, DOWN, 1), (3, by_first, OUT, 3),
            (4, by_diag, OUT, 1), (4, spread, UP, 3), (5, by_second, OUT, 3), (5, by_first, UP, 1),
            (6, spread, DOWN, 2), (6, by_diag, OUT, 2), (7, by_first, UP, 2), (8, by_diag, OUT, 3),
            (8, by_second, UP, 1), (9, by_second, UP, 2), (9, spread, DOWN, 3), (10, by_first, UP, 3),
            (11, by_diag, UP, 1), (11, by_first, DOWN, 1), (12, by_second, UP, 3), (12, by_diag, UP, 2),
            (13, by_first, DOWN, 2), (14, by_second, DOWN, 1), (14, by_diag, UP, 3), (15, by_second, DOWN, 2),
        )

        def attend(i, _):
            g = lax.rem(c + 1 + i, n_ctx)
            for h in range(heads):
                q = qaug[g, h]
                top = jnp.full((1, rows), -jnp.inf, f32)
                for j in range(2):
                    s = jnp.dot(kaug[h, j * keys : (j + 1) * keys, :], q, preferred_element_type=f32)
                    s_buf[j * keys : (j + 1) * keys, :] = s
                    top = jnp.maximum(top, jnp.max(s, axis=0, keepdims=True))
                out = jnp.zeros((hd + 16, rows), f32)
                for j in range(2):
                    p = jnp.exp(s_buf[j * keys : (j + 1) * keys, :] - top).astype(bf16)
                    out = out + jnp.dot(vt[h, :, j * keys : (j + 1) * keys], p, preferred_element_type=f32)
                total = out[hd : hd + 1]
                o = out[0:hd] / total
                lse = top + jnp.log(total)
                o_all[g, h * hd : (h + 1) * hd, :] = o
                ob_stage[g, h * hd : (h + 1) * hd, :] = o.astype(bf16)
                qaug[g, h, hd : hd + 16, :] = jnp.concatenate([qneg[g], three_rows(-lse, rows)], axis=0).astype(bf16)
                for slot, event, w, distance in plan:
                    if slot % heads == h:
                        pl.when(i == slot // heads)(functools.partial(event, w, distance))

            @pl.when(i < n_ctx - 1)
            def _():
                send(ob_stage.at[g], my_heads(ob_land), ob_send.at[g], ob_recv.at[c], g, z)

            return 0

        lax.fori_loop(0, n_ctx, attend, 0)

    def my_heads(ref):
        return ref.at[pl.ds(pl.multiple_of(c * span, 16), span)]

    def heads_of(ref, g):
        return ref.at[pl.ds(pl.multiple_of(g * span, 16), span)]

    vm = pltpu.VMEM
    pl.run_scoped(
        attention_forward,
        vm((heads, hd + 16, length), bf16), vm((n_ctx, 8, rows), f32), vm((length, rows), f32),
    )
    own_o = pltpu.make_async_copy(ob_stage.at[c], my_heads(ob_land), local_sem.at[4])
    own_o.start()

    mine = pl.ds(pl.multiple_of(core * half, 128), half)
    theirs = pl.ds(pl.multiple_of((1 - core) * half, 128), half)
    my_top = f_bit * two + s_bit * cut
    near, far = z + 1 - 2 * lax.rem(z, 2), z + 2 - 4 * (z // 2)

    def pair_at(w):
        return big.at[pl.ds(2 * w * shard, 2 * shard)]

    def add_pair(w):
        arrive(pair_at(w), p_send.at[w], p_recv.at[w], c, z)
        for s in range(n_wsh):
            other = big.at[:, pl.ds(s % 2 * half, half)]
            add_rows(acc.at[w, s], 0, other, (2 * w + s // 2) * shard, shard, 64)

    def pair_sum(w):
        add_pair(w)
        at = pl.ds(pl.multiple_of((1 - f_bit) * two, 16), two)
        send(acc.at[w, :, at], land_f.at[w], f_send.at[w], f_recv.at[w], first, z)

    def deep_pair_sum(w):
        add_pair(w)
        for j in range(2):
            s = 2 * j + lax.rem(near, 2)
            send(acc.at[w, s], deep_near.at[j], zn_send.at[w, j], zn_recv.at[w, j], c, near)

    def deep_near_sum(w):
        for j in range(2):
            arrive(deep_near.at[j], zn_send.at[w, j], zn_recv.at[w, j], c, z)
            add_rows(acc.at[w, 2 * j + lax.rem(z, 2)], 0, deep_near.at[j], 0, shard, 80)
        send(acc.at[w, far], deep_far, zf_send.at[w], zf_recv.at[w], c, far)

    def deep_far_sum(w):
        arrive(deep_far, zf_send.at[w], zf_recv.at[w], c, z)
        add_rows(acc.at[w, z], 0, deep_far, 0, shard, 80)
        at = pl.ds(pl.multiple_of((1 - f_bit) * two, 16), two)
        send(acc.at[w, z, at], deep_f, f_send.at[w], f_recv.at[w], first, z)

    def deep_first_sum(w):
        arrive(deep_f, f_send.at[w], f_recv.at[w], c, z)
        add_rows(acc.at[w, z], f_bit * two, deep_f, 0, two, 80)
        at = pl.ds(pl.multiple_of(f_bit * two + (1 - s_bit) * cut, 16), cut)
        send(acc.at[w, z, at], deep_s, s_send.at[w], s_recv.at[w], second, z)

    def deep_second_sum(w):
        arrive(deep_s, s_send.at[w], s_recv.at[w], c, z)
        add_rows(acc.at[w, z], my_top, deep_s, 0, cut, 80)
        planes[w].start(final_piece(w))
        pltpu.make_async_copy(final_piece(w), out_piece(w, c), local_sem.at[8 + w]).start()

    def first_sum(w):
        arrive(land_f.at[w], f_send.at[w], f_recv.at[w], c, z)
        for s in range(n_wsh):
            add_rows(acc.at[w, s], f_bit * two, land_f.at[w, s], 0, two, 80)
        at = pl.ds(pl.multiple_of(f_bit * two + (1 - s_bit) * cut, 16), cut)
        send(acc.at[w, :, at], land_s.at[w], s_send.at[w], s_recv.at[w], second, z)

    def second_sum(w):
        arrive(land_s.at[w], s_send.at[w], s_recv.at[w], c, z)
        for s in range(n_wsh):
            add_rows(acc.at[w, s], my_top, land_s.at[w, s], 0, cut, 80)
        at = pl.ds(pl.multiple_of(my_top, 16), cut)
        for j in range(2):
            s = 2 * j + lax.rem(near, 2)
            send(acc.at[w, s, at], land_near.at[w, j], zn_send.at[w, j], zn_recv.at[w, j], c, near)

    def near_sum(w):
        for j in range(2):
            arrive(land_near.at[w, j], zn_send.at[w, j], zn_recv.at[w, j], c, z)
            add_rows(acc.at[w, 2 * j + lax.rem(z, 2)], my_top, land_near.at[w, j], 0, cut, 80)
        at = pl.ds(pl.multiple_of(my_top, 16), cut)
        send(acc.at[w, far, at], land_far.at[w], zf_send.at[w], zf_recv.at[w], c, far)

    def out_piece(w, b):
        b_core, b_x, b_y = lax.rem(b, 2), lax.rem(b // 2, 2), b // 4
        r = (1 - b_core) * (2 * b_x + b_y) + b_core * (2 * b_y + b_x)
        return dw3_out.at[w, pl.ds(pl.multiple_of(r * cut, 16), cut), columns(b)]

    planes = [
        Plane(lambda b, w=w: out_piece(w, b), c, z, around, g_send.at[w], g_recv.at[w]) for w in range(3)
    ]

    def final_piece(w):
        return acc.at[w, z, pl.ds(pl.multiple_of(my_top, 16), cut)]

    def far_sum(w):
        arrive(land_far.at[w], zf_send.at[w], zf_recv.at[w], c, z)
        add_rows(acc.at[w, z], my_top, land_far.at[w], 0, cut, 80)
        planes[w].start(final_piece(w))
        pltpu.make_async_copy(final_piece(w), out_piece(w, c), local_sem.at[8 + w]).start()

    def feed_forward(x1, h2, a, gu, ob, turned, ga, inv2, outb, stage):
        def tiles(step, size=256):
            for top in range(0, width, size):
                step(slice(top, top + size))

        def turn(source, target):
            def one(at):
                target[at, :] = source[:, at].T

            tiles(one, 128)

        def weight_gradient(w, left_t, right):
            for s in range(n_wsh):
                stage[w, s // 2 * shard : (s // 2 + 1) * shard, s % 2 * half : (s % 2 + 1) * half] = jnp.dot(
                    left_t[s * shard : (s + 1) * shard, :], right[:, theirs], preferred_element_type=f32
                ).astype(bf16)
            send(stage.at[w], pair_at(w), p_send.at[w], p_recv.at[w], sib, z)
            for s in range(n_wsh):
                at = slice(s * shard, (s + 1) * shard)
                acc[w, s] = jnp.dot(left_t[at, :], right[:, mine], preferred_element_type=f32).astype(bf16)

        by_first(DOWN, 3)
        for distance in range(1, n_wsh):
            shards_at(OUT, distance, all_others)
        own_o.wait()
        for k in range(1, n_ctx):
            g = lax.rem(c + k, n_ctx)
            arrive(heads_of(ob_land, g), ob_send.at[0], ob_recv.at[g], c, z)

        def turn_ob(at):
            ob[:, at] = ob_land[at, :].T

        tiles(turn_ob, 128)
        by_diag(DOWN, 1)
        by_second(DOWN, 3)
        own_full[OUT].wait()

        def mix(at):
            x1[:, at] = tok[:, at].astype(f32) + jnp.dot(ob[...], w_full[OUT, :, at], preferred_element_type=f32)

        tiles(mix)
        by_diag(DOWN, 2)

        def norm_rows(i, _):
            at = pl.ds(pl.multiple_of(i * 32, 32), 32)
            t = x1[at, :]
            inverse = lax.rsqrt(jnp.mean(t * t, -1, keepdims=True) + EPS)
            inv2[at, :] = jnp.broadcast_to(inverse, (32, 128))
            h2[at, :] = (t * inverse * gains[1:2, :]).astype(bf16)
            return 0

        lax.fori_loop(0, rows // 32, norm_rows, 0)
        by_diag(DOWN, 3)
        for distance in range(1, n_wsh):
            shards_at(UP, distance, all_others)
        own_full[UP].wait()

        def lift(at):
            dh[:, at] = jnp.dot(h2[...], w_full[UP, :, at], preferred_element_type=f32)

        tiles(lift)
        own_cot.wait()
        for distance in range(1, n_wsh):
            shards_at(DOWN, distance, all_others)
        own_full[DOWN].wait()

        def hidden(at):
            up = dh[:, at]
            da = lax.dot_general(
                cot[...], w_full[DOWN, at, :], (((1,), (1,)), ((), ())), preferred_element_type=f32
            )
            sig = 1.0 / (1.0 + jnp.exp(-up))
            act = up * sig
            a[:, at] = act.astype(bf16)
            turned[at, :] = act.T.astype(bf16)
            gu[:, at] = (da * sig * (1.0 + up * (1.0 - sig))).astype(bf16)

        tiles(hidden)
        weight_gradient(DOWN, turned, cot)

        def back(at):
            dh[:, at] = lax.dot_general(
                gu[...], w_full[UP, at, :], (((1,), (1,)), ((), ())), preferred_element_type=f32
            )

        tiles(back)

        def norm_back_rows(i, total):
            at = pl.ds(pl.multiple_of(i * 16, 16), 16)
            inverse = inv2[at, 0:1]
            normed = x1[at, :] * inverse
            grad = dh[at, :]
            both = grad * normed
            slope = jnp.mean(both * gains[1:2, :], -1, keepdims=True)
            result = cot[at, :].astype(f32) + inverse * (grad * gains[1:2, :] - normed * slope)
            dx[at, :] = result
            ga[at, :] = result.astype(bf16)
            return total + both

        gain_sum = lax.fori_loop(0, rows // 16, norm_back_rows, jnp.zeros((16, width), f32))
        vec[:, 0:width] = jnp.sum(gain_sum, axis=0, keepdims=True)

        def back_out(at):
            go_stage[at, :] = lax.dot_general(
                w_full[OUT, at, :], ga[...], (((1,), (1,)), ((), ())), preferred_element_type=f32
            ).astype(bf16)

        tiles(back_out)
        for w in range(3):
            lines[w].finish(my_piece[w])
            for distance in range(1, n_wsh):
                shards_at(w, distance, Plane.finish)
        for k in range(1, n_ctx):
            g = lax.rem(c + k, n_ctx)
            send(heads_of(go_stage, g), go_land.at[c], go_send.at[k], go_recv.at[c], g, z)
        pltpu.make_async_copy(my_heads(go_stage), go_land.at[c], local_sem.at[5]).start()
        deep_pair_sum(DOWN)
        turn(h2, turned)
        weight_gradient(UP, turned, gu)
        weight_gradient(OUT, ob_land, ga)
        pair_sum(UP)

        def finish(at):
            outb[:, at] = (
                x1[:, at] + jnp.dot(a[...], w_full[DOWN, :, at], preferred_element_type=f32)
            ).astype(bf16)

        tiles(finish)
        own_out = pltpu.make_async_copy(outb, out_out, local_sem.at[6])
        own_out.start()
        pair_sum(OUT)
        own_out.wait()
        for w in range(3):
            left(stage.at[w], p_send.at[w], p_recv.at[w], c, z)

    wide = (rows, width)
    pl.run_scoped(
        feed_forward,
        vm(wide, f32), vm(wide, bf16), vm(wide, bf16), vm(wide, bf16), vm(wide, bf16),
        vm((width, rows), bf16), vm(wide, bf16), vm((rows, 128), f32), vm(wide, bf16),
        vm((3, 2 * shard, width), bf16),
    )

    def attention_backward(goaug, go_tm, q_tm, dk, dv, dqkv):
        per = width // rows

        def block(i):
            return w_full.at[i // per, :, pl.ds(pl.multiple_of(lax.rem(i, per) * rows, 128), rows)]

        def part_p(i):
            return block(i)

        def part_f(i):
            return block(n_ctx // 2 + i)

        part_s = block(jnp.int32(n_ctx // 2 + 2))

        def part(b):
            return block(n_ctx // 2 + 3 + b)

        dk[...] = jnp.zeros_like(dk)
        dv[...] = jnp.zeros_like(dv)
        dqkv[3 * span :, :] = jnp.zeros((dqkv.shape[0] - 3 * span, length), bf16)
        gain_col = gain_column()

        def prepare(g):
            at = pl.ds(pl.multiple_of(g * rows, 16), rows)
            for h in range(heads):
                go = go_land[g, h * hd : (h + 1) * hd, :]
                wide = go.astype(f32)
                delta = jnp.sum(wide * o_all[g, h * hd : (h + 1) * hd, :], axis=0, keepdims=True)
                tail = jnp.concatenate([three_rows(-delta, rows), jnp.zeros((120 - hd, rows), f32)], axis=0)
                goaug[g, h, 0:hd, :] = go
                goaug[g, h, hd:128, :] = tail.astype(bf16)
                go_tm[h, at, :] = jnp.concatenate([wide, jnp.zeros((128 - hd, rows), f32)], axis=0).T.astype(bf16)
                q = qaug[g, h, 0:hd, :].astype(f32)
                q_tm[h, at, :] = jnp.concatenate([q, jnp.zeros((128 - hd, rows), f32)], axis=0).T.astype(bf16)

        pltpu.make_async_copy(my_heads(go_stage), go_land.at[c], local_sem.at[5]).wait()
        prepare(c)

        def prepare_other(k, _):
            g = lax.rem(c + k, n_ctx)
            arrive(go_land.at[g], go_send.at[0], go_recv.at[g], c, z)
            prepare(g)
            return 0

        lax.fori_loop(1, n_ctx, prepare_other, 0)
        three = 3 * hd
        starts, size = windows(width, n_wsh)

        def head_gradients(h, events):
            def attend(g, _):
                at = pl.ds(pl.multiple_of(g * rows, 16), rows)
                p = jnp.exp(jnp.dot(kaug[h], qaug[g, h], preferred_element_type=f32))
                ds = (p * jnp.dot(vaug[h], goaug[g, h], preferred_element_type=f32)).astype(bf16)
                dq = jnp.dot(kt[h], ds, preferred_element_type=f32)
                dk[h] += jnp.dot(ds, q_tm[h, at, :], preferred_element_type=f32)
                dv[h] += jnp.dot(p.astype(bf16), go_tm[h, at, :], preferred_element_type=f32)
                scale_acc[...] += dq * qraw[g, h * hd : (h + 1) * hd, :]
                lanes = pl.ds(pl.multiple_of(g * rows, 128), rows)
                dqkv[h * three : h * three + hd, lanes] = (dq * gain_col).astype(bf16)
                for step, event in events:
                    pl.when(g == step)(event)
                return 0

            lax.fori_loop(0, n_ctx, attend, 0)

            def settle(g, _):
                at = pl.ds(pl.multiple_of(g * rows, 16), rows)
                lanes = pl.ds(pl.multiple_of(g * rows, 128), rows)
                for i, source in enumerate((dk, dv)):
                    turned = source[h, at, :].T
                    top = h * three + (i + 1) * hd
                    dqkv[top : top + hd, lanes] = turned[0:hd].astype(bf16)
                return 0

            lax.fori_loop(0, n_ctx, settle, 0)

        def head_windows(h):
            for s in range(n_wsh):
                total = jnp.zeros((three, size), f32)
                for b in range(n_ctx):
                    total = total + jnp.dot(
                        dqkv[h * three : (h + 1) * three, b * rows : (b + 1) * rows],
                        h1_all[b, :, starts[s] : starts[s] + size], preferred_element_type=f32,
                    )
                win_out[h, s] = total.astype(bf16)
            for j in range(2):
                s = 2 * j + lax.rem(near, 2)
                send(win_out.at[h, s], win_near.at[h, j], wn_send.at[h, j], wn_recv.at[h, j], c, near)

        def near_window(h):
            for j in range(2):
                arrive(win_near.at[h, j], wn_send.at[h, j], wn_recv.at[h, j], c, z)
                add_rows(win_out.at[h, 2 * j + lax.rem(z, 2)], 0, win_near.at[h, j], 0, three, 80)
            send(win_out.at[h, far], win_far.at[h], wf_send.at[h], wf_recv.at[h], c, far)

        plane_w = [
            Plane(lambda b, h=h: dwqkv_out.at[b, h], c, z, around, wg_send.at[h], wg_recv.at[h]) for h in range(heads)
        ]

        def own_window(h):
            return pltpu.make_async_copy(win_out.at[h, z], dwqkv_out.at[c, h], load_sem.at[h])

        def far_window(h):
            arrive(win_far.at[h], wf_send.at[h], wf_recv.at[h], c, z)
            add_rows(win_out.at[h, z], 0, win_far.at[h], 0, three, 80)
            plane_w[h].start(win_out.at[h, z])
            own_window(h).start()

        head_gradients(0, ((6, lambda: first_sum(UP)),))
        head_windows(0)
        head_gradients(1, (
            (1, lambda: second_sum(UP)), (2, lambda: deep_near_sum(DOWN)), (4, lambda: first_sum(OUT)),
            (5, lambda: near_sum(UP)), (6, lambda: near_window(0)), (7, lambda: second_sum(OUT)),
        ))

        def partial(b):
            lanes = pl.ds(pl.multiple_of(b * rows, 128), rows)
            part(b)[...] = jnp.dot(w_c[...], dqkv[:, lanes], preferred_element_type=f32).astype(bf16)

        def to_sib(i, _):
            b = 2 * i + (1 - core)
            partial(b)
            send(part(b), part_p(i), hp_send.at[i], hp_recv.at[i], sib, z)
            return 0

        lax.fori_loop(0, n_ctx // 2, to_sib, 0)
        head_windows(1)

        def own_core(i, _):
            partial(2 * i + core)
            return 0

        lax.fori_loop(0, n_ctx // 2, own_core, 0)

        def scale_row():
            scale_sum = jnp.sum(scale_acc[...], axis=1, keepdims=True)
            return jnp.concatenate(
                [jnp.broadcast_to(scale_sum, (hd, 128)), jnp.zeros((128 - hd, 128), f32)], axis=0
            ).T[0:1, :]

        def pair(i, b):
            arrive(part_p(b // 2), hp_send.at[0], hp_recv.at[b // 2], c, z)
            add_rows(part(b), 0, part_p(b // 2), 0, width, 128)
            if i < 2:
                slot = s_bit if i == 0 else 1 - s_bit
                send(part(b), part_f(slot), hf_send.at[i], hf_recv.at[slot], first, z)

        pair(1, diag)
        pair(0, first)
        deep_far_sum(DOWN)
        far_sum(UP)
        near_sum(OUT)
        vec[:, width:] = scale_row()
        for k in range(1, n_ctx):
            g = lax.rem(c + k, n_ctx)
            send(vec, vec_plane.at[c], vp_send.at[k], vp_recv.at[c], g, z)
        far_window(0)
        pair(2, second)
        pair(3, c)
        deep_first_sum(DOWN)
        near_window(1)
        planes[UP].from_first()
        far_sum(OUT)
        planes[UP].from_second()
        arrive(part_f(1 - s_bit), hf_send.at[0], hf_recv.at[1 - s_bit], c, z)
        add_rows(part(second), 0, part_f(1 - s_bit), 0, width, 128)
        send(part(second), part_s, hs_send.at[0], hs_recv.at[0], second, z)
        deep_second_sum(DOWN)
        arrive(part_f(s_bit), hf_send.at[0], hf_recv.at[s_bit], c, z)
        add_rows(part(c), 0, part_f(s_bit), 0, width, 128)
        far_window(1)
        plane_w[0].from_first()
        plane_w[0].from_second()
        planes[UP].from_diag()
        total = vec[...]
        for k in range(1, n_ctx):
            g = lax.rem(c + k, n_ctx)
            arrive(vec_plane.at[g], vp_send.at[0], vp_recv.at[g], c, z)
            total = total + vec_plane[g]
        vec_mid[...] = total
        for k in range(1, n_wsh):
            send(vec_mid, vec_line.at[z], vl_send.at[k], vl_recv.at[z], c, lax.rem(z + k, n_wsh))
        planes[OUT].from_first()
        planes[OUT].from_second()
        planes[DOWN].from_first()
        planes[DOWN].from_second()
        arrive(part_s, hs_send.at[0], hs_recv.at[0], c, z)

        mine_part = part(c)

        def turn_dh(i, _):
            at = pl.ds(pl.multiple_of(i * 128, 128), 128)
            dh[:, at] = (mine_part[at, :].astype(f32) + part_s[at, :].astype(f32)).T
            return 0

        lax.fori_loop(0, width // 128, turn_dh, 0)

        def last_rows(i, total):
            at = pl.ds(pl.multiple_of(i * 16, 16), 16)
            t = tok[at, :].astype(f32)
            inverse = lax.rsqrt(jnp.mean(t * t, -1, keepdims=True) + EPS)
            normed = t * inverse
            grad = dh[at, :]
            both = grad * normed
            slope = jnp.mean(both * gains[0:1, :], -1, keepdims=True)
            gtok[at, :] = (dx[at, :] + inverse * (grad * gains[0:1, :] - normed * slope)).astype(bf16)
            return total + both

        gain_sum = lax.fori_loop(0, rows // 16, last_rows, jnp.zeros((16, width), f32))
        row[...] = jnp.sum(gain_sum, axis=0, keepdims=True)
        for k in range(1, n_ctx):
            g = lax.rem(c + k, n_ctx)
            send(row, row_plane.at[c], rp_send.at[k], rp_recv.at[c], g, z)
        own_gtok = pltpu.make_async_copy(gtok, gtok_out, local_sem.at[11])
        own_gtok.start()
        plane_w[0].from_diag()
        planes[OUT].from_diag()
        planes[DOWN].from_diag()
        plane_w[1].from_first()
        plane_w[1].from_second()
        total = row[...]
        for k in range(1, n_ctx):
            g = lax.rem(c + k, n_ctx)
            arrive(row_plane.at[g], rp_send.at[0], rp_recv.at[g], c, z)
            total = total + row_plane[g]
        row_mid[...] = total
        for k in range(1, n_wsh):
            send(row_mid, row_line.at[z], rl_send.at[k], rl_recv.at[z], c, lax.rem(z + k, n_wsh))
        plane_w[1].from_diag()
        whole = vec_mid[...]
        for k in range(1, n_wsh):
            s = lax.rem(z + k, n_wsh)
            arrive(vec_line.at[s], vl_send.at[0], vl_recv.at[s], c, z)
            whole = whole + vec_line[s]
        vec_sum[...] = jnp.zeros_like(vec_sum)
        vec_sum[1:2, :] = whole[:, 0:width]
        vec_sum[2:3, 0:128] = whole[:, width:]
        for k in range(1, n_wsh):
            s = lax.rem(z + k, n_wsh)
            arrive(row_line.at[s], rl_send.at[0], rl_recv.at[s], c, z)
            total = total + row_line[s]
        vec_sum[0:1, :] = total
        own_vec = pltpu.make_async_copy(vec_sum, vec_out, local_sem.at[12])
        own_vec.start()
        for plane in planes + plane_w:
            all_others(plane)
            plane.finish()
        for i in range(n_ctx // 2):
            left(part(c), hp_send.at[i], hp_recv.at[i], c, z)
        for i in range(2):
            left(part(c), hf_send.at[i], hf_recv.at[i], c, z)
        left(part(c), hs_send.at[0], hs_recv.at[0], c, z)
        for copy in (own_gtok, own_vec, *[own_window(h) for h in range(heads)]):
            copy.wait()

    pl.run_scoped(
        attention_backward,
        vm((n_ctx, heads, 128, rows), bf16), vm((heads, length, 128), bf16), vm((heads, length, 128), bf16),
        vm((heads, length, 128), f32), vm((heads, length, 128), f32), vm((w_c.shape[1], length), bf16),
    )

    wline.finish(wqkv_ref)
    for k in range(1, n_wsh):
        left(pack_ref, pk_send.at[k], pk_recv.at[z], c, z)
        left(vec, vl_send.at[k], vl_recv.at[0], c, z)
        left(row, rl_send.at[k], rl_recv.at[0], c, z)
    for k in range(1, n_ctx):
        g = lax.rem(c + k, n_ctx)
        left(ob_stage.at[g], ob_send.at[g], ob_recv.at[g], c, z)
        left(go_land.at[0], go_send.at[k], go_recv.at[0], c, z)
        left(vec, vp_send.at[k], vp_recv.at[0], c, z)
        left(row, rp_send.at[k], rp_recv.at[0], c, z)
    for w in range(3):
        pltpu.make_async_copy(final_piece(w), out_piece(w, c), local_sem.at[8 + w]).wait()
        left(deep_f if w == DOWN else land_f.at[w], f_send.at[w], f_recv.at[w], c, z)
        left(deep_s if w == DOWN else land_s.at[w], s_send.at[w], s_recv.at[w], c, z)
        for j in range(2):
            left(deep_near.at[j] if w == DOWN else land_near.at[w, j], zn_send.at[w, j], zn_recv.at[w, j], c, z)
        left(deep_far if w == DOWN else land_far.at[w], zf_send.at[w], zf_recv.at[w], c, z)
    for h in range(heads):
        for j in range(2):
            left(win_near.at[h, j], wn_send.at[h, j], wn_recv.at[h, j], c, z)
        left(win_far.at[h], wf_send.at[h], wf_recv.at[h], c, z)


def whole_call(dims, tok, cot, wqkv, w3, pack, order, lengths):
    n_ctx, n_wsh, hd, heads = dims
    rows, width = tok.shape
    span, length, shard = hd * heads, rows * n_ctx, width // n_wsh
    half, cut = width // 2, shard // (n_ctx // 2)
    f32, bf16 = jnp.float32, jnp.bfloat16
    hbm = pl.BlockSpec(memory_space=pl.ANY)
    smem = pl.BlockSpec(memory_space=pltpu.SMEM)
    shape = jax.ShapeDtypeStruct
    dma = pltpu.SemaphoreType.DMA
    vm = pltpu.VMEM
    size = windows(width, n_wsh)[1]
    wide = (rows, width)
    outs = (
        shape(wide, bf16), shape(wide, bf16),
        shape((3, shard, width), bf16), shape((n_ctx, heads, 3 * hd, size), bf16), shape((8, width), f32),
    )
    scratch = [
        vm((n_ctx, rows, width), bf16), vm((3, width, width), bf16), vm((length, width), bf16),
        vm((width, wqkv.shape[1]), bf16), vm((n_wsh,) + pack.shape, f32), vm((8, width), f32),
        vm((heads, length, 128), bf16), vm((heads, length, 128), bf16), vm((heads, hd, length), bf16),
        vm((n_ctx, heads, 128, rows), bf16), vm((n_ctx, span, rows), f32), vm((n_ctx, span, rows), f32),
        vm((n_ctx, span, rows), bf16), vm((width, rows), bf16), vm((width, rows), bf16), vm((n_ctx, span, rows), bf16),
        vm((3, n_wsh, shard, half), bf16), vm((2, n_wsh, 2 * cut, half), bf16), vm((2, n_wsh, cut, half), bf16),
        vm((2, 2, cut, half), bf16), vm((2, cut, half), bf16),
        vm((2, shard, half), bf16), vm((shard, half), bf16), vm((2 * cut, half), bf16), vm((cut, half), bf16),
        vm((heads, n_wsh, 3 * hd, size), bf16), vm((heads, 2, 3 * hd, size), bf16), vm((heads, 3 * hd, size), bf16),
        vm(wide, f32), vm(wide, f32), vm(wide, bf16), vm(wide, bf16), vm(wide, bf16),
        vm((1, width + 128), f32), vm((n_ctx, 1, width + 128), f32), vm((n_wsh, 1, width + 128), f32),
        vm((1, width + 128), f32), vm((8, width), f32), vm((1, width), f32), vm((n_ctx, 1, width), f32), vm((n_wsh, 1, width), f32),
        vm((1, width), f32), vm((hd, rows), f32),
        dma((2, 7)), dma((2, n_ctx)), dma((2 * n_wsh,)), dma((n_wsh,)), dma((n_wsh,)), dma((n_wsh,)),
        dma((n_ctx,)), dma((n_ctx,)), dma((3, 2 * n_wsh)), dma((3, n_wsh)),
        dma((3, n_wsh, 7)), dma((3, n_wsh, n_ctx)),
        dma((n_ctx,)), dma((n_ctx,)), dma((3,)), dma((3,)), dma((3,)), dma((3,)), dma((3,)), dma((3,)),
        dma((3, 2)), dma((3, 2)), dma((3,)), dma((3,)), dma((3, 7)), dma((3, n_ctx)),
        dma((n_ctx // 2,)), dma((n_ctx // 2,)), dma((2,)), dma((2,)), dma((1,)), dma((1,)),
        dma((heads, 2)), dma((heads, 2)), dma((heads,)), dma((heads,)), dma((heads, 7)), dma((heads, n_ctx)),
        dma((n_ctx,)), dma((n_ctx,)), dma((n_wsh,)), dma((n_wsh,)),
        dma((n_ctx,)), dma((n_ctx,)), dma((n_wsh,)), dma((n_wsh,)), dma((13,)), dma((heads + 3,)),
    ]
    return pl.pallas_call(
        functools.partial(whole_kernel, dims),
        out_shape=outs,
        in_specs=[hbm] * 7 + [smem] * 2,
        out_specs=[hbm] * len(outs),
        scratch_shapes=scratch,
        compiler_params=pltpu.CompilerParams(
            collective_id=0, has_side_effects=True, vmem_limit_bytes=VMEM_BYTES
        ),
    )(tok, cot, wqkv, *w3, pack, order, lengths)


def finish_kernel(dims, dwqkv_ref, dw3_ref, *refs):
    outs, (pieces, plain, wide, turned, results, in_sem, out_sem) = refs[:6], refs[6:]
    n_ctx, n_wsh, hd, heads = dims
    z = lax.axis_index("wsh")
    f32 = jnp.float32
    shard, width = outs[0].shape
    starts, size = windows(width, n_wsh)
    offset = jnp.int32(0)
    for s in range(n_wsh):
        offset = jnp.where(z == s, s * shard - starts[s], offset)
    ins = [pltpu.make_async_copy(dw3_ref.at[w], plain.at[w], in_sem.at[w]) for w in range(3)]
    for i in range(3):
        at = pl.ds(i * hd, hd)
        ins.append(pltpu.make_async_copy(dwqkv_ref.at[:, :, at], pieces.at[i], in_sem.at[3 + i]))
    for copy in ins:
        copy.start()
    done = []

    def store(i):
        copy = pltpu.make_async_copy(results.at[i], outs[i], out_sem.at[i])
        copy.start()
        done.append(copy)

    for w in range(3):
        ins[w].wait()
        results[3 + w] = plain[w].astype(f32)
        store(3 + w)
    for i in range(3):
        ins[3 + i].wait()

        def lay(b, _):
            for h in range(heads):
                at = pl.ds(pl.multiple_of((b * heads + h) * hd, 16), hd)
                wide[at, :] = pieces[i, b, h].astype(f32)
            return 0

        lax.fori_loop(0, n_ctx, lay, 0)

        def turn(j, _):
            at = pl.ds(pl.multiple_of(j * 128, 128), 128)
            turned[:, at] = wide[at, :].T
            return 0

        lax.fori_loop(0, width // 128, turn, 0)
        results[i] = turned[pl.ds(pl.multiple_of(offset, 8), shard), :]
        store(i)
    for copy in done:
        copy.wait()


def finish_call(dims, dwqkv, dw3):
    n_ctx, n_wsh, hd, heads = dims
    shard, width = dw3.shape[1:]
    size = dwqkv.shape[3]
    f32, bf16 = jnp.float32, jnp.bfloat16
    hbm = pl.BlockSpec(memory_space=pl.ANY)
    dma = pltpu.SemaphoreType.DMA
    return pl.pallas_call(
        functools.partial(finish_kernel, dims),
        out_shape=(jax.ShapeDtypeStruct((shard, width), f32),) * 6,
        in_specs=[hbm] * 2,
        out_specs=[hbm] * 6,
        scratch_shapes=[
            pltpu.VMEM((3, n_ctx, heads, hd, size), bf16), pltpu.VMEM((3, shard, width), bf16),
            pltpu.VMEM((width, size), f32), pltpu.VMEM((size, width), f32), pltpu.VMEM((6, shard, width), f32),
            dma((6,)), dma((6,)),
        ],
        compiler_params=pltpu.CompilerParams(vmem_limit_bytes=VMEM_BYTES),
    )(dwqkv, dw3)


def head_split(
    tokens, cotangent, block_lengths, group_order, w_query, w_key, w_value, w_out, w_up, w_down,
    gain_attn, gain_mlp, query_scale,
):
    f32 = jnp.float32
    n_ctx, n_wsh = lax.axis_size("ctx"), lax.axis_size("wsh")
    c, z = lax.axis_index("ctx"), lax.axis_index("wsh")
    width = tokens.shape[2]
    hd, heads = width // H, H // n_ctx
    span, shard = hd * heads, width // n_wsh
    dims = (n_ctx, n_wsh, hd, heads)
    mine = [lax.dynamic_slice_in_dim(w, c * span, span, 1) for w in (w_query, w_key, w_value)]
    mine = [w[:, h * hd : (h + 1) * hd] for h in range(heads) for w in mine]
    lanes = -(-3 * span // 128) * 128
    wqkv = jnp.pad(jnp.concatenate(mine, 1), ((0, 0), (0, lanes - 3 * span)))
    lanes = -(-shard // 128) * 128
    pack = sum(
        jnp.pad(v.astype(f32)[None], ((i, 7 - i), (0, lanes - v.shape[0])))
        for i, v in enumerate((gain_attn, gain_mlp, query_scale))
    )
    outputs, gtok, dw3, dwqkv, sums = whole_call(
        dims, tokens[0], cotangent[0], wqkv, (w_out, w_up, w_down), pack, group_order, block_lengths
    )[:5]
    weight_grads = finish_call(dims, dwqkv, dw3)
    own = [lax.dynamic_slice_in_dim(sums[i], z * shard, shard, 0) for i in (0, 1)]
    scale_grad = (
        lax.dynamic_slice_in_dim(sums[2], z * (hd // n_wsh), hd // n_wsh, 0)
        * (LOG_BASE / math.sqrt(hd))
        * jax.nn.sigmoid(query_scale.astype(f32))
    )
    return (
        outputs.reshape(tokens.shape), gtok.reshape(tokens.shape), *weight_grads, own[0], own[1], scale_grad,
    )


def solution(mesh):
    in_specs = (
        P("wsh", "ctx", None),
        P("wsh", "ctx", None),
        P("wsh", None),
        P(),
        P("wsh", None),
        P("wsh", None),
        P("wsh", None),
        P("wsh", None),
        P("wsh", None),
        P("wsh", None),
        P("wsh"),
        P("wsh"),
        P("wsh"),
    )
    out_specs = (
        P("wsh", "ctx", None),
        P("wsh", "ctx", None),
        P("wsh", None),
        P("wsh", None),
        P("wsh", None),
        P("wsh", None),
        P("wsh", None),
        P("wsh", None),
        P("wsh"),
        P("wsh"),
        P("wsh"),
    )
    n_ctx, n_wsh = mesh.shape["ctx"], mesh.shape["wsh"]
    plan = head_split if (n_ctx, n_wsh) == (8, 4) else per_device
    return jax.shard_map(
        plan, mesh=mesh, in_specs=in_specs, out_specs=out_specs, check_vma=False
    )
```

```python
import functools
import math

import jax
import jax.numpy as jnp
from jax import lax
from jax.experimental import pallas as pl
from jax.experimental.pallas import tpu as pltpu
from jax.sharding import PartitionSpec as P

H = 16


EPS = 1e-06
LOG_BASE = 1.442695041


def row_step():
    return 512


def rows_at(array, block_no, step_rows):
    return lax.dynamic_slice_in_dim(array, block_no * step_rows, step_rows, 0)


def inverse_rms(values):
    return lax.rsqrt(jnp.mean(values * values, -1, keepdims=True) + EPS)


def norm_back(normed, inverse, grad):
    return inverse * (grad - normed * jnp.mean(grad * normed, -1, keepdims=True))


def split_heads(matrix):
    return matrix.reshape(matrix.shape[0], H, -1)


def outer_product(left, right):
    return lax.dot_general(
        left, right, (((0,), (0,)), ((), ())), preferred_element_type=jnp.float32
    )


def back_product(grad, weight):
    return lax.dot_general(
        grad, weight, (((1,), (1,)), ((), ())), preferred_element_type=jnp.float32
    )


def probabilities(query3, key3, query_marks, key_marks, log_totals):
    scores = jnp.einsum("qhd,khd->hqk", query3, key3, preferred_element_type=jnp.float32)
    allowed = key_marks[None, None, :] <= query_marks[None, :, None]
    return jnp.exp(jnp.where(allowed, scores - log_totals[:, :, None], -jnp.inf))


def score_grads(chances, grad_out3, value3, deltas):
    grad_chances = jnp.einsum("qhd,khd->hqk", grad_out3, value3, preferred_element_type=jnp.float32)
    return (chances * (grad_chances - deltas[:, :, None])).astype(jnp.bfloat16)


def per_device(
    tokens,
    cotangent,
    block_lengths,
    group_order,
    w_query,
    w_key,
    w_value,
    w_out,
    w_up,
    w_down,
    gain_attn,
    gain_mlp,
    query_scale,
):
    gathered = (
        lax.all_gather(w_query, "wsh", axis=0, tiled=True),
        lax.all_gather(w_key, "wsh", axis=0, tiled=True),
        lax.all_gather(w_value, "wsh", axis=0, tiled=True),
        lax.all_gather(w_out, "wsh", axis=0, tiled=True),
        lax.all_gather(w_up, "wsh", axis=0, tiled=True),
        lax.all_gather(w_down, "wsh", axis=0, tiled=True),
        lax.all_gather(gain_attn, "wsh", axis=0, tiled=True),
        lax.all_gather(gain_mlp, "wsh", axis=0, tiled=True),
        lax.all_gather(query_scale, "wsh", axis=0, tiled=True),
    )
    (
        full_query,
        full_key,
        full_value,
        full_out,
        full_up,
        full_down,
        norm_attn,
        norm_mlp,
        scale_param,
    ) = gathered
    tok_rows = tokens.shape[1]
    model_width = tokens.shape[2]
    length = tok_rows * lax.axis_size("ctx")
    device = lax.axis_index("ctx")
    head_size = scale_param.shape[0]
    f32 = jnp.float32
    bf16 = jnp.bfloat16
    inputs = tokens.reshape(tok_rows, model_width).astype(f32)
    positions = (
        group_order[:, None] * tok_rows + jnp.arange(tok_rows, dtype=jnp.int32)[None, :]
    ).reshape(length)
    bounds = jnp.cumsum(block_lengths[0])
    block_ids = jnp.sum((bounds[None, :] <= positions[:, None]).astype(jnp.int32), -1)
    query_ids = lax.dynamic_slice_in_dim(block_ids, device * tok_rows, tok_rows, 0)
    inverse_one = inverse_rms(inputs)
    normed_one = inputs * inverse_one
    hidden_one = (normed_one * norm_attn.astype(f32)).astype(bf16)
    query_raw = jnp.dot(hidden_one, full_query, preferred_element_type=f32).reshape(
        tok_rows, H, head_size
    )
    query_gain = LOG_BASE / math.sqrt(head_size) * jax.nn.softplus(scale_param.astype(f32))
    query3 = (query_raw * query_gain).astype(bf16)
    key_flat = jnp.dot(hidden_one, full_key, preferred_element_type=f32).astype(bf16)
    value_flat = jnp.dot(hidden_one, full_value, preferred_element_type=f32).astype(bf16)
    initial = (
        jnp.full((H, tok_rows), -1e30, f32),
        jnp.zeros((H, tok_rows), f32),
        jnp.zeros((tok_rows, H, head_size), f32),
    )
    key_rows = lax.all_gather(key_flat, "ctx", axis=0, tiled=True)
    value_rows = lax.all_gather(value_flat, "ctx", axis=0, tiled=True)
    row_count = key_rows.shape[0]
    step_rows = row_step()

    def one_block(block_no, looped):
        key_part = split_heads(rows_at(key_rows, block_no, step_rows))
        value_part = split_heads(rows_at(value_rows, block_no, step_rows))
        block_marks = rows_at(block_ids, block_no, step_rows)
        maxima, totals, running = looped
        scores = jnp.einsum("qhd,khd->hqk", query3, key_part, preferred_element_type=f32)
        allowed = block_marks[None, None, :] <= query_ids[None, :, None]
        scores = jnp.where(allowed, scores, -jnp.inf)
        raised = jnp.maximum(maxima, jnp.max(scores, -1))
        rescale = jnp.exp(maxima - raised)
        weights = jnp.exp(scores - raised[:, :, None])
        totals = totals * rescale + jnp.sum(weights, -1)
        running = running * rescale.T[:, :, None] + jnp.einsum(
            "hqk,khd->qhd", weights.astype(bf16), value_part, preferred_element_type=f32
        )
        return (raised, totals, running)

    maxima, totals, running = lax.fori_loop(0, row_count // step_rows, one_block, initial)
    log_totals = maxima + jnp.log(totals)
    attended = running / totals.T[:, :, None]
    attended_bf = attended.reshape(tok_rows, model_width).astype(bf16)
    mixed = inputs + jnp.dot(attended_bf, full_out, preferred_element_type=f32)
    inverse_two = inverse_rms(mixed)
    normed_two = mixed * inverse_two
    hidden_two = (normed_two * norm_mlp.astype(f32)).astype(bf16)
    up_raw = jnp.dot(hidden_two, full_up, preferred_element_type=f32)
    active = jax.nn.silu(up_raw).astype(bf16)
    outputs = mixed + jnp.dot(active, full_down, preferred_element_type=f32)
    grad_output = cotangent.reshape(tok_rows, model_width).astype(f32)
    grad_mlp = grad_output.astype(bf16)
    grad_active = back_product(grad_mlp, full_down)
    sigmoid_up = jax.nn.sigmoid(up_raw)
    grad_up_raw = (grad_active * sigmoid_up * (1.0 + up_raw * (1.0 - sigmoid_up))).astype(bf16)
    grad_hidden_two = back_product(grad_up_raw, full_up)
    grad_gain_mlp = jnp.sum(grad_hidden_two * normed_two, 0)
    grad_mixed = grad_output + norm_back(
        normed_two, inverse_two, grad_hidden_two * norm_mlp.astype(f32)
    )
    grad_branch = grad_mixed.astype(bf16)
    grad_att = back_product(grad_branch, full_out).astype(bf16)
    grad_att3 = split_heads(grad_att)
    deltas = jnp.sum(grad_att3.astype(f32) * attended, -1).T
    key_whole, value_whole = (
        lax.all_gather(key_flat, "ctx", axis=0, tiled=True),
        lax.all_gather(value_flat, "ctx", axis=0, tiled=True),
    )
    step_rows = row_step()
    block_total = length // step_rows

    def key_block(grad_q, block_parts):
        key_rows, value_rows, block_marks = block_parts
        key_part = split_heads(key_rows)
        value_part = split_heads(value_rows)
        zero_part = jnp.zeros((key_rows.shape[0], H, head_size), f32)
        chances = probabilities(query3, key_part, query_ids, block_marks, log_totals)
        slopes = score_grads(chances, grad_att3, value_part, deltas)
        new_grad = (grad_q, zero_part, zero_part)[0] + jnp.einsum(
            "hqk,khd->qhd", slopes, key_part, preferred_element_type=f32
        )
        grad_key_part = jnp.einsum("hqk,qhd->khd", slopes, query3, preferred_element_type=f32)
        grad_value_part = jnp.einsum(
            "hqk,qhd->khd", chances.astype(bf16), grad_att3, preferred_element_type=f32
        )
        return (new_grad, (grad_key_part, grad_value_part))

    grad_qs, (key_terms, value_terms) = lax.scan(
        key_block,
        jnp.zeros((tok_rows, H, head_size), f32),
        (
            key_whole.reshape(block_total, step_rows, model_width),
            value_whole.reshape(block_total, step_rows, model_width),
            block_ids.reshape(block_total, step_rows),
        ),
    )
    grad_key, grad_value = (
        lax.psum_scatter(
            key_terms.reshape(length, model_width).astype(jnp.bfloat16),
            "ctx",
            scatter_dimension=0,
            tiled=True,
        ).astype(jnp.float32),
        lax.psum_scatter(
            value_terms.reshape(length, model_width).astype(jnp.bfloat16),
            "ctx",
            scatter_dimension=0,
            tiled=True,
        ).astype(jnp.float32),
    )
    grad_key_bf = grad_key.astype(bf16)
    grad_value_bf = grad_value.astype(bf16)
    grad_query_bf = (grad_qs * query_gain).reshape(tok_rows, model_width).astype(bf16)
    grad_scale_param = (
        jnp.sum(grad_qs * query_raw, (0, 1))
        * (LOG_BASE / math.sqrt(head_size))
        * jax.nn.sigmoid(scale_param.astype(f32))
    )
    grad_hidden_one = (
        back_product(grad_query_bf, full_query)
        + back_product(grad_key_bf, full_key)
        + back_product(grad_value_bf, full_value)
    )
    grad_gain_attn = jnp.sum(grad_hidden_one * normed_one, 0)
    grad_inputs = grad_mixed + norm_back(
        normed_one, inverse_one, grad_hidden_one * norm_attn.astype(f32)
    )
    grad_queryw = outer_product(hidden_one, grad_query_bf)
    grad_keyw = outer_product(hidden_one, grad_key_bf)
    grad_valuew = outer_product(hidden_one, grad_value_bf)
    grad_outw = outer_product(attended_bf, grad_branch)
    grad_upw = outer_product(hidden_two, grad_up_raw)
    grad_downw = outer_product(active, grad_mlp)
    owned = (
        lax.psum_scatter(
            grad_queryw.astype(jnp.bfloat16), "wsh", scatter_dimension=0, tiled=True
        ).astype(jnp.float32),
        lax.psum_scatter(
            grad_keyw.astype(jnp.bfloat16), "wsh", scatter_dimension=0, tiled=True
        ).astype(jnp.float32),
        lax.psum_scatter(
            grad_valuew.astype(jnp.bfloat16), "wsh", scatter_dimension=0, tiled=True
        ).astype(jnp.float32),
        lax.psum_scatter(
            grad_outw.astype(jnp.bfloat16), "wsh", scatter_dimension=0, tiled=True
        ).astype(jnp.float32),
        lax.psum_scatter(
            grad_upw.astype(jnp.bfloat16), "wsh", scatter_dimension=0, tiled=True
        ).astype(jnp.float32),
        lax.psum_scatter(
            grad_downw.astype(jnp.bfloat16), "wsh", scatter_dimension=0, tiled=True
        ).astype(jnp.float32),
        lax.psum_scatter(
            grad_gain_attn.astype(jnp.bfloat16), "wsh", scatter_dimension=0, tiled=True
        ).astype(jnp.float32),
        lax.psum_scatter(
            grad_gain_mlp.astype(jnp.bfloat16), "wsh", scatter_dimension=0, tiled=True
        ).astype(jnp.float32),
        lax.psum_scatter(
            grad_scale_param.astype(jnp.bfloat16), "wsh", scatter_dimension=0, tiled=True
        ).astype(jnp.float32),
    )
    summed = (
        lax.psum(owned[0].astype(jnp.bfloat16), "ctx").astype(jnp.float32),
        lax.psum(owned[1].astype(jnp.bfloat16), "ctx").astype(jnp.float32),
        lax.psum(owned[2].astype(jnp.bfloat16), "ctx").astype(jnp.float32),
        lax.psum(owned[3].astype(jnp.bfloat16), "ctx").astype(jnp.float32),
        lax.psum(owned[4].astype(jnp.bfloat16), "ctx").astype(jnp.float32),
        lax.psum(owned[5].astype(jnp.bfloat16), "ctx").astype(jnp.float32),
        lax.psum(owned[6].astype(jnp.bfloat16), "ctx").astype(jnp.float32),
        lax.psum(owned[7].astype(jnp.bfloat16), "ctx").astype(jnp.float32),
        lax.psum(owned[8].astype(jnp.bfloat16), "ctx").astype(jnp.float32),
    )
    return (
        outputs.reshape(tokens.shape).astype(bf16),
        grad_inputs.reshape(tokens.shape).astype(bf16),
        summed[0],
        summed[1],
        summed[2],
        summed[3],
        summed[4],
        summed[5],
        summed[6],
        summed[7],
        summed[8],
    )


MESH = pl.DeviceIdType.MESH
NEG = -1e30
VMEM_BYTES = 62 * 1024 * 1024


def place():
    c, z = lax.axis_index("ctx"), lax.axis_index("wsh")
    core, x, y = lax.rem(c, 2), lax.rem(c // 2, 2), c // 4
    sib = c + 1 - 2 * core
    over_x, over_y = c + 2 - 4 * x, c + 4 - 8 * y
    first = over_x * (1 - core) + over_y * core
    second = over_y * (1 - core) + over_x * core
    diag = over_x + over_y - c
    return c, z, sib, first, second, diag


def greet(c, z, n_ctx, n_wsh):
    barrier = pltpu.get_barrier_semaphore()
    for k in range(1, n_ctx):
        pl.semaphore_signal(
            barrier, inc=1, device_id=(lax.rem(c + k, n_ctx), z), device_id_type=MESH
        )
    for k in range(1, n_wsh):
        pl.semaphore_signal(
            barrier, inc=1, device_id=(c, lax.rem(z + k, n_wsh)), device_id_type=MESH
        )


def met(n_ctx, n_wsh):
    pl.semaphore_wait(pltpu.get_barrier_semaphore(), n_ctx + n_wsh - 2)


def send(src, dst, send_sem, recv_sem, c, z):
    copy = pltpu.make_async_remote_copy(
        src_ref=src, dst_ref=dst, send_sem=send_sem, recv_sem=recv_sem,
        device_id=(c, z), device_id_type=MESH,
    )
    copy.start()
    return copy


def arrive(dst, send_sem, recv_sem, c, z):
    pltpu.make_async_remote_copy(
        src_ref=dst, dst_ref=dst, send_sem=send_sem, recv_sem=recv_sem,
        device_id=(c, z), device_id_type=MESH,
    ).wait_recv()


def left(src, send_sem, recv_sem, c, z):
    pltpu.make_async_remote_copy(
        src_ref=src, dst_ref=src, send_sem=send_sem, recv_sem=recv_sem,
        device_id=(c, z), device_id_type=MESH,
    ).wait_send()


class Line:
    def __init__(self, at, c, z, n, send_sem, recv_sem):
        self.at, self.c, self.z, self.n = at, c, z, n
        self.send_sem, self.recv_sem = send_sem, recv_sem

    def start(self, own):
        c, z = self.c, self.z

        @pl.when(z < self.n - 1)
        def _():
            send(own, self.at(z), self.send_sem.at[0], self.recv_sem.at[z], c, z + 1)

        @pl.when(z > 0)
        def _():
            send(own, self.at(z), self.send_sem.at[1], self.recv_sem.at[z], c, z - 1)

    def forward(self, distance, then=None):
        c, z, n = self.c, self.z, self.n
        below, above = z - distance, z + distance

        @pl.when(below >= 0)
        def _():
            arrive(self.at(below), self.send_sem.at[0], self.recv_sem.at[below], c, z)

            @pl.when(z < n - 1)
            def _():
                send(self.at(below), self.at(below), self.send_sem.at[2 * distance], self.recv_sem.at[below], c, z + 1)

            if then is not None:
                then(below)

        @pl.when(above < n)
        def _():
            arrive(self.at(above), self.send_sem.at[0], self.recv_sem.at[above], c, z)

            @pl.when(z > 0)
            def _():
                send(self.at(above), self.at(above), self.send_sem.at[2 * distance + 1], self.recv_sem.at[above], c, z - 1)

            if then is not None:
                then(above)

    def finish(self, own):
        c, z, n = self.c, self.z, self.n

        @pl.when(z < n - 1)
        def _():
            left(own, self.send_sem.at[0], self.recv_sem.at[z], c, z)

        @pl.when(z > 0)
        def _():
            left(own, self.send_sem.at[1], self.recv_sem.at[z], c, z)

        for distance in range(1, n):
            below, above = z - distance, z + distance

            @pl.when((below >= 0) & (z < n - 1))
            def _():
                left(self.at(below), self.send_sem.at[2 * distance], self.recv_sem.at[below], c, z)

            @pl.when((above < n) & (z > 0))
            def _():
                left(self.at(above), self.send_sem.at[2 * distance + 1], self.recv_sem.at[above], c, z)


class Plane:
    def __init__(self, at, c, z, around, send_sem, recv_sem):
        self.at, self.c, self.z = at, c, z
        self.sib, self.first, self.second, self.diag = around
        self.send_sem, self.recv_sem = send_sem, recv_sem

    def push(self, slot, block, target, src=None):
        src = self.at(block) if src is None else src
        send(src, self.at(block), self.send_sem.at[slot], self.recv_sem.at[block], target, self.z)

    def wait(self, block):
        arrive(self.at(block), self.send_sem.at[0], self.recv_sem.at[block], self.c, self.z)

    def start(self, own=None):
        self.push(0, self.c, self.first, own)
        self.push(1, self.c, self.second, own)
        self.push(2, self.c, self.sib, own)

    def from_first(self):
        self.wait(self.first)
        self.push(3, self.first, self.second)
        self.push(4, self.first, self.sib)

    def from_second(self):
        self.wait(self.second)
        self.push(5, self.second, self.sib)

    def from_diag(self):
        self.wait(self.diag)
        self.push(6, self.diag, self.sib)

    def others(self):
        shift = self.sib - self.c
        return (self.sib, self.second + shift, self.first + shift, self.diag + shift)

    def finish(self):
        for slot in range(7):
            left(self.at(self.c), self.send_sem.at[slot], self.recv_sem.at[self.c], self.c, self.z)


def block_ids_of(block, order_ref, lengths_ref, rows):
    n_blk = lengths_ref.shape[1]
    position = order_ref[block] * rows + lax.broadcasted_iota(jnp.int32, (8, rows), 1)
    ids = jnp.zeros((8, rows), jnp.int32)
    bound = jnp.int32(0)
    for b in range(n_blk):
        bound = bound + lengths_ref[0, b]
        ids = ids + jnp.where(position >= bound, 1, 0)
    return ids, lax.broadcasted_iota(jnp.int32, (8, rows), 0)


def three_rows(value, rows):
    f32 = jnp.float32
    high = value.astype(jnp.bfloat16).astype(f32)
    rest = value - high
    mid = rest.astype(jnp.bfloat16).astype(f32)
    low = rest - mid
    row = lax.broadcasted_iota(jnp.int32, (8, rows), 0)
    return jnp.where(row == 0, high, 0.0) + jnp.where(row == 1, mid, 0.0) + jnp.where(row == 2, low, 0.0)


def add_rows(target, at, other, other_at, rows, step):
    f32 = jnp.float32

    def some_rows(i, _):
        here = pl.ds(pl.multiple_of(at + i * step, 16), step)
        there = pl.ds(pl.multiple_of(other_at + i * step, 16), step)
        target[here, :] = (target[here, :].astype(f32) + other[there, :].astype(f32)).astype(target.dtype)
        return 0

    lax.fori_loop(0, rows // step, some_rows, 0)


def windows(width, n):
    part = width // n
    tiles = -(-part // 128) + (0 if part % 128 == 0 else 0)
    size = tiles * 128
    return [min(s * part // 128 * 128, width - size) for s in range(n)], size


def whole_kernel(
    dims,
    tok_ref, cot_ref, wq_ref, wk_ref, wv_ref, wout_ref, wup_ref, wdown_ref, pack_ref, order_ref, lengths_ref,
    out_out, gtok_out, dw3_out, dwqkv_out, vec_out,
    h1_all, w_full, big, w_c, w_own, packs, gains, kaug, vaug, kt, qaug, qraw, o_all, ob_stage, ob_land, go_stage, go_land,
    acc, land_f, land_s, land_near, land_far, deep_near, deep_far, deep_f, deep_s, win_out, win_near, win_far,
    dx, dh, tok, cot, gtok, vec, vec_plane, vec_line, vec_mid, vec_sum, row, row_plane, row_line, row_mid, scale_acc,
    tok_send, tok_recv, wz_send, wz_recv, pk_send, pk_recv, ob_send, ob_recv,
    w3z_send, w3z_recv, w3p_send, w3p_recv,
    go_send, go_recv, p_send, p_recv, f_send, f_recv, s_send, s_recv, zn_send, zn_recv, zf_send, zf_recv, g_send, g_recv,
    hp_send, hp_recv, hf_send, hf_recv, hs_send, hs_recv, wn_send, wn_recv, wf_send, wf_recv, wg_send, wg_recv,
    vp_send, vp_recv, vl_send, vl_recv, rp_send, rp_recv, rl_send, rl_recv, local_sem, load_sem, cols_sem,
):
    n_ctx, n_wsh, hd, heads = dims
    f32, bf16 = jnp.float32, jnp.bfloat16
    c, z, sib, first, second, diag = place()
    around = (sib, first, second, diag)
    core, x, y = lax.rem(c, 2), lax.rem(c // 2, 2), c // 4
    f_bit, s_bit = x * (1 - core) + y * core, y * (1 - core) + x * core
    rows, width = tok_ref.shape
    span, length = hd * heads, rows * n_ctx
    shard, half = width // n_wsh, width // 2
    two, cut = shard // 2, shard // (n_ctx // 2)
    w3_refs = (wout_ref, wup_ref, wdown_ref)
    OUT, UP, DOWN = 0, 1, 2
    own_tok = pltpu.make_async_copy(tok_ref, tok, local_sem.at[0])
    columns_in = [
        pltpu.make_async_copy(ref.at[:, pl.ds(side * half, half)], acc.at[i, side], cols_sem.at[i, side])
        for i, ref in enumerate((wq_ref, wk_ref, wv_ref))
        for side in range(2)
    ]
    own_pack = pltpu.make_async_copy(pack_ref, packs.at[z], local_sem.at[2])
    own_cot = pltpu.make_async_copy(cot_ref, cot, local_sem.at[3])
    own_full = [
        pltpu.make_async_copy(
            w3_refs[w], w_full.at[w, pl.ds(pl.multiple_of(z * shard, 16), shard)], load_sem.at[heads + w]
        )
        for w in range(3)
    ]
    for copy in (*columns_in, own_tok, own_pack, own_cot, *own_full):
        copy.start()
    greet(c, z, n_ctx, n_wsh)
    for copy in columns_in:
        copy.wait()
    for k in range(n_ctx):

        @pl.when(c == k)
        def _():
            for h in range(heads):
                side, at = divmod(k * span + h * hd, half)
                for i in range(3):
                    w_own[:, (3 * h + i) * hd : (3 * h + i + 1) * hd] = acc[i, side, :, at : at + hd]

    w_own[:, 3 * span :] = jnp.zeros((shard, w_own.shape[1] - 3 * span), bf16)
    own_w = pltpu.make_async_copy(w_own, w_c.at[pl.ds(pl.multiple_of(z * shard, 16), shard)], local_sem.at[1])
    own_w.start()
    met(n_ctx, n_wsh)

    part_rows = rows // 2
    tokens = [
        Plane(
            lambda b, i=i: big.at[pl.ds(pl.multiple_of(b * rows + i * part_rows, 16), part_rows)], c, z, around,
            tok_send.at[i], tok_recv.at[i],
        )
        for i in range(2)
    ]
    for i in range(2):
        tokens[i].start(tok_ref.at[pl.ds(i * part_rows, part_rows)])
    wline = Line(lambda s: w_c.at[pl.ds(pl.multiple_of(s * shard, 16), shard)], c, z, n_wsh, wz_send, wz_recv)
    for k in range(1, n_wsh):
        send(pack_ref, packs.at[z], pk_send.at[k], pk_recv.at[z], c, lax.rem(z + k, n_wsh))
    wline.start(w_own)
    scale_acc[...] = jnp.zeros_like(scale_acc)

    def columns(b):
        return pl.ds(pl.multiple_of(lax.rem(b, 2) * half, 128), half)

    def piece(w, s, b):
        top = pl.multiple_of(s * shard + (b // 2) * cut, 16)
        return w_full.at[w, pl.ds(top, cut), columns(b)]

    my_piece = [ref.at[pl.ds(pl.multiple_of((c // 2) * cut, 16), cut), columns(c)] for ref in w3_refs]
    lines = [
        Line(lambda s, w=w: piece(w, s, c), c, z, n_wsh, w3z_send.at[w], w3z_recv.at[w]) for w in range(3)
    ]

    def plane_of(w, s):
        k = lax.rem(s - z + n_wsh, n_wsh)
        return Plane(lambda b: piece(w, s, b), c, z, around, w3p_send.at[w, k], w3p_recv.at[w, k])

    def shards_at(w, distance, step):
        below, above = z - distance, z + distance

        @pl.when(below >= 0)
        def _():
            step(plane_of(w, below))

        @pl.when(above < n_wsh)
        def _():
            step(plane_of(w, above))

    def spread(w, distance):
        lines[w].forward(distance, lambda s: plane_of(w, s).start())

    def step_of(step):
        return lambda w, distance: shards_at(w, distance, step)

    by_first, by_second, by_diag = step_of(Plane.from_first), step_of(Plane.from_second), step_of(Plane.from_diag)

    def all_others(plane):
        for b in plane.others():
            plane.wait(b)

    own_tok.wait()
    own_pack.wait()
    for k in range(1, n_wsh):
        other = lax.rem(z + k, n_wsh)
        arrive(packs.at[other], pk_send.at[0], pk_recv.at[other], c, z)
    row8 = lax.broadcasted_iota(jnp.int32, (8, width), 0)
    total = jnp.zeros((8, width), f32)
    for s in range(n_wsh):
        wide = jnp.concatenate([packs[s], jnp.zeros((8, width - packs.shape[2]), f32)], axis=1)
        by_shard = pltpu.roll(wide, s * shard, 1) if s else wide
        by_dim = pltpu.roll(wide, s * (hd // n_wsh), 1) if s else wide
        total = total + jnp.where(row8 < 2, by_shard, by_dim)
    gains[...] = total

    def gain_column():
        scale = jnp.concatenate([gains[2:3, 0:128], jnp.zeros((7, 128), f32)], axis=0)
        soft = jnp.maximum(scale, 0.0) + jnp.log(1.0 + jnp.exp(-jnp.abs(scale)))
        return (LOG_BASE / math.sqrt(hd) * soft).T[0:hd, 0:1]

    def attention_forward(vt, qneg, s_buf):
        def norm_block(b, source, top):
            gain = gains[0:1, :]

            def some_rows(i, _):
                t = source[pl.ds(pl.multiple_of(top + i * 32, 32), 32), :].astype(f32)
                inverse = lax.rsqrt(jnp.mean(t * t, -1, keepdims=True) + EPS)
                h1_all[b, pl.ds(pl.multiple_of(i * 32, 32), 32), :] = (t * inverse * gain).astype(bf16)
                return 0

            lax.fori_loop(0, rows // 32, some_rows, 0)

        def norm_arrived(b):
            norm_block(b, big, b * rows)

        def arrived(b):
            for i in range(2):
                tokens[i].wait(b)
            norm_arrived(b)

        others = tokens[0].others()
        lines[OUT].start(my_piece[OUT])
        norm_block(c, tok, 0)
        arrived(others[0])
        tokens[0].from_first()
        wline.forward(1)
        lines[UP].start(my_piece[UP])
        tokens[1].from_first()
        norm_arrived(first)
        tokens[0].from_second()
        tokens[1].from_second()
        norm_arrived(second)
        spread(OUT, 1)
        wline.forward(2)
        lines[DOWN].start(my_piece[DOWN])
        arrived(others[1])
        arrived(others[2])
        tokens[0].from_diag()
        tokens[1].from_diag()
        norm_arrived(diag)
        arrived(others[3])
        spread(OUT, 2)
        wline.forward(3)
        own_w.wait()
        spread(UP, 1)
        gain_col = gain_column()

        def project(b, _):
            raw = jnp.dot(h1_all[b], w_c[...], preferred_element_type=f32).T
            at = pl.ds(pl.multiple_of(b * rows, 128), rows)
            ids, row = block_ids_of(b, order_ref, lengths_ref, rows)
            hot = jnp.where(ids == row, 1.0, 0.0)
            neg = jnp.where(row > ids, NEG, 0.0)
            ones = jnp.ones((8, rows), f32)
            qneg[b] = neg
            for h in range(heads):
                top = 3 * h * hd
                q = raw[top : top + hd]
                qraw[b, h * hd : (h + 1) * hd, :] = q
                q = q * gain_col
                qaug[b, h, 0:hd, :] = q.astype(bf16)
                qaug[b, h, hd : hd + 16, :] = jnp.concatenate([neg, jnp.zeros((8, rows), f32)], axis=0).astype(bf16)
                qaug[b, h, hd + 16 : 128, :] = jnp.zeros((112 - hd, rows), bf16)
                k = raw[top + hd : top + 2 * hd].astype(bf16)
                v = raw[top + 2 * hd : top + 3 * hd].astype(bf16)
                tail = jnp.zeros((112 - hd, rows), f32)
                kt[h, :, at] = k
                vt[h, 0:hd, at] = v
                vt[h, hd : hd + 16, at] = jnp.ones((16, rows), bf16)
                kaug[h, at, :] = jnp.concatenate([k.astype(f32), hot, ones, tail], axis=0).T.astype(bf16)
                vaug[h, at, :] = jnp.concatenate([v.astype(f32), ones, ones, tail], axis=0).T.astype(bf16)
            return 0

        lax.fori_loop(0, n_ctx, project, 0)
        for i in range(2):
            tokens[i].finish()
        keys = length // 2
        plan = (
            (0, spread, OUT, 3), (0, by_first, OUT, 1), (1, by_first, OUT, 2), (1, spread, UP, 2),
            (2, by_second, OUT, 1), (2, by_second, OUT, 2), (3, spread, DOWN, 1), (3, by_first, OUT, 3),
            (4, by_diag, OUT, 1), (4, spread, UP, 3), (5, by_second, OUT, 3), (5, by_first, UP, 1),
            (6, spread, DOWN, 2), (6, by_diag, OUT, 2), (7, by_first, UP, 2), (8, by_diag, OUT, 3),
            (8, by_second, UP, 1), (9, by_second, UP, 2), (9, spread, DOWN, 3), (10, by_first, UP, 3),
            (11, by_diag, UP, 1), (11, by_first, DOWN, 1), (12, by_second, UP, 3), (12, by_diag, UP, 2),
            (13, by_first, DOWN, 2), (14, by_second, DOWN, 1), (14, by_diag, UP, 3), (15, by_second, DOWN, 2),
        )

        def attend(i, _):
            g = lax.rem(c + 1 + i, n_ctx)
            for h in range(heads):
                q = qaug[g, h]
                top = jnp.full((1, rows), -jnp.inf, f32)
                for j in range(2):
                    s = jnp.dot(kaug[h, j * keys : (j + 1) * keys, :], q, preferred_element_type=f32)
                    s_buf[j * keys : (j + 1) * keys, :] = s
                    top = jnp.maximum(top, jnp.max(s, axis=0, keepdims=True))
                out = jnp.zeros((hd + 16, rows), f32)
                for j in range(2):
                    p = jnp.exp(s_buf[j * keys : (j + 1) * keys, :] - top).astype(bf16)
                    out = out + jnp.dot(vt[h, :, j * keys : (j + 1) * keys], p, preferred_element_type=f32)
                total = out[hd : hd + 1]
                o = out[0:hd] / total
                lse = top + jnp.log(total)
                o_all[g, h * hd : (h + 1) * hd, :] = o
                ob_stage[g, h * hd : (h + 1) * hd, :] = o.astype(bf16)
                qaug[g, h, hd : hd + 16, :] = jnp.concatenate([qneg[g], three_rows(-lse, rows)], axis=0).astype(bf16)
                for slot, event, w, distance in plan:
                    if slot % heads == h:
                        pl.when(i == slot // heads)(functools.partial(event, w, distance))

            @pl.when(i < n_ctx - 1)
            def _():
                send(ob_stage.at[g], my_heads(ob_land), ob_send.at[g], ob_recv.at[c], g, z)

            return 0

        lax.fori_loop(0, n_ctx, attend, 0)

    def my_heads(ref):
        return ref.at[pl.ds(pl.multiple_of(c * span, 16), span)]

    def heads_of(ref, g):
        return ref.at[pl.ds(pl.multiple_of(g * span, 16), span)]

    vm = pltpu.VMEM
    pl.run_scoped(
        attention_forward,
        vm((heads, hd + 16, length), bf16), vm((n_ctx, 8, rows), f32), vm((length, rows), f32),
    )
    own_o = pltpu.make_async_copy(ob_stage.at[c], my_heads(ob_land), local_sem.at[4])
    own_o.start()

    mine = pl.ds(pl.multiple_of(core * half, 128), half)
    theirs = pl.ds(pl.multiple_of((1 - core) * half, 128), half)
    my_top = f_bit * two + s_bit * cut
    near, far = z + 1 - 2 * lax.rem(z, 2), z + 2 - 4 * (z // 2)

    def pair_at(w):
        return big.at[pl.ds(2 * w * shard, 2 * shard)]

    def add_pair(w):
        arrive(pair_at(w), p_send.at[w], p_recv.at[w], c, z)
        for s in range(n_wsh):
            other = big.at[:, pl.ds(s % 2 * half, half)]
            add_rows(acc.at[w, s], 0, other, (2 * w + s // 2) * shard, shard, 64)

    def pair_sum(w):
        add_pair(w)
        at = pl.ds(pl.multiple_of((1 - f_bit) * two, 16), two)
        send(acc.at[w, :, at], land_f.at[w], f_send.at[w], f_recv.at[w], first, z)

    def deep_pair_sum(w):
        add_pair(w)
        for j in range(2):
            s = 2 * j + lax.rem(near, 2)
            send(acc.at[w, s], deep_near.at[j], zn_send.at[w, j], zn_recv.at[w, j], c, near)

    def deep_near_sum(w):
        for j in range(2):
            arrive(deep_near.at[j], zn_send.at[w, j], zn_recv.at[w, j], c, z)
            add_rows(acc.at[w, 2 * j + lax.rem(z, 2)], 0, deep_near.at[j], 0, shard, 80)
        send(acc.at[w, far], deep_far, zf_send.at[w], zf_recv.at[w], c, far)

    def deep_far_sum(w):
        arrive(deep_far, zf_send.at[w], zf_recv.at[w], c, z)
        add_rows(acc.at[w, z], 0, deep_far, 0, shard, 80)
        at = pl.ds(pl.multiple_of((1 - f_bit) * two, 16), two)
        send(acc.at[w, z, at], deep_f, f_send.at[w], f_recv.at[w], first, z)

    def deep_first_sum(w):
        arrive(deep_f, f_send.at[w], f_recv.at[w], c, z)
        add_rows(acc.at[w, z], f_bit * two, deep_f, 0, two, 80)
        at = pl.ds(pl.multiple_of(f_bit * two + (1 - s_bit) * cut, 16), cut)
        send(acc.at[w, z, at], deep_s, s_send.at[w], s_recv.at[w], second, z)

    def deep_second_sum(w):
        arrive(deep_s, s_send.at[w], s_recv.at[w], c, z)
        add_rows(acc.at[w, z], my_top, deep_s, 0, cut, 80)
        planes[w].start(final_piece(w))
        pltpu.make_async_copy(final_piece(w), out_piece(w, c), local_sem.at[8 + w]).start()

    def first_sum(w):
        arrive(land_f.at[w], f_send.at[w], f_recv.at[w], c, z)
        for s in range(n_wsh):
            add_rows(acc.at[w, s], f_bit * two, land_f.at[w, s], 0, two, 80)
        at = pl.ds(pl.multiple_of(f_bit * two + (1 - s_bit) * cut, 16), cut)
        send(acc.at[w, :, at], land_s.at[w], s_send.at[w], s_recv.at[w], second, z)

    def second_sum(w):
        arrive(land_s.at[w], s_send.at[w], s_recv.at[w], c, z)
        for s in range(n_wsh):
            add_rows(acc.at[w, s], my_top, land_s.at[w, s], 0, cut, 80)
        at = pl.ds(pl.multiple_of(my_top, 16), cut)
        for j in range(2):
            s = 2 * j + lax.rem(near, 2)
            send(acc.at[w, s, at], land_near.at[w, j], zn_send.at[w, j], zn_recv.at[w, j], c, near)

    def near_sum(w):
        for j in range(2):
            arrive(land_near.at[w, j], zn_send.at[w, j], zn_recv.at[w, j], c, z)
            add_rows(acc.at[w, 2 * j + lax.rem(z, 2)], my_top, land_near.at[w, j], 0, cut, 80)
        at = pl.ds(pl.multiple_of(my_top, 16), cut)
        send(acc.at[w, far, at], land_far.at[w], zf_send.at[w], zf_recv.at[w], c, far)

    def out_piece(w, b):
        b_core, b_x, b_y = lax.rem(b, 2), lax.rem(b // 2, 2), b // 4
        r = (1 - b_core) * (2 * b_x + b_y) + b_core * (2 * b_y + b_x)
        return dw3_out.at[w, pl.ds(pl.multiple_of(r * cut, 16), cut), columns(b)]

    planes = [
        Plane(lambda b, w=w: out_piece(w, b), c, z, around, g_send.at[w], g_recv.at[w]) for w in range(3)
    ]

    def final_piece(w):
        return acc.at[w, z, pl.ds(pl.multiple_of(my_top, 16), cut)]

    def far_sum(w):
        arrive(land_far.at[w], zf_send.at[w], zf_recv.at[w], c, z)
        add_rows(acc.at[w, z], my_top, land_far.at[w], 0, cut, 80)
        planes[w].start(final_piece(w))
        pltpu.make_async_copy(final_piece(w), out_piece(w, c), local_sem.at[8 + w]).start()

    def feed_forward(x1, h2, a, gu, ob, turned, ga, inv2, outb, stage):
        def tiles(step, size=256):
            for top in range(0, width, size):
                step(slice(top, top + size))

        def turn(source, target):
            def one(at):
                target[at, :] = source[:, at].T

            tiles(one, 128)

        def weight_gradient(w, left_t, right):
            for s in range(n_wsh):
                stage[w, s // 2 * shard : (s // 2 + 1) * shard, s % 2 * half : (s % 2 + 1) * half] = jnp.dot(
                    left_t[s * shard : (s + 1) * shard, :], right[:, theirs], preferred_element_type=f32
                ).astype(bf16)
            send(stage.at[w], pair_at(w), p_send.at[w], p_recv.at[w], sib, z)
            for s in range(n_wsh):
                at = slice(s * shard, (s + 1) * shard)
                acc[w, s] = jnp.dot(left_t[at, :], right[:, mine], preferred_element_type=f32).astype(bf16)

        by_first(DOWN, 3)
        for distance in range(1, n_wsh):
            shards_at(OUT, distance, all_others)
        own_o.wait()
        for k in range(1, n_ctx):
            g = lax.rem(c + k, n_ctx)
            arrive(heads_of(ob_land, g), ob_send.at[0], ob_recv.at[g], c, z)

        def turn_ob(at):
            ob[:, at] = ob_land[at, :].T

        tiles(turn_ob, 128)
        by_diag(DOWN, 1)
        by_second(DOWN, 3)
        own_full[OUT].wait()

        def mix(at):
            x1[:, at] = tok[:, at].astype(f32) + jnp.dot(ob[...], w_full[OUT, :, at], preferred_element_type=f32)

        tiles(mix)
        by_diag(DOWN, 2)

        def norm_rows(i, _):
            at = pl.ds(pl.multiple_of(i * 32, 32), 32)
            t = x1[at, :]
            inverse = lax.rsqrt(jnp.mean(t * t, -1, keepdims=True) + EPS)
            inv2[at, :] = jnp.broadcast_to(inverse, (32, 128))
            h2[at, :] = (t * inverse * gains[1:2, :]).astype(bf16)
            return 0

        lax.fori_loop(0, rows // 32, norm_rows, 0)
        by_diag(DOWN, 3)
        for distance in range(1, n_wsh):
            shards_at(UP, distance, all_others)
        own_full[UP].wait()

        def lift(at):
            dh[:, at] = jnp.dot(h2[...], w_full[UP, :, at], preferred_element_type=f32)

        tiles(lift)
        own_cot.wait()
        for distance in range(1, n_wsh):
            shards_at(DOWN, distance, all_others)
        own_full[DOWN].wait()

        def hidden(at):
            up = dh[:, at]
            da = lax.dot_general(
                cot[...], w_full[DOWN, at, :], (((1,), (1,)), ((), ())), preferred_element_type=f32
            )
            sig = 1.0 / (1.0 + jnp.exp(-up))
            act = up * sig
            a[:, at] = act.astype(bf16)
            turned[at, :] = act.T.astype(bf16)
            gu[:, at] = (da * sig * (1.0 + up * (1.0 - sig))).astype(bf16)

        tiles(hidden)

        def back(at):
            dh[:, at] = lax.dot_general(
                gu[...], w_full[UP, at, :], (((1,), (1,)), ((), ())), preferred_element_type=f32
            )

        tiles(back)

        def norm_back_rows(i, total):
            at = pl.ds(pl.multiple_of(i * 16, 16), 16)
            inverse = inv2[at, 0:1]
            normed = x1[at, :] * inverse
            grad = dh[at, :]
            both = grad * normed
            slope = jnp.mean(both * gains[1:2, :], -1, keepdims=True)
            result = cot[at, :].astype(f32) + inverse * (grad * gains[1:2, :] - normed * slope)
            dx[at, :] = result
            ga[at, :] = result.astype(bf16)
            return total + both

        gain_sum = lax.fori_loop(0, rows // 16, norm_back_rows, jnp.zeros((16, width), f32))
        vec[:, 0:width] = jnp.sum(gain_sum, axis=0, keepdims=True)

        def back_out(at):
            go_stage[at, :] = lax.dot_general(
                w_full[OUT, at, :], ga[...], (((1,), (1,)), ((), ())), preferred_element_type=f32
            ).astype(bf16)

        tiles(back_out)
        for w in range(3):
            lines[w].finish(my_piece[w])
            for distance in range(1, n_wsh):
                shards_at(w, distance, Plane.finish)
        for k in range(1, n_ctx):
            g = lax.rem(c + k, n_ctx)
            send(heads_of(go_stage, g), go_land.at[c], go_send.at[k], go_recv.at[c], g, z)
        pltpu.make_async_copy(my_heads(go_stage), go_land.at[c], local_sem.at[5]).start()
        weight_gradient(DOWN, turned, cot)
        turn(h2, turned)
        weight_gradient(UP, turned, gu)
        deep_pair_sum(DOWN)
        weight_gradient(OUT, ob_land, ga)
        pair_sum(UP)

        def finish(at):
            outb[:, at] = (
                x1[:, at] + jnp.dot(a[...], w_full[DOWN, :, at], preferred_element_type=f32)
            ).astype(bf16)

        tiles(finish)
        own_out = pltpu.make_async_copy(outb, out_out, local_sem.at[6])
        own_out.start()
        pair_sum(OUT)
        own_out.wait()
        for w in range(3):
            left(stage.at[w], p_send.at[w], p_recv.at[w], c, z)

    wide = (rows, width)
    pl.run_scoped(
        feed_forward,
        vm(wide, f32), vm(wide, bf16), vm(wide, bf16), vm(wide, bf16), vm(wide, bf16),
        vm((width, rows), bf16), vm(wide, bf16), vm((rows, 128), f32), vm(wide, bf16),
        vm((3, 2 * shard, width), bf16),
    )

    def attention_backward(goaug, go_tm, q_tm, dk, dv, dqkv):
        per = width // rows

        def block(i):
            return w_full.at[i // per, :, pl.ds(pl.multiple_of(lax.rem(i, per) * rows, 128), rows)]

        def part_p(i):
            return block(i)

        def part_f(i):
            return block(n_ctx // 2 + i)

        part_s = block(jnp.int32(n_ctx // 2 + 2))

        def part(b):
            return block(n_ctx // 2 + 3 + b)

        dk[...] = jnp.zeros_like(dk)
        dv[...] = jnp.zeros_like(dv)
        dqkv[3 * span :, :] = jnp.zeros((dqkv.shape[0] - 3 * span, length), bf16)
        gain_col = gain_column()

        def prepare(g):
            at = pl.ds(pl.multiple_of(g * rows, 16), rows)
            for h in range(heads):
                go = go_land[g, h * hd : (h + 1) * hd, :]
                wide = go.astype(f32)
                delta = jnp.sum(wide * o_all[g, h * hd : (h + 1) * hd, :], axis=0, keepdims=True)
                tail = jnp.concatenate([three_rows(-delta, rows), jnp.zeros((120 - hd, rows), f32)], axis=0)
                goaug[g, h, 0:hd, :] = go
                goaug[g, h, hd:128, :] = tail.astype(bf16)
                go_tm[h, at, :] = jnp.concatenate([wide, jnp.zeros((128 - hd, rows), f32)], axis=0).T.astype(bf16)
                q = qaug[g, h, 0:hd, :].astype(f32)
                q_tm[h, at, :] = jnp.concatenate([q, jnp.zeros((128 - hd, rows), f32)], axis=0).T.astype(bf16)

        pltpu.make_async_copy(my_heads(go_stage), go_land.at[c], local_sem.at[5]).wait()
        prepare(c)

        def prepare_other(k, _):
            g = lax.rem(c + k, n_ctx)
            arrive(go_land.at[g], go_send.at[0], go_recv.at[g], c, z)
            prepare(g)
            return 0

        lax.fori_loop(1, n_ctx, prepare_other, 0)
        three = 3 * hd
        starts, size = windows(width, n_wsh)

        def head_gradients(h, events):
            def attend(g, _):
                at = pl.ds(pl.multiple_of(g * rows, 16), rows)
                p = jnp.exp(jnp.dot(kaug[h], qaug[g, h], preferred_element_type=f32))
                ds = (p * jnp.dot(vaug[h], goaug[g, h], preferred_element_type=f32)).astype(bf16)
                dq = jnp.dot(kt[h], ds, preferred_element_type=f32)
                dk[h] += jnp.dot(ds, q_tm[h, at, :], preferred_element_type=f32)
                dv[h] += jnp.dot(p.astype(bf16), go_tm[h, at, :], preferred_element_type=f32)
                scale_acc[...] += dq * qraw[g, h * hd : (h + 1) * hd, :]
                lanes = pl.ds(pl.multiple_of(g * rows, 128), rows)
                dqkv[h * three : h * three + hd, lanes] = (dq * gain_col).astype(bf16)
                for step, event in events:
                    pl.when(g == step)(event)
                return 0

            lax.fori_loop(0, n_ctx, attend, 0)

            def settle(g, _):
                at = pl.ds(pl.multiple_of(g * rows, 16), rows)
                lanes = pl.ds(pl.multiple_of(g * rows, 128), rows)
                for i, source in enumerate((dk, dv)):
                    turned = source[h, at, :].T
                    top = h * three + (i + 1) * hd
                    dqkv[top : top + hd, lanes] = turned[0:hd].astype(bf16)
                return 0

            lax.fori_loop(0, n_ctx, settle, 0)

        def head_windows(h):
            for s in range(n_wsh):
                total = jnp.zeros((three, size), f32)
                for b in range(n_ctx):
                    total = total + jnp.dot(
                        dqkv[h * three : (h + 1) * three, b * rows : (b + 1) * rows],
                        h1_all[b, :, starts[s] : starts[s] + size], preferred_element_type=f32,
                    )
                win_out[h, s] = total.astype(bf16)
            for j in range(2):
                s = 2 * j + lax.rem(near, 2)
                send(win_out.at[h, s], win_near.at[h, j], wn_send.at[h, j], wn_recv.at[h, j], c, near)

        def near_window(h):
            for j in range(2):
                arrive(win_near.at[h, j], wn_send.at[h, j], wn_recv.at[h, j], c, z)
                add_rows(win_out.at[h, 2 * j + lax.rem(z, 2)], 0, win_near.at[h, j], 0, three, 80)
            send(win_out.at[h, far], win_far.at[h], wf_send.at[h], wf_recv.at[h], c, far)

        plane_w = [
            Plane(lambda b, h=h: dwqkv_out.at[b, h], c, z, around, wg_send.at[h], wg_recv.at[h]) for h in range(heads)
        ]

        def own_window(h):
            return pltpu.make_async_copy(win_out.at[h, z], dwqkv_out.at[c, h], load_sem.at[h])

        def far_window(h):
            arrive(win_far.at[h], wf_send.at[h], wf_recv.at[h], c, z)
            add_rows(win_out.at[h, z], 0, win_far.at[h], 0, three, 80)
            plane_w[h].start(win_out.at[h, z])
            own_window(h).start()

        head_gradients(0, ((6, lambda: first_sum(UP)),))
        head_windows(0)
        head_gradients(1, (
            (1, lambda: second_sum(UP)), (4, lambda: deep_near_sum(DOWN)), (5, lambda: first_sum(OUT)),
            (6, lambda: near_sum(UP)), (6, lambda: near_window(0)), (7, lambda: second_sum(OUT)),
        ))

        def partial(b):
            lanes = pl.ds(pl.multiple_of(b * rows, 128), rows)
            part(b)[...] = jnp.dot(w_c[...], dqkv[:, lanes], preferred_element_type=f32).astype(bf16)

        def to_sib(b):
            partial(b)
            send(part(b), part_p(b // 2), hp_send.at[b // 2], hp_recv.at[b // 2], sib, z)

        def scale_row():
            scale_sum = jnp.sum(scale_acc[...], axis=1, keepdims=True)
            return jnp.concatenate(
                [jnp.broadcast_to(scale_sum, (hd, 128)), jnp.zeros((128 - hd, 128), f32)], axis=0
            ).T[0:1, :]

        def pair(i, b):
            arrive(part_p(b // 2), hp_send.at[0], hp_recv.at[b // 2], c, z)
            add_rows(part(b), 0, part_p(b // 2), 0, width, 128)
            if i < 2:
                slot = s_bit if i == 0 else 1 - s_bit
                send(part(b), part_f(slot), hf_send.at[i], hf_recv.at[slot], first, z)

        shift = sib - c
        to_sib(diag + shift)
        to_sib(second + shift)
        partial(diag)
        to_sib(first + shift)
        pair(1, diag)
        partial(first)
        to_sib(sib)
        pair(0, first)
        partial(second)
        partial(c)
        head_windows(1)
        deep_far_sum(DOWN)
        far_sum(UP)
        near_sum(OUT)
        vec[:, width:] = scale_row()
        for k in range(1, n_ctx):
            g = lax.rem(c + k, n_ctx)
            send(vec, vec_plane.at[c], vp_send.at[k], vp_recv.at[c], g, z)
        far_window(0)
        pair(2, second)
        pair(3, c)
        deep_first_sum(DOWN)
        near_window(1)
        planes[UP].from_first()
        far_sum(OUT)
        planes[UP].from_second()
        arrive(part_f(1 - s_bit), hf_send.at[0], hf_recv.at[1 - s_bit], c, z)
        add_rows(part(second), 0, part_f(1 - s_bit), 0, width, 128)
        send(part(second), part_s, hs_send.at[0], hs_recv.at[0], second, z)
        deep_second_sum(DOWN)
        arrive(part_f(s_bit), hf_send.at[0], hf_recv.at[s_bit], c, z)
        add_rows(part(c), 0, part_f(s_bit), 0, width, 128)
        far_window(1)
        plane_w[0].from_first()
        plane_w[0].from_second()
        planes[UP].from_diag()
        total = vec[...]
        for k in range(1, n_ctx):
            g = lax.rem(c + k, n_ctx)
            arrive(vec_plane.at[g], vp_send.at[0], vp_recv.at[g], c, z)
            total = total + vec_plane[g]
        vec_mid[...] = total
        for k in range(1, n_wsh):
            send(vec_mid, vec_line.at[z], vl_send.at[k], vl_recv.at[z], c, lax.rem(z + k, n_wsh))
        planes[OUT].from_first()
        planes[OUT].from_second()
        planes[DOWN].from_first()
        planes[DOWN].from_second()
        arrive(part_s, hs_send.at[0], hs_recv.at[0], c, z)

        mine_part = part(c)

        def turn_dh(i, _):
            at = pl.ds(pl.multiple_of(i * 128, 128), 128)
            dh[:, at] = (mine_part[at, :].astype(f32) + part_s[at, :].astype(f32)).T
            return 0

        lax.fori_loop(0, width // 128, turn_dh, 0)

        def last_rows(i, total):
            at = pl.ds(pl.multiple_of(i * 16, 16), 16)
            t = tok[at, :].astype(f32)
            inverse = lax.rsqrt(jnp.mean(t * t, -1, keepdims=True) + EPS)
            normed = t * inverse
            grad = dh[at, :]
            both = grad * normed
            slope = jnp.mean(both * gains[0:1, :], -1, keepdims=True)
            gtok[at, :] = (dx[at, :] + inverse * (grad * gains[0:1, :] - normed * slope)).astype(bf16)
            return total + both

        gain_sum = lax.fori_loop(0, rows // 16, last_rows, jnp.zeros((16, width), f32))
        row[...] = jnp.sum(gain_sum, axis=0, keepdims=True)
        for k in range(1, n_ctx):
            g = lax.rem(c + k, n_ctx)
            send(row, row_plane.at[c], rp_send.at[k], rp_recv.at[c], g, z)
        own_gtok = pltpu.make_async_copy(gtok, gtok_out, local_sem.at[11])
        own_gtok.start()
        plane_w[0].from_diag()
        planes[OUT].from_diag()
        planes[DOWN].from_diag()
        plane_w[1].from_first()
        plane_w[1].from_second()
        total = row[...]
        for k in range(1, n_ctx):
            g = lax.rem(c + k, n_ctx)
            arrive(row_plane.at[g], rp_send.at[0], rp_recv.at[g], c, z)
            total = total + row_plane[g]
        row_mid[...] = total
        for k in range(1, n_wsh):
            send(row_mid, row_line.at[z], rl_send.at[k], rl_recv.at[z], c, lax.rem(z + k, n_wsh))
        plane_w[1].from_diag()
        whole = vec_mid[...]
        for k in range(1, n_wsh):
            s = lax.rem(z + k, n_wsh)
            arrive(vec_line.at[s], vl_send.at[0], vl_recv.at[s], c, z)
            whole = whole + vec_line[s]
        vec_sum[...] = jnp.zeros_like(vec_sum)
        vec_sum[1:2, :] = whole[:, 0:width]
        vec_sum[2:3, 0:128] = whole[:, width:]
        for k in range(1, n_wsh):
            s = lax.rem(z + k, n_wsh)
            arrive(row_line.at[s], rl_send.at[0], rl_recv.at[s], c, z)
            total = total + row_line[s]
        vec_sum[0:1, :] = total
        own_vec = pltpu.make_async_copy(vec_sum, vec_out, local_sem.at[12])
        own_vec.start()
        for plane in planes + plane_w:
            all_others(plane)
            plane.finish()
        for i in range(n_ctx // 2):
            left(part(c), hp_send.at[i], hp_recv.at[i], c, z)
        for i in range(2):
            left(part(c), hf_send.at[i], hf_recv.at[i], c, z)
        left(part(c), hs_send.at[0], hs_recv.at[0], c, z)
        for copy in (own_gtok, own_vec, *[own_window(h) for h in range(heads)]):
            copy.wait()

    pl.run_scoped(
        attention_backward,
        vm((n_ctx, heads, 128, rows), bf16), vm((heads, length, 128), bf16), vm((heads, length, 128), bf16),
        vm((heads, length, 128), f32), vm((heads, length, 128), f32), vm((w_c.shape[1], length), bf16),
    )

    wline.finish(w_own)
    for k in range(1, n_wsh):
        left(pack_ref, pk_send.at[k], pk_recv.at[z], c, z)
        left(vec, vl_send.at[k], vl_recv.at[0], c, z)
        left(row, rl_send.at[k], rl_recv.at[0], c, z)
    for k in range(1, n_ctx):
        g = lax.rem(c + k, n_ctx)
        left(ob_stage.at[g], ob_send.at[g], ob_recv.at[g], c, z)
        left(go_land.at[0], go_send.at[k], go_recv.at[0], c, z)
        left(vec, vp_send.at[k], vp_recv.at[0], c, z)
        left(row, rp_send.at[k], rp_recv.at[0], c, z)
    for w in range(3):
        pltpu.make_async_copy(final_piece(w), out_piece(w, c), local_sem.at[8 + w]).wait()
        left(deep_f if w == DOWN else land_f.at[w], f_send.at[w], f_recv.at[w], c, z)
        left(deep_s if w == DOWN else land_s.at[w], s_send.at[w], s_recv.at[w], c, z)
        for j in range(2):
            left(deep_near.at[j] if w == DOWN else land_near.at[w, j], zn_send.at[w, j], zn_recv.at[w, j], c, z)
        left(deep_far if w == DOWN else land_far.at[w], zf_send.at[w], zf_recv.at[w], c, z)
    for h in range(heads):
        for j in range(2):
            left(win_near.at[h, j], wn_send.at[h, j], wn_recv.at[h, j], c, z)
        left(win_far.at[h], wf_send.at[h], wf_recv.at[h], c, z)


def whole_call(dims, tok, cot, w6, pack, order, lengths):
    n_ctx, n_wsh, hd, heads = dims
    rows, width = tok.shape
    span, length, shard = hd * heads, rows * n_ctx, width // n_wsh
    half, cut = width // 2, shard // (n_ctx // 2)
    f32, bf16 = jnp.float32, jnp.bfloat16
    hbm = pl.BlockSpec(memory_space=pl.ANY)
    smem = pl.BlockSpec(memory_space=pltpu.SMEM)
    shape = jax.ShapeDtypeStruct
    dma = pltpu.SemaphoreType.DMA
    vm = pltpu.VMEM
    size = windows(width, n_wsh)[1]
    lanes = -(-3 * span // 128) * 128
    wide = (rows, width)
    outs = (
        shape(wide, bf16), shape(wide, bf16),
        shape((3, shard, width), bf16), shape((n_ctx, heads, 3 * hd, size), bf16), shape((8, width), f32),
    )
    scratch = [
        vm((n_ctx, rows, width), bf16), vm((3, width, width), bf16), vm((length, width), bf16),
        vm((width, lanes), bf16), vm((shard, lanes), bf16), vm((n_wsh,) + pack.shape, f32), vm((8, width), f32),
        vm((heads, length, 128), bf16), vm((heads, length, 128), bf16), vm((heads, hd, length), bf16),
        vm((n_ctx, heads, 128, rows), bf16), vm((n_ctx, span, rows), f32), vm((n_ctx, span, rows), f32),
        vm((n_ctx, span, rows), bf16), vm((width, rows), bf16), vm((width, rows), bf16), vm((n_ctx, span, rows), bf16),
        vm((3, n_wsh, shard, half), bf16), vm((2, n_wsh, 2 * cut, half), bf16), vm((2, n_wsh, cut, half), bf16),
        vm((2, 2, cut, half), bf16), vm((2, cut, half), bf16),
        vm((2, shard, half), bf16), vm((shard, half), bf16), vm((2 * cut, half), bf16), vm((cut, half), bf16),
        vm((heads, n_wsh, 3 * hd, size), bf16), vm((heads, 2, 3 * hd, size), bf16), vm((heads, 3 * hd, size), bf16),
        vm(wide, f32), vm(wide, f32), vm(wide, bf16), vm(wide, bf16), vm(wide, bf16),
        vm((1, width + 128), f32), vm((n_ctx, 1, width + 128), f32), vm((n_wsh, 1, width + 128), f32),
        vm((1, width + 128), f32), vm((8, width), f32), vm((1, width), f32), vm((n_ctx, 1, width), f32), vm((n_wsh, 1, width), f32),
        vm((1, width), f32), vm((hd, rows), f32),
        dma((2, 7)), dma((2, n_ctx)), dma((2 * n_wsh,)), dma((n_wsh,)), dma((n_wsh,)), dma((n_wsh,)),
        dma((n_ctx,)), dma((n_ctx,)), dma((3, 2 * n_wsh)), dma((3, n_wsh)),
        dma((3, n_wsh, 7)), dma((3, n_wsh, n_ctx)),
        dma((n_ctx,)), dma((n_ctx,)), dma((3,)), dma((3,)), dma((3,)), dma((3,)), dma((3,)), dma((3,)),
        dma((3, 2)), dma((3, 2)), dma((3,)), dma((3,)), dma((3, 7)), dma((3, n_ctx)),
        dma((n_ctx // 2,)), dma((n_ctx // 2,)), dma((2,)), dma((2,)), dma((1,)), dma((1,)),
        dma((heads, 2)), dma((heads, 2)), dma((heads,)), dma((heads,)), dma((heads, 7)), dma((heads, n_ctx)),
        dma((n_ctx,)), dma((n_ctx,)), dma((n_wsh,)), dma((n_wsh,)),
        dma((n_ctx,)), dma((n_ctx,)), dma((n_wsh,)), dma((n_wsh,)), dma((13,)), dma((heads + 3,)), dma((3, 2)),
    ]
    return pl.pallas_call(
        functools.partial(whole_kernel, dims),
        out_shape=outs,
        in_specs=[hbm] * 9 + [smem] * 2,
        out_specs=[hbm] * len(outs),
        scratch_shapes=scratch,
        compiler_params=pltpu.CompilerParams(
            collective_id=0, has_side_effects=True, vmem_limit_bytes=VMEM_BYTES
        ),
    )(tok, cot, *w6, pack, order, lengths)


def finish_kernel(dims, dwqkv_ref, dw3_ref, *refs):
    outs, (pieces, plain, wide, turned, results, in_sem, out_sem) = refs[:6], refs[6:]
    n_ctx, n_wsh, hd, heads = dims
    z = lax.axis_index("wsh")
    f32 = jnp.float32
    shard, width = outs[0].shape
    starts, size = windows(width, n_wsh)
    offset = jnp.int32(0)
    for s in range(n_wsh):
        offset = jnp.where(z == s, s * shard - starts[s], offset)
    ins = [pltpu.make_async_copy(dw3_ref.at[w], plain.at[w], in_sem.at[w]) for w in range(3)]
    for i in range(3):
        at = pl.ds(i * hd, hd)
        ins.append(pltpu.make_async_copy(dwqkv_ref.at[:, :, at], pieces.at[i], in_sem.at[3 + i]))
    for copy in ins:
        copy.start()
    done = []

    def store(i, result):
        copy = pltpu.make_async_copy(result, outs[i], out_sem.at[i])
        copy.start()
        done.append(copy)

    for w in range(3):
        ins[w].wait()
        results[w] = plain[w].astype(f32)
        store(3 + w, results.at[w])
    for i in range(3):
        ins[3 + i].wait()

        def lay(b, _):
            for h in range(heads):
                at = pl.ds(pl.multiple_of((b * heads + h) * hd, 16), hd)
                wide[at, :] = pieces[i, b, h].astype(f32)
            return 0

        lax.fori_loop(0, n_ctx, lay, 0)

        def turn(j, _):
            at = pl.ds(pl.multiple_of(j * 128, 128), 128)
            turned[i, :, at] = wide[at, :].T
            return 0

        lax.fori_loop(0, width // 128, turn, 0)
        store(i, turned.at[i, pl.ds(pl.multiple_of(offset, 8), shard)])
    for copy in done:
        copy.wait()


def finish_call(dims, dwqkv, dw3):
    n_ctx, n_wsh, hd, heads = dims
    shard, width = dw3.shape[1:]
    size = dwqkv.shape[3]
    f32, bf16 = jnp.float32, jnp.bfloat16
    hbm = pl.BlockSpec(memory_space=pl.ANY)
    dma = pltpu.SemaphoreType.DMA
    return pl.pallas_call(
        functools.partial(finish_kernel, dims),
        out_shape=(jax.ShapeDtypeStruct((shard, width), f32),) * 6,
        in_specs=[hbm] * 2,
        out_specs=[hbm] * 6,
        scratch_shapes=[
            pltpu.VMEM((3, n_ctx, heads, hd, size), bf16), pltpu.VMEM((3, shard, width), bf16),
            pltpu.VMEM((width, size), f32), pltpu.VMEM((3, size, width), f32), pltpu.VMEM((3, shard, width), f32),
            dma((6,)), dma((6,)),
        ],
        compiler_params=pltpu.CompilerParams(vmem_limit_bytes=VMEM_BYTES),
    )(dwqkv, dw3)


def head_split(
    tokens, cotangent, block_lengths, group_order, w_query, w_key, w_value, w_out, w_up, w_down,
    gain_attn, gain_mlp, query_scale,
):
    f32 = jnp.float32
    n_ctx, n_wsh = lax.axis_size("ctx"), lax.axis_size("wsh")
    z = lax.axis_index("wsh")
    width = tokens.shape[2]
    hd, heads = width // H, H // n_ctx
    shard = width // n_wsh
    dims = (n_ctx, n_wsh, hd, heads)
    lanes = -(-shard // 128) * 128
    pack = sum(
        jnp.pad(v.astype(f32)[None], ((i, 7 - i), (0, lanes - v.shape[0])))
        for i, v in enumerate((gain_attn, gain_mlp, query_scale))
    )
    outputs, gtok, dw3, dwqkv, sums = whole_call(
        dims, tokens[0], cotangent[0], (w_query, w_key, w_value, w_out, w_up, w_down), pack, group_order, block_lengths
    )[:5]
    weight_grads = finish_call(dims, dwqkv, dw3)
    own = [lax.dynamic_slice_in_dim(sums[i], z * shard, shard, 0) for i in (0, 1)]
    scale_grad = (
        lax.dynamic_slice_in_dim(sums[2], z * (hd // n_wsh), hd // n_wsh, 0)
        * (LOG_BASE / math.sqrt(hd))
        * jax.nn.sigmoid(query_scale.astype(f32))
    )
    return (
        outputs.reshape(tokens.shape), gtok.reshape(tokens.shape), *weight_grads, own[0], own[1], scale_grad,
    )


def solution(mesh):
    in_specs = (
        P("wsh", "ctx", None),
        P("wsh", "ctx", None),
        P("wsh", None),
        P(),
        P("wsh", None),
        P("wsh", None),
        P("wsh", None),
        P("wsh", None),
        P("wsh", None),
        P("wsh", None),
        P("wsh"),
        P("wsh"),
        P("wsh"),
    )
    out_specs = (
        P("wsh", "ctx", None),
        P("wsh", "ctx", None),
        P("wsh", None),
        P("wsh", None),
        P("wsh", None),
        P("wsh", None),
        P("wsh", None),
        P("wsh", None),
        P("wsh"),
        P("wsh"),
        P("wsh"),
    )
    n_ctx, n_wsh = mesh.shape["ctx"], mesh.shape["wsh"]
    plan = head_split if (n_ctx, n_wsh) == (8, 4) else per_device
    return jax.shard_map(
        plan, mesh=mesh, in_specs=in_specs, out_specs=out_specs, check_vma=False
    )
```

```python
import functools
import math

import jax
import jax.numpy as jnp
from jax import lax
from jax.experimental import pallas as pl
from jax.experimental.pallas import tpu as pltpu
from jax.sharding import PartitionSpec as P

H = 16


EPS = 1e-06
LOG_BASE = 1.442695041


def row_step():
    return 512


def rows_at(array, block_no, step_rows):
    return lax.dynamic_slice_in_dim(array, block_no * step_rows, step_rows, 0)


def inverse_rms(values):
    return lax.rsqrt(jnp.mean(values * values, -1, keepdims=True) + EPS)


def norm_back(normed, inverse, grad):
    return inverse * (grad - normed * jnp.mean(grad * normed, -1, keepdims=True))


def split_heads(matrix):
    return matrix.reshape(matrix.shape[0], H, -1)


def outer_product(left, right):
    return lax.dot_general(
        left, right, (((0,), (0,)), ((), ())), preferred_element_type=jnp.float32
    )


def back_product(grad, weight):
    return lax.dot_general(
        grad, weight, (((1,), (1,)), ((), ())), preferred_element_type=jnp.float32
    )


def probabilities(query3, key3, query_marks, key_marks, log_totals):
    scores = jnp.einsum("qhd,khd->hqk", query3, key3, preferred_element_type=jnp.float32)
    allowed = key_marks[None, None, :] <= query_marks[None, :, None]
    return jnp.exp(jnp.where(allowed, scores - log_totals[:, :, None], -jnp.inf))


def score_grads(chances, grad_out3, value3, deltas):
    grad_chances = jnp.einsum("qhd,khd->hqk", grad_out3, value3, preferred_element_type=jnp.float32)
    return (chances * (grad_chances - deltas[:, :, None])).astype(jnp.bfloat16)


def per_device(
    tokens,
    cotangent,
    block_lengths,
    group_order,
    w_query,
    w_key,
    w_value,
    w_out,
    w_up,
    w_down,
    gain_attn,
    gain_mlp,
    query_scale,
):
    gathered = (
        lax.all_gather(w_query, "wsh", axis=0, tiled=True),
        lax.all_gather(w_key, "wsh", axis=0, tiled=True),
        lax.all_gather(w_value, "wsh", axis=0, tiled=True),
        lax.all_gather(w_out, "wsh", axis=0, tiled=True),
        lax.all_gather(w_up, "wsh", axis=0, tiled=True),
        lax.all_gather(w_down, "wsh", axis=0, tiled=True),
        lax.all_gather(gain_attn, "wsh", axis=0, tiled=True),
        lax.all_gather(gain_mlp, "wsh", axis=0, tiled=True),
        lax.all_gather(query_scale, "wsh", axis=0, tiled=True),
    )
    (
        full_query,
        full_key,
        full_value,
        full_out,
        full_up,
        full_down,
        norm_attn,
        norm_mlp,
        scale_param,
    ) = gathered
    tok_rows = tokens.shape[1]
    model_width = tokens.shape[2]
    length = tok_rows * lax.axis_size("ctx")
    device = lax.axis_index("ctx")
    head_size = scale_param.shape[0]
    f32 = jnp.float32
    bf16 = jnp.bfloat16
    inputs = tokens.reshape(tok_rows, model_width).astype(f32)
    positions = (
        group_order[:, None] * tok_rows + jnp.arange(tok_rows, dtype=jnp.int32)[None, :]
    ).reshape(length)
    bounds = jnp.cumsum(block_lengths[0])
    block_ids = jnp.sum((bounds[None, :] <= positions[:, None]).astype(jnp.int32), -1)
    query_ids = lax.dynamic_slice_in_dim(block_ids, device * tok_rows, tok_rows, 0)
    inverse_one = inverse_rms(inputs)
    normed_one = inputs * inverse_one
    hidden_one = (normed_one * norm_attn.astype(f32)).astype(bf16)
    query_raw = jnp.dot(hidden_one, full_query, preferred_element_type=f32).reshape(
        tok_rows, H, head_size
    )
    query_gain = LOG_BASE / math.sqrt(head_size) * jax.nn.softplus(scale_param.astype(f32))
    query3 = (query_raw * query_gain).astype(bf16)
    key_flat = jnp.dot(hidden_one, full_key, preferred_element_type=f32).astype(bf16)
    value_flat = jnp.dot(hidden_one, full_value, preferred_element_type=f32).astype(bf16)
    initial = (
        jnp.full((H, tok_rows), -1e30, f32),
        jnp.zeros((H, tok_rows), f32),
        jnp.zeros((tok_rows, H, head_size), f32),
    )
    key_rows = lax.all_gather(key_flat, "ctx", axis=0, tiled=True)
    value_rows = lax.all_gather(value_flat, "ctx", axis=0, tiled=True)
    row_count = key_rows.shape[0]
    step_rows = row_step()

    def one_block(block_no, looped):
        key_part = split_heads(rows_at(key_rows, block_no, step_rows))
        value_part = split_heads(rows_at(value_rows, block_no, step_rows))
        block_marks = rows_at(block_ids, block_no, step_rows)
        maxima, totals, running = looped
        scores = jnp.einsum("qhd,khd->hqk", query3, key_part, preferred_element_type=f32)
        allowed = block_marks[None, None, :] <= query_ids[None, :, None]
        scores = jnp.where(allowed, scores, -jnp.inf)
        raised = jnp.maximum(maxima, jnp.max(scores, -1))
        rescale = jnp.exp(maxima - raised)
        weights = jnp.exp(scores - raised[:, :, None])
        totals = totals * rescale + jnp.sum(weights, -1)
        running = running * rescale.T[:, :, None] + jnp.einsum(
            "hqk,khd->qhd", weights.astype(bf16), value_part, preferred_element_type=f32
        )
        return (raised, totals, running)

    maxima, totals, running = lax.fori_loop(0, row_count // step_rows, one_block, initial)
    log_totals = maxima + jnp.log(totals)
    attended = running / totals.T[:, :, None]
    attended_bf = attended.reshape(tok_rows, model_width).astype(bf16)
    mixed = inputs + jnp.dot(attended_bf, full_out, preferred_element_type=f32)
    inverse_two = inverse_rms(mixed)
    normed_two = mixed * inverse_two
    hidden_two = (normed_two * norm_mlp.astype(f32)).astype(bf16)
    up_raw = jnp.dot(hidden_two, full_up, preferred_element_type=f32)
    active = jax.nn.silu(up_raw).astype(bf16)
    outputs = mixed + jnp.dot(active, full_down, preferred_element_type=f32)
    grad_output = cotangent.reshape(tok_rows, model_width).astype(f32)
    grad_mlp = grad_output.astype(bf16)
    grad_active = back_product(grad_mlp, full_down)
    sigmoid_up = jax.nn.sigmoid(up_raw)
    grad_up_raw = (grad_active * sigmoid_up * (1.0 + up_raw * (1.0 - sigmoid_up))).astype(bf16)
    grad_hidden_two = back_product(grad_up_raw, full_up)
    grad_gain_mlp = jnp.sum(grad_hidden_two * normed_two, 0)
    grad_mixed = grad_output + norm_back(
        normed_two, inverse_two, grad_hidden_two * norm_mlp.astype(f32)
    )
    grad_branch = grad_mixed.astype(bf16)
    grad_att = back_product(grad_branch, full_out).astype(bf16)
    grad_att3 = split_heads(grad_att)
    deltas = jnp.sum(grad_att3.astype(f32) * attended, -1).T
    key_whole, value_whole = (
        lax.all_gather(key_flat, "ctx", axis=0, tiled=True),
        lax.all_gather(value_flat, "ctx", axis=0, tiled=True),
    )
    step_rows = row_step()
    block_total = length // step_rows

    def key_block(grad_q, block_parts):
        key_rows, value_rows, block_marks = block_parts
        key_part = split_heads(key_rows)
        value_part = split_heads(value_rows)
        zero_part = jnp.zeros((key_rows.shape[0], H, head_size), f32)
        chances = probabilities(query3, key_part, query_ids, block_marks, log_totals)
        slopes = score_grads(chances, grad_att3, value_part, deltas)
        new_grad = (grad_q, zero_part, zero_part)[0] + jnp.einsum(
            "hqk,khd->qhd", slopes, key_part, preferred_element_type=f32
        )
        grad_key_part = jnp.einsum("hqk,qhd->khd", slopes, query3, preferred_element_type=f32)
        grad_value_part = jnp.einsum(
            "hqk,qhd->khd", chances.astype(bf16), grad_att3, preferred_element_type=f32
        )
        return (new_grad, (grad_key_part, grad_value_part))

    grad_qs, (key_terms, value_terms) = lax.scan(
        key_block,
        jnp.zeros((tok_rows, H, head_size), f32),
        (
            key_whole.reshape(block_total, step_rows, model_width),
            value_whole.reshape(block_total, step_rows, model_width),
            block_ids.reshape(block_total, step_rows),
        ),
    )
    grad_key, grad_value = (
        lax.psum_scatter(
            key_terms.reshape(length, model_width).astype(jnp.bfloat16),
            "ctx",
            scatter_dimension=0,
            tiled=True,
        ).astype(jnp.float32),
        lax.psum_scatter(
            value_terms.reshape(length, model_width).astype(jnp.bfloat16),
            "ctx",
            scatter_dimension=0,
            tiled=True,
        ).astype(jnp.float32),
    )
    grad_key_bf = grad_key.astype(bf16)
    grad_value_bf = grad_value.astype(bf16)
    grad_query_bf = (grad_qs * query_gain).reshape(tok_rows, model_width).astype(bf16)
    grad_scale_param = (
        jnp.sum(grad_qs * query_raw, (0, 1))
        * (LOG_BASE / math.sqrt(head_size))
        * jax.nn.sigmoid(scale_param.astype(f32))
    )
    grad_hidden_one = (
        back_product(grad_query_bf, full_query)
        + back_product(grad_key_bf, full_key)
        + back_product(grad_value_bf, full_value)
    )
    grad_gain_attn = jnp.sum(grad_hidden_one * normed_one, 0)
    grad_inputs = grad_mixed + norm_back(
        normed_one, inverse_one, grad_hidden_one * norm_attn.astype(f32)
    )
    grad_queryw = outer_product(hidden_one, grad_query_bf)
    grad_keyw = outer_product(hidden_one, grad_key_bf)
    grad_valuew = outer_product(hidden_one, grad_value_bf)
    grad_outw = outer_product(attended_bf, grad_branch)
    grad_upw = outer_product(hidden_two, grad_up_raw)
    grad_downw = outer_product(active, grad_mlp)
    owned = (
        lax.psum_scatter(
            grad_queryw.astype(jnp.bfloat16), "wsh", scatter_dimension=0, tiled=True
        ).astype(jnp.float32),
        lax.psum_scatter(
            grad_keyw.astype(jnp.bfloat16), "wsh", scatter_dimension=0, tiled=True
        ).astype(jnp.float32),
        lax.psum_scatter(
            grad_valuew.astype(jnp.bfloat16), "wsh", scatter_dimension=0, tiled=True
        ).astype(jnp.float32),
        lax.psum_scatter(
            grad_outw.astype(jnp.bfloat16), "wsh", scatter_dimension=0, tiled=True
        ).astype(jnp.float32),
        lax.psum_scatter(
            grad_upw.astype(jnp.bfloat16), "wsh", scatter_dimension=0, tiled=True
        ).astype(jnp.float32),
        lax.psum_scatter(
            grad_downw.astype(jnp.bfloat16), "wsh", scatter_dimension=0, tiled=True
        ).astype(jnp.float32),
        lax.psum_scatter(
            grad_gain_attn.astype(jnp.bfloat16), "wsh", scatter_dimension=0, tiled=True
        ).astype(jnp.float32),
        lax.psum_scatter(
            grad_gain_mlp.astype(jnp.bfloat16), "wsh", scatter_dimension=0, tiled=True
        ).astype(jnp.float32),
        lax.psum_scatter(
            grad_scale_param.astype(jnp.bfloat16), "wsh", scatter_dimension=0, tiled=True
        ).astype(jnp.float32),
    )
    summed = (
        lax.psum(owned[0].astype(jnp.bfloat16), "ctx").astype(jnp.float32),
        lax.psum(owned[1].astype(jnp.bfloat16), "ctx").astype(jnp.float32),
        lax.psum(owned[2].astype(jnp.bfloat16), "ctx").astype(jnp.float32),
        lax.psum(owned[3].astype(jnp.bfloat16), "ctx").astype(jnp.float32),
        lax.psum(owned[4].astype(jnp.bfloat16), "ctx").astype(jnp.float32),
        lax.psum(owned[5].astype(jnp.bfloat16), "ctx").astype(jnp.float32),
        lax.psum(owned[6].astype(jnp.bfloat16), "ctx").astype(jnp.float32),
        lax.psum(owned[7].astype(jnp.bfloat16), "ctx").astype(jnp.float32),
        lax.psum(owned[8].astype(jnp.bfloat16), "ctx").astype(jnp.float32),
    )
    return (
        outputs.reshape(tokens.shape).astype(bf16),
        grad_inputs.reshape(tokens.shape).astype(bf16),
        summed[0],
        summed[1],
        summed[2],
        summed[3],
        summed[4],
        summed[5],
        summed[6],
        summed[7],
        summed[8],
    )


MESH = pl.DeviceIdType.MESH
NEG = -1e30
VMEM_BYTES = 62 * 1024 * 1024


def place():
    c, z = lax.axis_index("ctx"), lax.axis_index("wsh")
    core, x, y = lax.rem(c, 2), lax.rem(c // 2, 2), c // 4
    sib = c + 1 - 2 * core
    over_x, over_y = c + 2 - 4 * x, c + 4 - 8 * y
    first = over_x * (1 - core) + over_y * core
    second = over_y * (1 - core) + over_x * core
    diag = over_x + over_y - c
    return c, z, sib, first, second, diag


def greet(c, z, n_ctx, n_wsh):
    barrier = pltpu.get_barrier_semaphore()
    for k in range(1, n_ctx):
        pl.semaphore_signal(
            barrier, inc=1, device_id=(lax.rem(c + k, n_ctx), z), device_id_type=MESH
        )
    for k in range(1, n_wsh):
        pl.semaphore_signal(
            barrier, inc=1, device_id=(c, lax.rem(z + k, n_wsh)), device_id_type=MESH
        )


def met(n_ctx, n_wsh):
    pl.semaphore_wait(pltpu.get_barrier_semaphore(), n_ctx + n_wsh - 2)


def send(src, dst, send_sem, recv_sem, c, z):
    copy = pltpu.make_async_remote_copy(
        src_ref=src, dst_ref=dst, send_sem=send_sem, recv_sem=recv_sem,
        device_id=(c, z), device_id_type=MESH,
    )
    copy.start()
    return copy


def arrive(dst, send_sem, recv_sem, c, z):
    pltpu.make_async_remote_copy(
        src_ref=dst, dst_ref=dst, send_sem=send_sem, recv_sem=recv_sem,
        device_id=(c, z), device_id_type=MESH,
    ).wait_recv()


def left(src, send_sem, recv_sem, c, z):
    pltpu.make_async_remote_copy(
        src_ref=src, dst_ref=src, send_sem=send_sem, recv_sem=recv_sem,
        device_id=(c, z), device_id_type=MESH,
    ).wait_send()


class Line:
    def __init__(self, at, c, z, n, send_sem, recv_sem):
        self.at, self.c, self.z, self.n = at, c, z, n
        self.send_sem, self.recv_sem = send_sem, recv_sem

    def start(self, own):
        c, z = self.c, self.z

        @pl.when(z < self.n - 1)
        def _():
            send(own, self.at(z), self.send_sem.at[0], self.recv_sem.at[z], c, z + 1)

        @pl.when(z > 0)
        def _():
            send(own, self.at(z), self.send_sem.at[1], self.recv_sem.at[z], c, z - 1)

    def forward(self, distance, then=None):
        c, z, n = self.c, self.z, self.n
        below, above = z - distance, z + distance

        @pl.when(below >= 0)
        def _():
            arrive(self.at(below), self.send_sem.at[0], self.recv_sem.at[below], c, z)

            @pl.when(z < n - 1)
            def _():
                send(self.at(below), self.at(below), self.send_sem.at[2 * distance], self.recv_sem.at[below], c, z + 1)

            if then is not None:
                then(below)

        @pl.when(above < n)
        def _():
            arrive(self.at(above), self.send_sem.at[0], self.recv_sem.at[above], c, z)

            @pl.when(z > 0)
            def _():
                send(self.at(above), self.at(above), self.send_sem.at[2 * distance + 1], self.recv_sem.at[above], c, z - 1)

            if then is not None:
                then(above)

    def finish(self, own):
        c, z, n = self.c, self.z, self.n

        @pl.when(z < n - 1)
        def _():
            left(own, self.send_sem.at[0], self.recv_sem.at[z], c, z)

        @pl.when(z > 0)
        def _():
            left(own, self.send_sem.at[1], self.recv_sem.at[z], c, z)

        for distance in range(1, n):
            below, above = z - distance, z + distance

            @pl.when((below >= 0) & (z < n - 1))
            def _():
                left(self.at(below), self.send_sem.at[2 * distance], self.recv_sem.at[below], c, z)

            @pl.when((above < n) & (z > 0))
            def _():
                left(self.at(above), self.send_sem.at[2 * distance + 1], self.recv_sem.at[above], c, z)


class Plane:
    def __init__(self, at, c, z, around, send_sem, recv_sem):
        self.at, self.c, self.z = at, c, z
        self.sib, self.first, self.second, self.diag = around
        self.send_sem, self.recv_sem = send_sem, recv_sem

    def push(self, slot, block, target, src=None):
        src = self.at(block) if src is None else src
        send(src, self.at(block), self.send_sem.at[slot], self.recv_sem.at[block], target, self.z)

    def wait(self, block):
        arrive(self.at(block), self.send_sem.at[0], self.recv_sem.at[block], self.c, self.z)

    def start(self, own=None):
        self.push(0, self.c, self.first, own)
        self.push(1, self.c, self.second, own)
        self.push(2, self.c, self.sib, own)

    def from_first(self):
        self.wait(self.first)
        self.push(3, self.first, self.second)
        self.push(4, self.first, self.sib)

    def from_second(self):
        self.wait(self.second)
        self.push(5, self.second, self.sib)

    def from_diag(self):
        self.wait(self.diag)
        self.push(6, self.diag, self.sib)

    def others(self):
        shift = self.sib - self.c
        return (self.sib, self.second + shift, self.first + shift, self.diag + shift)

    def finish(self):
        for slot in range(7):
            left(self.at(self.c), self.send_sem.at[slot], self.recv_sem.at[self.c], self.c, self.z)


def block_ids_of(block, order_ref, lengths_ref, rows):
    n_blk = lengths_ref.shape[1]
    position = order_ref[block] * rows + lax.broadcasted_iota(jnp.int32, (8, rows), 1)
    ids = jnp.zeros((8, rows), jnp.int32)
    bound = jnp.int32(0)
    for b in range(n_blk):
        bound = bound + lengths_ref[0, b]
        ids = ids + jnp.where(position >= bound, 1, 0)
    return ids, lax.broadcasted_iota(jnp.int32, (8, rows), 0)


def three_rows(value, rows):
    f32 = jnp.float32
    high = value.astype(jnp.bfloat16).astype(f32)
    rest = value - high
    mid = rest.astype(jnp.bfloat16).astype(f32)
    low = rest - mid
    row = lax.broadcasted_iota(jnp.int32, (8, rows), 0)
    return jnp.where(row == 0, high, 0.0) + jnp.where(row == 1, mid, 0.0) + jnp.where(row == 2, low, 0.0)


def add_rows(target, at, other, other_at, rows, step):
    f32 = jnp.float32

    def some_rows(i, _):
        here = pl.ds(pl.multiple_of(at + i * step, 16), step)
        there = pl.ds(pl.multiple_of(other_at + i * step, 16), step)
        target[here, :] = (target[here, :].astype(f32) + other[there, :].astype(f32)).astype(target.dtype)
        return 0

    lax.fori_loop(0, rows // step, some_rows, 0)


def windows(width, n):
    part = width // n
    tiles = -(-part // 128) + (0 if part % 128 == 0 else 0)
    size = tiles * 128
    return [min(s * part // 128 * 128, width - size) for s in range(n)], size


def whole_kernel(
    dims,
    tok_ref, cot_ref, wq_ref, wk_ref, wv_ref, wout_ref, wup_ref, wdown_ref, pack_ref, order_ref, lengths_ref,
    out_out, gtok_out, dw3_out, dwqkv_out, vec_out,
    h1_all, w_full, big, w_c, w_own, packs, gains, kaug, vaug, kt, qaug, qraw, o_all, ob_stage, ob_land, go_stage, go_land,
    acc, land_f, land_s, land_near, land_far, deep_near, deep_far, deep_f, deep_s, win_out, win_near, win_far,
    dx, dh, tok, cot, gtok, vec, vec_plane, vec_line, vec_mid, vec_sum, row, row_plane, row_line, row_mid, scale_acc,
    tok_send, tok_recv, wz_send, wz_recv, pk_send, pk_recv, ob_send, ob_recv,
    w3z_send, w3z_recv, w3p_send, w3p_recv,
    go_send, go_recv, p_send, p_recv, f_send, f_recv, s_send, s_recv, zn_send, zn_recv, zf_send, zf_recv, g_send, g_recv,
    hp_send, hp_recv, hf_send, hf_recv, hs_send, hs_recv, wn_send, wn_recv, wf_send, wf_recv, wg_send, wg_recv,
    vp_send, vp_recv, vl_send, vl_recv, rp_send, rp_recv, rl_send, rl_recv, sl_send, sl_recv, sx_send, sx_recv, local_sem, load_sem, cols_sem,
):
    n_ctx, n_wsh, hd, heads = dims
    f32, bf16 = jnp.float32, jnp.bfloat16
    c, z, sib, first, second, diag = place()
    around = (sib, first, second, diag)
    core, x, y = lax.rem(c, 2), lax.rem(c // 2, 2), c // 4
    f_bit, s_bit = x * (1 - core) + y * core, y * (1 - core) + x * core
    rows, width = tok_ref.shape
    span, length = hd * heads, rows * n_ctx
    shard, half = width // n_wsh, width // 2
    two, cut = shard // 2, shard // (n_ctx // 2)
    w3_refs = (wout_ref, wup_ref, wdown_ref)
    OUT, UP, DOWN = 0, 1, 2
    own_tok = pltpu.make_async_copy(tok_ref, tok, local_sem.at[0])
    columns_in = [
        pltpu.make_async_copy(ref.at[:, pl.ds(side * half, half)], acc.at[i, side], cols_sem.at[i, side])
        for i, ref in enumerate((wq_ref, wk_ref, wv_ref))
        for side in range(2)
    ]
    own_pack = pltpu.make_async_copy(pack_ref, packs.at[z], local_sem.at[2])
    own_cot = pltpu.make_async_copy(cot_ref, cot, local_sem.at[3])
    own_full = [
        pltpu.make_async_copy(
            w3_refs[w], w_full.at[w, pl.ds(pl.multiple_of(z * shard, 16), shard)], load_sem.at[heads + w]
        )
        for w in range(3)
    ]
    for copy in (*columns_in, own_tok, own_pack, own_cot, *own_full):
        copy.start()
    greet(c, z, n_ctx, n_wsh)
    for copy in columns_in:
        copy.wait()
    for k in range(n_ctx):

        @pl.when(c == k)
        def _():
            for h in range(heads):
                side, at = divmod(k * span + h * hd, half)
                for i in range(3):
                    w_own[:, (3 * h + i) * hd : (3 * h + i + 1) * hd] = acc[i, side, :, at : at + hd]

    w_own[:, 3 * span :] = jnp.zeros((shard, w_own.shape[1] - 3 * span), bf16)
    own_w = pltpu.make_async_copy(w_own, w_c.at[pl.ds(pl.multiple_of(z * shard, 16), shard)], local_sem.at[1])
    own_w.start()
    met(n_ctx, n_wsh)

    part_rows = rows // 2
    tokens = [
        Plane(
            lambda b, i=i: big.at[pl.ds(pl.multiple_of(b * rows + i * part_rows, 16), part_rows)], c, z, around,
            tok_send.at[i], tok_recv.at[i],
        )
        for i in range(2)
    ]
    for i in range(2):
        tokens[i].start(tok_ref.at[pl.ds(i * part_rows, part_rows)])
    wline = Line(lambda s: w_c.at[pl.ds(pl.multiple_of(s * shard, 16), shard)], c, z, n_wsh, wz_send, wz_recv)
    for k in range(1, n_wsh):
        send(pack_ref, packs.at[z], pk_send.at[k], pk_recv.at[z], c, lax.rem(z + k, n_wsh))
    wline.start(w_own)
    scale_acc[...] = jnp.zeros_like(scale_acc)

    def columns(b):
        return pl.ds(pl.multiple_of(lax.rem(b, 2) * half, 128), half)

    straight = shard * 2 // 5
    cuts = (cut, cut, (shard - straight) // (n_ctx // 2))

    def piece(w, s, b):
        top = pl.multiple_of(s * shard + (b // 2) * cuts[w], 16)
        return w_full.at[w, pl.ds(top, cuts[w]), columns(b)]

    def straight_rows(s, of_core):
        top = s * shard + shard - straight + of_core * (straight // 2)
        return w_full.at[DOWN, pl.ds(pl.multiple_of(top, 16), straight // 2)]

    my_straight = wdown_ref.at[pl.ds(pl.multiple_of(shard - straight + core * (straight // 2), 16), straight // 2)]
    straight_line = Line(lambda s: straight_rows(s, core), c, z, n_wsh, sl_send, sl_recv)

    def to_other_core(s):
        k = lax.rem(s - z + n_wsh, n_wsh)
        send(straight_rows(s, core), straight_rows(s, core), sx_send.at[k], sx_recv.at[k], sib, z)

    def go_straight(w, distance):
        straight_line.forward(distance, to_other_core)


    my_piece = [
        ref.at[pl.ds(pl.multiple_of((c // 2) * cuts[w], 16), cuts[w]), columns(c)] for w, ref in enumerate(w3_refs)
    ]
    lines = [
        Line(lambda s, w=w: piece(w, s, c), c, z, n_wsh, w3z_send.at[w], w3z_recv.at[w]) for w in range(3)
    ]

    def plane_of(w, s):
        k = lax.rem(s - z + n_wsh, n_wsh)
        return Plane(lambda b: piece(w, s, b), c, z, around, w3p_send.at[w, k], w3p_recv.at[w, k])

    def shards_at(w, distance, step):
        below, above = z - distance, z + distance

        @pl.when(below >= 0)
        def _():
            step(plane_of(w, below))

        @pl.when(above < n_wsh)
        def _():
            step(plane_of(w, above))

    def spread(w, distance):
        lines[w].forward(distance, lambda s: plane_of(w, s).start())

    def step_of(step):
        return lambda w, distance: shards_at(w, distance, step)

    by_first, by_second, by_diag = step_of(Plane.from_first), step_of(Plane.from_second), step_of(Plane.from_diag)

    def all_others(plane):
        for b in plane.others():
            plane.wait(b)

    own_tok.wait()
    own_pack.wait()
    for k in range(1, n_wsh):
        other = lax.rem(z + k, n_wsh)
        arrive(packs.at[other], pk_send.at[0], pk_recv.at[other], c, z)
    row8 = lax.broadcasted_iota(jnp.int32, (8, width), 0)
    total = jnp.zeros((8, width), f32)
    for s in range(n_wsh):
        wide = jnp.concatenate([packs[s], jnp.zeros((8, width - packs.shape[2]), f32)], axis=1)
        by_shard = pltpu.roll(wide, s * shard, 1) if s else wide
        by_dim = pltpu.roll(wide, s * (hd // n_wsh), 1) if s else wide
        total = total + jnp.where(row8 < 2, by_shard, by_dim)
    gains[...] = total

    def gain_column():
        scale = jnp.concatenate([gains[2:3, 0:128], jnp.zeros((7, 128), f32)], axis=0)
        soft = jnp.maximum(scale, 0.0) + jnp.log(1.0 + jnp.exp(-jnp.abs(scale)))
        return (LOG_BASE / math.sqrt(hd) * soft).T[0:hd, 0:1]

    def attention_forward(vt, qneg, s_buf):
        def norm_block(b, source, top):
            gain = gains[0:1, :]

            def some_rows(i, _):
                t = source[pl.ds(pl.multiple_of(top + i * 32, 32), 32), :].astype(f32)
                inverse = lax.rsqrt(jnp.mean(t * t, -1, keepdims=True) + EPS)
                h1_all[b, pl.ds(pl.multiple_of(i * 32, 32), 32), :] = (t * inverse * gain).astype(bf16)
                return 0

            lax.fori_loop(0, rows // 32, some_rows, 0)

        def norm_arrived(b):
            norm_block(b, big, b * rows)

        def arrived(b):
            for i in range(2):
                tokens[i].wait(b)
            norm_arrived(b)

        others = tokens[0].others()
        lines[OUT].start(my_piece[OUT])
        norm_block(c, tok, 0)
        arrived(others[0])
        tokens[0].from_first()
        wline.forward(1)
        lines[UP].start(my_piece[UP])
        tokens[1].from_first()
        norm_arrived(first)
        tokens[0].from_second()
        tokens[1].from_second()
        norm_arrived(second)
        spread(OUT, 1)
        wline.forward(2)
        lines[DOWN].start(my_piece[DOWN])
        straight_line.start(my_straight)
        arrived(others[1])
        arrived(others[2])
        tokens[0].from_diag()
        tokens[1].from_diag()
        norm_arrived(diag)
        arrived(others[3])
        spread(OUT, 2)
        wline.forward(3)
        own_w.wait()
        spread(UP, 1)
        gain_col = gain_column()

        def project(b, _):
            raw = jnp.dot(h1_all[b], w_c[...], preferred_element_type=f32).T
            at = pl.ds(pl.multiple_of(b * rows, 128), rows)
            ids, row = block_ids_of(b, order_ref, lengths_ref, rows)
            hot = jnp.where(ids == row, 1.0, 0.0)
            neg = jnp.where(row > ids, NEG, 0.0)
            ones = jnp.ones((8, rows), f32)
            qneg[b] = neg
            for h in range(heads):
                top = 3 * h * hd
                q = raw[top : top + hd]
                qraw[b, h * hd : (h + 1) * hd, :] = q
                q = q * gain_col
                qaug[b, h, 0:hd, :] = q.astype(bf16)
                qaug[b, h, hd : hd + 16, :] = jnp.concatenate([neg, jnp.zeros((8, rows), f32)], axis=0).astype(bf16)
                qaug[b, h, hd + 16 : 128, :] = jnp.zeros((112 - hd, rows), bf16)
                k = raw[top + hd : top + 2 * hd].astype(bf16)
                v = raw[top + 2 * hd : top + 3 * hd].astype(bf16)
                tail = jnp.zeros((112 - hd, rows), f32)
                kt[h, :, at] = k
                vt[h, 0:hd, at] = v
                vt[h, hd : hd + 16, at] = jnp.ones((16, rows), bf16)
                kaug[h, at, :] = jnp.concatenate([k.astype(f32), hot, ones, tail], axis=0).T.astype(bf16)
                vaug[h, at, :] = jnp.concatenate([v.astype(f32), ones, ones, tail], axis=0).T.astype(bf16)
            return 0

        lax.fori_loop(0, n_ctx, project, 0)
        for i in range(2):
            tokens[i].finish()
        keys = length // 2
        plan = (
            (0, spread, OUT, 3), (0, by_first, OUT, 1), (1, by_first, OUT, 2), (1, spread, UP, 2),
            (2, by_second, OUT, 1), (2, by_second, OUT, 2), (3, spread, DOWN, 1), (3, go_straight, DOWN, 1), (3, by_first, OUT, 3),
            (4, by_diag, OUT, 1), (4, spread, UP, 3), (5, by_second, OUT, 3), (5, by_first, UP, 1),
            (6, spread, DOWN, 2), (6, go_straight, DOWN, 2), (6, by_diag, OUT, 2), (7, by_first, UP, 2), (8, by_diag, OUT, 3),
            (8, by_second, UP, 1), (9, by_second, UP, 2), (9, spread, DOWN, 3), (9, go_straight, DOWN, 3), (10, by_first, UP, 3),
            (11, by_diag, UP, 1), (11, by_first, DOWN, 1), (12, by_second, UP, 3), (12, by_diag, UP, 2),
            (13, by_first, DOWN, 2), (14, by_second, DOWN, 1), (14, by_diag, UP, 3), (15, by_second, DOWN, 2),
        )

        def attend(i, _):
            g = lax.rem(c + 1 + i, n_ctx)
            for h in range(heads):
                q = qaug[g, h]
                top = jnp.full((1, rows), -jnp.inf, f32)
                for j in range(2):
                    s = jnp.dot(kaug[h, j * keys : (j + 1) * keys, :], q, preferred_element_type=f32)
                    s_buf[j * keys : (j + 1) * keys, :] = s
                    top = jnp.maximum(top, jnp.max(s, axis=0, keepdims=True))
                out = jnp.zeros((hd + 16, rows), f32)
                for j in range(2):
                    p = jnp.exp(s_buf[j * keys : (j + 1) * keys, :] - top).astype(bf16)
                    out = out + jnp.dot(vt[h, :, j * keys : (j + 1) * keys], p, preferred_element_type=f32)
                total = out[hd : hd + 1]
                o = out[0:hd] / total
                lse = top + jnp.log(total)
                o_all[g, h * hd : (h + 1) * hd, :] = o
                ob_stage[g, h * hd : (h + 1) * hd, :] = o.astype(bf16)
                qaug[g, h, hd : hd + 16, :] = jnp.concatenate([qneg[g], three_rows(-lse, rows)], axis=0).astype(bf16)
                for slot, event, w, distance in plan:
                    if slot % heads == h:
                        pl.when(i == slot // heads)(functools.partial(event, w, distance))

            @pl.when(i < n_ctx - 1)
            def _():
                send(ob_stage.at[g], my_heads(ob_land), ob_send.at[g], ob_recv.at[c], g, z)

            return 0

        lax.fori_loop(0, n_ctx, attend, 0)

    def my_heads(ref):
        return ref.at[pl.ds(pl.multiple_of(c * span, 16), span)]

    def heads_of(ref, g):
        return ref.at[pl.ds(pl.multiple_of(g * span, 16), span)]

    vm = pltpu.VMEM
    pl.run_scoped(
        attention_forward,
        vm((heads, hd + 16, length), bf16), vm((n_ctx, 8, rows), f32), vm((length, rows), f32),
    )
    own_o = pltpu.make_async_copy(ob_stage.at[c], my_heads(ob_land), local_sem.at[4])
    own_o.start()

    mine = pl.ds(pl.multiple_of(core * half, 128), half)
    theirs = pl.ds(pl.multiple_of((1 - core) * half, 128), half)
    my_top = f_bit * two + s_bit * cut
    near, far = z + 1 - 2 * lax.rem(z, 2), z + 2 - 4 * (z // 2)

    def pair_at(w):
        return big.at[pl.ds(2 * w * shard, 2 * shard)]

    def add_pair(w):
        arrive(pair_at(w), p_send.at[w], p_recv.at[w], c, z)
        for s in range(n_wsh):
            other = big.at[:, pl.ds(s % 2 * half, half)]
            add_rows(acc.at[w, s], 0, other, (2 * w + s // 2) * shard, shard, 64)

    def pair_sum(w):
        add_pair(w)
        at = pl.ds(pl.multiple_of((1 - f_bit) * two, 16), two)
        send(acc.at[w, :, at], land_f.at[w], f_send.at[w], f_recv.at[w], first, z)

    def deep_pair_sum(w):
        add_pair(w)
        for j in range(2):
            s = 2 * j + lax.rem(near, 2)
            send(acc.at[w, s], deep_near.at[j], zn_send.at[w, j], zn_recv.at[w, j], c, near)

    def deep_near_sum(w):
        for j in range(2):
            arrive(deep_near.at[j], zn_send.at[w, j], zn_recv.at[w, j], c, z)
            add_rows(acc.at[w, 2 * j + lax.rem(z, 2)], 0, deep_near.at[j], 0, shard, 80)
        send(acc.at[w, far], deep_far, zf_send.at[w], zf_recv.at[w], c, far)

    def deep_far_sum(w):
        arrive(deep_far, zf_send.at[w], zf_recv.at[w], c, z)
        add_rows(acc.at[w, z], 0, deep_far, 0, shard, 80)
        at = pl.ds(pl.multiple_of((1 - f_bit) * two, 16), two)
        send(acc.at[w, z, at], deep_f, f_send.at[w], f_recv.at[w], first, z)

    def deep_first_sum(w):
        arrive(deep_f, f_send.at[w], f_recv.at[w], c, z)
        add_rows(acc.at[w, z], f_bit * two, deep_f, 0, two, 80)
        at = pl.ds(pl.multiple_of(f_bit * two + (1 - s_bit) * cut, 16), cut)
        send(acc.at[w, z, at], deep_s, s_send.at[w], s_recv.at[w], second, z)

    def deep_second_sum(w):
        arrive(deep_s, s_send.at[w], s_recv.at[w], c, z)
        add_rows(acc.at[w, z], my_top, deep_s, 0, cut, 80)
        planes[w].start(final_piece(w))
        pltpu.make_async_copy(final_piece(w), out_piece(w, c), local_sem.at[8 + w]).start()

    def first_sum(w):
        arrive(land_f.at[w], f_send.at[w], f_recv.at[w], c, z)
        for s in range(n_wsh):
            add_rows(acc.at[w, s], f_bit * two, land_f.at[w, s], 0, two, 80)
        at = pl.ds(pl.multiple_of(f_bit * two + (1 - s_bit) * cut, 16), cut)
        send(acc.at[w, :, at], land_s.at[w], s_send.at[w], s_recv.at[w], second, z)

    def second_sum(w):
        arrive(land_s.at[w], s_send.at[w], s_recv.at[w], c, z)
        for s in range(n_wsh):
            add_rows(acc.at[w, s], my_top, land_s.at[w, s], 0, cut, 80)
        at = pl.ds(pl.multiple_of(my_top, 16), cut)
        for j in range(2):
            s = 2 * j + lax.rem(near, 2)
            send(acc.at[w, s, at], land_near.at[w, j], zn_send.at[w, j], zn_recv.at[w, j], c, near)

    def near_sum(w):
        for j in range(2):
            arrive(land_near.at[w, j], zn_send.at[w, j], zn_recv.at[w, j], c, z)
            add_rows(acc.at[w, 2 * j + lax.rem(z, 2)], my_top, land_near.at[w, j], 0, cut, 80)
        at = pl.ds(pl.multiple_of(my_top, 16), cut)
        send(acc.at[w, far, at], land_far.at[w], zf_send.at[w], zf_recv.at[w], c, far)

    def out_piece(w, b):
        b_core, b_x, b_y = lax.rem(b, 2), lax.rem(b // 2, 2), b // 4
        r = (1 - b_core) * (2 * b_x + b_y) + b_core * (2 * b_y + b_x)
        return dw3_out.at[w, pl.ds(pl.multiple_of(r * cut, 16), cut), columns(b)]

    planes = [
        Plane(lambda b, w=w: out_piece(w, b), c, z, around, g_send.at[w], g_recv.at[w]) for w in range(3)
    ]

    def final_piece(w):
        return acc.at[w, z, pl.ds(pl.multiple_of(my_top, 16), cut)]

    def far_sum(w):
        arrive(land_far.at[w], zf_send.at[w], zf_recv.at[w], c, z)
        add_rows(acc.at[w, z], my_top, land_far.at[w], 0, cut, 80)
        planes[w].start(final_piece(w))
        pltpu.make_async_copy(final_piece(w), out_piece(w, c), local_sem.at[8 + w]).start()

    def feed_forward(x1, h2, a, gu, ob, turned, ga, inv2, outb, stage):
        def tiles(step, size=256):
            for top in range(0, width, size):
                step(slice(top, top + size))

        def turn(source, target):
            def one(at):
                target[at, :] = source[:, at].T

            tiles(one, 128)

        def weight_gradient(w, left_t, right):
            for s in range(n_wsh):
                stage[w, s // 2 * shard : (s // 2 + 1) * shard, s % 2 * half : (s % 2 + 1) * half] = jnp.dot(
                    left_t[s * shard : (s + 1) * shard, :], right[:, theirs], preferred_element_type=f32
                ).astype(bf16)
            send(stage.at[w], pair_at(w), p_send.at[w], p_recv.at[w], sib, z)
            for s in range(n_wsh):
                at = slice(s * shard, (s + 1) * shard)
                acc[w, s] = jnp.dot(left_t[at, :], right[:, mine], preferred_element_type=f32).astype(bf16)

        by_first(DOWN, 3)
        for distance in range(1, n_wsh):
            shards_at(OUT, distance, all_others)
        own_o.wait()
        for k in range(1, n_ctx):
            g = lax.rem(c + k, n_ctx)
            arrive(heads_of(ob_land, g), ob_send.at[0], ob_recv.at[g], c, z)

        def turn_ob(at):
            ob[:, at] = ob_land[at, :].T

        tiles(turn_ob, 128)
        by_diag(DOWN, 1)
        by_second(DOWN, 3)
        own_full[OUT].wait()

        def mix(at):
            x1[:, at] = tok[:, at].astype(f32) + jnp.dot(ob[...], w_full[OUT, :, at], preferred_element_type=f32)

        tiles(mix)
        by_diag(DOWN, 2)

        def norm_rows(i, _):
            at = pl.ds(pl.multiple_of(i * 32, 32), 32)
            t = x1[at, :]
            inverse = lax.rsqrt(jnp.mean(t * t, -1, keepdims=True) + EPS)
            inv2[at, :] = jnp.broadcast_to(inverse, (32, 128))
            h2[at, :] = (t * inverse * gains[1:2, :]).astype(bf16)
            return 0

        lax.fori_loop(0, rows // 32, norm_rows, 0)
        by_diag(DOWN, 3)
        for distance in range(1, n_wsh):
            shards_at(UP, distance, all_others)
        own_full[UP].wait()

        def lift(at):
            dh[:, at] = jnp.dot(h2[...], w_full[UP, :, at], preferred_element_type=f32)

        tiles(lift)
        own_cot.wait()
        for distance in range(1, n_wsh):
            shards_at(DOWN, distance, all_others)
        for k in range(1, n_wsh):
            s = lax.rem(z + k, n_wsh)
            arrive(straight_rows(s, 1 - core), sx_send.at[0], sx_recv.at[k], c, z)
        own_full[DOWN].wait()

        def hidden(at):
            up = dh[:, at]
            da = lax.dot_general(
                cot[...], w_full[DOWN, at, :], (((1,), (1,)), ((), ())), preferred_element_type=f32
            )
            sig = 1.0 / (1.0 + jnp.exp(-up))
            act = up * sig
            a[:, at] = act.astype(bf16)
            turned[at, :] = act.T.astype(bf16)
            gu[:, at] = (da * sig * (1.0 + up * (1.0 - sig))).astype(bf16)

        tiles(hidden)

        def back(at):
            dh[:, at] = lax.dot_general(
                gu[...], w_full[UP, at, :], (((1,), (1,)), ((), ())), preferred_element_type=f32
            )

        tiles(back)

        def norm_back_rows(i, total):
            at = pl.ds(pl.multiple_of(i * 16, 16), 16)
            inverse = inv2[at, 0:1]
            normed = x1[at, :] * inverse
            grad = dh[at, :]
            both = grad * normed
            slope = jnp.mean(both * gains[1:2, :], -1, keepdims=True)
            result = cot[at, :].astype(f32) + inverse * (grad * gains[1:2, :] - normed * slope)
            dx[at, :] = result
            ga[at, :] = result.astype(bf16)
            return total + both

        gain_sum = lax.fori_loop(0, rows // 16, norm_back_rows, jnp.zeros((16, width), f32))
        vec[:, 0:width] = jnp.sum(gain_sum, axis=0, keepdims=True)

        def back_out(at):
            go_stage[at, :] = lax.dot_general(
                w_full[OUT, at, :], ga[...], (((1,), (1,)), ((), ())), preferred_element_type=f32
            ).astype(bf16)

        tiles(back_out)
        straight_line.finish(my_straight)
        for k in range(1, n_wsh):
            left(my_straight, sx_send.at[k], sx_recv.at[k], c, z)
        for w in range(3):
            lines[w].finish(my_piece[w])
            for distance in range(1, n_wsh):
                shards_at(w, distance, Plane.finish)
        for k in range(1, n_ctx):
            g = lax.rem(c + k, n_ctx)
            send(heads_of(go_stage, g), go_land.at[c], go_send.at[k], go_recv.at[c], g, z)
        pltpu.make_async_copy(my_heads(go_stage), go_land.at[c], local_sem.at[5]).start()
        weight_gradient(DOWN, turned, cot)
        turn(h2, turned)
        weight_gradient(UP, turned, gu)
        deep_pair_sum(DOWN)
        weight_gradient(OUT, ob_land, ga)
        pair_sum(UP)

        def finish(at):
            outb[:, at] = (
                x1[:, at] + jnp.dot(a[...], w_full[DOWN, :, at], preferred_element_type=f32)
            ).astype(bf16)

        tiles(finish)
        own_out = pltpu.make_async_copy(outb, out_out, local_sem.at[6])
        own_out.start()
        pair_sum(OUT)
        own_out.wait()
        for w in range(3):
            left(stage.at[w], p_send.at[w], p_recv.at[w], c, z)

    wide = (rows, width)
    pl.run_scoped(
        feed_forward,
        vm(wide, f32), vm(wide, bf16), vm(wide, bf16), vm(wide, bf16), vm(wide, bf16),
        vm((width, rows), bf16), vm(wide, bf16), vm((rows, 128), f32), vm(wide, bf16),
        vm((3, 2 * shard, width), bf16),
    )

    def attention_backward(goaug, go_tm, q_tm, dk, dv, dqkv):
        per = width // rows

        def block(i):
            return w_full.at[i // per, :, pl.ds(pl.multiple_of(lax.rem(i, per) * rows, 128), rows)]

        def part_p(i):
            return block(i)

        def part_f(i):
            return block(n_ctx // 2 + i)

        part_s = block(jnp.int32(n_ctx // 2 + 2))

        def part(b):
            return block(n_ctx // 2 + 3 + b)

        dk[...] = jnp.zeros_like(dk)
        dv[...] = jnp.zeros_like(dv)
        dqkv[3 * span :, :] = jnp.zeros((dqkv.shape[0] - 3 * span, length), bf16)
        gain_col = gain_column()

        def prepare(g):
            at = pl.ds(pl.multiple_of(g * rows, 16), rows)
            for h in range(heads):
                go = go_land[g, h * hd : (h + 1) * hd, :]
                wide = go.astype(f32)
                delta = jnp.sum(wide * o_all[g, h * hd : (h + 1) * hd, :], axis=0, keepdims=True)
                tail = jnp.concatenate([three_rows(-delta, rows), jnp.zeros((120 - hd, rows), f32)], axis=0)
                goaug[g, h, 0:hd, :] = go
                goaug[g, h, hd:128, :] = tail.astype(bf16)
                go_tm[h, at, :] = jnp.concatenate([wide, jnp.zeros((128 - hd, rows), f32)], axis=0).T.astype(bf16)
                q = qaug[g, h, 0:hd, :].astype(f32)
                q_tm[h, at, :] = jnp.concatenate([q, jnp.zeros((128 - hd, rows), f32)], axis=0).T.astype(bf16)

        pltpu.make_async_copy(my_heads(go_stage), go_land.at[c], local_sem.at[5]).wait()
        prepare(c)

        def prepare_other(k, _):
            g = lax.rem(c + k, n_ctx)
            arrive(go_land.at[g], go_send.at[0], go_recv.at[g], c, z)
            prepare(g)
            return 0

        lax.fori_loop(1, n_ctx, prepare_other, 0)
        three = 3 * hd
        starts, size = windows(width, n_wsh)

        def head_gradients(h, events):
            def attend(g, _):
                at = pl.ds(pl.multiple_of(g * rows, 16), rows)
                p = jnp.exp(jnp.dot(kaug[h], qaug[g, h], preferred_element_type=f32))
                ds = (p * jnp.dot(vaug[h], goaug[g, h], preferred_element_type=f32)).astype(bf16)
                dq = jnp.dot(kt[h], ds, preferred_element_type=f32)
                dk[h] += jnp.dot(ds, q_tm[h, at, :], preferred_element_type=f32)
                dv[h] += jnp.dot(p.astype(bf16), go_tm[h, at, :], preferred_element_type=f32)
                scale_acc[...] += dq * qraw[g, h * hd : (h + 1) * hd, :]
                lanes = pl.ds(pl.multiple_of(g * rows, 128), rows)
                dqkv[h * three : h * three + hd, lanes] = (dq * gain_col).astype(bf16)
                for step, event in events:
                    pl.when(g == step)(event)
                return 0

            lax.fori_loop(0, n_ctx, attend, 0)

            def settle(g, _):
                at = pl.ds(pl.multiple_of(g * rows, 16), rows)
                lanes = pl.ds(pl.multiple_of(g * rows, 128), rows)
                for i, source in enumerate((dk, dv)):
                    turned = source[h, at, :].T
                    top = h * three + (i + 1) * hd
                    dqkv[top : top + hd, lanes] = turned[0:hd].astype(bf16)
                return 0

            lax.fori_loop(0, n_ctx, settle, 0)

        def head_windows(h):
            for s in range(n_wsh):
                total = jnp.zeros((three, size), f32)
                for b in range(n_ctx):
                    total = total + jnp.dot(
                        dqkv[h * three : (h + 1) * three, b * rows : (b + 1) * rows],
                        h1_all[b, :, starts[s] : starts[s] + size], preferred_element_type=f32,
                    )
                win_out[h, s] = total.astype(bf16)
            for j in range(2):
                s = 2 * j + lax.rem(near, 2)
                send(win_out.at[h, s], win_near.at[h, j], wn_send.at[h, j], wn_recv.at[h, j], c, near)

        def near_window(h):
            for j in range(2):
                arrive(win_near.at[h, j], wn_send.at[h, j], wn_recv.at[h, j], c, z)
                add_rows(win_out.at[h, 2 * j + lax.rem(z, 2)], 0, win_near.at[h, j], 0, three, 80)
            send(win_out.at[h, far], win_far.at[h], wf_send.at[h], wf_recv.at[h], c, far)

        plane_w = [
            Plane(lambda b, h=h: dwqkv_out.at[b, h], c, z, around, wg_send.at[h], wg_recv.at[h]) for h in range(heads)
        ]

        def own_window(h):
            return pltpu.make_async_copy(win_out.at[h, z], dwqkv_out.at[c, h], load_sem.at[h])

        def far_window(h):
            arrive(win_far.at[h], wf_send.at[h], wf_recv.at[h], c, z)
            add_rows(win_out.at[h, z], 0, win_far.at[h], 0, three, 80)
            plane_w[h].start(win_out.at[h, z])
            own_window(h).start()

        head_gradients(0, ((6, lambda: first_sum(UP)),))
        head_windows(0)
        head_gradients(1, (
            (1, lambda: second_sum(UP)), (4, lambda: deep_near_sum(DOWN)), (5, lambda: first_sum(OUT)),
            (6, lambda: near_sum(UP)), (6, lambda: near_window(0)), (7, lambda: second_sum(OUT)),
        ))

        def partial(b):
            lanes = pl.ds(pl.multiple_of(b * rows, 128), rows)
            part(b)[...] = jnp.dot(w_c[...], dqkv[:, lanes], preferred_element_type=f32).astype(bf16)

        def to_sib(b):
            partial(b)
            send(part(b), part_p(b // 2), hp_send.at[b // 2], hp_recv.at[b // 2], sib, z)

        def scale_row():
            scale_sum = jnp.sum(scale_acc[...], axis=1, keepdims=True)
            return jnp.concatenate(
                [jnp.broadcast_to(scale_sum, (hd, 128)), jnp.zeros((128 - hd, 128), f32)], axis=0
            ).T[0:1, :]

        def pair(i, b):
            arrive(part_p(b // 2), hp_send.at[0], hp_recv.at[b // 2], c, z)
            add_rows(part(b), 0, part_p(b // 2), 0, width, 128)
            if i < 2:
                slot = s_bit if i == 0 else 1 - s_bit
                send(part(b), part_f(slot), hf_send.at[i], hf_recv.at[slot], first, z)

        shift = sib - c
        to_sib(diag + shift)
        to_sib(second + shift)
        partial(diag)
        to_sib(first + shift)
        pair(1, diag)
        partial(first)
        to_sib(sib)
        pair(0, first)
        partial(second)
        partial(c)
        head_windows(1)
        deep_far_sum(DOWN)
        far_sum(UP)
        near_sum(OUT)
        vec[:, width:] = scale_row()
        for k in range(1, n_ctx):
            g = lax.rem(c + k, n_ctx)
            send(vec, vec_plane.at[c], vp_send.at[k], vp_recv.at[c], g, z)
        far_window(0)
        pair(2, second)
        pair(3, c)
        deep_first_sum(DOWN)
        near_window(1)
        planes[UP].from_first()
        far_sum(OUT)
        planes[UP].from_second()
        arrive(part_f(1 - s_bit), hf_send.at[0], hf_recv.at[1 - s_bit], c, z)
        add_rows(part(second), 0, part_f(1 - s_bit), 0, width, 128)
        send(part(second), part_s, hs_send.at[0], hs_recv.at[0], second, z)
        deep_second_sum(DOWN)
        arrive(part_f(s_bit), hf_send.at[0], hf_recv.at[s_bit], c, z)
        add_rows(part(c), 0, part_f(s_bit), 0, width, 128)
        far_window(1)
        plane_w[0].from_first()
        plane_w[0].from_second()
        planes[UP].from_diag()
        total = vec[...]
        for k in range(1, n_ctx):
            g = lax.rem(c + k, n_ctx)
            arrive(vec_plane.at[g], vp_send.at[0], vp_recv.at[g], c, z)
            total = total + vec_plane[g]
        vec_mid[...] = total
        for k in range(1, n_wsh):
            send(vec_mid, vec_line.at[z], vl_send.at[k], vl_recv.at[z], c, lax.rem(z + k, n_wsh))
        planes[OUT].from_first()
        planes[OUT].from_second()
        planes[DOWN].from_first()
        planes[DOWN].from_second()
        arrive(part_s, hs_send.at[0], hs_recv.at[0], c, z)

        mine_part = part(c)

        def turn_dh(i, _):
            at = pl.ds(pl.multiple_of(i * 128, 128), 128)
            dh[:, at] = (mine_part[at, :].astype(f32) + part_s[at, :].astype(f32)).T
            return 0

        lax.fori_loop(0, width // 128, turn_dh, 0)

        def last_rows(i, total):
            at = pl.ds(pl.multiple_of(i * 16, 16), 16)
            t = tok[at, :].astype(f32)
            inverse = lax.rsqrt(jnp.mean(t * t, -1, keepdims=True) + EPS)
            normed = t * inverse
            grad = dh[at, :]
            both = grad * normed
            slope = jnp.mean(both * gains[0:1, :], -1, keepdims=True)
            gtok[at, :] = (dx[at, :] + inverse * (grad * gains[0:1, :] - normed * slope)).astype(bf16)
            return total + both

        gain_sum = lax.fori_loop(0, rows // 16, last_rows, jnp.zeros((16, width), f32))
        row[...] = jnp.sum(gain_sum, axis=0, keepdims=True)
        for k in range(1, n_ctx):
            g = lax.rem(c + k, n_ctx)
            send(row, row_plane.at[c], rp_send.at[k], rp_recv.at[c], g, z)
        own_gtok = pltpu.make_async_copy(gtok, gtok_out, local_sem.at[11])
        own_gtok.start()
        plane_w[0].from_diag()
        planes[OUT].from_diag()
        planes[DOWN].from_diag()
        plane_w[1].from_first()
        plane_w[1].from_second()
        total = row[...]
        for k in range(1, n_ctx):
            g = lax.rem(c + k, n_ctx)
            arrive(row_plane.at[g], rp_send.at[0], rp_recv.at[g], c, z)
            total = total + row_plane[g]
        row_mid[...] = total
        for k in range(1, n_wsh):
            send(row_mid, row_line.at[z], rl_send.at[k], rl_recv.at[z], c, lax.rem(z + k, n_wsh))
        plane_w[1].from_diag()
        whole = vec_mid[...]
        for k in range(1, n_wsh):
            s = lax.rem(z + k, n_wsh)
            arrive(vec_line.at[s], vl_send.at[0], vl_recv.at[s], c, z)
            whole = whole + vec_line[s]
        vec_sum[...] = jnp.zeros_like(vec_sum)
        vec_sum[1:2, :] = whole[:, 0:width]
        vec_sum[2:3, 0:128] = whole[:, width:]
        for k in range(1, n_wsh):
            s = lax.rem(z + k, n_wsh)
            arrive(row_line.at[s], rl_send.at[0], rl_recv.at[s], c, z)
            total = total + row_line[s]
        vec_sum[0:1, :] = total
        own_vec = pltpu.make_async_copy(vec_sum, vec_out, local_sem.at[12])
        own_vec.start()
        for plane in planes + plane_w:
            all_others(plane)
            plane.finish()
        for i in range(n_ctx // 2):
            left(part(c), hp_send.at[i], hp_recv.at[i], c, z)
        for i in range(2):
            left(part(c), hf_send.at[i], hf_recv.at[i], c, z)
        left(part(c), hs_send.at[0], hs_recv.at[0], c, z)
        for copy in (own_gtok, own_vec, *[own_window(h) for h in range(heads)]):
            copy.wait()

    pl.run_scoped(
        attention_backward,
        vm((n_ctx, heads, 128, rows), bf16), vm((heads, length, 128), bf16), vm((heads, length, 128), bf16),
        vm((heads, length, 128), f32), vm((heads, length, 128), f32), vm((w_c.shape[1], length), bf16),
    )

    wline.finish(w_own)
    for k in range(1, n_wsh):
        left(pack_ref, pk_send.at[k], pk_recv.at[z], c, z)
        left(vec, vl_send.at[k], vl_recv.at[0], c, z)
        left(row, rl_send.at[k], rl_recv.at[0], c, z)
    for k in range(1, n_ctx):
        g = lax.rem(c + k, n_ctx)
        left(ob_stage.at[g], ob_send.at[g], ob_recv.at[g], c, z)
        left(go_land.at[0], go_send.at[k], go_recv.at[0], c, z)
        left(vec, vp_send.at[k], vp_recv.at[0], c, z)
        left(row, rp_send.at[k], rp_recv.at[0], c, z)
    for w in range(3):
        pltpu.make_async_copy(final_piece(w), out_piece(w, c), local_sem.at[8 + w]).wait()
        left(deep_f if w == DOWN else land_f.at[w], f_send.at[w], f_recv.at[w], c, z)
        left(deep_s if w == DOWN else land_s.at[w], s_send.at[w], s_recv.at[w], c, z)
        for j in range(2):
            left(deep_near.at[j] if w == DOWN else land_near.at[w, j], zn_send.at[w, j], zn_recv.at[w, j], c, z)
        left(deep_far if w == DOWN else land_far.at[w], zf_send.at[w], zf_recv.at[w], c, z)
    for h in range(heads):
        for j in range(2):
            left(win_near.at[h, j], wn_send.at[h, j], wn_recv.at[h, j], c, z)
        left(win_far.at[h], wf_send.at[h], wf_recv.at[h], c, z)


def whole_call(dims, tok, cot, w6, pack, order, lengths):
    n_ctx, n_wsh, hd, heads = dims
    rows, width = tok.shape
    span, length, shard = hd * heads, rows * n_ctx, width // n_wsh
    half, cut = width // 2, shard // (n_ctx // 2)
    f32, bf16 = jnp.float32, jnp.bfloat16
    hbm = pl.BlockSpec(memory_space=pl.ANY)
    smem = pl.BlockSpec(memory_space=pltpu.SMEM)
    shape = jax.ShapeDtypeStruct
    dma = pltpu.SemaphoreType.DMA
    vm = pltpu.VMEM
    size = windows(width, n_wsh)[1]
    lanes = -(-3 * span // 128) * 128
    wide = (rows, width)
    outs = (
        shape(wide, bf16), shape(wide, bf16),
        shape((3, shard, width), bf16), shape((n_ctx, heads, 3 * hd, size), bf16), shape((8, width), f32),
    )
    scratch = [
        vm((n_ctx, rows, width), bf16), vm((3, width, width), bf16), vm((length, width), bf16),
        vm((width, lanes), bf16), vm((shard, lanes), bf16), vm((n_wsh,) + pack.shape, f32), vm((8, width), f32),
        vm((heads, length, 128), bf16), vm((heads, length, 128), bf16), vm((heads, hd, length), bf16),
        vm((n_ctx, heads, 128, rows), bf16), vm((n_ctx, span, rows), f32), vm((n_ctx, span, rows), f32),
        vm((n_ctx, span, rows), bf16), vm((width, rows), bf16), vm((width, rows), bf16), vm((n_ctx, span, rows), bf16),
        vm((3, n_wsh, shard, half), bf16), vm((2, n_wsh, 2 * cut, half), bf16), vm((2, n_wsh, cut, half), bf16),
        vm((2, 2, cut, half), bf16), vm((2, cut, half), bf16),
        vm((2, shard, half), bf16), vm((shard, half), bf16), vm((2 * cut, half), bf16), vm((cut, half), bf16),
        vm((heads, n_wsh, 3 * hd, size), bf16), vm((heads, 2, 3 * hd, size), bf16), vm((heads, 3 * hd, size), bf16),
        vm(wide, f32), vm(wide, f32), vm(wide, bf16), vm(wide, bf16), vm(wide, bf16),
        vm((1, width + 128), f32), vm((n_ctx, 1, width + 128), f32), vm((n_wsh, 1, width + 128), f32),
        vm((1, width + 128), f32), vm((8, width), f32), vm((1, width), f32), vm((n_ctx, 1, width), f32), vm((n_wsh, 1, width), f32),
        vm((1, width), f32), vm((hd, rows), f32),
        dma((2, 7)), dma((2, n_ctx)), dma((2 * n_wsh,)), dma((n_wsh,)), dma((n_wsh,)), dma((n_wsh,)),
        dma((n_ctx,)), dma((n_ctx,)), dma((3, 2 * n_wsh)), dma((3, n_wsh)),
        dma((3, n_wsh, 7)), dma((3, n_wsh, n_ctx)),
        dma((n_ctx,)), dma((n_ctx,)), dma((3,)), dma((3,)), dma((3,)), dma((3,)), dma((3,)), dma((3,)),
        dma((3, 2)), dma((3, 2)), dma((3,)), dma((3,)), dma((3, 7)), dma((3, n_ctx)),
        dma((n_ctx // 2,)), dma((n_ctx // 2,)), dma((2,)), dma((2,)), dma((1,)), dma((1,)),
        dma((heads, 2)), dma((heads, 2)), dma((heads,)), dma((heads,)), dma((heads, 7)), dma((heads, n_ctx)),
        dma((n_ctx,)), dma((n_ctx,)), dma((n_wsh,)), dma((n_wsh,)),
        dma((n_ctx,)), dma((n_ctx,)), dma((n_wsh,)), dma((n_wsh,)), dma((2 * n_wsh,)), dma((n_wsh,)), dma((n_wsh,)), dma((n_wsh,)),
        dma((13,)), dma((heads + 3,)), dma((3, 2)),
    ]
    return pl.pallas_call(
        functools.partial(whole_kernel, dims),
        out_shape=outs,
        in_specs=[hbm] * 9 + [smem] * 2,
        out_specs=[hbm] * len(outs),
        scratch_shapes=scratch,
        compiler_params=pltpu.CompilerParams(
            collective_id=0, has_side_effects=True, vmem_limit_bytes=VMEM_BYTES
        ),
    )(tok, cot, *w6, pack, order, lengths)


def finish_kernel(dims, dwqkv_ref, dw3_ref, *refs):
    tok_refs, outs, tok_outs = refs[:2], refs[2:8], refs[8:10]
    pieces, plain, wide, turned, results, tok_buf, in_sem, out_sem = refs[10:]
    n_ctx, n_wsh, hd, heads = dims
    z = lax.axis_index("wsh")
    f32 = jnp.float32
    shard, width = outs[0].shape
    starts, size = windows(width, n_wsh)
    offset = jnp.int32(0)
    for s in range(n_wsh):
        offset = jnp.where(z == s, s * shard - starts[s], offset)
    ins = [pltpu.make_async_copy(dw3_ref.at[w], plain.at[w], in_sem.at[w]) for w in range(3)]
    for i in range(3):
        at = pl.ds(i * hd, hd)
        ins.append(pltpu.make_async_copy(dwqkv_ref.at[:, :, at], pieces.at[i], in_sem.at[3 + i]))
    tok_ins = [pltpu.make_async_copy(tok_refs[i], tok_buf.at[i], in_sem.at[6 + i]) for i in range(2)]
    for copy in ins + tok_ins:
        copy.start()
    done = []

    def store(i, result):
        copy = pltpu.make_async_copy(result, outs[i], out_sem.at[i])
        copy.start()
        done.append(copy)

    for w in range(3):
        ins[w].wait()
        results[w] = plain[w].astype(f32)
        store(3 + w, results.at[w])
    for i in range(3):
        ins[3 + i].wait()

        def lay(b, _):
            for h in range(heads):
                at = pl.ds(pl.multiple_of((b * heads + h) * hd, 16), hd)
                wide[at, :] = pieces[i, b, h].astype(f32)
            return 0

        lax.fori_loop(0, n_ctx, lay, 0)

        def turn(j, _):
            at = pl.ds(pl.multiple_of(j * 128, 128), 128)
            turned[i, :, at] = wide[at, :].T
            return 0

        lax.fori_loop(0, width // 128, turn, 0)
        store(i, turned.at[i, pl.ds(pl.multiple_of(offset, 8), shard)])
    for i in range(2):
        tok_ins[i].wait()
        copy = pltpu.make_async_copy(tok_buf.at[i], tok_outs[i], out_sem.at[6 + i])
        copy.start()
        done.append(copy)
    for copy in done:
        copy.wait()


def finish_call(dims, dwqkv, dw3, outputs, gtok):
    n_ctx, n_wsh, hd, heads = dims
    shard, width = dw3.shape[1:]
    size = dwqkv.shape[3]
    f32, bf16 = jnp.float32, jnp.bfloat16
    hbm = pl.BlockSpec(memory_space=pl.ANY)
    dma = pltpu.SemaphoreType.DMA
    return pl.pallas_call(
        functools.partial(finish_kernel, dims),
        out_shape=(jax.ShapeDtypeStruct((shard, width), f32),) * 6 + (jax.ShapeDtypeStruct(gtok.shape, bf16),) * 2,
        in_specs=[hbm] * 4,
        out_specs=[hbm] * 8,
        scratch_shapes=[
            pltpu.VMEM((3, n_ctx, heads, hd, size), bf16), pltpu.VMEM((3, shard, width), bf16),
            pltpu.VMEM((width, size), f32), pltpu.VMEM((3, size, width), f32), pltpu.VMEM((3, shard, width), f32),
            pltpu.VMEM((2,) + gtok.shape, bf16), dma((8,)), dma((8,)),
        ],
        compiler_params=pltpu.CompilerParams(vmem_limit_bytes=VMEM_BYTES),
    )(dwqkv, dw3, outputs, gtok)


def head_split(
    tokens, cotangent, block_lengths, group_order, w_query, w_key, w_value, w_out, w_up, w_down,
    gain_attn, gain_mlp, query_scale,
):
    f32 = jnp.float32
    n_ctx, n_wsh = lax.axis_size("ctx"), lax.axis_size("wsh")
    z = lax.axis_index("wsh")
    width = tokens.shape[2]
    hd, heads = width // H, H // n_ctx
    shard = width // n_wsh
    dims = (n_ctx, n_wsh, hd, heads)
    lanes = -(-shard // 128) * 128
    pack = sum(
        jnp.pad(v.astype(f32)[None], ((i, 7 - i), (0, lanes - v.shape[0])))
        for i, v in enumerate((gain_attn, gain_mlp, query_scale))
    )
    outputs, gtok, dw3, dwqkv, sums = whole_call(
        dims, tokens[0], cotangent[0], (w_query, w_key, w_value, w_out, w_up, w_down), pack, group_order, block_lengths
    )[:5]
    *weight_grads, outputs, gtok = finish_call(dims, dwqkv, dw3, outputs, gtok)
    own = [lax.dynamic_slice_in_dim(sums[i], z * shard, shard, 0) for i in (0, 1)]
    scale_grad = (
        lax.dynamic_slice_in_dim(sums[2], z * (hd // n_wsh), hd // n_wsh, 0)
        * (LOG_BASE / math.sqrt(hd))
        * jax.nn.sigmoid(query_scale.astype(f32))
    )
    return (
        outputs.reshape(tokens.shape), gtok.reshape(tokens.shape), *weight_grads, own[0], own[1], scale_grad,
    )


def solution(mesh):
    in_specs = (
        P("wsh", "ctx", None),
        P("wsh", "ctx", None),
        P("wsh", None),
        P(),
        P("wsh", None),
        P("wsh", None),
        P("wsh", None),
        P("wsh", None),
        P("wsh", None),
        P("wsh", None),
        P("wsh"),
        P("wsh"),
        P("wsh"),
    )
    out_specs = (
        P("wsh", "ctx", None),
        P("wsh", "ctx", None),
        P("wsh", None),
        P("wsh", None),
        P("wsh", None),
        P("wsh", None),
        P("wsh", None),
        P("wsh", None),
        P("wsh"),
        P("wsh"),
        P("wsh"),
    )
    n_ctx, n_wsh = mesh.shape["ctx"], mesh.shape["wsh"]
    plan = head_split if (n_ctx, n_wsh) == (8, 4) else per_device
    return jax.shard_map(
        plan, mesh=mesh, in_specs=in_specs, out_specs=out_specs, check_vma=False
    )
```

```python
import functools
import math

import jax
import jax.numpy as jnp
from jax import lax
from jax.experimental import pallas as pl
from jax.experimental.pallas import tpu as pltpu
from jax.sharding import PartitionSpec as P

H = 16


EPS = 1e-06
LOG_BASE = 1.442695041


def row_step():
    return 512


def rows_at(array, block_no, step_rows):
    return lax.dynamic_slice_in_dim(array, block_no * step_rows, step_rows, 0)


def inverse_rms(values):
    return lax.rsqrt(jnp.mean(values * values, -1, keepdims=True) + EPS)


def norm_back(normed, inverse, grad):
    return inverse * (grad - normed * jnp.mean(grad * normed, -1, keepdims=True))


def split_heads(matrix):
    return matrix.reshape(matrix.shape[0], H, -1)


def outer_product(left, right):
    return lax.dot_general(
        left, right, (((0,), (0,)), ((), ())), preferred_element_type=jnp.float32
    )


def back_product(grad, weight):
    return lax.dot_general(
        grad, weight, (((1,), (1,)), ((), ())), preferred_element_type=jnp.float32
    )


def probabilities(query3, key3, query_marks, key_marks, log_totals):
    scores = jnp.einsum("qhd,khd->hqk", query3, key3, preferred_element_type=jnp.float32)
    allowed = key_marks[None, None, :] <= query_marks[None, :, None]
    return jnp.exp(jnp.where(allowed, scores - log_totals[:, :, None], -jnp.inf))


def score_grads(chances, grad_out3, value3, deltas):
    grad_chances = jnp.einsum("qhd,khd->hqk", grad_out3, value3, preferred_element_type=jnp.float32)
    return (chances * (grad_chances - deltas[:, :, None])).astype(jnp.bfloat16)


def per_device(
    tokens,
    cotangent,
    block_lengths,
    group_order,
    w_query,
    w_key,
    w_value,
    w_out,
    w_up,
    w_down,
    gain_attn,
    gain_mlp,
    query_scale,
):
    gathered = (
        lax.all_gather(w_query, "wsh", axis=0, tiled=True),
        lax.all_gather(w_key, "wsh", axis=0, tiled=True),
        lax.all_gather(w_value, "wsh", axis=0, tiled=True),
        lax.all_gather(w_out, "wsh", axis=0, tiled=True),
        lax.all_gather(w_up, "wsh", axis=0, tiled=True),
        lax.all_gather(w_down, "wsh", axis=0, tiled=True),
        lax.all_gather(gain_attn, "wsh", axis=0, tiled=True),
        lax.all_gather(gain_mlp, "wsh", axis=0, tiled=True),
        lax.all_gather(query_scale, "wsh", axis=0, tiled=True),
    )
    (
        full_query,
        full_key,
        full_value,
        full_out,
        full_up,
        full_down,
        norm_attn,
        norm_mlp,
        scale_param,
    ) = gathered
    tok_rows = tokens.shape[1]
    model_width = tokens.shape[2]
    length = tok_rows * lax.axis_size("ctx")
    device = lax.axis_index("ctx")
    head_size = scale_param.shape[0]
    f32 = jnp.float32
    bf16 = jnp.bfloat16
    inputs = tokens.reshape(tok_rows, model_width).astype(f32)
    positions = (
        group_order[:, None] * tok_rows + jnp.arange(tok_rows, dtype=jnp.int32)[None, :]
    ).reshape(length)
    bounds = jnp.cumsum(block_lengths[0])
    block_ids = jnp.sum((bounds[None, :] <= positions[:, None]).astype(jnp.int32), -1)
    query_ids = lax.dynamic_slice_in_dim(block_ids, device * tok_rows, tok_rows, 0)
    inverse_one = inverse_rms(inputs)
    normed_one = inputs * inverse_one
    hidden_one = (normed_one * norm_attn.astype(f32)).astype(bf16)
    query_raw = jnp.dot(hidden_one, full_query, preferred_element_type=f32).reshape(
        tok_rows, H, head_size
    )
    query_gain = LOG_BASE / math.sqrt(head_size) * jax.nn.softplus(scale_param.astype(f32))
    query3 = (query_raw * query_gain).astype(bf16)
    key_flat = jnp.dot(hidden_one, full_key, preferred_element_type=f32).astype(bf16)
    value_flat = jnp.dot(hidden_one, full_value, preferred_element_type=f32).astype(bf16)
    initial = (
        jnp.full((H, tok_rows), -1e30, f32),
        jnp.zeros((H, tok_rows), f32),
        jnp.zeros((tok_rows, H, head_size), f32),
    )
    key_rows = lax.all_gather(key_flat, "ctx", axis=0, tiled=True)
    value_rows = lax.all_gather(value_flat, "ctx", axis=0, tiled=True)
    row_count = key_rows.shape[0]
    step_rows = row_step()

    def one_block(block_no, looped):
        key_part = split_heads(rows_at(key_rows, block_no, step_rows))
        value_part = split_heads(rows_at(value_rows, block_no, step_rows))
        block_marks = rows_at(block_ids, block_no, step_rows)
        maxima, totals, running = looped
        scores = jnp.einsum("qhd,khd->hqk", query3, key_part, preferred_element_type=f32)
        allowed = block_marks[None, None, :] <= query_ids[None, :, None]
        scores = jnp.where(allowed, scores, -jnp.inf)
        raised = jnp.maximum(maxima, jnp.max(scores, -1))
        rescale = jnp.exp(maxima - raised)
        weights = jnp.exp(scores - raised[:, :, None])
        totals = totals * rescale + jnp.sum(weights, -1)
        running = running * rescale.T[:, :, None] + jnp.einsum(
            "hqk,khd->qhd", weights.astype(bf16), value_part, preferred_element_type=f32
        )
        return (raised, totals, running)

    maxima, totals, running = lax.fori_loop(0, row_count // step_rows, one_block, initial)
    log_totals = maxima + jnp.log(totals)
    attended = running / totals.T[:, :, None]
    attended_bf = attended.reshape(tok_rows, model_width).astype(bf16)
    mixed = inputs + jnp.dot(attended_bf, full_out, preferred_element_type=f32)
    inverse_two = inverse_rms(mixed)
    normed_two = mixed * inverse_two
    hidden_two = (normed_two * norm_mlp.astype(f32)).astype(bf16)
    up_raw = jnp.dot(hidden_two, full_up, preferred_element_type=f32)
    active = jax.nn.silu(up_raw).astype(bf16)
    outputs = mixed + jnp.dot(active, full_down, preferred_element_type=f32)
    grad_output = cotangent.reshape(tok_rows, model_width).astype(f32)
    grad_mlp = grad_output.astype(bf16)
    grad_active = back_product(grad_mlp, full_down)
    sigmoid_up = jax.nn.sigmoid(up_raw)
    grad_up_raw = (grad_active * sigmoid_up * (1.0 + up_raw * (1.0 - sigmoid_up))).astype(bf16)
    grad_hidden_two = back_product(grad_up_raw, full_up)
    grad_gain_mlp = jnp.sum(grad_hidden_two * normed_two, 0)
    grad_mixed = grad_output + norm_back(
        normed_two, inverse_two, grad_hidden_two * norm_mlp.astype(f32)
    )
    grad_branch = grad_mixed.astype(bf16)
    grad_att = back_product(grad_branch, full_out).astype(bf16)
    grad_att3 = split_heads(grad_att)
    deltas = jnp.sum(grad_att3.astype(f32) * attended, -1).T
    key_whole, value_whole = (
        lax.all_gather(key_flat, "ctx", axis=0, tiled=True),
        lax.all_gather(value_flat, "ctx", axis=0, tiled=True),
    )
    step_rows = row_step()
    block_total = length // step_rows

    def key_block(grad_q, block_parts):
        key_rows, value_rows, block_marks = block_parts
        key_part = split_heads(key_rows)
        value_part = split_heads(value_rows)
        zero_part = jnp.zeros((key_rows.shape[0], H, head_size), f32)
        chances = probabilities(query3, key_part, query_ids, block_marks, log_totals)
        slopes = score_grads(chances, grad_att3, value_part, deltas)
        new_grad = (grad_q, zero_part, zero_part)[0] + jnp.einsum(
            "hqk,khd->qhd", slopes, key_part, preferred_element_type=f32
        )
        grad_key_part = jnp.einsum("hqk,qhd->khd", slopes, query3, preferred_element_type=f32)
        grad_value_part = jnp.einsum(
            "hqk,qhd->khd", chances.astype(bf16), grad_att3, preferred_element_type=f32
        )
        return (new_grad, (grad_key_part, grad_value_part))

    grad_qs, (key_terms, value_terms) = lax.scan(
        key_block,
        jnp.zeros((tok_rows, H, head_size), f32),
        (
            key_whole.reshape(block_total, step_rows, model_width),
            value_whole.reshape(block_total, step_rows, model_width),
            block_ids.reshape(block_total, step_rows),
        ),
    )
    grad_key, grad_value = (
        lax.psum_scatter(
            key_terms.reshape(length, model_width).astype(jnp.bfloat16),
            "ctx",
            scatter_dimension=0,
            tiled=True,
        ).astype(jnp.float32),
        lax.psum_scatter(
            value_terms.reshape(length, model_width).astype(jnp.bfloat16),
            "ctx",
            scatter_dimension=0,
            tiled=True,
        ).astype(jnp.float32),
    )
    grad_key_bf = grad_key.astype(bf16)
    grad_value_bf = grad_value.astype(bf16)
    grad_query_bf = (grad_qs * query_gain).reshape(tok_rows, model_width).astype(bf16)
    grad_scale_param = (
        jnp.sum(grad_qs * query_raw, (0, 1))
        * (LOG_BASE / math.sqrt(head_size))
        * jax.nn.sigmoid(scale_param.astype(f32))
    )
    grad_hidden_one = (
        back_product(grad_query_bf, full_query)
        + back_product(grad_key_bf, full_key)
        + back_product(grad_value_bf, full_value)
    )
    grad_gain_attn = jnp.sum(grad_hidden_one * normed_one, 0)
    grad_inputs = grad_mixed + norm_back(
        normed_one, inverse_one, grad_hidden_one * norm_attn.astype(f32)
    )
    grad_queryw = outer_product(hidden_one, grad_query_bf)
    grad_keyw = outer_product(hidden_one, grad_key_bf)
    grad_valuew = outer_product(hidden_one, grad_value_bf)
    grad_outw = outer_product(attended_bf, grad_branch)
    grad_upw = outer_product(hidden_two, grad_up_raw)
    grad_downw = outer_product(active, grad_mlp)
    owned = (
        lax.psum_scatter(
            grad_queryw.astype(jnp.bfloat16), "wsh", scatter_dimension=0, tiled=True
        ).astype(jnp.float32),
        lax.psum_scatter(
            grad_keyw.astype(jnp.bfloat16), "wsh", scatter_dimension=0, tiled=True
        ).astype(jnp.float32),
        lax.psum_scatter(
            grad_valuew.astype(jnp.bfloat16), "wsh", scatter_dimension=0, tiled=True
        ).astype(jnp.float32),
        lax.psum_scatter(
            grad_outw.astype(jnp.bfloat16), "wsh", scatter_dimension=0, tiled=True
        ).astype(jnp.float32),
        lax.psum_scatter(
            grad_upw.astype(jnp.bfloat16), "wsh", scatter_dimension=0, tiled=True
        ).astype(jnp.float32),
        lax.psum_scatter(
            grad_downw.astype(jnp.bfloat16), "wsh", scatter_dimension=0, tiled=True
        ).astype(jnp.float32),
        lax.psum_scatter(
            grad_gain_attn.astype(jnp.bfloat16), "wsh", scatter_dimension=0, tiled=True
        ).astype(jnp.float32),
        lax.psum_scatter(
            grad_gain_mlp.astype(jnp.bfloat16), "wsh", scatter_dimension=0, tiled=True
        ).astype(jnp.float32),
        lax.psum_scatter(
            grad_scale_param.astype(jnp.bfloat16), "wsh", scatter_dimension=0, tiled=True
        ).astype(jnp.float32),
    )
    summed = (
        lax.psum(owned[0].astype(jnp.bfloat16), "ctx").astype(jnp.float32),
        lax.psum(owned[1].astype(jnp.bfloat16), "ctx").astype(jnp.float32),
        lax.psum(owned[2].astype(jnp.bfloat16), "ctx").astype(jnp.float32),
        lax.psum(owned[3].astype(jnp.bfloat16), "ctx").astype(jnp.float32),
        lax.psum(owned[4].astype(jnp.bfloat16), "ctx").astype(jnp.float32),
        lax.psum(owned[5].astype(jnp.bfloat16), "ctx").astype(jnp.float32),
        lax.psum(owned[6].astype(jnp.bfloat16), "ctx").astype(jnp.float32),
        lax.psum(owned[7].astype(jnp.bfloat16), "ctx").astype(jnp.float32),
        lax.psum(owned[8].astype(jnp.bfloat16), "ctx").astype(jnp.float32),
    )
    return (
        outputs.reshape(tokens.shape).astype(bf16),
        grad_inputs.reshape(tokens.shape).astype(bf16),
        summed[0],
        summed[1],
        summed[2],
        summed[3],
        summed[4],
        summed[5],
        summed[6],
        summed[7],
        summed[8],
    )


MESH = pl.DeviceIdType.MESH
NEG = -1e30
VMEM_BYTES = 62 * 1024 * 1024


def place():
    c, z = lax.axis_index("ctx"), lax.axis_index("wsh")
    core, x, y = lax.rem(c, 2), lax.rem(c // 2, 2), c // 4
    sib = c + 1 - 2 * core
    over_x, over_y = c + 2 - 4 * x, c + 4 - 8 * y
    first = over_x * (1 - core) + over_y * core
    second = over_y * (1 - core) + over_x * core
    diag = over_x + over_y - c
    return c, z, sib, first, second, diag


def greet(c, z, n_ctx, n_wsh):
    barrier = pltpu.get_barrier_semaphore()
    for k in range(1, n_ctx):
        pl.semaphore_signal(
            barrier, inc=1, device_id=(lax.rem(c + k, n_ctx), z), device_id_type=MESH
        )
    for k in range(1, n_wsh):
        pl.semaphore_signal(
            barrier, inc=1, device_id=(c, lax.rem(z + k, n_wsh)), device_id_type=MESH
        )


def met(n_ctx, n_wsh):
    pl.semaphore_wait(pltpu.get_barrier_semaphore(), n_ctx + n_wsh - 2)


def send(src, dst, send_sem, recv_sem, c, z):
    copy = pltpu.make_async_remote_copy(
        src_ref=src, dst_ref=dst, send_sem=send_sem, recv_sem=recv_sem,
        device_id=(c, z), device_id_type=MESH,
    )
    copy.start()
    return copy


def arrive(dst, send_sem, recv_sem, c, z):
    pltpu.make_async_remote_copy(
        src_ref=dst, dst_ref=dst, send_sem=send_sem, recv_sem=recv_sem,
        device_id=(c, z), device_id_type=MESH,
    ).wait_recv()


def left(src, send_sem, recv_sem, c, z):
    pltpu.make_async_remote_copy(
        src_ref=src, dst_ref=src, send_sem=send_sem, recv_sem=recv_sem,
        device_id=(c, z), device_id_type=MESH,
    ).wait_send()


class Line:
    def __init__(self, at, c, z, n, send_sem, recv_sem):
        self.at, self.c, self.z, self.n = at, c, z, n
        self.send_sem, self.recv_sem = send_sem, recv_sem

    def start(self, own):
        c, z = self.c, self.z

        @pl.when(z < self.n - 1)
        def _():
            send(own, self.at(z), self.send_sem.at[0], self.recv_sem.at[z], c, z + 1)

        @pl.when(z > 0)
        def _():
            send(own, self.at(z), self.send_sem.at[1], self.recv_sem.at[z], c, z - 1)

    def forward(self, distance, then=None):
        c, z, n = self.c, self.z, self.n
        below, above = z - distance, z + distance

        @pl.when(below >= 0)
        def _():
            arrive(self.at(below), self.send_sem.at[0], self.recv_sem.at[below], c, z)

            @pl.when(z < n - 1)
            def _():
                send(self.at(below), self.at(below), self.send_sem.at[2 * distance], self.recv_sem.at[below], c, z + 1)

            if then is not None:
                then(below)

        @pl.when(above < n)
        def _():
            arrive(self.at(above), self.send_sem.at[0], self.recv_sem.at[above], c, z)

            @pl.when(z > 0)
            def _():
                send(self.at(above), self.at(above), self.send_sem.at[2 * distance + 1], self.recv_sem.at[above], c, z - 1)

            if then is not None:
                then(above)

    def finish(self, own):
        c, z, n = self.c, self.z, self.n

        @pl.when(z < n - 1)
        def _():
            left(own, self.send_sem.at[0], self.recv_sem.at[z], c, z)

        @pl.when(z > 0)
        def _():
            left(own, self.send_sem.at[1], self.recv_sem.at[z], c, z)

        for distance in range(1, n):
            below, above = z - distance, z + distance

            @pl.when((below >= 0) & (z < n - 1))
            def _():
                left(self.at(below), self.send_sem.at[2 * distance], self.recv_sem.at[below], c, z)

            @pl.when((above < n) & (z > 0))
            def _():
                left(self.at(above), self.send_sem.at[2 * distance + 1], self.recv_sem.at[above], c, z)


class Plane:
    def __init__(self, at, c, z, around, send_sem, recv_sem):
        self.at, self.c, self.z = at, c, z
        self.sib, self.first, self.second, self.diag = around
        self.send_sem, self.recv_sem = send_sem, recv_sem

    def push(self, slot, block, target, src=None):
        src = self.at(block) if src is None else src
        send(src, self.at(block), self.send_sem.at[slot], self.recv_sem.at[block], target, self.z)

    def wait(self, block):
        arrive(self.at(block), self.send_sem.at[0], self.recv_sem.at[block], self.c, self.z)

    def start(self, own=None):
        self.push(0, self.c, self.first, own)
        self.push(1, self.c, self.second, own)
        self.push(2, self.c, self.sib, own)

    def from_first(self):
        self.wait(self.first)
        self.push(3, self.first, self.second)
        self.push(4, self.first, self.sib)

    def from_second(self):
        self.wait(self.second)
        self.push(5, self.second, self.sib)

    def from_diag(self):
        self.wait(self.diag)
        self.push(6, self.diag, self.sib)

    def others(self):
        shift = self.sib - self.c
        return (self.sib, self.second + shift, self.first + shift, self.diag + shift)

    def finish(self):
        for slot in range(7):
            left(self.at(self.c), self.send_sem.at[slot], self.recv_sem.at[self.c], self.c, self.z)


def block_ids_of(block, order_ref, lengths_ref, rows):
    n_blk = lengths_ref.shape[1]
    position = order_ref[block] * rows + lax.broadcasted_iota(jnp.int32, (8, rows), 1)
    ids = jnp.zeros((8, rows), jnp.int32)
    bound = jnp.int32(0)
    for b in range(n_blk):
        bound = bound + lengths_ref[0, b]
        ids = ids + jnp.where(position >= bound, 1, 0)
    return ids, lax.broadcasted_iota(jnp.int32, (8, rows), 0)


def three_rows(value, rows):
    f32 = jnp.float32
    high = value.astype(jnp.bfloat16).astype(f32)
    rest = value - high
    mid = rest.astype(jnp.bfloat16).astype(f32)
    low = rest - mid
    row = lax.broadcasted_iota(jnp.int32, (8, rows), 0)
    return jnp.where(row == 0, high, 0.0) + jnp.where(row == 1, mid, 0.0) + jnp.where(row == 2, low, 0.0)


def add_rows(target, at, other, other_at, rows, step):
    f32 = jnp.float32

    def some_rows(i, _):
        here = pl.ds(pl.multiple_of(at + i * step, 16), step)
        there = pl.ds(pl.multiple_of(other_at + i * step, 16), step)
        target[here, :] = (target[here, :].astype(f32) + other[there, :].astype(f32)).astype(target.dtype)
        return 0

    lax.fori_loop(0, rows // step, some_rows, 0)


def windows(width, n):
    part = width // n
    tiles = -(-part // 128) + (0 if part % 128 == 0 else 0)
    size = tiles * 128
    return [min(s * part // 128 * 128, width - size) for s in range(n)], size


def whole_kernel(
    dims,
    tok_ref, cot_ref, wq_ref, wk_ref, wv_ref, wout_ref, wup_ref, wdown_ref, pack_ref, order_ref, lengths_ref,
    out_out, gtok_out, dw3_out, dwqkv_out, vec_out,
    h1_all, w_full, big, w_c, w_own, packs, gains, kaug, vaug, kt, qaug, qraw, o_all, ob_stage, ob_land, go_stage, go_land,
    acc, land_f, land_s, land_near, land_far, deep_near, deep_far, deep_f, deep_s, win_out, win_near, win_far,
    dx, dh, tok, cot, gtok, vec, vec_plane, vec_line, vec_mid, vec_sum, row, row_plane, row_line, row_mid, scale_acc,
    tok_send, tok_recv, wz_send, wz_recv, pk_send, pk_recv, ob_send, ob_recv,
    w3z_send, w3z_recv, w3p_send, w3p_recv,
    go_send, go_recv, p_send, p_recv, f_send, f_recv, s_send, s_recv, zn_send, zn_recv, zf_send, zf_recv, g_send, g_recv,
    hp_send, hp_recv, hf_send, hf_recv, hs_send, hs_recv, wn_send, wn_recv, wf_send, wf_recv, wg_send, wg_recv,
    vp_send, vp_recv, vl_send, vl_recv, rp_send, rp_recv, rl_send, rl_recv, sl_send, sl_recv, sx_send, sx_recv, local_sem, load_sem, cols_sem,
):
    n_ctx, n_wsh, hd, heads = dims
    f32, bf16 = jnp.float32, jnp.bfloat16
    c, z, sib, first, second, diag = place()
    around = (sib, first, second, diag)
    core, x, y = lax.rem(c, 2), lax.rem(c // 2, 2), c // 4
    f_bit, s_bit = x * (1 - core) + y * core, y * (1 - core) + x * core
    rows, width = tok_ref.shape
    span, length = hd * heads, rows * n_ctx
    shard, half = width // n_wsh, width // 2
    two, cut = shard // 2, shard // (n_ctx // 2)
    w3_refs = (wout_ref, wup_ref, wdown_ref)
    OUT, UP, DOWN = 0, 1, 2
    own_tok = pltpu.make_async_copy(tok_ref, tok, local_sem.at[0])
    columns_in = [
        pltpu.make_async_copy(ref.at[:, pl.ds(side * half, half)], acc.at[i, side], cols_sem.at[i, side])
        for i, ref in enumerate((wq_ref, wk_ref, wv_ref))
        for side in range(2)
    ]
    own_pack = pltpu.make_async_copy(pack_ref, packs.at[z], local_sem.at[2])
    own_cot = pltpu.make_async_copy(cot_ref, cot, local_sem.at[3])
    own_full = [
        pltpu.make_async_copy(
            w3_refs[w], w_full.at[w, pl.ds(pl.multiple_of(z * shard, 16), shard)], load_sem.at[heads + w]
        )
        for w in range(3)
    ]
    for copy in (*columns_in, own_tok, own_pack, own_cot, *own_full):
        copy.start()
    greet(c, z, n_ctx, n_wsh)
    for copy in columns_in:
        copy.wait()
    for k in range(n_ctx):

        @pl.when(c == k)
        def _():
            for h in range(heads):
                side, at = divmod(k * span + h * hd, half)
                for i in range(3):
                    w_own[:, (3 * h + i) * hd : (3 * h + i + 1) * hd] = acc[i, side, :, at : at + hd]

    w_own[:, 3 * span :] = jnp.zeros((shard, w_own.shape[1] - 3 * span), bf16)
    own_w = pltpu.make_async_copy(w_own, w_c.at[pl.ds(pl.multiple_of(z * shard, 16), shard)], local_sem.at[1])
    own_w.start()
    met(n_ctx, n_wsh)

    part_rows = rows // 2
    tokens = [
        Plane(
            lambda b, i=i: big.at[pl.ds(pl.multiple_of(b * rows + i * part_rows, 16), part_rows)], c, z, around,
            tok_send.at[i], tok_recv.at[i],
        )
        for i in range(2)
    ]
    for i in range(2):
        tokens[i].start(tok_ref.at[pl.ds(i * part_rows, part_rows)])
    wline = Line(lambda s: w_c.at[pl.ds(pl.multiple_of(s * shard, 16), shard)], c, z, n_wsh, wz_send, wz_recv)
    for k in range(1, n_wsh):
        send(pack_ref, packs.at[z], pk_send.at[k], pk_recv.at[z], c, lax.rem(z + k, n_wsh))
    wline.start(w_own)
    scale_acc[...] = jnp.zeros_like(scale_acc)

    def columns(b):
        return pl.ds(pl.multiple_of(lax.rem(b, 2) * half, 128), half)

    straight = shard * 3 // 5
    cuts = (cut, cut, (shard - straight) // (n_ctx // 2))

    def piece(w, s, b):
        top = pl.multiple_of(s * shard + (b // 2) * cuts[w], 16)
        return w_full.at[w, pl.ds(top, cuts[w]), columns(b)]

    def straight_rows(s, of_core):
        top = s * shard + shard - straight + of_core * (straight // 2)
        return w_full.at[DOWN, pl.ds(pl.multiple_of(top, 16), straight // 2)]

    my_straight = wdown_ref.at[pl.ds(pl.multiple_of(shard - straight + core * (straight // 2), 16), straight // 2)]
    straight_line = Line(lambda s: straight_rows(s, core), c, z, n_wsh, sl_send, sl_recv)

    def to_other_core(s):
        k = lax.rem(s - z + n_wsh, n_wsh)
        send(straight_rows(s, core), straight_rows(s, core), sx_send.at[k], sx_recv.at[k], sib, z)

    def go_straight(w, distance):
        straight_line.forward(distance, to_other_core)


    my_piece = [
        ref.at[pl.ds(pl.multiple_of((c // 2) * cuts[w], 16), cuts[w]), columns(c)] for w, ref in enumerate(w3_refs)
    ]
    lines = [
        Line(lambda s, w=w: piece(w, s, c), c, z, n_wsh, w3z_send.at[w], w3z_recv.at[w]) for w in range(3)
    ]

    def plane_of(w, s):
        k = lax.rem(s - z + n_wsh, n_wsh)
        return Plane(lambda b: piece(w, s, b), c, z, around, w3p_send.at[w, k], w3p_recv.at[w, k])

    def shards_at(w, distance, step):
        below, above = z - distance, z + distance

        @pl.when(below >= 0)
        def _():
            step(plane_of(w, below))

        @pl.when(above < n_wsh)
        def _():
            step(plane_of(w, above))

    def spread(w, distance):
        lines[w].forward(distance, lambda s: plane_of(w, s).start())

    def step_of(step):
        return lambda w, distance: shards_at(w, distance, step)

    by_first, by_second, by_diag = step_of(Plane.from_first), step_of(Plane.from_second), step_of(Plane.from_diag)

    def all_others(plane):
        for b in plane.others():
            plane.wait(b)

    own_tok.wait()
    own_pack.wait()
    for k in range(1, n_wsh):
        other = lax.rem(z + k, n_wsh)
        arrive(packs.at[other], pk_send.at[0], pk_recv.at[other], c, z)
    row8 = lax.broadcasted_iota(jnp.int32, (8, width), 0)
    total = jnp.zeros((8, width), f32)
    for s in range(n_wsh):
        wide = jnp.concatenate([packs[s], jnp.zeros((8, width - packs.shape[2]), f32)], axis=1)
        by_shard = pltpu.roll(wide, s * shard, 1) if s else wide
        by_dim = pltpu.roll(wide, s * (hd // n_wsh), 1) if s else wide
        total = total + jnp.where(row8 < 2, by_shard, by_dim)
    gains[...] = total

    def gain_column():
        scale = jnp.concatenate([gains[2:3, 0:128], jnp.zeros((7, 128), f32)], axis=0)
        soft = jnp.maximum(scale, 0.0) + jnp.log(1.0 + jnp.exp(-jnp.abs(scale)))
        return (LOG_BASE / math.sqrt(hd) * soft).T[0:hd, 0:1]

    def attention_forward(vt, qneg, s_buf):
        def norm_block(b, source, top):
            gain = gains[0:1, :]

            def some_rows(i, _):
                t = source[pl.ds(pl.multiple_of(top + i * 32, 32), 32), :].astype(f32)
                inverse = lax.rsqrt(jnp.mean(t * t, -1, keepdims=True) + EPS)
                h1_all[b, pl.ds(pl.multiple_of(i * 32, 32), 32), :] = (t * inverse * gain).astype(bf16)
                return 0

            lax.fori_loop(0, rows // 32, some_rows, 0)

        def norm_arrived(b):
            norm_block(b, big, b * rows)

        def arrived(b):
            for i in range(2):
                tokens[i].wait(b)
            norm_arrived(b)

        others = tokens[0].others()
        lines[OUT].start(my_piece[OUT])
        norm_block(c, tok, 0)
        arrived(others[0])
        tokens[0].from_first()
        wline.forward(1)
        lines[UP].start(my_piece[UP])
        tokens[1].from_first()
        norm_arrived(first)
        tokens[0].from_second()
        tokens[1].from_second()
        norm_arrived(second)
        spread(OUT, 1)
        wline.forward(2)
        lines[DOWN].start(my_piece[DOWN])
        arrived(others[1])
        arrived(others[2])
        tokens[0].from_diag()
        tokens[1].from_diag()
        norm_arrived(diag)
        arrived(others[3])
        spread(OUT, 2)
        wline.forward(3)
        own_w.wait()
        straight_line.start(my_straight)
        spread(UP, 1)
        gain_col = gain_column()

        def project(b, _):
            raw = jnp.dot(h1_all[b], w_c[...], preferred_element_type=f32).T
            at = pl.ds(pl.multiple_of(b * rows, 128), rows)
            ids, row = block_ids_of(b, order_ref, lengths_ref, rows)
            hot = jnp.where(ids == row, 1.0, 0.0)
            neg = jnp.where(row > ids, NEG, 0.0)
            ones = jnp.ones((8, rows), f32)
            qneg[b] = neg
            for h in range(heads):
                top = 3 * h * hd
                q = raw[top : top + hd]
                qraw[b, h * hd : (h + 1) * hd, :] = q
                q = q * gain_col
                qaug[b, h, 0:hd, :] = q.astype(bf16)
                qaug[b, h, hd : hd + 16, :] = jnp.concatenate([neg, jnp.zeros((8, rows), f32)], axis=0).astype(bf16)
                qaug[b, h, hd + 16 : 128, :] = jnp.zeros((112 - hd, rows), bf16)
                k = raw[top + hd : top + 2 * hd].astype(bf16)
                v = raw[top + 2 * hd : top + 3 * hd].astype(bf16)
                tail = jnp.zeros((112 - hd, rows), f32)
                kt[h, :, at] = k
                vt[h, 0:hd, at] = v
                vt[h, hd : hd + 16, at] = jnp.ones((16, rows), bf16)
                kaug[h, at, :] = jnp.concatenate([k.astype(f32), hot, ones, tail], axis=0).T.astype(bf16)
                vaug[h, at, :] = jnp.concatenate([v.astype(f32), ones, ones, tail], axis=0).T.astype(bf16)
            return 0

        lax.fori_loop(0, n_ctx, project, 0)
        for i in range(2):
            tokens[i].finish()
        keys = length // 2
        plan = (
            (0, spread, OUT, 3), (0, by_first, OUT, 1), (1, by_first, OUT, 2), (1, spread, UP, 2),
            (2, by_second, OUT, 1), (2, by_second, OUT, 2), (3, spread, DOWN, 1), (3, go_straight, DOWN, 1), (3, by_first, OUT, 3),
            (4, by_diag, OUT, 1), (4, spread, UP, 3), (5, by_second, OUT, 3), (5, by_first, UP, 1),
            (6, spread, DOWN, 2), (6, go_straight, DOWN, 2), (6, by_diag, OUT, 2), (7, by_first, UP, 2), (8, by_diag, OUT, 3),
            (8, by_second, UP, 1), (9, by_second, UP, 2), (9, spread, DOWN, 3), (9, go_straight, DOWN, 3), (10, by_first, UP, 3),
            (11, by_diag, UP, 1), (11, by_first, DOWN, 1), (12, by_second, UP, 3), (12, by_diag, UP, 2),
            (13, by_first, DOWN, 2), (14, by_second, DOWN, 1), (14, by_diag, UP, 3), (15, by_second, DOWN, 2),
        )

        def attend(i, _):
            g = lax.rem(c + 1 + i, n_ctx)
            for h in range(heads):
                q = qaug[g, h]
                top = jnp.full((1, rows), -jnp.inf, f32)
                for j in range(2):
                    s = jnp.dot(kaug[h, j * keys : (j + 1) * keys, :], q, preferred_element_type=f32)
                    s_buf[j * keys : (j + 1) * keys, :] = s
                    top = jnp.maximum(top, jnp.max(s, axis=0, keepdims=True))
                out = jnp.zeros((hd + 16, rows), f32)
                for j in range(2):
                    p = jnp.exp(s_buf[j * keys : (j + 1) * keys, :] - top).astype(bf16)
                    out = out + jnp.dot(vt[h, :, j * keys : (j + 1) * keys], p, preferred_element_type=f32)
                total = out[hd : hd + 1]
                o = out[0:hd] / total
                lse = top + jnp.log(total)
                o_all[g, h * hd : (h + 1) * hd, :] = o
                ob_stage[g, h * hd : (h + 1) * hd, :] = o.astype(bf16)
                qaug[g, h, hd : hd + 16, :] = jnp.concatenate([qneg[g], three_rows(-lse, rows)], axis=0).astype(bf16)
                for slot, event, w, distance in plan:
                    if slot % heads == h:
                        pl.when(i == slot // heads)(functools.partial(event, w, distance))

            @pl.when(i < n_ctx - 1)
            def _():
                send(ob_stage.at[g], my_heads(ob_land), ob_send.at[g], ob_recv.at[c], g, z)

            return 0

        lax.fori_loop(0, n_ctx, attend, 0)

    def my_heads(ref):
        return ref.at[pl.ds(pl.multiple_of(c * span, 16), span)]

    def heads_of(ref, g):
        return ref.at[pl.ds(pl.multiple_of(g * span, 16), span)]

    vm = pltpu.VMEM
    pl.run_scoped(
        attention_forward,
        vm((heads, hd + 16, length), bf16), vm((n_ctx, 8, rows), f32), vm((length, rows), f32),
    )
    own_o = pltpu.make_async_copy(ob_stage.at[c], my_heads(ob_land), local_sem.at[4])
    own_o.start()

    mine = pl.ds(pl.multiple_of(core * half, 128), half)
    theirs = pl.ds(pl.multiple_of((1 - core) * half, 128), half)
    my_top = f_bit * two + s_bit * cut
    near, far = z + 1 - 2 * lax.rem(z, 2), z + 2 - 4 * (z // 2)

    def pair_at(w):
        return big.at[pl.ds(2 * w * shard, 2 * shard)]

    def add_pair(w):
        arrive(pair_at(w), p_send.at[w], p_recv.at[w], c, z)
        for s in range(n_wsh):
            other = big.at[:, pl.ds(s % 2 * half, half)]
            add_rows(acc.at[w, s], 0, other, (2 * w + s // 2) * shard, shard, 64)

    def pair_sum(w):
        add_pair(w)
        at = pl.ds(pl.multiple_of((1 - f_bit) * two, 16), two)
        send(acc.at[w, :, at], land_f.at[w], f_send.at[w], f_recv.at[w], first, z)

    def deep_pair_sum(w):
        add_pair(w)
        for j in range(2):
            s = 2 * j + lax.rem(near, 2)
            send(acc.at[w, s], deep_near.at[j], zn_send.at[w, j], zn_recv.at[w, j], c, near)

    def deep_near_sum(w):
        for j in range(2):
            arrive(deep_near.at[j], zn_send.at[w, j], zn_recv.at[w, j], c, z)
            add_rows(acc.at[w, 2 * j + lax.rem(z, 2)], 0, deep_near.at[j], 0, shard, 80)
        send(acc.at[w, far], deep_far, zf_send.at[w], zf_recv.at[w], c, far)

    def deep_far_sum(w):
        arrive(deep_far, zf_send.at[w], zf_recv.at[w], c, z)
        add_rows(acc.at[w, z], 0, deep_far, 0, shard, 80)
        at = pl.ds(pl.multiple_of((1 - f_bit) * two, 16), two)
        send(acc.at[w, z, at], deep_f, f_send.at[w], f_recv.at[w], first, z)

    def deep_first_sum(w):
        arrive(deep_f, f_send.at[w], f_recv.at[w], c, z)
        add_rows(acc.at[w, z], f_bit * two, deep_f, 0, two, 80)
        at = pl.ds(pl.multiple_of(f_bit * two + (1 - s_bit) * cut, 16), cut)
        send(acc.at[w, z, at], deep_s, s_send.at[w], s_recv.at[w], second, z)

    def deep_second_sum(w):
        arrive(deep_s, s_send.at[w], s_recv.at[w], c, z)
        add_rows(acc.at[w, z], my_top, deep_s, 0, cut, 80)
        planes[w].start(final_piece(w))
        pltpu.make_async_copy(final_piece(w), out_piece(w, c), local_sem.at[8 + w]).start()

    def first_sum(w):
        arrive(land_f.at[w], f_send.at[w], f_recv.at[w], c, z)
        for s in range(n_wsh):
            add_rows(acc.at[w, s], f_bit * two, land_f.at[w, s], 0, two, 80)
        at = pl.ds(pl.multiple_of(f_bit * two + (1 - s_bit) * cut, 16), cut)
        send(acc.at[w, :, at], land_s.at[w], s_send.at[w], s_recv.at[w], second, z)

    def second_sum(w):
        arrive(land_s.at[w], s_send.at[w], s_recv.at[w], c, z)
        for s in range(n_wsh):
            add_rows(acc.at[w, s], my_top, land_s.at[w, s], 0, cut, 80)
        at = pl.ds(pl.multiple_of(my_top, 16), cut)
        for j in range(2):
            s = 2 * j + lax.rem(near, 2)
            send(acc.at[w, s, at], land_near.at[w, j], zn_send.at[w, j], zn_recv.at[w, j], c, near)

    def near_sum(w):
        for j in range(2):
            arrive(land_near.at[w, j], zn_send.at[w, j], zn_recv.at[w, j], c, z)
            add_rows(acc.at[w, 2 * j + lax.rem(z, 2)], my_top, land_near.at[w, j], 0, cut, 80)
        at = pl.ds(pl.multiple_of(my_top, 16), cut)
        send(acc.at[w, far, at], land_far.at[w], zf_send.at[w], zf_recv.at[w], c, far)

    def out_piece(w, b):
        b_core, b_x, b_y = lax.rem(b, 2), lax.rem(b // 2, 2), b // 4
        r = (1 - b_core) * (2 * b_x + b_y) + b_core * (2 * b_y + b_x)
        return dw3_out.at[w, pl.ds(pl.multiple_of(r * cut, 16), cut), columns(b)]

    planes = [
        Plane(lambda b, w=w: out_piece(w, b), c, z, around, g_send.at[w], g_recv.at[w]) for w in range(3)
    ]

    def final_piece(w):
        return acc.at[w, z, pl.ds(pl.multiple_of(my_top, 16), cut)]

    def far_sum(w):
        arrive(land_far.at[w], zf_send.at[w], zf_recv.at[w], c, z)
        add_rows(acc.at[w, z], my_top, land_far.at[w], 0, cut, 80)
        planes[w].start(final_piece(w))
        pltpu.make_async_copy(final_piece(w), out_piece(w, c), local_sem.at[8 + w]).start()

    def feed_forward(x1, h2, a, gu, ob, turned, ga, inv2, outb, stage):
        def tiles(step, size=256):
            for top in range(0, width, size):
                step(slice(top, top + size))

        def turn(source, target):
            def one(at):
                target[at, :] = source[:, at].T

            tiles(one, 128)

        def weight_gradient(w, left_t, right):
            for s in range(n_wsh):
                stage[w, s // 2 * shard : (s // 2 + 1) * shard, s % 2 * half : (s % 2 + 1) * half] = jnp.dot(
                    left_t[s * shard : (s + 1) * shard, :], right[:, theirs], preferred_element_type=f32
                ).astype(bf16)
            send(stage.at[w], pair_at(w), p_send.at[w], p_recv.at[w], sib, z)
            for s in range(n_wsh):
                at = slice(s * shard, (s + 1) * shard)
                acc[w, s] = jnp.dot(left_t[at, :], right[:, mine], preferred_element_type=f32).astype(bf16)

        by_first(DOWN, 3)
        for distance in range(1, n_wsh):
            shards_at(OUT, distance, all_others)
        own_o.wait()
        for k in range(1, n_ctx):
            g = lax.rem(c + k, n_ctx)
            arrive(heads_of(ob_land, g), ob_send.at[0], ob_recv.at[g], c, z)

        def turn_ob(at):
            ob[:, at] = ob_land[at, :].T

        tiles(turn_ob, 128)
        by_diag(DOWN, 1)
        by_second(DOWN, 3)
        own_full[OUT].wait()

        def mix(at):
            x1[:, at] = tok[:, at].astype(f32) + jnp.dot(ob[...], w_full[OUT, :, at], preferred_element_type=f32)

        tiles(mix)
        by_diag(DOWN, 2)

        def norm_rows(i, _):
            at = pl.ds(pl.multiple_of(i * 32, 32), 32)
            t = x1[at, :]
            inverse = lax.rsqrt(jnp.mean(t * t, -1, keepdims=True) + EPS)
            inv2[at, :] = jnp.broadcast_to(inverse, (32, 128))
            h2[at, :] = (t * inverse * gains[1:2, :]).astype(bf16)
            return 0

        lax.fori_loop(0, rows // 32, norm_rows, 0)
        by_diag(DOWN, 3)
        for distance in range(1, n_wsh):
            shards_at(UP, distance, all_others)
        own_full[UP].wait()

        def lift(at):
            dh[:, at] = jnp.dot(h2[...], w_full[UP, :, at], preferred_element_type=f32)

        tiles(lift)
        own_cot.wait()
        for distance in range(1, n_wsh):
            shards_at(DOWN, distance, all_others)
        for k in range(1, n_wsh):
            s = lax.rem(z + k, n_wsh)
            arrive(straight_rows(s, 1 - core), sx_send.at[0], sx_recv.at[k], c, z)
        own_full[DOWN].wait()

        def hidden(at):
            up = dh[:, at]
            da = lax.dot_general(
                cot[...], w_full[DOWN, at, :], (((1,), (1,)), ((), ())), preferred_element_type=f32
            )
            sig = 1.0 / (1.0 + jnp.exp(-up))
            act = up * sig
            a[:, at] = act.astype(bf16)
            turned[at, :] = act.T.astype(bf16)
            gu[:, at] = (da * sig * (1.0 + up * (1.0 - sig))).astype(bf16)

        tiles(hidden)

        def back(at):
            dh[:, at] = lax.dot_general(
                gu[...], w_full[UP, at, :], (((1,), (1,)), ((), ())), preferred_element_type=f32
            )

        tiles(back)

        def norm_back_rows(i, total):
            at = pl.ds(pl.multiple_of(i * 16, 16), 16)
            inverse = inv2[at, 0:1]
            normed = x1[at, :] * inverse
            grad = dh[at, :]
            both = grad * normed
            slope = jnp.mean(both * gains[1:2, :], -1, keepdims=True)
            result = cot[at, :].astype(f32) + inverse * (grad * gains[1:2, :] - normed * slope)
            dx[at, :] = result
            ga[at, :] = result.astype(bf16)
            return total + both

        gain_sum = lax.fori_loop(0, rows // 16, norm_back_rows, jnp.zeros((16, width), f32))
        vec[:, 0:width] = jnp.sum(gain_sum, axis=0, keepdims=True)

        def back_out(at):
            go_stage[at, :] = lax.dot_general(
                w_full[OUT, at, :], ga[...], (((1,), (1,)), ((), ())), preferred_element_type=f32
            ).astype(bf16)

        tiles(back_out)
        straight_line.finish(my_straight)
        for k in range(1, n_wsh):
            left(my_straight, sx_send.at[k], sx_recv.at[k], c, z)
        for w in range(3):
            lines[w].finish(my_piece[w])
            for distance in range(1, n_wsh):
                shards_at(w, distance, Plane.finish)
        for k in range(1, n_ctx):
            g = lax.rem(c + k, n_ctx)
            send(heads_of(go_stage, g), go_land.at[c], go_send.at[k], go_recv.at[c], g, z)
        pltpu.make_async_copy(my_heads(go_stage), go_land.at[c], local_sem.at[5]).start()
        weight_gradient(DOWN, turned, cot)
        turn(h2, turned)
        weight_gradient(UP, turned, gu)
        deep_pair_sum(DOWN)
        weight_gradient(OUT, ob_land, ga)
        pair_sum(UP)

        def finish(at):
            outb[:, at] = (
                x1[:, at] + jnp.dot(a[...], w_full[DOWN, :, at], preferred_element_type=f32)
            ).astype(bf16)

        tiles(finish)
        own_out = pltpu.make_async_copy(outb, out_out, local_sem.at[6])
        own_out.start()
        pair_sum(OUT)
        own_out.wait()
        for w in range(3):
            left(stage.at[w], p_send.at[w], p_recv.at[w], c, z)

    wide = (rows, width)
    pl.run_scoped(
        feed_forward,
        vm(wide, f32), vm(wide, bf16), vm(wide, bf16), vm(wide, bf16), vm(wide, bf16),
        vm((width, rows), bf16), vm(wide, bf16), vm((rows, 128), f32), vm(wide, bf16),
        vm((3, 2 * shard, width), bf16),
    )

    def attention_backward(goaug, go_tm, q_tm, dk, dv, dqkv):
        per = width // rows

        def block(i):
            return w_full.at[i // per, :, pl.ds(pl.multiple_of(lax.rem(i, per) * rows, 128), rows)]

        def part_p(i):
            return block(i)

        def part_f(i):
            return block(n_ctx // 2 + i)

        part_s = block(jnp.int32(n_ctx // 2 + 2))

        def part(b):
            return block(n_ctx // 2 + 3 + b)

        dk[...] = jnp.zeros_like(dk)
        dv[...] = jnp.zeros_like(dv)
        dqkv[3 * span :, :] = jnp.zeros((dqkv.shape[0] - 3 * span, length), bf16)
        gain_col = gain_column()

        def prepare(g):
            at = pl.ds(pl.multiple_of(g * rows, 16), rows)
            for h in range(heads):
                go = go_land[g, h * hd : (h + 1) * hd, :]
                wide = go.astype(f32)
                delta = jnp.sum(wide * o_all[g, h * hd : (h + 1) * hd, :], axis=0, keepdims=True)
                tail = jnp.concatenate([three_rows(-delta, rows), jnp.zeros((120 - hd, rows), f32)], axis=0)
                goaug[g, h, 0:hd, :] = go
                goaug[g, h, hd:128, :] = tail.astype(bf16)
                go_tm[h, at, :] = jnp.concatenate([wide, jnp.zeros((128 - hd, rows), f32)], axis=0).T.astype(bf16)
                q = qaug[g, h, 0:hd, :].astype(f32)
                q_tm[h, at, :] = jnp.concatenate([q, jnp.zeros((128 - hd, rows), f32)], axis=0).T.astype(bf16)

        pltpu.make_async_copy(my_heads(go_stage), go_land.at[c], local_sem.at[5]).wait()
        prepare(c)

        def prepare_other(k, _):
            g = lax.rem(c + k, n_ctx)
            arrive(go_land.at[g], go_send.at[0], go_recv.at[g], c, z)
            prepare(g)
            return 0

        lax.fori_loop(1, n_ctx, prepare_other, 0)
        three = 3 * hd
        starts, size = windows(width, n_wsh)

        def head_gradients(h, events):
            def attend(g, _):
                at = pl.ds(pl.multiple_of(g * rows, 16), rows)
                p = jnp.exp(jnp.dot(kaug[h], qaug[g, h], preferred_element_type=f32))
                ds = (p * jnp.dot(vaug[h], goaug[g, h], preferred_element_type=f32)).astype(bf16)
                dq = jnp.dot(kt[h], ds, preferred_element_type=f32)
                dk[h] += jnp.dot(ds, q_tm[h, at, :], preferred_element_type=f32)
                dv[h] += jnp.dot(p.astype(bf16), go_tm[h, at, :], preferred_element_type=f32)
                scale_acc[...] += dq * qraw[g, h * hd : (h + 1) * hd, :]
                lanes = pl.ds(pl.multiple_of(g * rows, 128), rows)
                dqkv[h * three : h * three + hd, lanes] = (dq * gain_col).astype(bf16)
                for step, event in events:
                    pl.when(g == step)(event)
                return 0

            lax.fori_loop(0, n_ctx, attend, 0)

            def settle(g, _):
                at = pl.ds(pl.multiple_of(g * rows, 16), rows)
                lanes = pl.ds(pl.multiple_of(g * rows, 128), rows)
                for i, source in enumerate((dk, dv)):
                    turned = source[h, at, :].T
                    top = h * three + (i + 1) * hd
                    dqkv[top : top + hd, lanes] = turned[0:hd].astype(bf16)
                return 0

            lax.fori_loop(0, n_ctx, settle, 0)

        def head_windows(h):
            for s in range(n_wsh):
                total = jnp.zeros((three, size), f32)
                for b in range(n_ctx):
                    total = total + jnp.dot(
                        dqkv[h * three : (h + 1) * three, b * rows : (b + 1) * rows],
                        h1_all[b, :, starts[s] : starts[s] + size], preferred_element_type=f32,
                    )
                win_out[h, s] = total.astype(bf16)
            for j in range(2):
                s = 2 * j + lax.rem(near, 2)
                send(win_out.at[h, s], win_near.at[h, j], wn_send.at[h, j], wn_recv.at[h, j], c, near)

        def near_window(h):
            for j in range(2):
                arrive(win_near.at[h, j], wn_send.at[h, j], wn_recv.at[h, j], c, z)
                add_rows(win_out.at[h, 2 * j + lax.rem(z, 2)], 0, win_near.at[h, j], 0, three, 80)
            send(win_out.at[h, far], win_far.at[h], wf_send.at[h], wf_recv.at[h], c, far)

        plane_w = [
            Plane(lambda b, h=h: dwqkv_out.at[b, h], c, z, around, wg_send.at[h], wg_recv.at[h]) for h in range(heads)
        ]

        def own_window(h):
            return pltpu.make_async_copy(win_out.at[h, z], dwqkv_out.at[c, h], load_sem.at[h])

        def far_window(h):
            arrive(win_far.at[h], wf_send.at[h], wf_recv.at[h], c, z)
            add_rows(win_out.at[h, z], 0, win_far.at[h], 0, three, 80)
            plane_w[h].start(win_out.at[h, z])
            own_window(h).start()

        head_gradients(0, ((6, lambda: first_sum(UP)),))
        head_windows(0)
        head_gradients(1, (
            (1, lambda: second_sum(UP)), (4, lambda: deep_near_sum(DOWN)), (5, lambda: first_sum(OUT)),
            (6, lambda: near_sum(UP)), (6, lambda: near_window(0)), (7, lambda: second_sum(OUT)),
        ))

        def partial(b):
            lanes = pl.ds(pl.multiple_of(b * rows, 128), rows)
            part(b)[...] = jnp.dot(w_c[...], dqkv[:, lanes], preferred_element_type=f32).astype(bf16)

        def to_sib(b):
            partial(b)
            send(part(b), part_p(b // 2), hp_send.at[b // 2], hp_recv.at[b // 2], sib, z)

        def scale_row():
            scale_sum = jnp.sum(scale_acc[...], axis=1, keepdims=True)
            return jnp.concatenate(
                [jnp.broadcast_to(scale_sum, (hd, 128)), jnp.zeros((128 - hd, 128), f32)], axis=0
            ).T[0:1, :]

        def pair(i, b):
            arrive(part_p(b // 2), hp_send.at[0], hp_recv.at[b // 2], c, z)
            add_rows(part(b), 0, part_p(b // 2), 0, width, 128)
            if i < 2:
                slot = s_bit if i == 0 else 1 - s_bit
                send(part(b), part_f(slot), hf_send.at[i], hf_recv.at[slot], first, z)

        shift = sib - c
        to_sib(diag + shift)
        to_sib(second + shift)
        partial(diag)
        to_sib(first + shift)
        pair(1, diag)
        partial(first)
        to_sib(sib)
        pair(0, first)
        partial(second)
        partial(c)
        head_windows(1)
        deep_far_sum(DOWN)
        far_sum(UP)
        near_sum(OUT)
        vec[:, width:] = scale_row()
        for k in range(1, n_ctx):
            g = lax.rem(c + k, n_ctx)
            send(vec, vec_plane.at[c], vp_send.at[k], vp_recv.at[c], g, z)
        far_window(0)
        pair(2, second)
        pair(3, c)
        deep_first_sum(DOWN)
        near_window(1)
        planes[UP].from_first()
        far_sum(OUT)
        planes[UP].from_second()
        arrive(part_f(1 - s_bit), hf_send.at[0], hf_recv.at[1 - s_bit], c, z)
        add_rows(part(second), 0, part_f(1 - s_bit), 0, width, 128)
        send(part(second), part_s, hs_send.at[0], hs_recv.at[0], second, z)
        deep_second_sum(DOWN)
        arrive(part_f(s_bit), hf_send.at[0], hf_recv.at[s_bit], c, z)
        add_rows(part(c), 0, part_f(s_bit), 0, width, 128)
        far_window(1)
        plane_w[0].from_first()
        plane_w[0].from_second()
        planes[UP].from_diag()
        total = vec[...]
        for k in range(1, n_ctx):
            g = lax.rem(c + k, n_ctx)
            arrive(vec_plane.at[g], vp_send.at[0], vp_recv.at[g], c, z)
            total = total + vec_plane[g]
        vec_mid[...] = total
        for k in range(1, n_wsh):
            send(vec_mid, vec_line.at[z], vl_send.at[k], vl_recv.at[z], c, lax.rem(z + k, n_wsh))
        planes[OUT].from_first()
        planes[OUT].from_second()
        planes[DOWN].from_first()
        planes[DOWN].from_second()
        arrive(part_s, hs_send.at[0], hs_recv.at[0], c, z)

        mine_part = part(c)

        def turn_dh(i, _):
            at = pl.ds(pl.multiple_of(i * 128, 128), 128)
            dh[:, at] = (mine_part[at, :].astype(f32) + part_s[at, :].astype(f32)).T
            return 0

        lax.fori_loop(0, width // 128, turn_dh, 0)

        def last_rows(i, total):
            at = pl.ds(pl.multiple_of(i * 16, 16), 16)
            t = tok[at, :].astype(f32)
            inverse = lax.rsqrt(jnp.mean(t * t, -1, keepdims=True) + EPS)
            normed = t * inverse
            grad = dh[at, :]
            both = grad * normed
            slope = jnp.mean(both * gains[0:1, :], -1, keepdims=True)
            gtok[at, :] = (dx[at, :] + inverse * (grad * gains[0:1, :] - normed * slope)).astype(bf16)
            return total + both

        gain_sum = lax.fori_loop(0, rows // 16, last_rows, jnp.zeros((16, width), f32))
        row[...] = jnp.sum(gain_sum, axis=0, keepdims=True)
        for k in range(1, n_ctx):
            g = lax.rem(c + k, n_ctx)
            send(row, row_plane.at[c], rp_send.at[k], rp_recv.at[c], g, z)
        own_gtok = pltpu.make_async_copy(gtok, gtok_out, local_sem.at[11])
        own_gtok.start()
        plane_w[0].from_diag()
        planes[OUT].from_diag()
        planes[DOWN].from_diag()
        plane_w[1].from_first()
        plane_w[1].from_second()
        total = row[...]
        for k in range(1, n_ctx):
            g = lax.rem(c + k, n_ctx)
            arrive(row_plane.at[g], rp_send.at[0], rp_recv.at[g], c, z)
            total = total + row_plane[g]
        row_mid[...] = total
        for k in range(1, n_wsh):
            send(row_mid, row_line.at[z], rl_send.at[k], rl_recv.at[z], c, lax.rem(z + k, n_wsh))
        plane_w[1].from_diag()
        whole = vec_mid[...]
        for k in range(1, n_wsh):
            s = lax.rem(z + k, n_wsh)
            arrive(vec_line.at[s], vl_send.at[0], vl_recv.at[s], c, z)
            whole = whole + vec_line[s]
        vec_sum[...] = jnp.zeros_like(vec_sum)
        vec_sum[1:2, :] = whole[:, 0:width]
        vec_sum[2:3, 0:128] = whole[:, width:]
        for k in range(1, n_wsh):
            s = lax.rem(z + k, n_wsh)
            arrive(row_line.at[s], rl_send.at[0], rl_recv.at[s], c, z)
            total = total + row_line[s]
        vec_sum[0:1, :] = total
        own_vec = pltpu.make_async_copy(vec_sum, vec_out, local_sem.at[12])
        own_vec.start()
        for plane in planes + plane_w:
            all_others(plane)
            plane.finish()
        for i in range(n_ctx // 2):
            left(part(c), hp_send.at[i], hp_recv.at[i], c, z)
        for i in range(2):
            left(part(c), hf_send.at[i], hf_recv.at[i], c, z)
        left(part(c), hs_send.at[0], hs_recv.at[0], c, z)
        for copy in (own_gtok, own_vec, *[own_window(h) for h in range(heads)]):
            copy.wait()

    pl.run_scoped(
        attention_backward,
        vm((n_ctx, heads, 128, rows), bf16), vm((heads, length, 128), bf16), vm((heads, length, 128), bf16),
        vm((heads, length, 128), f32), vm((heads, length, 128), f32), vm((w_c.shape[1], length), bf16),
    )

    wline.finish(w_own)
    for k in range(1, n_wsh):
        left(pack_ref, pk_send.at[k], pk_recv.at[z], c, z)
        left(vec, vl_send.at[k], vl_recv.at[0], c, z)
        left(row, rl_send.at[k], rl_recv.at[0], c, z)
    for k in range(1, n_ctx):
        g = lax.rem(c + k, n_ctx)
        left(ob_stage.at[g], ob_send.at[g], ob_recv.at[g], c, z)
        left(go_land.at[0], go_send.at[k], go_recv.at[0], c, z)
        left(vec, vp_send.at[k], vp_recv.at[0], c, z)
        left(row, rp_send.at[k], rp_recv.at[0], c, z)
    for w in range(3):
        pltpu.make_async_copy(final_piece(w), out_piece(w, c), local_sem.at[8 + w]).wait()
        left(deep_f if w == DOWN else land_f.at[w], f_send.at[w], f_recv.at[w], c, z)
        left(deep_s if w == DOWN else land_s.at[w], s_send.at[w], s_recv.at[w], c, z)
        for j in range(2):
            left(deep_near.at[j] if w == DOWN else land_near.at[w, j], zn_send.at[w, j], zn_recv.at[w, j], c, z)
        left(deep_far if w == DOWN else land_far.at[w], zf_send.at[w], zf_recv.at[w], c, z)
    for h in range(heads):
        for j in range(2):
            left(win_near.at[h, j], wn_send.at[h, j], wn_recv.at[h, j], c, z)
        left(win_far.at[h], wf_send.at[h], wf_recv.at[h], c, z)


def whole_call(dims, tok, cot, w6, pack, order, lengths):
    n_ctx, n_wsh, hd, heads = dims
    rows, width = tok.shape
    span, length, shard = hd * heads, rows * n_ctx, width // n_wsh
    half, cut = width // 2, shard // (n_ctx // 2)
    f32, bf16 = jnp.float32, jnp.bfloat16
    hbm = pl.BlockSpec(memory_space=pl.ANY)
    smem = pl.BlockSpec(memory_space=pltpu.SMEM)
    shape = jax.ShapeDtypeStruct
    dma = pltpu.SemaphoreType.DMA
    vm = pltpu.VMEM
    size = windows(width, n_wsh)[1]
    lanes = -(-3 * span // 128) * 128
    wide = (rows, width)
    outs = (
        shape(wide, bf16), shape(wide, bf16),
        shape((3, shard, width), bf16), shape((n_ctx, heads, 3 * hd, size), bf16), shape((8, width), f32),
    )
    scratch = [
        vm((n_ctx, rows, width), bf16), vm((3, width, width), bf16), vm((length, width), bf16),
        vm((width, lanes), bf16), vm((shard, lanes), bf16), vm((n_wsh,) + pack.shape, f32), vm((8, width), f32),
        vm((heads, length, 128), bf16), vm((heads, length, 128), bf16), vm((heads, hd, length), bf16),
        vm((n_ctx, heads, 128, rows), bf16), vm((n_ctx, span, rows), f32), vm((n_ctx, span, rows), f32),
        vm((n_ctx, span, rows), bf16), vm((width, rows), bf16), vm((width, rows), bf16), vm((n_ctx, span, rows), bf16),
        vm((3, n_wsh, shard, half), bf16), vm((2, n_wsh, 2 * cut, half), bf16), vm((2, n_wsh, cut, half), bf16),
        vm((2, 2, cut, half), bf16), vm((2, cut, half), bf16),
        vm((2, shard, half), bf16), vm((shard, half), bf16), vm((2 * cut, half), bf16), vm((cut, half), bf16),
        vm((heads, n_wsh, 3 * hd, size), bf16), vm((heads, 2, 3 * hd, size), bf16), vm((heads, 3 * hd, size), bf16),
        vm(wide, f32), vm(wide, f32), vm(wide, bf16), vm(wide, bf16), vm(wide, bf16),
        vm((1, width + 128), f32), vm((n_ctx, 1, width + 128), f32), vm((n_wsh, 1, width + 128), f32),
        vm((1, width + 128), f32), vm((8, width), f32), vm((1, width), f32), vm((n_ctx, 1, width), f32), vm((n_wsh, 1, width), f32),
        vm((1, width), f32), vm((hd, rows), f32),
        dma((2, 7)), dma((2, n_ctx)), dma((2 * n_wsh,)), dma((n_wsh,)), dma((n_wsh,)), dma((n_wsh,)),
        dma((n_ctx,)), dma((n_ctx,)), dma((3, 2 * n_wsh)), dma((3, n_wsh)),
        dma((3, n_wsh, 7)), dma((3, n_wsh, n_ctx)),
        dma((n_ctx,)), dma((n_ctx,)), dma((3,)), dma((3,)), dma((3,)), dma((3,)), dma((3,)), dma((3,)),
        dma((3, 2)), dma((3, 2)), dma((3,)), dma((3,)), dma((3, 7)), dma((3, n_ctx)),
        dma((n_ctx // 2,)), dma((n_ctx // 2,)), dma((2,)), dma((2,)), dma((1,)), dma((1,)),
        dma((heads, 2)), dma((heads, 2)), dma((heads,)), dma((heads,)), dma((heads, 7)), dma((heads, n_ctx)),
        dma((n_ctx,)), dma((n_ctx,)), dma((n_wsh,)), dma((n_wsh,)),
        dma((n_ctx,)), dma((n_ctx,)), dma((n_wsh,)), dma((n_wsh,)), dma((2 * n_wsh,)), dma((n_wsh,)), dma((n_wsh,)), dma((n_wsh,)),
        dma((13,)), dma((heads + 3,)), dma((3, 2)),
    ]
    return pl.pallas_call(
        functools.partial(whole_kernel, dims),
        out_shape=outs,
        in_specs=[hbm] * 9 + [smem] * 2,
        out_specs=[hbm] * len(outs),
        scratch_shapes=scratch,
        compiler_params=pltpu.CompilerParams(
            collective_id=0, has_side_effects=True, vmem_limit_bytes=VMEM_BYTES
        ),
    )(tok, cot, *w6, pack, order, lengths)


def finish_kernel(dims, dwqkv_ref, dw3_ref, *refs):
    tok_refs, outs, tok_outs = refs[:2], refs[2:8], refs[8:10]
    pieces, plain, wide, turned, results, tok_buf, in_sem, out_sem = refs[10:]
    n_ctx, n_wsh, hd, heads = dims
    z = lax.axis_index("wsh")
    f32 = jnp.float32
    shard, width = outs[0].shape
    starts, size = windows(width, n_wsh)
    offset = jnp.int32(0)
    for s in range(n_wsh):
        offset = jnp.where(z == s, s * shard - starts[s], offset)
    ins = [pltpu.make_async_copy(dw3_ref.at[w], plain.at[w], in_sem.at[w]) for w in range(3)]
    for i in range(3):
        at = pl.ds(i * hd, hd)
        ins.append(pltpu.make_async_copy(dwqkv_ref.at[:, :, at], pieces.at[i], in_sem.at[3 + i]))
    tok_ins = [pltpu.make_async_copy(tok_refs[i], tok_buf.at[i], in_sem.at[6 + i]) for i in range(2)]
    for copy in ins + tok_ins:
        copy.start()
    done = []

    def store(i, result):
        copy = pltpu.make_async_copy(result, outs[i], out_sem.at[i])
        copy.start()
        done.append(copy)

    for w in range(3):
        ins[w].wait()
        results[w] = plain[w].astype(f32)
        store(3 + w, results.at[w])
    for i in range(3):
        ins[3 + i].wait()

        def lay(b, _):
            for h in range(heads):
                at = pl.ds(pl.multiple_of((b * heads + h) * hd, 16), hd)
                wide[at, :] = pieces[i, b, h].astype(f32)
            return 0

        lax.fori_loop(0, n_ctx, lay, 0)

        def turn(j, _):
            at = pl.ds(pl.multiple_of(j * 128, 128), 128)
            turned[i, :, at] = wide[at, :].T
            return 0

        lax.fori_loop(0, width // 128, turn, 0)
        store(i, turned.at[i, pl.ds(pl.multiple_of(offset, 8), shard)])
    for i in range(2):
        tok_ins[i].wait()
        copy = pltpu.make_async_copy(tok_buf.at[i], tok_outs[i], out_sem.at[6 + i])
        copy.start()
        done.append(copy)
    for copy in done:
        copy.wait()


def finish_call(dims, dwqkv, dw3, outputs, gtok):
    n_ctx, n_wsh, hd, heads = dims
    shard, width = dw3.shape[1:]
    size = dwqkv.shape[3]
    f32, bf16 = jnp.float32, jnp.bfloat16
    hbm = pl.BlockSpec(memory_space=pl.ANY)
    dma = pltpu.SemaphoreType.DMA
    return pl.pallas_call(
        functools.partial(finish_kernel, dims),
        out_shape=(jax.ShapeDtypeStruct((shard, width), f32),) * 6 + (jax.ShapeDtypeStruct(gtok.shape, bf16),) * 2,
        in_specs=[hbm] * 4,
        out_specs=[hbm] * 8,
        scratch_shapes=[
            pltpu.VMEM((3, n_ctx, heads, hd, size), bf16), pltpu.VMEM((3, shard, width), bf16),
            pltpu.VMEM((width, size), f32), pltpu.VMEM((3, size, width), f32), pltpu.VMEM((3, shard, width), f32),
            pltpu.VMEM((2,) + gtok.shape, bf16), dma((8,)), dma((8,)),
        ],
        compiler_params=pltpu.CompilerParams(vmem_limit_bytes=VMEM_BYTES),
    )(dwqkv, dw3, outputs, gtok)


def head_split(
    tokens, cotangent, block_lengths, group_order, w_query, w_key, w_value, w_out, w_up, w_down,
    gain_attn, gain_mlp, query_scale,
):
    f32 = jnp.float32
    n_ctx, n_wsh = lax.axis_size("ctx"), lax.axis_size("wsh")
    z = lax.axis_index("wsh")
    width = tokens.shape[2]
    hd, heads = width // H, H // n_ctx
    shard = width // n_wsh
    dims = (n_ctx, n_wsh, hd, heads)
    lanes = -(-shard // 128) * 128
    pack = sum(
        jnp.pad(v.astype(f32)[None], ((i, 7 - i), (0, lanes - v.shape[0])))
        for i, v in enumerate((gain_attn, gain_mlp, query_scale))
    )
    outputs, gtok, dw3, dwqkv, sums = whole_call(
        dims, tokens[0], cotangent[0], (w_query, w_key, w_value, w_out, w_up, w_down), pack, group_order, block_lengths
    )[:5]
    *weight_grads, outputs, gtok = finish_call(dims, dwqkv, dw3, outputs, gtok)
    own = [lax.dynamic_slice_in_dim(sums[i], z * shard, shard, 0) for i in (0, 1)]
    scale_grad = (
        lax.dynamic_slice_in_dim(sums[2], z * (hd // n_wsh), hd // n_wsh, 0)
        * (LOG_BASE / math.sqrt(hd))
        * jax.nn.sigmoid(query_scale.astype(f32))
    )
    return (
        outputs.reshape(tokens.shape), gtok.reshape(tokens.shape), *weight_grads, own[0], own[1], scale_grad,
    )


def solution(mesh):
    in_specs = (
        P("wsh", "ctx", None),
        P("wsh", "ctx", None),
        P("wsh", None),
        P(),
        P("wsh", None),
        P("wsh", None),
        P("wsh", None),
        P("wsh", None),
        P("wsh", None),
        P("wsh", None),
        P("wsh"),
        P("wsh"),
        P("wsh"),
    )
    out_specs = (
        P("wsh", "ctx", None),
        P("wsh", "ctx", None),
        P("wsh", None),
        P("wsh", None),
        P("wsh", None),
        P("wsh", None),
        P("wsh", None),
        P("wsh", None),
        P("wsh"),
        P("wsh"),
        P("wsh"),
    )
    n_ctx, n_wsh = mesh.shape["ctx"], mesh.shape["wsh"]
    plan = head_split if (n_ctx, n_wsh) == (8, 4) else per_device
    return jax.shard_map(
        plan, mesh=mesh, in_specs=in_specs, out_specs=out_specs, check_vma=False
    )
```
